32 devices in a mesh: blk: 8 (over y, x, core), expert: 4 (over z).
Axes of the slice: x: 2, y: 2, z: 4, core: 2. Of those that a mesh axis runs over, the one named last changes fastest.
Arguments:
- queries: bfloat16 [16, 72, 1024], P('expert', None, 'blk'), may hold values from -6 to 6
- keys: bfloat16 [16, 72, 1024], P('expert', None, 'blk'), may hold values from -6 to 6
- values: bfloat16 [16, 72, 1024], P('expert', None, 'blk'), may hold values from -24 to 24
- image_ids: int32 [256], P('blk'), may hold values from 0 to 2, as said below
- placement: int32 [256, 1], P('blk'), may hold values from 0 to 7; in each aligned block of 32 rows (0 to 31, 32 to 63, ...) at most 16 rows name the same one
- merge_gain: float32 [16, 288], P('expert'), may hold values from 0.1 to 1.9
- merge_weight: bfloat16 [16, 288, 2048], P('expert'), may hold values from -0.09375 to 0.09375
- text: bfloat16 [1024, 2048], P('blk'), may hold values from -6 to 6
- norm_gain: float32 [2048], replicated, may hold values from 0.1 to 1.9
- w_gate: bfloat16 [8, 3072, 2048], P('blk', 'expert'), may hold values from -0.125 to 0.125
- w_up: bfloat16 [8, 3072, 2048], P('blk', 'expert'), may hold values from -0.125 to 0.125
- w_down: bfloat16 [8, 3072, 2048], P('blk', 'expert'), may hold values from -0.15625 to 0.15625
- routes: int32 [1024, 8], P('blk'), may hold values from 0 to 127, all different within a row; in each aligned block of 128 rows (0 to 127, 128 to 255, ...) at most 10 rows name the same one
- route_gates: float32 [1024, 8], P('blk'), may hold values from 0.2 to 1
- cotangent: bfloat16 [1024, 2048], P('blk'), may hold values from -6 to 6
Outputs:
- llm_out: bfloat16 [1024, 2048], P('blk')
- attn_grad: float32 [16, 72, 1024], P('expert', None, 'blk')
The draws below stay inside these ranges and needn't reach their ends.
Inputs may be any that keep to these rules, and one draw needn't show every extreme that they name: `image_ids`: three images in order: ids never fall along the sequence; image 0 holds from 16 to 31 merged rows and image 2 from 17 to 32. `placement`: among the 32 rows of one encoder index no shard is named more than 16 times. `routes`: each token names 8 different experts; among the 128 tokens of one shard no expert is named more than 10 times.
All inputs are finite; a program needn't handle non-finite values.
Results may differ from the reference program's by a relative error of at most 0.03.
Values may be sent and summed in bfloat16 or wider, within the bound.
No kernel may reach another device: no remote copies, remote signals or barrier semaphores. Data moves between devices by JAX's collectives and lax.ppermute only.
A program may use at most 64 MiB of HBM per device.

```python
import math
import jax
import jax.numpy as jnp
import numpy as np
from jax import lax

HEADS = 16
HD = 72
DW = 2048
FF = 1536
EXPERTS = 128
TOPK = 8
LTOK_DEV = 128
SEQ = 1024
MROWS_DEV = 32
MSEQ = 256
LTOK = 1024
CAPV = 16
CAPX = 10
EXP_WIN = 16
N_BLK = 8
N_EXPERT = 4


def draw_queries(key, part):
    key = jax.random.fold_in(key, 1)
    return jnp.clip(jax.random.normal(key, (HEADS, HD, SEQ)), -4.0, 4.0).astype(jnp.bfloat16)


def draw_keys(key, part):
    key = jax.random.fold_in(key, 2)
    return jnp.clip(jax.random.normal(key, (HEADS, HD, SEQ)), -4.0, 4.0).astype(jnp.bfloat16)


def draw_values(key, part):
    key = jax.random.fold_in(key, 3)
    head_rise = jnp.arange(HEADS, dtype=jnp.float32)[:, None, None] / max(HEADS - 1, 1)
    base_draw = jnp.clip(jax.random.normal(key, (HEADS, HD, SEQ)), -4.0, 4.0)
    return (base_draw * 2.0 * 3.0 ** head_rise).astype(jnp.bfloat16)


def draw_image_ids(key, part):
    key = jax.random.fold_in(key, 4)
    first_end = jax.random.randint(jax.random.fold_in(key, 1), (), MSEQ // 16, MSEQ // 8)
    second = jax.random.randint(jax.random.fold_in(key, 2), (), MSEQ - MSEQ // 8, MSEQ - MSEQ // 16)
    row_index = jnp.arange(MSEQ, dtype=jnp.int32)
    return (row_index >= first_end).astype(jnp.int32) + (row_index >= second).astype(jnp.int32)


def shard_levels(key, shape, cuts, smallest, high):
    level = 1.0
    for dim, blocks in cuts:
        steps = jax.random.uniform(jax.random.fold_in(jax.random.fold_in(key, 6), dim), (blocks,), jnp.float32, smallest / len(cuts), high / len(cuts))
        level = level * jnp.repeat(jnp.exp(steps), shape[dim] // blocks).reshape((-1,) + (1,) * (len(shape) - 1 - dim))
    return level


def routed_block(stream_key, own, number, rows, number_of, top, bound, lean):
    ranking = jax.random.permutation(stream_key, number_of)
    crowded, usual = shares(number_of, rows * top, bound, lean, True), shares(number_of, rows * top, bound, lean, False)
    places = jnp.arange(number_of)

    def named(lengths, rotation):
        used = int((lengths > 0).sum())
        fixed = max(1, used // 4)
        shifted = fixed + (places - fixed + rotation * (used - fixed)) % max(1, number_of - fixed)
        return jnp.zeros((number_of,), jnp.int32).at[ranking[jnp.where(places < fixed, places, shifted)]].set(jnp.asarray(lengths, jnp.int32))

    lengths = jnp.where(number % 4 == 0, named(crowded, number // 4), named(usual, number - number // 4 - 1))
    mixed = jax.random.permutation(jax.random.fold_in(own, 3), number_of)
    donor, sink = mixed[0:number_of // 2 * 2:2], mixed[1:number_of // 2 * 2:2]
    room = jnp.minimum(lengths[donor] - 1, bound - lengths[sink]) // 2
    room = jnp.where((donor == ranking[0]) | (sink == ranking[0]) | (lengths[sink] == 0), 0, jnp.maximum(room, 0))
    shifted = jax.random.randint(jax.random.fold_in(own, 4), (number_of // 2,), 0, 1 << 20) % (room + 1)
    lengths = lengths.at[donor].add(-shifted).at[sink].add(shifted)
    items = jnp.searchsorted(jnp.cumsum(lengths), jnp.arange(rows * top), side="right").astype(jnp.int32)
    listing = items.reshape(top, rows).T
    listing = listing[jax.random.permutation(jax.random.fold_in(own, 1), rows)]
    rotation = jax.random.randint(jax.random.fold_in(own, 2), (rows, 1), 0, top)
    return jnp.take_along_axis(listing, (jnp.arange(top)[None, :] + rotation) % top, axis=1)


def shares(number_of, total, most, slope, full):
    weights = [(1 << 20) // math.isqrt(grade ** slope) + 1 for grade in range(1, number_of + 1)]
    largest = most if full else min(most, max(-(-total // number_of), total * weights[0] // sum(weights)))
    least = 1 if total - largest >= number_of - 1 else 0
    given, spare = [largest] + [least] * (number_of - 1), total - largest - least * (number_of - 1)
    while spare > 0:
        free = [i for i in range(1, number_of) if given[i] < largest] or [i for i in range(1, number_of) if given[i] < most]
        pool, budget = sum([weights[i] for i in free]), spare
        for i in free:
            addition = min(most - given[i], max(1, budget * weights[i] // pool), spare)
            given[i] = given[i] + addition
            spare = spare - addition
    return np.array(given)


def noise(rng, extent, width, most, shards=(), kind=jnp.bfloat16):
    array = jax.random.normal(rng, extent, jnp.float32) * width
    if len(shards) > 0:
        array = shard_levels(rng, extent, shards, -0.22, 0.18) * array
    return jnp.clip(array, min=-most, max=most).astype(kind)


def setup_inputs(seed: int = 0) -> dict:
    key_of = jax.random.split(jax.random.key(seed), 16)
    queries = draw_queries(jax.random.fold_in(key_of[15], 71), 0)
    keys = draw_keys(jax.random.fold_in(key_of[15], 71), 0)
    values = draw_values(jax.random.fold_in(key_of[15], 71), 0)
    image_ids = draw_image_ids(jax.random.fold_in(key_of[15], 71), 0)
    placement_keys = jax.random.split(jax.random.fold_in(key_of[4], 1), MSEQ // MROWS_DEV)
    placement_turns = jax.random.permutation(jax.random.fold_in(key_of[4], 3), MSEQ // MROWS_DEV)
    placement = jax.vmap(lambda own, number: routed_block(jax.random.fold_in(key_of[4], 2), own, number, MROWS_DEV, N_BLK, 1, CAPV, 2))(placement_keys, placement_turns).reshape((MSEQ, 1))
    merge_gain = jnp.clip(1.0 + 0.18 * jax.random.normal(key_of[5], (HEADS, 4 * HD), jnp.float32), 0.1, 1.9)
    merge_weight = noise(key_of[6], (HEADS, 4 * HD, DW), (HEADS * 4 * HD) ** -0.5, 0.09375, ((0, 4),))
    text = noise(key_of[7], (LTOK, DW), 1.0, 6.0, ((0, 8),))
    norm_gain = jnp.clip(1.0 + 0.18 * jax.random.normal(key_of[8], (DW,), jnp.float32), 0.1, 1.9)
    w_gate = noise(key_of[9], (EXP_WIN // 2, 2 * FF, DW), DW ** -0.5, 0.125, ((0, 8), (1, 4)))
    w_up = noise(key_of[10], (EXP_WIN // 2, 2 * FF, DW), DW ** -0.5, 0.125, ((0, 8), (1, 4)))
    w_down = noise(key_of[11], (EXP_WIN // 2, 2 * FF, DW), FF ** -0.5, 0.15625, ((0, 8), (1, 4)))
    routes_keys = jax.random.split(jax.random.fold_in(key_of[12], 1), LTOK // LTOK_DEV)
    routes_turns = jax.random.permutation(jax.random.fold_in(key_of[12], 3), LTOK // LTOK_DEV)
    routes = jax.vmap(lambda own, number: routed_block(jax.random.fold_in(key_of[12], 2), own, number, LTOK_DEV, EXPERTS, TOPK, CAPX, 2))(routes_keys, routes_turns).reshape((LTOK, TOPK))
    route_gates = jnp.clip(jnp.exp(math.log(1.0) - 1.609438 * jax.random.uniform(key_of[13], (LTOK, TOPK), jnp.float32) ** shard_levels(key_of[13], (LTOK, TOPK), ((0, 8),), -0.2, 0.2)), 0.2, 1.0)
    cotangent = noise(key_of[14], (LTOK, DW), 1.0, 6.0, ((0, 8),))
    return dict(queries=queries, keys=keys, values=values, image_ids=image_ids, placement=placement, merge_gain=merge_gain, merge_weight=merge_weight, text=text, norm_gain=norm_gain, w_gate=w_gate, w_up=w_up, w_down=w_down, routes=routes, route_gates=route_gates, cotangent=cotangent)


EPS = 1e-06

def attend(queries, keys, values, image_ids):
    patch_ids = jnp.repeat(image_ids, 4)
    block_rows = min(256, SEQ)
    score_scale = HD ** (-0.5)
    key_table = keys.astype(jnp.float32)
    value_table = values.astype(jnp.float32)

    def one_block(first_row):
        query_part = lax.dynamic_slice_in_dim(queries, first_row, block_rows, 2).astype(jnp.float32)
        query_ids = lax.dynamic_slice_in_dim(patch_ids, first_row, block_rows, 0)
        scores = jnp.einsum('hdq,hdk->hqk', query_part, key_table) * score_scale
        same_image = query_ids[:, None] == patch_ids[None, :]
        scores = jnp.where(same_image[None], scores, -1e+30)
        row_max = lax.optimization_barrier(jnp.max(scores, axis=-1, keepdims=True))
        weights = jnp.exp(scores - row_max)
        row_total = lax.optimization_barrier(jnp.sum(weights, axis=-1))
        rounded = lax.optimization_barrier(weights.astype(jnp.bfloat16))
        mixed_rows = jnp.einsum('hqk,hdk->hdq', rounded.astype(jnp.float32), value_table)
        return mixed_rows / row_total[:, None, :]
    starts = (jnp.arange(SEQ // block_rows) * block_rows).astype(jnp.int32)
    pieces = lax.map(one_block, starts)
    return jnp.transpose(pieces, (1, 2, 0, 3)).reshape(HEADS, HD, SEQ).astype(jnp.bfloat16)

def merge_rows(attn):
    spread = jnp.transpose(attn, (2, 0, 1)).reshape(MSEQ, 4, HEADS, HD)
    return jnp.transpose(spread, (0, 2, 1, 3)).reshape(MSEQ, HEADS * 4 * HD)

def split_rows(merged):
    spread = merged.reshape(MSEQ, HEADS, 4, HD).transpose(0, 2, 1, 3).reshape(SEQ, HEADS, HD)
    return jnp.transpose(spread, (1, 2, 0))

def rms_norm(inputs, norm_gain):
    return inputs * lax.rsqrt(lax.optimization_barrier(jnp.mean(inputs * inputs, axis=-1, keepdims=True)) + EPS) * norm_gain

def by_shards(pairs):
    group_count = N_EXPERT // 2
    shard_width = FF // group_count
    total_parts = None
    for act_part, weight_part in pairs:
        row_count = act_part.shape[0]
        term = jnp.einsum('rjf,jfd->rjd', act_part.reshape(row_count, group_count, shard_width).astype(jnp.float32), weight_part.reshape(group_count, shard_width, DW).astype(jnp.float32))
        total_parts = term if total_parts is None else total_parts + term
    rounded = lax.optimization_barrier(total_parts.astype(jnp.bfloat16))
    return lax.optimization_barrier(jnp.sum(rounded.astype(jnp.float32), axis=1))

def reference(queries, keys, values, image_ids, placement, merge_gain, merge_weight, text, norm_gain, w_gate, w_up, w_down, routes, route_gates, cotangent):
    attn = attend(queries, keys, values, image_ids)
    full_width = HEADS * 4 * HD
    merged = merge_rows(attn).astype(jnp.float32)
    row_mean = lax.optimization_barrier(jnp.sum(merged, axis=1)) / full_width
    mean_square = lax.optimization_barrier(jnp.sum(merged * merged, axis=1)) / full_width
    inv_std = lax.rsqrt(mean_square - row_mean * row_mean + EPS)
    normed = (merged - row_mean[:, None]) * inv_std[:, None]
    gain_flat = merge_gain.reshape(full_width)
    scaled = (normed * gain_flat).astype(jnp.bfloat16)
    weight_flat = merge_weight.reshape(full_width, DW)
    vision = jnp.dot(scaled, weight_flat, preferred_element_type=jnp.float32).astype(jnp.bfloat16)
    dest_shard = placement[:, 0].astype(jnp.int32)
    dest_hits = (dest_shard[:, None] == jnp.arange(N_BLK, dtype=jnp.int32)[None, :]).astype(jnp.int32)
    earlier = jnp.cumsum(dest_hits, axis=0).astype(jnp.int32) - dest_hits
    slot_index = lax.optimization_barrier(jnp.sum(earlier * dest_hits, axis=1)).astype(jnp.int32)
    position = (dest_shard * LTOK_DEV + slot_index).astype(jnp.int32)
    hidden_in = text.at[position].set(vision)
    inputs_f32 = hidden_in.astype(jnp.float32)
    normed_h, norm_pull = jax.vjp(lambda inputs: rms_norm(inputs, norm_gain), inputs_f32)
    h_rows = normed_h.astype(jnp.bfloat16)
    cot_rows = cotangent.astype(jnp.float32)
    pair_expert = routes.reshape(-1)
    pair_gate = route_gates.reshape(-1)
    max_rows = N_BLK * CAPX
    gate_all = w_gate.reshape(EXP_WIN, FF, DW)
    up_all = w_up.reshape(EXP_WIN, FF, DW)
    down_all = w_down.reshape(EXP_WIN, FF, DW)

    def one_expert(state_carry, expert_id):
        expert_sum, hidden_grad = state_carry
        chosen = pair_expert == expert_id
        pair_index = jnp.nonzero(chosen, size=max_rows, fill_value=0)[0].astype(jnp.int32)
        live_mask = (jnp.arange(max_rows) < jnp.sum(chosen.astype(jnp.int32))).astype(jnp.float32)
        token_index = (pair_index // TOPK).astype(jnp.int32)
        pair_weight = pair_gate[pair_index] * live_mask
        expert_rows = h_rows[token_index]
        gate_mat = gate_all[expert_id]
        up_mat = up_all[expert_id]
        down_mat = down_all[expert_id]
        gate_pre = jnp.dot(expert_rows, gate_mat.T, preferred_element_type=jnp.float32)
        up_proj = jnp.dot(expert_rows, up_mat.T, preferred_element_type=jnp.float32)
        activated = (jax.nn.silu(gate_pre) * up_proj).astype(jnp.bfloat16)
        down_part = by_shards(((activated, down_mat),))
        expert_sum = expert_sum.at[token_index].add(down_part * pair_weight[:, None])
        back_rows = (cot_rows[token_index] * pair_weight[:, None]).astype(jnp.bfloat16)
        act_grad = jnp.dot(back_rows, down_mat.T, preferred_element_type=jnp.float32)
        sigmoid_gate = jax.nn.sigmoid(gate_pre)
        gate_grad = (act_grad * up_proj * sigmoid_gate * (1.0 + gate_pre * (1.0 - sigmoid_gate))).astype(jnp.bfloat16)
        up_grad = (act_grad * gate_pre * sigmoid_gate).astype(jnp.bfloat16)
        row_grad = by_shards(((gate_grad, gate_mat), (up_grad, up_mat)))
        hidden_grad = hidden_grad.at[token_index].add(row_grad * live_mask[:, None])
        return ((expert_sum, hidden_grad), None)
    zero_rows = jnp.zeros((LTOK, DW), jnp.float32)
    (expert_sum, hidden_grad), unused_out = lax.scan(one_expert, (zero_rows, zero_rows), jnp.arange(EXP_WIN, dtype=jnp.int32))
    llm_out = (inputs_f32 + expert_sum).astype(jnp.bfloat16)
    input_grad = cot_rows + norm_pull(hidden_grad)[0]
    vision_grad = input_grad[position].astype(jnp.bfloat16)
    scaled_grad = jnp.dot(vision_grad, weight_flat.T, preferred_element_type=jnp.float32)
    normed_grad = scaled_grad * gain_flat
    grad_mean = lax.optimization_barrier(jnp.sum(normed_grad, axis=1)) / full_width
    cross_mean = lax.optimization_barrier(jnp.sum(normed_grad * normed, axis=1)) / full_width
    merged_grad = inv_std[:, None] * (normed_grad - grad_mean[:, None] - normed * cross_mean[:, None])
    return (llm_out, split_rows(merged_grad))
```

```python
import jax
import jax.numpy as jnp
from jax import lax
from jax.sharding import PartitionSpec as P

CAPX = 10


EPS = 1e-06


def block_ranks(hit_table):
    before = jnp.cumsum(hit_table, axis=0) - hit_table
    return jnp.sum(before * hit_table, axis=1)


def swap(value, axis, step):
    count = lax.axis_size(axis)
    return lax.ppermute(value, axis, [(i, i ^ step) for i in range(count)])


def gather_near(value, axis):
    count = lax.axis_size(axis)
    return [value] + [swap(value, axis, step) for step in range(1, count)]


def exchange(blocks, axis):
    count = lax.axis_size(axis)
    parts = [blocks[0]] + [swap(blocks[step], axis, step) for step in range(1, count)]
    return jnp.stack(parts)


def in_order(stacked, axis):
    count = lax.axis_size(axis)
    return stacked[jnp.arange(count, dtype=jnp.int32) ^ lax.axis_index(axis)]


def small_sum(value, axis):
    parts = gather_near(value, axis)
    return sum(parts[1:], parts[0])


def wide_sum(value, axis):
    count = lax.axis_size(axis)
    rows, width = value.shape
    pieces = in_order(value.reshape(count, rows // count, width), axis)
    mine = exchange(pieces, axis).astype(jnp.float32).sum(axis=0).astype(value.dtype)
    whole = jnp.stack(gather_near(mine, axis))
    return in_order(whole, axis).reshape(rows, width)


def body(
    queries,
    keys,
    values,
    image_ids,
    placement,
    merge_gain,
    merge_weight,
    text,
    norm_gain,
    w_gate,
    w_up,
    w_down,
    routes,
    route_gates,
    cotangent,
):
    blocks = lax.axis_size("blk")
    my_index = lax.axis_index("blk")
    expert_size = lax.axis_size("expert")
    expert_index = lax.axis_index("expert")
    heads_here, head_size, patches = queries.shape
    merged_rows = image_ids.shape[0]
    llm_rows, model_width = text.shape
    top_count = routes.shape[1]
    along_width = (((1,), (1,)), ((), ()))
    marks = jnp.stack(gather_near(jnp.stack([image_ids, placement[:, 0]]), "blk"))
    near_ids = jnp.repeat(marks[:, 0].reshape(-1), 4)
    all_dest = in_order(marks[:, 1], "blk").reshape(-1)
    my_ids = near_ids[:patches]
    score_scale = head_size ** (-0.5)
    run_max = jnp.full((heads_here, patches), -1e30, jnp.float32)
    key_part = jnp.concatenate(gather_near(keys, "blk"), axis=2)
    value_part = jnp.concatenate(gather_near(values, "blk"), axis=2)
    scores = (
        jnp.einsum("hdq,hdk->hqk", queries, key_part, preferred_element_type=jnp.float32)
        * score_scale
    )
    scores = jnp.where((my_ids[:, None] == near_ids[None, :])[None], scores, -1e30)
    new_max = jnp.maximum(run_max, jnp.max(scores, axis=-1))
    weights = jnp.exp(scores - new_max[:, :, None])
    run_sum = jnp.sum(weights, axis=-1)
    weighted = jnp.einsum(
        "hqk,hdk->hdq", weights.astype(jnp.bfloat16), value_part, preferred_element_type=jnp.float32
    )
    run_max, run_sum, weighted = (new_max, run_sum, weighted)
    attn = (weighted / run_sum[:, None, :]).astype(jnp.bfloat16)
    spread = jnp.transpose(attn, (2, 0, 1)).reshape(merged_rows, 4, heads_here, head_size)
    merged = (
        jnp.transpose(spread, (0, 2, 1, 3))
        .reshape(merged_rows, heads_here * 4 * head_size)
        .astype(jnp.float32)
    )
    full_width = expert_size * merged.shape[1]
    row_sums, row_squares = small_sum(
        jnp.stack([jnp.sum(merged, axis=1), jnp.sum(merged * merged, axis=1)]), "expert"
    )
    row_mean = row_sums / full_width
    inv_std = lax.rsqrt(row_squares / full_width - row_mean * row_mean + EPS)
    normed = (merged - row_mean[:, None]) * inv_std[:, None]
    gain_flat = merge_gain.reshape(-1)
    scaled = (normed * gain_flat).astype(jnp.bfloat16)
    weight_flat = merge_weight.reshape(-1, merge_weight.shape[2])
    merger_part = jnp.dot(scaled, weight_flat, preferred_element_type=jnp.float32)
    vision = wide_sum(merger_part.astype(jnp.bfloat16), "expert")
    cap_rows = llm_rows // blocks
    long_rows = all_dest.shape[0]
    dest_hits = (all_dest[:, None] == jnp.arange(blocks, dtype=jnp.int32)[None, :]).astype(
        jnp.int32
    )
    slot_index = block_ranks(dest_hits)
    grouped = dest_hits.reshape(blocks, merged_rows, blocks)
    inner_before = jnp.cumsum(grouped, axis=1) - grouped
    block_rank = jnp.sum(inner_before * grouped, axis=2).reshape(long_rows)
    my_dest = lax.dynamic_slice_in_dim(all_dest, my_index * merged_rows, merged_rows, 0)
    local_rank = lax.dynamic_slice_in_dim(block_rank, my_index * merged_rows, merged_rows, 0)
    send_rows = (
        jnp.zeros((blocks, cap_rows, model_width), jnp.bfloat16)
        .at[my_dest ^ my_index, local_rank]
        .set(vision)
    )
    arrived = exchange(send_rows, "blk")
    source_block = jnp.arange(long_rows, dtype=jnp.int32) // merged_rows
    arrival = (source_block ^ my_index) * cap_rows + block_rank
    slot_target = jnp.where(all_dest == my_index, slot_index, llm_rows)
    slot_source = jnp.zeros((llm_rows,), jnp.int32).at[slot_target].set(arrival, mode="drop")
    slot_vision = jnp.zeros((llm_rows,), jnp.bool_).at[slot_target].set(True, mode="drop")
    flat_arrived = arrived.reshape(blocks * cap_rows, model_width)
    hidden_in = jnp.where(slot_vision[:, None], flat_arrived[slot_source], text)
    inputs_f32 = hidden_in.astype(jnp.float32)

    def rms_norm(inputs):
        return (
            inputs * lax.rsqrt(jnp.mean(inputs * inputs, axis=-1, keepdims=True) + EPS) * norm_gain
        )

    normed_h, norm_pull = jax.vjp(rms_norm, inputs_f32)
    h_rows = normed_h.astype(jnp.bfloat16)
    group_count = expert_size // 2
    member = expert_index // group_count
    window = 2 * blocks
    pair_expert = routes.reshape(-1)
    pair_hits = (pair_expert[:, None] == jnp.arange(window, dtype=jnp.int32)[None, :]).astype(
        jnp.int32
    )
    pair_rank = block_ranks(pair_hits)
    pair_live = (pair_expert < window) & (pair_expert % 2 == member)
    slot_count = blocks * CAPX
    pair_slot = jnp.where(pair_live, (pair_expert // 2 ^ my_index) * CAPX + pair_rank, slot_count)
    pair_token = jnp.arange(llm_rows * top_count, dtype=jnp.int32) // top_count
    pair_gate = jnp.where(pair_live, route_gates.reshape(-1), 0.0)
    slot_token = jnp.zeros((slot_count,), jnp.int32).at[pair_slot].set(pair_token, mode="drop")
    slot_gate = jnp.zeros((slot_count,), jnp.float32).at[pair_slot].set(pair_gate, mode="drop")
    slot_live = jnp.zeros((slot_count,), jnp.float32).at[pair_slot].set(1.0, mode="drop")

    def dispatch(slot_rows):
        buffer = jnp.where(slot_live[:, None] > 0.0, slot_rows, jnp.zeros_like(slot_rows))
        landed = exchange(buffer.reshape(blocks, CAPX, model_width), "blk")
        return landed.reshape(slot_count, model_width)

    def combine(landed, slot_weight):
        weighted_rows = (
            landed.reshape(slot_count, model_width).astype(jnp.float32) * slot_weight[:, None]
        )
        return jnp.zeros((llm_rows, model_width), jnp.float32).at[slot_token].add(weighted_rows)

    def to_owner(partial_value, slot_weight):
        returned = exchange(
            partial_value.astype(jnp.bfloat16).reshape(blocks, CAPX, model_width), "blk"
        )
        combined = combine(returned, slot_weight)
        return wide_sum(combined.astype(jnp.bfloat16), "expert").astype(jnp.float32)

    gate_rows = w_gate[0]
    up_rows = w_up[0]
    down_rows = w_down[0]
    expert_rows = dispatch(h_rows[slot_token])
    gate_pre = lax.dot_general(
        expert_rows, gate_rows, along_width, preferred_element_type=jnp.float32
    )
    up_proj = lax.dot_general(expert_rows, up_rows, along_width, preferred_element_type=jnp.float32)
    activated = (jax.nn.silu(gate_pre) * up_proj).astype(jnp.bfloat16)
    down_part = jnp.dot(activated, down_rows, preferred_element_type=jnp.float32)
    expert_sum = to_owner(down_part, slot_gate)
    llm_out = (inputs_f32 + expert_sum).astype(jnp.bfloat16)
    cot_rows = cotangent.astype(jnp.float32)
    back_rows = dispatch((cot_rows[slot_token] * slot_gate[:, None]).astype(jnp.bfloat16))
    act_grad = lax.dot_general(
        back_rows, down_rows, along_width, preferred_element_type=jnp.float32
    )
    sigmoid_gate = jax.nn.sigmoid(gate_pre)
    gate_grad = (
        act_grad * up_proj * sigmoid_gate * (1.0 + gate_pre * (1.0 - sigmoid_gate))
    ).astype(jnp.bfloat16)
    up_grad = (act_grad * gate_pre * sigmoid_gate).astype(jnp.bfloat16)
    row_grad = jnp.dot(gate_grad, gate_rows, preferred_element_type=jnp.float32) + jnp.dot(
        up_grad, up_rows, preferred_element_type=jnp.float32
    )
    hidden_grad = to_owner(row_grad, slot_live)
    input_grad = (cot_rows + norm_pull(hidden_grad)[0]).astype(jnp.bfloat16)
    back_target = jnp.where(slot_vision, slot_source, blocks * cap_rows)
    grad_buffer = (
        jnp.zeros((blocks * cap_rows, model_width), jnp.bfloat16)
        .at[back_target]
        .set(input_grad, mode="drop")
    )
    returned_rows = exchange(grad_buffer.reshape(blocks, cap_rows, model_width), "blk")
    vision_grad = returned_rows[my_dest ^ my_index, local_rank]
    scaled_grad = lax.dot_general(
        vision_grad, weight_flat, along_width, preferred_element_type=jnp.float32
    )
    normed_grad = scaled_grad * gain_flat
    grad_sum, cross_sum = small_sum(
        jnp.stack([jnp.sum(normed_grad, axis=1), jnp.sum(normed_grad * normed, axis=1)]),
        "expert",
    )
    merged_grad = inv_std[:, None] * (
        normed_grad - (grad_sum / full_width)[:, None] - normed * (cross_sum / full_width)[:, None]
    )
    unfolded = (
        merged_grad.reshape(merged_rows, heads_here, 4, head_size)
        .transpose(0, 2, 1, 3)
        .reshape(patches, heads_here, head_size)
    )
    attn_grad = jnp.transpose(unfolded, (1, 2, 0))
    return (llm_out, attn_grad)


def solution(mesh):
    return jax.shard_map(
        body,
        mesh=mesh,
        in_specs=(
            P("expert", None, "blk"),
            P("expert", None, "blk"),
            P("expert", None, "blk"),
            P("blk"),
            P("blk", None),
            P("expert", None),
            P("expert", None, None),
            P("blk", None),
            P(),
            P("blk", "expert", None),
            P("blk", "expert", None),
            P("blk", "expert", None),
            P("blk", None),
            P("blk", None),
            P("blk", None),
        ),
        out_specs=(P("blk", None), P("expert", None, "blk")),
        check_vma=False,
    )
```

```python
import functools

import jax
import jax.numpy as jnp
from jax import lax
from jax.experimental import pallas as pl
from jax.experimental.pallas import tpu as pltpu
from jax.sharding import PartitionSpec as P

CAPX = 10
SLOTS = 16
SEND = 32
EPS = 1e-06
VMEM_BYTES = 40 * 1024 * 1024
F32 = jnp.float32
BF16 = jnp.bfloat16


def iota(shape, dim):
    return lax.broadcasted_iota(jnp.int32, shape, dim)


def dot(a, b):
    return jnp.dot(a.astype(BF16), b.astype(BF16), preferred_element_type=F32)


def dot_nt(a, b):
    return lax.dot_general(a, b, (((1,), (1,)), ((), ())), preferred_element_type=F32)


def dot_tn(a, b):
    return lax.dot_general(a, b, (((0,), (0,)), ((), ())), preferred_element_type=F32)


def three(value):
    first = value.astype(BF16).astype(F32)
    second = (value - first).astype(BF16).astype(F32)
    return first, second, value - first - second


def put_scalars(columns, rows):
    lane = iota((rows, 128), 1)
    out = jnp.zeros((rows, 128), F32)
    place = 0
    for column in columns:
        for piece in three(column):
            out = jnp.where(lane == place, piece, out)
            place += 1
    return out


def get_scalar(block, which):
    lane = iota(block.shape, 1)
    return jnp.sum(jnp.where(lane // 3 == which, block, 0.0), axis=1, keepdims=True)


def plan_kernel(
    ids_ref, meta_ref, routes_ref, gates_ref, text_ref, gain_ref, cot_ref,
    send_ref, slots_ref, placed_ref, comb_ref, *, groups, merged_rows, row_share,
):
    blocks = meta_ref.shape[0]
    tokens = text_ref.shape[0]
    rows = blocks * merged_rows
    me, expert_index = ids_ref[0], ids_ref[1]
    member = expert_index // groups
    meta = meta_ref[...].astype(jnp.int32)
    field = iota(meta.shape, 1)
    mine = 2 * me + member
    hit = jnp.sum(((meta == mine) & (field < 8)).astype(F32), axis=1)
    dest = jnp.sum(jnp.where(field == 9, meta, 0).astype(F32), axis=1)
    before = (iota((tokens, tokens), 0) < iota((tokens, tokens), 1)).astype(BF16)
    rank = dot(hit, before)
    spread = (iota((128, rows), 0) == iota((128, rows), 1) % merged_rows).astype(BF16)
    own_block = iota((blocks, rows), 1) // merged_rows == iota((blocks, rows), 0)
    dest_row = jnp.sum(jnp.where(own_block, dot(dest, spread), 0.0), axis=0, keepdims=True)
    dest_row = dest_row.astype(jnp.int32)
    dest_hit = (iota((blocks, rows), 0) == dest_row).astype(F32)
    rows_before = (iota((rows, rows), 0) < iota((rows, rows), 1)).astype(BF16)
    slot = jnp.sum(dest_hit * dot(dest_hit, rows_before), axis=0, keepdims=True).astype(jnp.int32)
    at_token = (iota((tokens, rows), 0) == slot).astype(F32)
    row_hit = jnp.sum(dest_hit * dot(hit, at_token), axis=0, keepdims=True)
    row_rank = jnp.sum(dest_hit * dot(rank, at_token), axis=0, keepdims=True).astype(jnp.int32)
    slot_id = dest_row * SLOTS + row_rank
    slot_count = slots_ref.shape[0]
    chosen = (iota((slot_count, rows), 0) == slot_id) & (row_hit > 0.5)
    slots_ref[...] = chosen.astype(F32).astype(BF16)
    placed = jnp.where(dest_row == me, at_token, 0.0).astype(BF16)
    placed_ref[...] = placed

    pair_of = 2 * iota((blocks, tokens), 0) + member
    out_hit = jnp.zeros((blocks, tokens), F32)
    out_gate = jnp.zeros((blocks, tokens), F32)
    for k in range(routes_ref.shape[0]):
        same = pair_of == routes_ref[k : k + 1, :]
        out_hit = out_hit + same.astype(F32)
        out_gate = out_gate + jnp.where(same, gates_ref[k : k + 1, :], 0.0)
    out_rank = dot(out_hit, before)

    def expand(stride):
        count = blocks * stride
        pick = (iota((count, blocks), 0) // stride == iota((count, blocks), 1)).astype(BF16)
        gate = sum(dot(pick, piece) for piece in three(out_gate))
        return dot(pick, out_hit), dot(pick, out_rank).astype(jnp.int32), gate

    hits, ranks, gates = expand(SLOTS)
    live = jnp.where(ranks == iota(hits.shape, 0) % SLOTS, hits, 0.0)
    weight = live * gates
    high = weight.astype(BF16)
    comb_ref[0] = high
    comb_ref[1] = (weight - high.astype(F32)).astype(BF16)

    hits, ranks, gates = expand(SEND)
    place = iota(hits.shape, 0) % SEND
    input_pick = jnp.where((place < CAPX) & (ranks == place), hits, 0.0)
    back_pick = jnp.where((place >= CAPX) & (place < 2 * CAPX) & (ranks == place - CAPX), hits, 0.0)
    back_gate = jnp.sum(back_pick * gates, axis=1, keepdims=True)
    send_rows = blocks * SEND
    source = iota((send_rows, rows), 0)
    kept = source % SEND - 2 * CAPX
    wanted = source // SEND * merged_rows + expert_index * row_share + kept
    row_pick = (kept >= 0) & (kept < row_share) & (iota((send_rows, rows), 1) == wanted)
    cot_pick = dot_nt(row_pick.astype(F32).astype(BF16), placed)
    cot_row = iota((send_rows, 1), 0) % SEND >= 2 * CAPX
    factor = jnp.where(cot_row, 1.0, back_gate)
    text = text_ref[...].astype(F32)
    scale = lax.rsqrt(jnp.mean(text * text, axis=1, keepdims=True) + EPS)
    h_rows = (text * scale * gain_ref[...]).astype(BF16)
    send = dot(input_pick, h_rows) + factor * dot(back_pick + cot_pick, cot_ref[...])
    send_ref[...] = send.astype(BF16)


def attend_kernel(
    query_ref, near_ref, id_ref, gain_ref, weight_ref, message_ref, merged_ref, *, share, row_share
):
    heads, size, patches = query_ref.shape
    blocks = near_ref.shape[0]
    rows = merged_ref.shape[0]
    features = merged_ref.shape[1]
    width = weight_ref.shape[1]
    depth = heads * size
    near = [near_ref[j].astype(F32) for j in range(blocks)]
    key_ids = jnp.concatenate([part[2 * depth + 8 : 2 * depth + 9] for part in near], axis=1)
    same = id_ref[...] == key_ids
    spread = jnp.zeros((patches, features), F32)
    place_row, place_col = iota((size, features), 0), iota((size, features), 1)
    for head in range(heads):
        first = head * size
        keys = jnp.concatenate([part[first : first + size] for part in near], axis=1)
        first = depth + head * size
        values = jnp.concatenate([part[first : first + size] for part in near], axis=1)
        query = query_ref[head].astype(F32).T.astype(BF16)
        scores = dot(query, keys) * (size**-0.5)
        scores = jnp.where(same, scores, -1e30)
        weights = jnp.exp(scores - jnp.max(scores, axis=1, keepdims=True))
        total = jnp.sum(weights, axis=1, keepdims=True)
        attn = dot_nt(weights.astype(BF16), values.astype(BF16)) / total
        place = (place_col % size == place_row) & (place_col // (4 * size) == head)
        spread = spread + dot(attn, place.astype(F32))
    spot = iota((patches, features), 1) // size % 4 == iota((patches, features), 0) % 4
    fold = (iota((rows, patches), 1) // 4 == iota((rows, patches), 0)).astype(F32)
    merged = dot(fold, jnp.where(spot, spread, 0.0))
    merged_ref[...] = merged.astype(BF16)
    local_mean = jnp.sum(merged, axis=1, keepdims=True) / features
    centered = merged - local_mean
    squares = jnp.sum(centered * centered, axis=1, keepdims=True)
    gain = gain_ref[...]
    gain_high = gain.astype(BF16).astype(F32)
    extra = iota((8, features), 0)
    gain_rows = jnp.where(extra == 0, gain_high, jnp.where(extra == 1, gain - gain_high, 0.0))
    left = jnp.concatenate([centered * gain, gain_rows], axis=0)
    product = dot(left, weight_ref[...])
    gain_sum = product[rows : rows + 1] + product[rows + 1 : rows + 2]
    piece = width // row_share
    pieces = [gain_sum[:, j * piece : (j + 1) * piece] for j in range(row_share)]
    message_ref[:, :width] = product[:rows].astype(BF16)
    message_ref[:, width : width + piece] = jnp.concatenate(pieces * share, axis=0).astype(BF16)
    message_ref[:, width + piece :] = put_scalars([local_mean, squares], rows).astype(BF16)


def merge_kernel(message_ref, out_ref, *, width, features):
    share, row_share, _ = message_ref.shape
    piece = width // row_share
    parts = [message_ref[j].astype(F32) for j in range(share)]
    scalars = [part[:, width + piece :] for part in parts]
    means = [get_scalar(block, 0) for block in scalars]
    squares = [get_scalar(block, 1) for block in scalars]
    mean = sum(means) / share
    spread = sum(q + features * (m - mean) * (m - mean) for q, m in zip(squares, means))
    inv_std = lax.rsqrt(spread / (share * features) + EPS)
    total = jnp.zeros((row_share, width), F32)
    for part, local in zip(parts, means):
        tail = part[:, width : width + piece]
        gain_sum = jnp.concatenate([tail[j : j + 1] for j in range(row_share)], axis=1)
        total = total + part[:, :width] + (local - mean) * gain_sum
    vision = (total * inv_std).astype(BF16)
    scalar = put_scalars([mean, inv_std], row_share).astype(BF16)
    for j in range(share):
        out_ref[j, :, :width] = vision
        out_ref[j, :, width:] = scalar


def slot_pick(slot_count, send_rows, shift):
    row, col = iota((slot_count, send_rows), 0), iota((slot_count, send_rows), 1)
    place = row % SLOTS
    pick = (col == row // SLOTS * SEND + place + shift) & (place < CAPX)
    return pick.astype(F32)


def forward_kernel(
    vision_ref, early_ref, slots_ref, gain_ref, gate_ref, up_ref, down_ref,
    gate_out, up_out, down_out, h_ref, sum_ref,
):
    step = pl.program_id(0)
    slot_count, send_rows = slots_ref.shape[0], early_ref.shape[0]
    width = early_ref.shape[1]

    @pl.when(step == 0)
    def _():
        chosen = slots_ref[...]
        is_vision = jnp.sum(chosen.astype(F32), axis=1, keepdims=True) > 0.5
        inputs = dot(chosen, vision_ref[:, :width])
        scale = lax.rsqrt(jnp.mean(inputs * inputs, axis=1, keepdims=True) + EPS)
        normed = inputs * scale * gain_ref[...]
        text_rows = dot(slot_pick(slot_count, send_rows, 0), early_ref[...])
        h_ref[...] = jnp.where(is_vision, normed, text_rows).astype(BF16)
        sum_ref[...] = jnp.zeros_like(sum_ref)

    gate_pre = dot_nt(h_ref[...], gate_ref[...])
    up_proj = dot_nt(h_ref[...], up_ref[...])
    gate_out[...] = gate_pre
    up_out[...] = up_proj
    activated = (gate_pre * jax.nn.sigmoid(gate_pre) * up_proj).astype(BF16)
    sum_ref[...] += dot(activated, down_ref[...])

    @pl.when(step == pl.num_programs(0) - 1)
    def _():
        down_out[...] = sum_ref[...].astype(BF16)


def backward_kernel(
    early_ref, slots_ref, gate_in, up_in, gate_ref, up_ref, down_ref, out_ref, back_ref, sum_ref
):
    step = pl.program_id(0)
    slot_count, send_rows = slots_ref.shape[0], early_ref.shape[0]

    @pl.when(step == 0)
    def _():
        back_ref[...] = dot(slot_pick(slot_count, send_rows, CAPX), early_ref[...]).astype(BF16)
        sum_ref[...] = jnp.zeros_like(sum_ref)

    act_grad = dot_nt(back_ref[...], down_ref[...])
    gate_pre, up_proj = gate_in[...], up_in[...]
    sigmoid = jax.nn.sigmoid(gate_pre)
    gate_grad = act_grad * up_proj * sigmoid * (1.0 + gate_pre * (1.0 - sigmoid))
    up_grad = act_grad * gate_pre * sigmoid
    sum_ref[...] += dot(gate_grad, gate_ref[...]) + dot(up_grad, up_ref[...])

    @pl.when(step == pl.num_programs(0) - 1)
    def _():
        out_ref[...] = dot_tn(slots_ref[...], sum_ref[...].astype(BF16)).astype(BF16)


def combine_kernel(rows_ref, comb_ref, out_ref):
    rows = rows_ref[...]
    out_ref[...] = (dot_tn(comb_ref[0], rows) + dot_tn(comb_ref[1], rows)).astype(BF16)


def finish_kernel(ids_ref, part_ref, placed_ref, vision_ref, text_ref, out_ref):
    share, count, width = part_ref.shape
    first = pl.multiple_of(ids_ref[1] * count, count)
    placed = placed_ref[...]
    pick = iota((count, placed.shape[0]), 1) == iota((count, placed.shape[0]), 0) + first
    pick = pick.astype(F32)
    placed = dot(pick, placed)
    is_vision = jnp.sum(placed, axis=1, keepdims=True) > 0.5
    inputs = jnp.where(is_vision, dot(placed, vision_ref[:, :width]), dot(pick, text_ref[...]))
    total = inputs
    for j in range(share):
        total = total + part_ref[j].astype(F32)
    total = total.astype(BF16)
    for j in range(share):
        out_ref[j] = total


def gather_sum_kernel(part_ref, out_ref):
    total = part_ref[0].astype(F32)
    for j in range(1, part_ref.shape[0]):
        total = total + part_ref[j].astype(F32)
    out_ref[...] = total.astype(BF16)


def norm_grad_kernel(part_ref, own_ref, early_ref, gain_ref, out_ref):
    share, row_share, width = part_ref.shape
    hidden = part_ref[0].astype(F32)
    for j in range(1, share):
        hidden = hidden + part_ref[j].astype(F32)
    send_rows = early_ref.shape[0]
    pick = iota((row_share, send_rows), 1) % SEND == iota((row_share, send_rows), 0) + 2 * CAPX
    cotangent = dot(pick.astype(F32), early_ref[...])
    inputs = own_ref[0, :, :width].astype(F32)
    scale = lax.rsqrt(jnp.mean(inputs * inputs, axis=1, keepdims=True) + EPS)
    pulled = hidden * gain_ref[...]
    cross = jnp.mean(pulled * inputs, axis=1, keepdims=True)
    grad = cotangent + scale * pulled - inputs * (scale * scale * scale) * cross
    grad = grad.astype(BF16)
    for j in range(share):
        out_ref[j] = grad


def merge_grad_kernel(grad_ref, weight_ref, gain_ref, merged_ref, scalar_ref, out_ref, sums_ref):
    normed_grad = dot_nt(grad_ref[...], weight_ref[...]) * gain_ref[...]
    out_ref[...] = normed_grad
    scalars = scalar_ref[...].astype(F32)
    normed = (merged_ref[...].astype(F32) - get_scalar(scalars, 0)) * get_scalar(scalars, 1)
    first = jnp.sum(normed_grad, axis=1, keepdims=True)
    second = jnp.sum(normed_grad * normed, axis=1, keepdims=True)
    lane = iota(sums_ref.shape[1:], 1)
    sums = jnp.where(lane == 0, first, jnp.where(lane == 1, second, 0.0))
    for j in range(sums_ref.shape[0]):
        sums_ref[j] = sums


def unfold_kernel(sums_ref, grad_ref, merged_ref, scalar_ref, out_ref, *, size):
    rows, features = grad_ref.shape
    depth, patches = out_ref.shape
    share = sums_ref.shape[0]
    sums = sums_ref[0]
    for j in range(1, share):
        sums = sums + sums_ref[j]
    sums = sums / (share * features)
    lane = iota(sums.shape, 1)
    grad_mean = jnp.sum(jnp.where(lane == 0, sums, 0.0), axis=1, keepdims=True)
    cross_mean = jnp.sum(jnp.where(lane == 1, sums, 0.0), axis=1, keepdims=True)
    scalars = scalar_ref[...].astype(F32)
    inv_std = get_scalar(scalars, 1)
    normed = (merged_ref[...].astype(F32) - get_scalar(scalars, 0)) * inv_std
    grad = inv_std * (grad_ref[...] - grad_mean - normed * cross_mean)
    high = grad.astype(BF16)
    low = (grad - high.astype(F32)).astype(BF16)
    unfold = (iota((patches, rows), 0) // 4 == iota((patches, rows), 1)).astype(F32)
    spot = iota((patches, features), 1) // size % 4 == iota((patches, features), 0) % 4
    row, col = iota((depth, features), 0), iota((depth, features), 1)
    place = (col // (4 * size) == row // size) & (col % size == row % size)
    place = place.astype(F32).astype(BF16)
    out = jnp.zeros((depth, patches), F32)
    for piece in (high, low):
        wide = jnp.where(spot, dot(unfold, piece), 0.0).astype(BF16)
        out = out + dot_nt(place, wide)
    out_ref[...] = out


def whole(memory_space=pltpu.VMEM):
    return pl.BlockSpec(memory_space=memory_space)


def run(kernel, outs, *args, scalars=0, cost=None, name=None):
    specs = [whole(pltpu.SMEM)] * scalars + [whole()] * (len(args) - scalars)
    return pl.pallas_call(
        kernel,
        out_shape=outs,
        in_specs=specs,
        out_specs=jax.tree.map(lambda _: whole(), outs),
        compiler_params=pltpu.CompilerParams(vmem_limit_bytes=VMEM_BYTES),
        name=name,
    )(*args)


def shape(dims, dtype=BF16):
    return jax.ShapeDtypeStruct(dims, dtype)


def trade(value, axis):
    return lax.all_to_all(value, axis, split_axis=0, concat_axis=0, tiled=True)


def body(
    queries, keys, values, image_ids, placement, merge_gain, merge_weight, text, norm_gain,
    w_gate, w_up, w_down, routes, route_gates, cotangent,
):
    blocks = lax.axis_size("blk")
    share = lax.axis_size("expert")
    ids = jnp.stack([lax.axis_index("blk"), lax.axis_index("expert")]).astype(jnp.int32)
    heads, size, patches = queries.shape
    depth = heads * size
    rows = image_ids.shape[0]
    row_share = rows // share
    tokens, width = text.shape
    all_rows = blocks * rows
    features = heads * 4 * size
    hidden = w_gate.shape[1]
    slot_count = blocks * SLOTS
    groups = share // 2

    patch_ids = jnp.repeat(image_ids, 4)
    routes_t = routes.T
    gates_t = route_gates.T
    meta = jnp.concatenate(
        [
            routes_t.astype(BF16),
            patch_ids[None].astype(BF16),
            jnp.pad(placement[:, 0][None].astype(BF16), ((0, 0), (0, 128 - rows))),
            jnp.zeros((6, 128), BF16),
        ]
    )
    local = jnp.concatenate([keys.reshape(depth, patches), values.reshape(depth, patches), meta])
    near = lax.all_gather(local, "blk", axis=0)

    gain_row = norm_gain[None]
    send, slots, placed, comb = run(
        functools.partial(plan_kernel, groups=groups, merged_rows=rows, row_share=row_share),
        (
            shape((blocks * SEND, width)),
            shape((slot_count, all_rows)),
            shape((tokens, all_rows)),
            shape((2, slot_count, tokens)),
        ),
        ids, near[:, 2 * depth :], routes_t, gates_t, text, gain_row, cotangent,
        scalars=1, name="plan",
    )
    early = trade(send.reshape(blocks, SEND, width), "blk").reshape(blocks * SEND, width)

    weight_flat = merge_weight.reshape(features, width)
    gain_flat = merge_gain.reshape(1, features)
    message_width = width + width // row_share + 128
    message, merged = run(
        functools.partial(attend_kernel, share=share, row_share=row_share),
        (shape((rows, message_width)), shape((rows, features))),
        queries, near, patch_ids[:, None].astype(F32), gain_flat, weight_flat, name="attend",
    )
    message = trade(message.reshape(share, row_share, message_width), "expert")
    own = run(
        functools.partial(merge_kernel, width=width, features=features),
        shape((share, row_share, width + 128)),
        message, name="merge",
    )
    block_rows = trade(own, "expert").reshape(rows, width + 128)
    scalars = block_rows[:, width:]
    vision = lax.all_gather(block_rows, "blk", axis=0).reshape(all_rows, width + 128)

    tile = 256 if hidden % 256 == 0 else hidden
    weight_spec = pl.BlockSpec((None, tile, width), lambda i: (0, i, 0))
    hidden_spec = pl.BlockSpec((slot_count, tile), lambda i: (0, i))

    def fixed(*dims):
        return pl.BlockSpec(dims, lambda i: (0,) * len(dims))

    params = pltpu.CompilerParams(
        vmem_limit_bytes=VMEM_BYTES, dimension_semantics=("arbitrary",)
    )
    gate_pre, up_proj, down_part = pl.pallas_call(
        forward_kernel,
        grid=(hidden // tile,),
        in_specs=[
            fixed(all_rows, width + 128), fixed(blocks * SEND, width), fixed(slot_count, all_rows),
            fixed(1, width), weight_spec, weight_spec, weight_spec,
        ],
        out_specs=[hidden_spec, hidden_spec, fixed(slot_count, width)],
        out_shape=[
            shape((slot_count, hidden), F32), shape((slot_count, hidden), F32),
            shape((slot_count, width)),
        ],
        scratch_shapes=[pltpu.VMEM((slot_count, width), BF16), pltpu.VMEM((slot_count, width), F32)],
        compiler_params=params,
        name="forward",
    )(vision, early, slots, gain_row, w_gate, w_up, w_down)
    returned = trade(down_part.reshape(blocks, SLOTS, width), "blk")
    row_grad = pl.pallas_call(
        backward_kernel,
        grid=(hidden // tile,),
        in_specs=[
            fixed(blocks * SEND, width), fixed(slot_count, all_rows), hidden_spec, hidden_spec,
            weight_spec, weight_spec, weight_spec,
        ],
        out_specs=fixed(all_rows, width),
        out_shape=shape((all_rows, width)),
        scratch_shapes=[pltpu.VMEM((slot_count, width), BF16), pltpu.VMEM((slot_count, width), F32)],
        compiler_params=params,
        name="backward",
    )(early, slots, gate_pre, up_proj, w_gate, w_up, w_down)
    row_grad = trade(row_grad.reshape(blocks, rows, width), "blk")

    combined = run(
        combine_kernel, shape((tokens, width)), returned.reshape(slot_count, width), comb,
        name="combine",
    )
    combined = trade(combined.reshape(share, tokens // share, width), "expert")
    grad_sum = run(gather_sum_kernel, shape((rows, width)), row_grad, name="gather_sum")
    grad_sum = trade(grad_sum.reshape(share, row_share, width), "expert")
    vision_grad = run(
        norm_grad_kernel, shape((share, row_share, width)), grad_sum, own, early, gain_row,
        name="norm_grad",
    )
    vision_grad = trade(vision_grad, "expert").reshape(rows, width)
    normed_grad, sums = run(
        merge_grad_kernel,
        (shape((rows, features), F32), shape((share, rows, 128), F32)),
        vision_grad, weight_flat, gain_flat, merged, scalars, name="merge_grad",
    )
    sums = trade(sums, "expert")
    finished = run(
        finish_kernel, shape((share, tokens // share, width)), ids, combined, placed, vision, text,
        scalars=1, name="finish",
    )
    llm_out = trade(finished, "expert").reshape(tokens, width)
    attn_grad = run(
        functools.partial(unfold_kernel, size=size), shape((depth, patches), F32),
        sums, normed_grad, merged, scalars, name="unfold",
    )
    return llm_out, attn_grad.reshape(heads, size, patches)


def solution(mesh):
    return jax.shard_map(
        body,
        mesh=mesh,
        in_specs=(
            P("expert", None, "blk"),
            P("expert", None, "blk"),
            P("expert", None, "blk"),
            P("blk"),
            P("blk", None),
            P("expert", None),
            P("expert", None, None),
            P("blk", None),
            P(),
            P("blk", "expert", None),
            P("blk", "expert", None),
            P("blk", "expert", None),
            P("blk", None),
            P("blk", None),
            P("blk", None),
        ),
        out_specs=(P("blk", None), P("expert", None, "blk")),
        check_vma=False,
    )
```

```python
import functools

import jax
import jax.numpy as jnp
from jax import lax
from jax.experimental import pallas as pl
from jax.experimental.pallas import tpu as pltpu
from jax.sharding import PartitionSpec as P

CAPX = 10
SLOTS = 16
SEND = 32
EPS = 1e-06
VMEM_BYTES = 24 * 1024 * 1024
BIG_VMEM = 56 * 1024 * 1024
F32 = jnp.float32
BF16 = jnp.bfloat16


def iota(shape, dim):
    return lax.broadcasted_iota(jnp.int32, shape, dim)


def dot(a, b):
    return jnp.dot(a.astype(BF16), b.astype(BF16), preferred_element_type=F32)


def dot_nt(a, b):
    return lax.dot_general(a, b, (((1,), (1,)), ((), ())), preferred_element_type=F32)


def dot_tn(a, b):
    return lax.dot_general(a, b, (((0,), (0,)), ((), ())), preferred_element_type=F32)


def three(value):
    first = value.astype(BF16).astype(F32)
    second = (value - first).astype(BF16).astype(F32)
    return first, second, value - first - second


def put_scalars(columns, rows):
    lane = iota((rows, 128), 1)
    out = jnp.zeros((rows, 128), F32)
    place = 0
    for column in columns:
        for piece in three(column):
            out = jnp.where(lane == place, piece, out)
            place += 1
    return out


def get_scalar(block, which):
    lane = iota(block.shape, 1)
    return jnp.sum(jnp.where(lane // 3 == which, block, 0.0), axis=1, keepdims=True)


def pack_kernel(keys_ref, values_ref, images_ref, placement_ref, routes_ref, out_ref):
    rows = images_ref.shape[1]
    depth, patches = keys_ref.shape
    repeat = (iota((rows, patches), 0) == iota((rows, patches), 1) // 4).astype(F32)
    keep = (iota((rows, patches), 0) == iota((rows, patches), 1)).astype(F32)
    patch_ids = dot(images_ref[...].astype(F32), repeat)
    dest = dot(placement_ref[...].astype(F32), keep)
    line = iota((8, patches), 0)
    rest = jnp.where(line == 0, patch_ids, jnp.where(line == 1, dest, 0.0))
    parts = [keys_ref[...], values_ref[...], routes_ref[...], rest]
    out_ref[...] = jnp.concatenate([part.astype(F32) for part in parts], axis=0).astype(BF16)


def plan_kernel(*refs, blocks, groups, merged_rows, row_share):
    ids_ref, *near_refs = refs[: blocks + 1]
    routes_ref, gates_ref, text_ref, gain_ref, cot_ref = refs[blocks + 1 : blocks + 6]
    slots_ref, placed_ref, comb_ref, *send_refs = refs[blocks + 6 :]
    tokens = text_ref.shape[0]
    share = merged_rows // row_share
    rows = blocks * merged_rows
    me, expert_index = ids_ref[0], ids_ref[1]
    member = expert_index // groups
    meta = [ref[...].astype(F32) for ref in near_refs]
    mine = (2 * me + member).astype(F32)
    hits = [jnp.sum((part[:8] == mine).astype(F32), axis=0, keepdims=True) for part in meta]
    hit = jnp.concatenate(hits, axis=0)
    dest = jnp.concatenate([part[9:10] for part in meta], axis=0)
    before = (iota((tokens, tokens), 0) < iota((tokens, tokens), 1)).astype(BF16)
    rank = dot(hit, before)

    def row_of(col):
        inner = col % merged_rows
        return ((inner // row_share) ^ expert_index) * row_share + inner % row_share

    def place_of(col):
        return ((col // merged_rows) ^ me) * merged_rows + row_of(col)

    spread = (iota((128, rows), 0) == row_of(iota((128, rows), 1))).astype(F32)
    own_block = iota((blocks, rows), 1) // merged_rows == iota((blocks, rows), 0)
    dest_row = jnp.sum(jnp.where(own_block, dot(dest, spread), 0.0), axis=0, keepdims=True)
    dest_row = dest_row.astype(jnp.int32) ^ me
    dest_hit = (iota((blocks, rows), 0) == dest_row).astype(F32)
    rows_before = place_of(iota((rows, rows), 0)) < place_of(iota((rows, rows), 1))
    earlier = dot(dest_hit, rows_before.astype(F32))
    slot = jnp.sum(dest_hit * earlier, axis=0, keepdims=True).astype(jnp.int32)
    at_token = (iota((tokens, rows), 0) == slot).astype(F32)
    row_hit = jnp.sum(dest_hit * dot(hit, at_token), axis=0, keepdims=True)
    row_rank = jnp.sum(dest_hit * dot(rank, at_token), axis=0, keepdims=True).astype(jnp.int32)
    slot_id = dest_row * SLOTS + row_rank
    slot_count = slots_ref.shape[0]
    chosen = (iota((slot_count, rows), 0) == slot_id) & (row_hit > 0.5)
    slots_ref[...] = chosen.astype(F32).astype(BF16)
    placed = jnp.where(dest_row == 0, at_token, 0.0).astype(BF16)
    placed_ref[...] = placed

    pair_of = 2 * (iota((blocks, tokens), 0) ^ me) + member
    out_hit = jnp.zeros((blocks, tokens), F32)
    out_gate = jnp.zeros((blocks, tokens), F32)
    for k in range(routes_ref.shape[0]):
        same = pair_of == routes_ref[k : k + 1, :]
        out_hit = out_hit + same.astype(F32)
        out_gate = out_gate + jnp.where(same, gates_ref[k : k + 1, :], 0.0)
    out_rank = dot(out_hit, before)

    def expand(stride):
        count = blocks * stride
        pick = (iota((count, blocks), 0) // stride == iota((count, blocks), 1)).astype(BF16)
        gate = sum(dot(pick, piece) for piece in three(out_gate))
        return dot(pick, out_hit), dot(pick, out_rank).astype(jnp.int32), gate

    hits, ranks, gates = expand(SLOTS)
    live = jnp.where(ranks == iota(hits.shape, 0) % SLOTS, hits, 0.0)
    weight = live * gates
    high = weight.astype(BF16).astype(F32)
    part = tokens // share
    col = iota((tokens, tokens), 1)
    turned = (iota((tokens, tokens), 0) == ((col // part) ^ expert_index) * part + col % part)
    turned = turned.astype(F32)
    comb_ref[0] = dot(high, turned).astype(BF16)
    comb_ref[1] = dot(weight - high, turned).astype(BF16)

    hits, ranks, gates = expand(SEND)
    place = iota(hits.shape, 0) % SEND
    input_pick = jnp.where((place < CAPX) & (ranks == place), hits, 0.0)
    back_pick = jnp.where((place >= CAPX) & (place < 2 * CAPX) & (ranks == place - CAPX), hits, 0.0)
    back_gate = jnp.sum(back_pick * gates, axis=1, keepdims=True)
    send_rows = blocks * SEND
    source = iota((send_rows, rows), 0)
    kept = source % SEND - 2 * CAPX
    wanted = source // SEND * merged_rows + kept
    row_pick = (kept >= 0) & (kept < row_share) & (iota((send_rows, rows), 1) == wanted)
    cot_pick = dot_nt(row_pick.astype(F32).astype(BF16), placed)
    cot_row = iota((send_rows, 1), 0) % SEND >= 2 * CAPX
    factor = jnp.where(cot_row, 1.0, back_gate)
    text = text_ref[...].astype(F32)
    scale = lax.rsqrt(jnp.mean(text * text, axis=1, keepdims=True) + EPS)
    h_rows = (text * scale * gain_ref[...]).astype(BF16)
    send = dot(input_pick, h_rows) + factor * dot(back_pick + cot_pick, cot_ref[...])
    send = send.astype(BF16)
    for k in range(blocks):
        send_refs[k][...] = send[k * SEND : (k + 1) * SEND]


def attend_kernel(*refs, blocks, share, row_share):
    ids_ref, query_ref, gain_ref, weight_hbm = refs[:4]
    near_refs = refs[4 : 4 + blocks]
    merged_ref, *message_refs = refs[4 + blocks : 5 + blocks + share]
    weight_ref, weight_sem = refs[5 + blocks + share :]
    weight_copy = pltpu.make_async_copy(weight_hbm, weight_ref, weight_sem)
    weight_copy.start()
    heads, size, patches = query_ref.shape
    rows, features = merged_ref.shape
    width = weight_ref.shape[1]
    depth = heads * size
    near = [ref[...].astype(F32) for ref in near_refs]
    key_ids = jnp.concatenate([part[2 * depth + 8 : 2 * depth + 9] for part in near], axis=1)
    eye = iota((patches, patches), 0) == iota((patches, patches), 1)
    own_ids = jnp.sum(jnp.where(eye, key_ids[:, :patches], 0.0), axis=1, keepdims=True)
    same = own_ids == key_ids
    spread = jnp.zeros((patches, features), F32)
    place_row, place_col = iota((size, features), 0), iota((size, features), 1)
    for head in range(heads):
        first = head * size
        keys = jnp.concatenate([part[first : first + size] for part in near], axis=1)
        first = depth + head * size
        values = jnp.concatenate([part[first : first + size] for part in near], axis=1)
        query = query_ref[head].astype(F32).T.astype(BF16)
        scores = dot(query, keys) * (size**-0.5)
        scores = jnp.where(same, scores, -1e30)
        weights = jnp.exp(scores - jnp.max(scores, axis=1, keepdims=True))
        total = jnp.sum(weights, axis=1, keepdims=True)
        attn = dot_nt(weights.astype(BF16), values.astype(BF16)) / total
        place = (place_col % size == place_row) & (place_col // (4 * size) == head)
        spread = spread + dot(attn, place.astype(F32))
    spot = iota((patches, features), 1) // size % 4 == iota((patches, features), 0) % 4
    line = iota((rows, patches), 0)
    line = ((line // row_share) ^ ids_ref[1]) * row_share + line % row_share
    fold = (iota((rows, patches), 1) // 4 == line).astype(F32)
    merged = dot(fold, jnp.where(spot, spread, 0.0))
    merged_ref[...] = merged.astype(BF16)
    local_mean = jnp.sum(merged, axis=1, keepdims=True) / features
    centered = merged - local_mean
    squares = jnp.sum(centered * centered, axis=1, keepdims=True)
    gain = gain_ref[...]
    gain_high = gain.astype(BF16).astype(F32)
    extra = iota((8, features), 0)
    gain_rows = jnp.where(extra == 0, gain_high, jnp.where(extra == 1, gain - gain_high, 0.0))
    left = jnp.concatenate([centered * gain, gain_rows], axis=0)
    weight_copy.wait()
    product = dot(left, weight_ref[...])
    gain_sum = product[rows : rows + 1] + product[rows + 1 : rows + 2]
    piece = width // row_share
    pieces = [gain_sum[:, j * piece : (j + 1) * piece] for j in range(row_share)]
    pieces = jnp.concatenate(pieces, axis=0).astype(BF16)
    scalars = put_scalars([local_mean, squares], rows).astype(BF16)
    for k in range(share):
        mine = slice(k * row_share, (k + 1) * row_share)
        message_refs[k][:, :width] = product[mine].astype(BF16)
        message_refs[k][:, width : width + piece] = pieces
        message_refs[k][:, width + piece :] = scalars[mine]


def merge_kernel(*refs, width, features):
    *message_refs, out_ref = refs
    share, row_share = len(message_refs), out_ref.shape[0]
    piece = width // row_share
    parts = [ref[...].astype(F32) for ref in message_refs]
    scalars = [part[:, width + piece :] for part in parts]
    means = [get_scalar(block, 0) for block in scalars]
    squares = [get_scalar(block, 1) for block in scalars]
    mean = sum(means) / share
    spread = sum(q + features * (m - mean) * (m - mean) for q, m in zip(squares, means))
    inv_std = lax.rsqrt(spread / (share * features) + EPS)
    total = jnp.zeros((row_share, width), F32)
    for part, local in zip(parts, means):
        tail = part[:, width : width + piece]
        gain_sum = jnp.concatenate([tail[j : j + 1] for j in range(row_share)], axis=1)
        total = total + part[:, :width] + (local - mean) * gain_sum
    out_ref[:, :width] = (total * inv_std).astype(BF16)
    out_ref[:, width:] = put_scalars([mean, inv_std], row_share).astype(BF16)


def stack_kernel(*refs):
    *part_refs, out_ref = refs
    out_ref[...] = stacked(part_refs)


def stacked(part_refs):
    return jnp.concatenate([ref[...].astype(F32) for ref in part_refs], axis=0).astype(BF16)


def slot_pick(slot_count, send_rows, shift):
    row, col = iota((slot_count, send_rows), 0), iota((slot_count, send_rows), 1)
    place = row % SLOTS
    pick = (col == row // SLOTS * SEND + place + shift) & (place < CAPX)
    return pick.astype(F32)


def experts_kernel(*refs, blocks):
    slots_ref, gain_ref, gate_hbm, up_hbm, down_hbm = refs[:5]
    vision_refs = refs[5 : 5 + blocks]
    early_refs = refs[5 + blocks : 5 + 2 * blocks]
    even_ref, odd_ref, *down_refs = refs[5 + 2 * blocks : 7 + 3 * blocks]
    weight_ref, h_ref, back_ref, down_sum, grad_sum, sems = refs[7 + 3 * blocks :]
    tiles, _, tile, width = weight_ref.shape
    slot_count = slots_ref.shape[0]

    def copy(i, which):
        source = (gate_hbm, up_hbm, down_hbm)[which].at[0, pl.ds(i * tile, tile)]
        return pltpu.make_async_copy(source, weight_ref.at[i, which], sems.at[i, which])

    for i in range(tiles):
        for which in range(3):
            copy(i, which).start()
    chosen = slots_ref[...]
    is_vision = jnp.sum(chosen.astype(F32), axis=1, keepdims=True) > 0.5
    vision = jnp.concatenate([ref[:, :width] for ref in vision_refs], axis=0)
    inputs = dot(chosen, vision)
    scale = lax.rsqrt(jnp.mean(inputs * inputs, axis=1, keepdims=True) + EPS)
    normed = inputs * scale * gain_ref[...]
    early = jnp.concatenate([ref[...] for ref in early_refs], axis=0)
    text_rows = dot(slot_pick(slot_count, early.shape[0], 0), early)
    h_ref[...] = jnp.where(is_vision, normed, text_rows).astype(BF16)
    back_ref[...] = dot(slot_pick(slot_count, early.shape[0], CAPX), early).astype(BF16)
    down_sum[...] = jnp.zeros_like(down_sum)
    grad_sum[...] = jnp.zeros_like(grad_sum)

    @pl.loop(0, tiles)
    def _(i):
        copy(i, 0).wait()
        gate_pre = dot_nt(h_ref[...], weight_ref[i, 0])
        copy(i, 1).wait()
        up_proj = dot_nt(h_ref[...], weight_ref[i, 1])
        copy(i, 2).wait()
        act_grad = dot_nt(back_ref[...], weight_ref[i, 2])
        sigmoid = jax.nn.sigmoid(gate_pre)
        gate_grad = act_grad * up_proj * sigmoid * (1.0 + gate_pre * (1.0 - sigmoid))
        up_grad = act_grad * gate_pre * sigmoid
        grad_sum[...] += dot(gate_grad, weight_ref[i, 0]) + dot(up_grad, weight_ref[i, 1])
        activated = gate_pre * sigmoid * up_proj
        down_sum[...] += dot(activated, weight_ref[i, 2])

    grads = dot_tn(chosen, grad_sum[...].astype(BF16)).astype(BF16)
    rows = grads.shape[0] // blocks
    for k in range(blocks):
        to_ref = odd_ref if k % 2 else even_ref
        to_ref[k // 2 * rows : (k // 2 + 1) * rows] = grads[k * rows : (k + 1) * rows]
        down_refs[k][...] = down_sum[k * SLOTS : (k + 1) * SLOTS].astype(BF16)


def pair_sum_kernel(own_ref, sibling_ref, *out_refs):
    rows = out_refs[0].shape[0]
    for k, out_ref in enumerate(out_refs):
        mine = slice(k * rows, (k + 1) * rows)
        out_ref[...] = (own_ref[mine].astype(F32) + sibling_ref[mine].astype(F32)).astype(BF16)


def total_of(part_refs):
    total = part_refs[0][...].astype(F32)
    for ref in part_refs[1:]:
        total = total + ref[...].astype(F32)
    return total


def chip_sum_kernel(*refs, count):
    out_refs = refs[count:]
    total = total_of(refs[:count])
    rows = out_refs[0].shape[0]
    for k, out_ref in enumerate(out_refs):
        out_ref[...] = total[k * rows : (k + 1) * rows].astype(BF16)


def combine_kernel(comb_ref, *refs, count):
    rows = jnp.concatenate([ref[...] for ref in refs[:count]], axis=0)
    total = (dot_tn(comb_ref[0], rows) + dot_tn(comb_ref[1], rows)).astype(BF16)
    out_refs = refs[count:]
    part = out_refs[0].shape[0]
    for k, out_ref in enumerate(out_refs):
        out_ref[...] = total[k * part : (k + 1) * part]


def finish_kernel(ids_ref, placed_ref, text_ref, *refs, blocks):
    vision_refs, part_refs, out_ref = refs[:blocks], refs[blocks:-1], refs[-1]
    count, width = out_ref.shape
    tokens = placed_ref.shape[0]
    first = ids_ref[1] * count
    pick = iota((count, tokens), 1) == iota((count, tokens), 0) + first
    pick = pick.astype(F32)
    placed = dot(pick, placed_ref[...])
    is_vision = jnp.sum(placed, axis=1, keepdims=True) > 0.5
    vision = jnp.concatenate([ref[:, :width] for ref in vision_refs], axis=0)
    inputs = jnp.where(is_vision, dot(placed, vision), dot(pick, text_ref[...]))
    out_ref[...] = (inputs + total_of(part_refs)).astype(BF16)


def lay_kernel(ids_ref, *refs):
    *part_refs, out_ref = refs
    count = part_refs[0].shape[0]
    for k, ref in enumerate(part_refs):
        first = pl.multiple_of((ids_ref[1] ^ k) * count, count)
        out_ref[pl.ds(first, count), :] = ref[...]


def norm_grad_kernel(own_ref, gain_ref, *refs, blocks):
    early_refs, part_refs, out_ref = refs[:blocks], refs[blocks:-1], refs[-1]
    row_share, width = out_ref.shape
    hidden = total_of(part_refs)
    early = jnp.concatenate([ref[...] for ref in early_refs], axis=0)
    send_rows = early.shape[0]
    pick = iota((row_share, send_rows), 1) % SEND == iota((row_share, send_rows), 0) + 2 * CAPX
    cotangent = dot(pick.astype(F32), early)
    inputs = own_ref[:, :width].astype(F32)
    scale = lax.rsqrt(jnp.mean(inputs * inputs, axis=1, keepdims=True) + EPS)
    pulled = hidden * gain_ref[...]
    cross = jnp.mean(pulled * inputs, axis=1, keepdims=True)
    grad = cotangent + scale * pulled - inputs * (scale * scale * scale) * cross
    out_ref[...] = grad.astype(BF16)


def merge_grad_kernel(*refs, share):
    gain_ref, merged_ref, scalar_ref, weight_hbm = refs[:4]
    part_refs = refs[4 : 4 + share]
    out_ref, sums_ref, weight_ref, sems = refs[4 + share :]
    width = weight_ref.shape[1]
    chunk = weight_ref.shape[0] // sems.shape[0]
    copies = []
    for i in range(sems.shape[0]):
        mine = pl.ds(i * chunk, chunk)
        copies.append(
            pltpu.make_async_copy(weight_hbm.at[mine], weight_ref.at[mine], sems.at[i])
        )
        copies[-1].start()
    grad = stacked(part_refs)
    scalars = scalar_ref[:, width:].astype(F32)
    normed = (merged_ref[...].astype(F32) - get_scalar(scalars, 0)) * get_scalar(scalars, 1)
    first, second = 0.0, 0.0
    for i, copy in enumerate(copies):
        copy.wait()
        mine = slice(i * chunk, (i + 1) * chunk)
        normed_grad = dot_nt(grad, weight_ref[mine]) * gain_ref[:, mine]
        out_ref[:, mine] = normed_grad
        first = first + jnp.sum(normed_grad, axis=1, keepdims=True)
        second = second + jnp.sum(normed_grad * normed[:, mine], axis=1, keepdims=True)
    lane = iota(sums_ref.shape, 1)
    sums_ref[...] = jnp.where(lane == 0, first, jnp.where(lane == 1, second, 0.0))


def unfold_kernel(ids_ref, grad_ref, merged_ref, scalar_ref, *refs, size):
    *sums_refs, out_ref = refs
    rows, features = grad_ref.shape
    depth, patches = out_ref.shape
    share = len(sums_refs)
    row_share = rows // share
    sums = sums_refs[0][...]
    for k in range(1, share):
        theirs = [sums_refs[k][(j ^ k) * row_share : ((j ^ k) + 1) * row_share] for j in range(share)]
        sums = sums + jnp.concatenate(theirs, axis=0)
    sums = sums / (share * features)
    lane = iota(sums.shape, 1)
    grad_mean = jnp.sum(jnp.where(lane == 0, sums, 0.0), axis=1, keepdims=True)
    cross_mean = jnp.sum(jnp.where(lane == 1, sums, 0.0), axis=1, keepdims=True)
    scalars = scalar_ref[:, scalar_ref.shape[1] - 128 :].astype(F32)
    inv_std = get_scalar(scalars, 1)
    normed = (merged_ref[...].astype(F32) - get_scalar(scalars, 0)) * inv_std
    grad = inv_std * (grad_ref[...] - grad_mean - normed * cross_mean)
    high = grad.astype(BF16)
    low = (grad - high.astype(F32)).astype(BF16)
    line = iota((patches, rows), 1)
    line = ((line // row_share) ^ ids_ref[1]) * row_share + line % row_share
    unfold = (iota((patches, rows), 0) // 4 == line).astype(F32)
    spot = iota((patches, features), 1) // size % 4 == iota((patches, features), 0) % 4
    row, col = iota((depth, features), 0), iota((depth, features), 1)
    place = (col // (4 * size) == row // size) & (col % size == row % size)
    place = place.astype(F32).astype(BF16)
    out = jnp.zeros((depth, patches), F32)
    for piece in (high, low):
        wide = jnp.where(spot, dot(unfold, piece), 0.0).astype(BF16)
        out = out + dot_nt(place, wide)
    out_ref[...] = out


def whole(memory_space=pltpu.VMEM):
    return pl.BlockSpec(memory_space=memory_space)


def run(kernel, outs, *args, scalars=0, far=(), scratch=(), vmem=VMEM_BYTES, name=None):
    specs = [whole(pltpu.SMEM)] * scalars + [whole()] * (len(args) - scalars)
    for place in far:
        specs[place] = whole(pl.ANY)
    return pl.pallas_call(
        kernel,
        out_shape=outs,
        in_specs=specs,
        out_specs=jax.tree.map(lambda _: whole(), outs),
        scratch_shapes=scratch,
        compiler_params=pltpu.CompilerParams(vmem_limit_bytes=vmem),
        name=name,
    )(*args)


def shape(dims, dtype=BF16):
    return jax.ShapeDtypeStruct(dims, dtype)


def swap(value, axis, step):
    count = lax.axis_size(axis)
    return lax.ppermute(value, axis, [(i, i ^ step) for i in range(count)])


def trade(parts, axis):
    return [parts[0]] + [swap(parts[k], axis, k) for k in range(1, len(parts))]


def spread_out(value, axis):
    return trade([value] * lax.axis_size(axis), axis)


def gather_blocks(value):
    near = {0: value}
    for k in range(2, lax.axis_size("blk"), 2):
        near[k] = swap(value, "blk", k)
    for k in list(near):
        near[k + 1] = swap(near[k], "blk", 1)
    return [near[k] for k in sorted(near)]


def body(
    queries, keys, values, image_ids, placement, merge_gain, merge_weight, text, norm_gain,
    w_gate, w_up, w_down, routes, route_gates, cotangent,
):
    blocks = lax.axis_size("blk")
    share = lax.axis_size("expert")
    ids = jnp.stack([lax.axis_index("blk"), lax.axis_index("expert")]).astype(jnp.int32)
    heads, size, patches = queries.shape
    depth = heads * size
    rows = image_ids.shape[0]
    row_share = rows // share
    tokens, width = text.shape
    part = tokens // share
    all_rows = blocks * rows
    features = heads * 4 * size
    hidden = w_gate.shape[1]
    slot_count = blocks * SLOTS
    groups = share // 2
    routes_t, gates_t, gain_row = routes.T, route_gates.T, norm_gain[None]

    local = run(
        pack_kernel, shape((2 * depth + 16, patches)),
        keys.reshape(depth, patches), values.reshape(depth, patches),
        image_ids[None], placement.reshape(1, rows), routes_t, name="pack",
    )
    near = gather_blocks(local)

    def fixed(*dims):
        return pl.BlockSpec(dims, lambda i: (0,) * len(dims))

    meta_spec = pl.BlockSpec((16, patches), lambda i: (2 * depth // 16, 0))
    plan_outs = [
        shape((slot_count, all_rows)), shape((tokens, all_rows)), shape((2, slot_count, tokens)),
    ] + [shape((SEND, width))] * blocks
    slots, placed, comb, *send = pl.pallas_call(
        functools.partial(
            plan_kernel, blocks=blocks, groups=groups, merged_rows=rows, row_share=row_share
        ),
        grid=(1,),
        in_specs=[whole(pltpu.SMEM)] + [meta_spec] * blocks
        + [
            fixed(*routes_t.shape), fixed(*gates_t.shape), fixed(tokens, width), fixed(1, width),
            fixed(tokens, width),
        ],
        out_specs=[fixed(*out.shape) for out in plan_outs],
        out_shape=plan_outs,
        compiler_params=pltpu.CompilerParams(vmem_limit_bytes=VMEM_BYTES),
        name="plan",
    )(ids, *near, routes_t, gates_t, text, gain_row, cotangent)
    early = trade(send, "blk")

    weight_flat = merge_weight.reshape(features, width)
    gain_flat = merge_gain.reshape(1, features)
    message_width = width + width // row_share + 128
    merged, *message = run(
        functools.partial(attend_kernel, blocks=blocks, share=share, row_share=row_share),
        [shape((rows, features))] + [shape((row_share, message_width))] * share,
        ids, queries, gain_flat, weight_flat, *near,
        scalars=1, far=(3,), vmem=BIG_VMEM,
        scratch=[pltpu.VMEM((features, width), BF16), pltpu.SemaphoreType.DMA(())],
        name="attend",
    )
    message = trade(message, "expert")
    own = run(
        functools.partial(merge_kernel, width=width, features=features),
        shape((row_share, width + 128)), *message, name="merge",
    )
    block_rows = run(
        stack_kernel, shape((rows, width + 128)), *spread_out(own, "expert"), name="stack"
    )
    vision = gather_blocks(block_rows)

    tile = 256 if hidden % 256 == 0 else hidden
    tiles = hidden // tile
    even, odd, *down = run(
        functools.partial(experts_kernel, blocks=blocks),
        [shape((all_rows // 2, width))] * 2 + [shape((SLOTS, width))] * blocks,
        slots, gain_row, w_gate, w_up, w_down, *vision, *early,
        far=(2, 3, 4), vmem=BIG_VMEM,
        scratch=[
            pltpu.VMEM((tiles, 3, tile, width), BF16),
            pltpu.VMEM((slot_count, width), BF16),
            pltpu.VMEM((slot_count, width), BF16),
            pltpu.VMEM((slot_count, width), F32),
            pltpu.VMEM((slot_count, width), F32),
            pltpu.SemaphoreType.DMA((tiles, 3)),
        ],
        name="experts",
    )
    grads = run(
        pair_sum_kernel, [shape((rows, width))] * (blocks // 2), even, swap(odd, "blk", 1),
        name="pair_sum",
    )
    grads = [grads[0]] + [swap(grads[k], "blk", 2 * k) for k in range(1, blocks // 2)]
    returned = trade(down, "blk")
    grads = run(
        functools.partial(chip_sum_kernel, count=blocks // 2),
        [shape((row_share, width))] * share, *grads, name="chip_sum",
    )
    grads = trade(grads, "expert")
    combined = run(
        functools.partial(combine_kernel, count=blocks), [shape((part, width))] * share,
        comb, *returned, name="combine",
    )
    combined = trade(combined, "expert")
    vision_grad = run(
        functools.partial(norm_grad_kernel, blocks=blocks), shape((row_share, width)),
        own, gain_row, *early, *grads, name="norm_grad",
    )
    vision_grad = spread_out(vision_grad, "expert")
    chunk = 384 if features % 384 == 0 else features
    normed_grad, sums = run(
        functools.partial(merge_grad_kernel, share=share),
        [shape((rows, features), F32), shape((rows, 128), F32)],
        gain_flat, merged, block_rows, weight_flat, *vision_grad,
        far=(3,), vmem=BIG_VMEM,
        scratch=[
            pltpu.VMEM((features, width), BF16), pltpu.SemaphoreType.DMA((features // chunk,))
        ],
        name="merge_grad",
    )
    sums = spread_out(sums, "expert")
    finished = run(
        functools.partial(finish_kernel, blocks=blocks), shape((part, width)),
        ids, placed, text, *vision, *combined, scalars=1, name="finish",
    )
    llm_out = run(
        lay_kernel, shape((tokens, width)), ids, *spread_out(finished, "expert"), scalars=1,
        name="lay",
    )
    attn_grad = run(
        functools.partial(unfold_kernel, size=size), shape((depth, patches), F32),
        ids, normed_grad, merged, block_rows, *sums, scalars=1, name="unfold",
    )
    return llm_out, attn_grad.reshape(heads, size, patches)


def solution(mesh):
    return jax.shard_map(
        body,
        mesh=mesh,
        in_specs=(
            P("expert", None, "blk"),
            P("expert", None, "blk"),
            P("expert", None, "blk"),
            P("blk"),
            P("blk", None),
            P("expert", None),
            P("expert", None, None),
            P("blk", None),
            P(),
            P("blk", "expert", None),
            P("blk", "expert", None),
            P("blk", "expert", None),
            P("blk", None),
            P("blk", None),
            P("blk", None),
        ),
        out_specs=(P("blk", None), P("expert", None, "blk")),
        check_vma=False,
    )
```

```python
import functools

import jax
import jax.numpy as jnp
from jax import lax
from jax.experimental import pallas as pl
from jax.experimental.pallas import tpu as pltpu
from jax.sharding import PartitionSpec as P

CAPX = 10
SLOTS = 16
SEND = 32
EPS = 1e-06
VMEM_BYTES = 24 * 1024 * 1024
F32 = jnp.float32
BF16 = jnp.bfloat16


def iota(shape, dim):
    return lax.broadcasted_iota(jnp.int32, shape, dim)


def dot(a, b):
    return jnp.dot(a.astype(BF16), b.astype(BF16), preferred_element_type=F32)


def dot_nt(a, b):
    return lax.dot_general(a, b, (((1,), (1,)), ((), ())), preferred_element_type=F32)


def dot_tn(a, b):
    return lax.dot_general(a, b, (((0,), (0,)), ((), ())), preferred_element_type=F32)


def three(value):
    first = value.astype(BF16).astype(F32)
    second = (value - first).astype(BF16).astype(F32)
    return first, second, value - first - second


def put_scalars(columns, rows):
    lane = iota((rows, 128), 1)
    out = jnp.zeros((rows, 128), F32)
    place = 0
    for column in columns:
        for piece in three(column):
            out = jnp.where(lane == place, piece, out)
            place += 1
    return out


def get_scalar(block, which):
    lane = iota(block.shape, 1)
    return jnp.sum(jnp.where(lane // 3 == which, block, 0.0), axis=1, keepdims=True)


def pack_kernel(*refs):
    far_refs, out_ref, near_refs, sems = refs[:5], refs[5], refs[6:11], refs[11]
    copies = [
        pltpu.make_async_copy(far, near, sems.at[i])
        for i, (far, near) in enumerate(zip(far_refs, near_refs))
    ]
    for copy in copies:
        copy.start()
    for copy in copies:
        copy.wait()
    keys_ref, values_ref, images_ref, placement_ref, routes_ref = near_refs
    rows = images_ref.shape[1]
    patches = keys_ref.shape[1]
    repeat = (iota((rows, patches), 0) == iota((rows, patches), 1) // 4).astype(F32)
    keep = (iota((rows, patches), 0) == iota((rows, patches), 1)).astype(F32)
    patch_ids = dot(images_ref[...].astype(F32), repeat)
    dest = dot(placement_ref[...].astype(F32), keep)
    line = iota((8, patches), 0)
    rest = jnp.where(line == 0, patch_ids, jnp.where(line == 1, dest, 0.0))
    parts = [keys_ref[...], values_ref[...], routes_ref[...], rest]
    out_ref[...] = jnp.concatenate([part.astype(F32) for part in parts], axis=0).astype(BF16)


def hold_kernel(*refs):
    count = (len(refs) - 1) // 2
    copies = []
    sems = refs[-1]
    for i in range(count):
        far_ref, near_ref = refs[i], refs[count + i]
        chunk = far_ref.shape[0] // sems.shape[1]
        for j in range(sems.shape[1]):
            mine = pl.ds(j * chunk, chunk)
            copies.append(pltpu.make_async_copy(far_ref.at[mine], near_ref.at[mine], sems.at[i, j]))
            copies[-1].start()
    for copy in copies:
        copy.wait()


def plan_kernel(*refs, blocks, groups, merged_rows, row_share):
    near_refs = refs[:blocks]
    routes_ref, gates_ref, text_ref, gain_ref, cot_ref, _ = refs[blocks : blocks + 6]
    slots_ref, placed_ref, comb_ref, send_ref = refs[blocks + 6 :]
    tokens = text_ref.shape[0]
    share = merged_rows // row_share
    rows = blocks * merged_rows
    me, expert_index = lax.axis_index("blk"), lax.axis_index("expert")
    member = expert_index // groups
    meta = [ref[...].astype(F32) for ref in near_refs]
    mine = (2 * me + member).astype(F32)
    hits = [jnp.sum((part[:8] == mine).astype(F32), axis=0, keepdims=True) for part in meta]
    hit = jnp.concatenate(hits, axis=0)
    dest = jnp.concatenate([part[9:10] for part in meta], axis=0)
    before = (iota((tokens, tokens), 0) < iota((tokens, tokens), 1)).astype(BF16)
    rank = dot(hit, before)

    def row_of(col):
        inner = col % merged_rows
        return ((inner // row_share) ^ expert_index) * row_share + inner % row_share

    def place_of(col):
        return ((col // merged_rows) ^ me) * merged_rows + row_of(col)

    spread = (iota((128, rows), 0) == row_of(iota((128, rows), 1))).astype(F32)
    own_block = iota((blocks, rows), 1) // merged_rows == iota((blocks, rows), 0)
    dest_row = jnp.sum(jnp.where(own_block, dot(dest, spread), 0.0), axis=0, keepdims=True)
    dest_row = dest_row.astype(jnp.int32) ^ me
    dest_hit = (iota((blocks, rows), 0) == dest_row).astype(F32)
    rows_before = place_of(iota((rows, rows), 0)) < place_of(iota((rows, rows), 1))
    earlier = dot(dest_hit, rows_before.astype(F32))
    slot = jnp.sum(dest_hit * earlier, axis=0, keepdims=True).astype(jnp.int32)
    at_token = (iota((tokens, rows), 0) == slot).astype(F32)
    row_hit = jnp.sum(dest_hit * dot(hit, at_token), axis=0, keepdims=True)
    row_rank = jnp.sum(dest_hit * dot(rank, at_token), axis=0, keepdims=True).astype(jnp.int32)
    slot_id = (dest_row ^ me) * SLOTS + row_rank
    slot_count = slots_ref.shape[0]
    chosen = (iota((slot_count, rows), 0) == slot_id) & (row_hit > 0.5)
    slots_ref[...] = chosen.astype(F32).astype(BF16)
    placed = jnp.where(dest_row == 0, at_token, 0.0).astype(BF16)
    placed_ref[...] = placed

    pair_of = 2 * iota((blocks, tokens), 0) + member
    out_hit = jnp.zeros((blocks, tokens), F32)
    out_gate = jnp.zeros((blocks, tokens), F32)
    for k in range(routes_ref.shape[0]):
        same = pair_of == routes_ref[k : k + 1, :]
        out_hit = out_hit + same.astype(F32)
        out_gate = out_gate + jnp.where(same, gates_ref[k : k + 1, :], 0.0)
    out_rank = dot(out_hit, before)

    def expand(stride):
        count = blocks * stride
        pick = (iota((count, blocks), 0) // stride == iota((count, blocks), 1)).astype(BF16)
        gate = sum(dot(pick, piece) for piece in three(out_gate))
        return dot(pick, out_hit), dot(pick, out_rank).astype(jnp.int32), gate

    hits, ranks, gates = expand(SLOTS)
    live = jnp.where(ranks == iota(hits.shape, 0) % SLOTS, hits, 0.0)
    weight = live * gates
    high = weight.astype(BF16).astype(F32)
    part = tokens // share
    col = iota((tokens, tokens), 1)
    turned = (col // part * 0).astype(jnp.int32)
    for place, k in enumerate(halving_order(share)):
        turned = jnp.where(col // part == place, k, turned)
    turned = (iota((tokens, tokens), 0) == (turned ^ expert_index) * part + col % part)
    turned = turned.astype(F32)
    comb_ref[0] = dot(high, turned).astype(BF16)
    comb_ref[1] = dot(weight - high, turned).astype(BF16)

    hits, ranks, gates = expand(SEND)
    place = iota(hits.shape, 0) % SEND
    input_pick = jnp.where((place < CAPX) & (ranks == place), hits, 0.0)
    back_pick = jnp.where((place >= CAPX) & (place < 2 * CAPX) & (ranks == place - CAPX), hits, 0.0)
    back_gate = jnp.sum(back_pick * gates, axis=1, keepdims=True)
    send_rows = blocks * SEND
    source = iota((send_rows, rows), 0)
    kept = source % SEND - 2 * CAPX
    wanted = ((source // SEND) ^ me) * merged_rows + kept
    row_pick = (kept >= 0) & (kept < row_share) & (iota((send_rows, rows), 1) == wanted)
    cot_pick = dot_nt(row_pick.astype(F32).astype(BF16), placed)
    cot_row = iota((send_rows, 1), 0) % SEND >= 2 * CAPX
    factor = jnp.where(cot_row, 1.0, back_gate)
    text = text_ref[...].astype(F32)
    scale = lax.rsqrt(jnp.mean(text * text, axis=1, keepdims=True) + EPS)
    h_rows = (text * scale * gain_ref[...]).astype(BF16)
    send = dot(input_pick, h_rows) + factor * dot(back_pick + cot_pick, cot_ref[...])
    send_ref[...] = send.astype(BF16)


def flat_gain(gain_ref):
    return jnp.concatenate([gain_ref[h : h + 1] for h in range(gain_ref.shape[0])], axis=1)


def attend_kernel(*refs, blocks, share, row_share):
    query_ref, gain_ref, weight_ref = refs[:3]
    near_refs = refs[3 : 3 + blocks]
    merged_ref, *message_refs = refs[3 + blocks :]
    heads, size, patches = query_ref.shape
    rows, features = merged_ref.shape
    width = weight_ref.shape[1]
    depth = heads * size
    near = [ref[...].astype(F32) for ref in near_refs]
    key_ids = jnp.concatenate([part[2 * depth + 8 : 2 * depth + 9] for part in near], axis=1)
    eye = iota((patches, patches), 0) == iota((patches, patches), 1)
    own_ids = jnp.sum(jnp.where(eye, key_ids[:, :patches], 0.0), axis=1, keepdims=True)
    same = own_ids == key_ids
    spread = jnp.zeros((patches, features), F32)
    place_row, place_col = iota((size, features), 0), iota((size, features), 1)
    for head in range(heads):
        first = head * size
        keys = jnp.concatenate([part[first : first + size] for part in near], axis=1)
        first = depth + head * size
        values = jnp.concatenate([part[first : first + size] for part in near], axis=1)
        query = query_ref[head].astype(F32).T.astype(BF16)
        scores = dot(query, keys) * (size**-0.5)
        scores = jnp.where(same, scores, -1e30)
        weights = jnp.exp(scores - jnp.max(scores, axis=1, keepdims=True))
        total = jnp.sum(weights, axis=1, keepdims=True)
        attn = dot_nt(weights.astype(BF16), values.astype(BF16)) / total
        place = (place_col % size == place_row) & (place_col // (4 * size) == head)
        spread = spread + dot(attn, place.astype(F32))
    spot = iota((patches, features), 1) // size % 4 == iota((patches, features), 0) % 4
    line = iota((rows, patches), 0)
    line = ((line // row_share) ^ lax.axis_index("expert")) * row_share + line % row_share
    fold = (iota((rows, patches), 1) // 4 == line).astype(F32)
    merged = dot(fold, jnp.where(spot, spread, 0.0))
    merged_ref[...] = merged.astype(BF16)
    local_mean = jnp.sum(merged, axis=1, keepdims=True) / features
    centered = merged - local_mean
    squares = jnp.sum(centered * centered, axis=1, keepdims=True)
    gain = flat_gain(gain_ref)
    gain_high = gain.astype(BF16).astype(F32)
    extra = iota((8, features), 0)
    gain_rows = jnp.where(extra == 0, gain_high, jnp.where(extra == 1, gain - gain_high, 0.0))
    left = jnp.concatenate([centered * gain, gain_rows], axis=0)
    product = dot(left, weight_ref[...])
    gain_sum = product[rows : rows + 1] + product[rows + 1 : rows + 2]
    piece = width // row_share
    pieces = [gain_sum[:, j * piece : (j + 1) * piece] for j in range(row_share)]
    pieces = jnp.concatenate(pieces, axis=0).astype(BF16)
    scalars = put_scalars([local_mean, squares], rows).astype(BF16)
    for k in range(share):
        mine = slice(k * row_share, (k + 1) * row_share)
        message_refs[k][:, :width] = product[mine].astype(BF16)
        message_refs[k][:, width : width + piece] = pieces
        message_refs[k][:, width + piece :] = scalars[mine]


def merge_kernel(*refs, width, features):
    *message_refs, out_ref = refs
    share, row_share = len(message_refs), out_ref.shape[0]
    piece = width // row_share
    parts = [ref[...].astype(F32) for ref in message_refs]
    scalars = [part[:, width + piece :] for part in parts]
    means = [get_scalar(block, 0) for block in scalars]
    squares = [get_scalar(block, 1) for block in scalars]
    mean = sum(means) / share
    spread = sum(q + features * (m - mean) * (m - mean) for q, m in zip(squares, means))
    inv_std = lax.rsqrt(spread / (share * features) + EPS)
    total = jnp.zeros((row_share, width), F32)
    for part, local in zip(parts, means):
        tail = part[:, width : width + piece]
        gain_sum = jnp.concatenate([tail[j : j + 1] for j in range(row_share)], axis=1)
        total = total + part[:, :width] + (local - mean) * gain_sum
    out_ref[:, :width] = (total * inv_std).astype(BF16)
    out_ref[:, width:] = put_scalars([mean, inv_std], row_share).astype(BF16)


def stack_kernel(*refs):
    *part_refs, out_ref = refs
    out_ref[...] = stacked(part_refs)


def stacked(part_refs):
    return jnp.concatenate([ref[...].astype(F32) for ref in part_refs], axis=0).astype(BF16)


def slot_pick(slot_count, send_rows, shift):
    row, col = iota((slot_count, send_rows), 0), iota((slot_count, send_rows), 1)
    place = row % SLOTS
    pick = (col == row // SLOTS * SEND + place + shift) & (place < CAPX)
    return pick.astype(F32)


def forward_kernel(*refs, blocks):
    slots_ref, gain_ref, gate_ref, up_ref, down_ref, early_ref = refs[:6]
    vision_refs = refs[6 : 6 + blocks]
    gate_out, up_out, down_out, h_ref, sum_ref = refs[6 + blocks :]
    hidden, width = gate_ref.shape
    slot_count = slots_ref.shape[0]
    chosen = slots_ref[...]
    is_vision = jnp.sum(chosen.astype(F32), axis=1, keepdims=True) > 0.5
    vision = jnp.concatenate([ref[:, :width] for ref in vision_refs], axis=0)
    inputs = dot(chosen, vision)
    scale = lax.rsqrt(jnp.mean(inputs * inputs, axis=1, keepdims=True) + EPS)
    normed = inputs * scale * gain_ref[...]
    early = early_ref[...]
    text_rows = dot(slot_pick(slot_count, early.shape[0], 0), early)
    h_ref[...] = jnp.where(is_vision, normed, text_rows).astype(BF16)
    tile = tile_of(hidden)
    for i in range(hidden // tile):
        mine = slice(i * tile, (i + 1) * tile)
        gate_pre = dot_nt(h_ref[...], gate_ref[mine])
        up_proj = dot_nt(h_ref[...], up_ref[mine])
        gate_out[:, mine] = gate_pre
        up_out[:, mine] = up_proj
        activated = gate_pre * jax.nn.sigmoid(gate_pre) * up_proj
        product = dot(activated, down_ref[mine])
        sum_ref[...] = product if i == 0 else sum_ref[...] + product
    down_out[...] = sum_ref[...].astype(BF16)


def backward_kernel(
    slots_ref, early_ref, gate_in, up_in, gate_ref, up_ref, down_ref, even_ref, odd_ref,
    back_ref, sum_ref, *, blocks,
):
    hidden = gate_ref.shape[0]
    slot_count = slots_ref.shape[0]
    early = early_ref[...]
    back_ref[...] = dot(slot_pick(slot_count, early.shape[0], CAPX), early).astype(BF16)
    tile = tile_of(hidden)
    for i in range(hidden // tile):
        mine = slice(i * tile, (i + 1) * tile)
        act_grad = dot_nt(back_ref[...], down_ref[mine])
        gate_pre, up_proj = gate_in[:, mine], up_in[:, mine]
        sigmoid = jax.nn.sigmoid(gate_pre)
        gate_grad = act_grad * up_proj * sigmoid * (1.0 + gate_pre * (1.0 - sigmoid))
        up_grad = act_grad * gate_pre * sigmoid
        product = dot(gate_grad, gate_ref[mine]) + dot(up_grad, up_ref[mine])
        sum_ref[...] = product if i == 0 else sum_ref[...] + product
    grads = dot_tn(slots_ref[...], sum_ref[...].astype(BF16)).astype(BF16)
    rows = grads.shape[0] // blocks
    for k in range(blocks):
        to_ref = odd_ref if k % 2 else even_ref
        to_ref[k // 2 * rows : (k // 2 + 1) * rows] = grads[k * rows : (k + 1) * rows]


def tile_of(hidden):
    return 256 if hidden % 256 == 0 else hidden


def halving_order(share):
    order = [0]
    step = share // 2
    while step:
        order = order + [k + step for k in order]
        step //= 2
    return [sum(1 << j for j in range(share.bit_length() - 1) if k >> j & 1) for k in order]


def pair_sum_kernel(own_ref, sibling_ref, *out_refs):
    rows = out_refs[0].shape[0]
    for k, out_ref in enumerate(out_refs):
        mine = slice(k * rows, (k + 1) * rows)
        out_ref[...] = (own_ref[mine].astype(F32) + sibling_ref[mine].astype(F32)).astype(BF16)


def total_of(part_refs):
    total = part_refs[0][...].astype(F32)
    for ref in part_refs[1:]:
        total = total + ref[...].astype(F32)
    return total


def chip_sum_kernel(*refs, count):
    out_refs = refs[count:]
    total = total_of(refs[:count])
    rows = out_refs[0].shape[0]
    for k, out_ref in enumerate(out_refs):
        out_ref[...] = total[k * rows : (k + 1) * rows].astype(BF16)


def combine_kernel(comb_ref, rows_ref, keep_ref, send_ref):
    rows = rows_ref[...]
    total = dot_tn(comb_ref[0], rows) + dot_tn(comb_ref[1], rows)
    half = keep_ref.shape[0]
    keep_ref[...] = total[:half]
    send_ref[...] = total[half:].astype(BF16)


def halve_kernel(own_ref, arrived_ref, keep_ref, send_ref):
    total = own_ref[...] + arrived_ref[...].astype(F32)
    half = keep_ref.shape[0]
    keep_ref[...] = total[:half]
    send_ref[...] = total[half:].astype(BF16)


def finish_kernel(placed_ref, text_ref, own_ref, arrived_ref, *refs):
    *vision_refs, out_ref = refs
    count, width = out_ref.shape
    tokens = placed_ref.shape[0]
    first = lax.axis_index("expert") * count
    pick = iota((count, tokens), 1) == iota((count, tokens), 0) + first
    pick = pick.astype(F32)
    placed = dot(pick, placed_ref[...])
    is_vision = jnp.sum(placed, axis=1, keepdims=True) > 0.5
    vision = jnp.concatenate([ref[:, :width] for ref in vision_refs], axis=0)
    inputs = jnp.where(is_vision, dot(placed, vision), dot(pick, text_ref[...]))
    out_ref[...] = (inputs + own_ref[...] + arrived_ref[...].astype(F32)).astype(BF16)


def lay_kernel(*refs):
    *part_refs, out_ref = refs
    count = part_refs[0].shape[0]
    for k, ref in enumerate(part_refs):
        first = pl.multiple_of((lax.axis_index("expert") ^ k) * count, count)
        out_ref[pl.ds(first, count), :] = ref[...]


def norm_grad_kernel(own_ref, gain_ref, early_ref, *refs):
    *part_refs, out_ref = refs
    row_share, width = out_ref.shape
    hidden = total_of(part_refs)
    early = early_ref[...]
    send_rows = early.shape[0]
    pick = iota((row_share, send_rows), 1) % SEND == iota((row_share, send_rows), 0) + 2 * CAPX
    cotangent = dot(pick.astype(F32), early)
    inputs = own_ref[:, :width].astype(F32)
    scale = lax.rsqrt(jnp.mean(inputs * inputs, axis=1, keepdims=True) + EPS)
    pulled = hidden * gain_ref[...]
    cross = jnp.mean(pulled * inputs, axis=1, keepdims=True)
    grad = cotangent + scale * pulled - inputs * (scale * scale * scale) * cross
    out_ref[...] = grad.astype(BF16)


def merge_grad_kernel(*refs):
    gain_ref, merged_ref, scalar_ref, weight_ref, *part_refs = refs[:-2]
    out_ref, sums_ref = refs[-2:]
    width = weight_ref.shape[1]
    normed_grad = dot_nt(stacked(part_refs), weight_ref[...]) * flat_gain(gain_ref)
    out_ref[...] = normed_grad
    scalars = scalar_ref[:, width:].astype(F32)
    normed = (merged_ref[...].astype(F32) - get_scalar(scalars, 0)) * get_scalar(scalars, 1)
    first = jnp.sum(normed_grad, axis=1, keepdims=True)
    second = jnp.sum(normed_grad * normed, axis=1, keepdims=True)
    lane = iota(sums_ref.shape, 1)
    sums_ref[...] = jnp.where(lane == 0, first, jnp.where(lane == 1, second, 0.0))


def unfold_kernel(grad_ref, merged_ref, scalar_ref, *refs, size):
    *sums_refs, out_ref = refs
    rows, features = grad_ref.shape
    depth, patches = out_ref.shape
    share = len(sums_refs)
    row_share = rows // share
    sums = sums_refs[0][...]
    for k in range(1, share):
        theirs = [sums_refs[k][(j ^ k) * row_share : ((j ^ k) + 1) * row_share] for j in range(share)]
        sums = sums + jnp.concatenate(theirs, axis=0)
    sums = sums / (share * features)
    lane = iota(sums.shape, 1)
    grad_mean = jnp.sum(jnp.where(lane == 0, sums, 0.0), axis=1, keepdims=True)
    cross_mean = jnp.sum(jnp.where(lane == 1, sums, 0.0), axis=1, keepdims=True)
    scalars = scalar_ref[:, scalar_ref.shape[1] - 128 :].astype(F32)
    inv_std = get_scalar(scalars, 1)
    normed = (merged_ref[...].astype(F32) - get_scalar(scalars, 0)) * inv_std
    grad = inv_std * (grad_ref[...] - grad_mean - normed * cross_mean)
    high = grad.astype(BF16)
    low = (grad - high.astype(F32)).astype(BF16)
    line = iota((patches, rows), 1)
    line = ((line // row_share) ^ lax.axis_index("expert")) * row_share + line % row_share
    unfold = (iota((patches, rows), 0) // 4 == line).astype(F32)
    spot = iota((patches, features), 1) // size % 4 == iota((patches, features), 0) % 4
    row, col = iota((depth, features), 0), iota((depth, features), 1)
    place = (col // (4 * size) == row // size) & (col % size == row % size)
    place = place.astype(F32).astype(BF16)
    out = jnp.zeros((depth, patches), F32)
    for piece in (high, low):
        wide = jnp.where(spot, dot(unfold, piece), 0.0).astype(BF16)
        out = out + dot_nt(place, wide)
    out_ref[...] = out


def whole(memory_space=pltpu.VMEM):
    return pl.BlockSpec(memory_space=memory_space)


def run(kernel, outs, *args, far=(), scratch=(), cost=1.0, name=None):
    specs = [whole()] * len(args)
    for place in far:
        specs[place] = whole(pltpu.HBM)
    return pl.pallas_call(
        kernel,
        out_shape=outs,
        in_specs=specs,
        out_specs=jax.tree.map(lambda _: whole(), outs),
        scratch_shapes=scratch,
        compiler_params=pltpu.CompilerParams(vmem_limit_bytes=VMEM_BYTES),
        cost_estimate=microseconds(cost),
        name=name,
    )(*args)


def microseconds(time):
    return pl.CostEstimate(flops=0, transcendentals=0, bytes_accessed=int(time * 3e6))


def shape(dims, dtype=BF16):
    return jax.ShapeDtypeStruct(dims, dtype)


def swap(value, axis, step):
    count = lax.axis_size(axis)
    return lax.ppermute(value, axis, [(i, i ^ step) for i in range(count)])


def trade(parts, axis):
    return [parts[0]] + [swap(parts[k], axis, k) for k in range(1, len(parts))]


def spread_out(value, axis):
    return trade([value] * lax.axis_size(axis), axis)


def gather_blocks(value):
    near = {0: value}
    for k in range(2, lax.axis_size("blk"), 2):
        near[k] = swap(value, "blk", k)
    for k in list(near):
        near[k + 1] = swap(near[k], "blk", 1)
    return [near[k] for k in sorted(near)]


def hold(arrays, after=None, name=None):
    if after is not None:
        *arrays, _ = lax.optimization_barrier((*arrays, after))
    chunks = 3 if arrays[0].shape[0] % 48 == 0 else 1
    return run(
        hold_kernel, [shape(array.shape) for array in arrays], *arrays,
        far=tuple(range(len(arrays))),
        scratch=[pltpu.SemaphoreType.DMA((len(arrays), chunks))],
        cost=sum(array.size for array in arrays) / 1e6, name=name,
    )


def send_all(value, axis):
    return lax.all_to_all(value, axis, split_axis=0, concat_axis=0, tiled=True)


def body(
    queries, keys, values, image_ids, placement, merge_gain, merge_weight, text, norm_gain,
    w_gate, w_up, w_down, routes, route_gates, cotangent,
):
    blocks = lax.axis_size("blk")
    share = lax.axis_size("expert")
    heads, size, patches = queries.shape
    depth = heads * size
    rows = image_ids.shape[0]
    row_share = rows // share
    tokens, width = text.shape
    part = tokens // share
    all_rows = blocks * rows
    features = heads * 4 * size
    hidden = w_gate.shape[1]
    slot_count = blocks * SLOTS
    groups = share // 2
    routes_t, gates_t, gain_row = routes.T, route_gates.T, norm_gain[None]

    small = [
        keys.reshape(depth, patches), values.reshape(depth, patches),
        image_ids[None], placement.reshape(1, rows), routes_t,
    ]
    local = run(
        pack_kernel, shape((2 * depth + 16, patches)), *small, far=range(5),
        scratch=[pltpu.VMEM(array.shape, array.dtype) for array in small]
        + [pltpu.SemaphoreType.DMA((5,))],
        name="pack",
    )
    near = gather_blocks(local)
    weight_flat = merge_weight.reshape(features, width)
    (weight_near,) = hold([weight_flat], name="hold_merge")

    message_width = width + width // row_share + 128
    merged, *message = run(
        functools.partial(attend_kernel, blocks=blocks, share=share, row_share=row_share),
        [shape((rows, features))] + [shape((row_share, message_width))] * share,
        queries, merge_gain, weight_near, *near, cost=4.0, name="attend",
    )

    def fixed(*dims):
        return pl.BlockSpec(dims, lambda i: (0,) * len(dims))

    meta_spec = pl.BlockSpec((16, patches), lambda i: (2 * depth // 16, 0))
    plan_outs = [
        shape((slot_count, all_rows)), shape((tokens, all_rows)), shape((2, slot_count, tokens)),
        shape((blocks * SEND, width)),
    ]
    slots, placed, comb, send = pl.pallas_call(
        functools.partial(
            plan_kernel, blocks=blocks, groups=groups, merged_rows=rows, row_share=row_share
        ),
        grid=(1,),
        in_specs=[meta_spec] * blocks
        + [
            fixed(*routes_t.shape), fixed(*gates_t.shape), fixed(tokens, width), fixed(1, width),
            fixed(tokens, width), whole(pl.ANY),
        ],
        out_specs=[fixed(*out.shape) for out in plan_outs],
        out_shape=plan_outs,
        compiler_params=pltpu.CompilerParams(vmem_limit_bytes=VMEM_BYTES),
        cost_estimate=microseconds(2.0),
        name="plan",
    )(*near, routes_t, gates_t, text, gain_row, cotangent, merged)
    early = send_all(send.reshape(blocks, SEND, width), "blk").reshape(blocks * SEND, width)

    message = trade(message, "expert")
    own = run(
        functools.partial(merge_kernel, width=width, features=features),
        shape((row_share, width + 128)), *message, cost=0.2, name="merge",
    )
    block_rows = run(
        stack_kernel, shape((rows, width + 128)), *spread_out(own, "expert"), cost=0.2, name="stack"
    )
    vision = gather_blocks(block_rows)
    gate_near, up_near, down_near = hold(
        [w_gate[0], w_up[0], w_down[0]], after=own, name="hold_experts"
    )

    gate_pre, up_proj, down = run(
        functools.partial(forward_kernel, blocks=blocks),
        [
            shape((slot_count, hidden), F32), shape((slot_count, hidden), F32),
            shape((slot_count, width)),
        ],
        slots, gain_row, gate_near, up_near, down_near, early, *vision,
        scratch=[pltpu.VMEM((slot_count, width), BF16), pltpu.VMEM((slot_count, width), F32)],
        cost=5.0, name="forward",
    )
    returned = send_all(down.reshape(blocks, SLOTS, width), "blk").reshape(slot_count, width)
    even, odd = run(
        functools.partial(backward_kernel, blocks=blocks),
        [shape((all_rows // 2, width))] * 2,
        slots, early, gate_pre, up_proj, gate_near, up_near, down_near,
        scratch=[pltpu.VMEM((slot_count, width), BF16), pltpu.VMEM((slot_count, width), F32)],
        cost=5.0, name="backward",
    )
    grads = run(
        pair_sum_kernel, [shape((rows, width))] * (blocks // 2), even, swap(odd, "blk", 1),
        cost=0.2, name="pair_sum",
    )
    grads = [grads[0]] + [swap(grads[k], "blk", 2 * k) for k in range(1, blocks // 2)]
    grads = run(
        functools.partial(chip_sum_kernel, count=blocks // 2),
        [shape((row_share, width))] * share, *grads, cost=0.2, name="chip_sum",
    )
    grads = trade(grads, "expert")
    vision_grad = run(
        norm_grad_kernel, shape((row_share, width)), own, gain_row, early, *grads,
        cost=0.3, name="norm_grad",
    )
    (weight_again,) = hold([weight_flat], after=down, name="hold_merge_again")
    normed_grad, sums = run(
        merge_grad_kernel,
        [shape((rows, features), F32), shape((rows, 128), F32)],
        merge_gain, merged, block_rows, weight_again, *spread_out(vision_grad, "expert"),
        cost=2.5, name="merge_grad",
    )
    sums = spread_out(sums, "expert")

    count = tokens // 2
    kept, sent = run(
        combine_kernel, [shape((count, width), F32), shape((count, width))], comb, returned,
        cost=0.5, name="combine",
    )
    step = 1
    while count > part:
        count //= 2
        kept, sent = run(
            halve_kernel, [shape((count, width), F32), shape((count, width))],
            kept, swap(sent, "expert", step), cost=0.3, name="halve",
        )
        step *= 2
    finished = run(
        finish_kernel, shape((part, width)),
        placed, text, kept, swap(sent, "expert", step), *vision, cost=1.0, name="finish",
    )
    laid = {0: finished}
    while step:
        laid.update({k + step: swap(laid[k], "expert", step) for k in list(laid)})
        step //= 2
    llm_out = run(
        lay_kernel, shape((tokens, width)), *[laid[k] for k in sorted(laid)], cost=1.0, name="lay"
    )
    attn_grad = run(
        functools.partial(unfold_kernel, size=size), shape((depth, patches), F32),
        normed_grad, merged, block_rows, *sums, cost=2.0, name="unfold",
    )
    return llm_out, attn_grad.reshape(heads, size, patches)


def solution(mesh):
    return jax.shard_map(
        body,
        mesh=mesh,
        in_specs=(
            P("expert", None, "blk"),
            P("expert", None, "blk"),
            P("expert", None, "blk"),
            P("blk"),
            P("blk", None),
            P("expert", None),
            P("expert", None, None),
            P("blk", None),
            P(),
            P("blk", "expert", None),
            P("blk", "expert", None),
            P("blk", "expert", None),
            P("blk", None),
            P("blk", None),
            P("blk", None),
        ),
        out_specs=(P("blk", None), P("expert", None, "blk")),
        check_vma=False,
    )
```

```python
import functools

import jax
import jax.numpy as jnp
from jax import lax
from jax.experimental import pallas as pl
from jax.experimental.pallas import tpu as pltpu
from jax.sharding import PartitionSpec as P

CAPX = 10
SLOTS = 16
SEND = 24
EPS = 1e-06
VMEM_BYTES = 16 * 1024 * 1024
PACK_BYTES = 60 * 1024 * 1024
ATTEND_BYTES = 58 * 1024 * 1024
F32 = jnp.float32
BF16 = jnp.bfloat16


def iota(shape, dim):
    return lax.broadcasted_iota(jnp.int32, shape, dim)


def dot(a, b):
    return jnp.dot(a.astype(BF16), b.astype(BF16), preferred_element_type=F32)


def dot_nt(a, b):
    return lax.dot_general(a, b, (((1,), (1,)), ((), ())), preferred_element_type=F32)


def dot_tn(a, b):
    return lax.dot_general(a, b, (((0,), (0,)), ((), ())), preferred_element_type=F32)


def three(value):
    first = value.astype(BF16).astype(F32)
    second = (value - first).astype(BF16).astype(F32)
    return first, second, value - first - second


def put_scalars(columns, rows):
    lane = iota((rows, 128), 1)
    out = jnp.zeros((rows, 128), F32)
    place = 0
    for column in columns:
        for piece in three(column):
            out = jnp.where(lane == place, piece, out)
            place += 1
    return out


def get_scalar(block, which):
    lane = iota(block.shape, 1)
    return jnp.sum(jnp.where(lane // 3 == which, block, 0.0), axis=1, keepdims=True)


def pack_kernel(*refs):
    far_refs, out_ref, near_refs, sems = refs[:5], refs[5], refs[6:11], refs[11]
    copies = [
        pltpu.make_async_copy(far, near, sems.at[i])
        for i, (far, near) in enumerate(zip(far_refs, near_refs))
    ]
    for copy in copies:
        copy.start()
    for copy in copies:
        copy.wait()
    keys_ref, values_ref, images_ref, placement_ref, routes_ref = near_refs
    rows = images_ref.shape[1]
    patches = keys_ref.shape[1]
    repeat = (iota((rows, patches), 0) == iota((rows, patches), 1) // 4).astype(F32)
    keep = (iota((rows, patches), 0) == iota((rows, patches), 1)).astype(F32)
    patch_ids = dot(images_ref[...].astype(F32), repeat)
    dest = dot(placement_ref[...].astype(F32), keep)
    line = iota((8, patches), 0)
    rest = jnp.where(line == 0, patch_ids, jnp.where(line == 1, dest, 0.0))
    parts = [keys_ref[...], values_ref[...], routes_ref[...], rest]
    out_ref[...] = jnp.concatenate([part.astype(F32) for part in parts], axis=0).astype(BF16)


def route_kernel(routes_ref, gates_ref, comb_ref, pick_ref, factor_ref, *, groups, share):
    blocks = comb_ref.shape[1] // SLOTS
    tokens = routes_ref.shape[1]
    me, expert_index = lax.axis_index("blk"), lax.axis_index("expert")
    member = expert_index // groups
    before = (iota((tokens, tokens), 0) < iota((tokens, tokens), 1)).astype(BF16)
    pair_of = 2 * (iota((blocks, tokens), 0) ^ me) + member
    out_hit = jnp.zeros((blocks, tokens), F32)
    out_gate = jnp.zeros((blocks, tokens), F32)
    for k in range(routes_ref.shape[0]):
        same = pair_of == routes_ref[k : k + 1, :]
        out_hit = out_hit + same.astype(F32)
        out_gate = out_gate + jnp.where(same, gates_ref[k : k + 1, :], 0.0)
    out_rank = dot(out_hit, before)

    def expand(stride):
        count = blocks * stride
        pick = (iota((count, blocks), 0) // stride == iota((count, blocks), 1)).astype(BF16)
        gate = sum(dot(pick, piece) for piece in three(out_gate))
        return dot(pick, out_hit), dot(pick, out_rank).astype(jnp.int32), gate

    hits, ranks, gates = expand(SLOTS)
    live = jnp.where(ranks == iota(hits.shape, 0) % SLOTS, hits, 0.0)
    weight = live * gates
    high = weight.astype(BF16).astype(F32)
    part = tokens // share
    col = iota((tokens, tokens), 1)
    turned = (col // part * 0).astype(jnp.int32)
    for place, k in enumerate(halving_order(share)):
        turned = jnp.where(col // part == place, k, turned)
    turned = (iota((tokens, tokens), 0) == (turned ^ expert_index) * part + col % part)
    turned = turned.astype(F32)
    comb_ref[0] = dot(high, turned).astype(BF16)
    comb_ref[1] = dot(weight - high, turned).astype(BF16)

    hits, ranks, gates = expand(SEND)
    place = iota(hits.shape, 0) % SEND
    input_pick = jnp.where((place < CAPX) & (ranks == place), hits, 0.0)
    back_pick = jnp.where((place >= CAPX) & (place < 2 * CAPX) & (ranks == place - CAPX), hits, 0.0)
    pick_ref[0] = input_pick.astype(BF16)
    pick_ref[1] = back_pick.astype(BF16)
    factor = jnp.sum(back_pick * gates, axis=1, keepdims=True)
    factor_ref[...] = jnp.broadcast_to(factor, factor_ref.shape)


def dispatch_kernel(pick_ref, factor_ref, text_ref, gain_ref, cot_ref, *send_refs):
    text = text_ref[...].astype(F32)
    scale = lax.rsqrt(jnp.mean(text * text, axis=1, keepdims=True) + EPS)
    h_rows = (text * scale * gain_ref[...]).astype(BF16)
    factor = factor_ref[:, :1]
    send = dot(pick_ref[0], h_rows) + factor * dot(pick_ref[1], cot_ref[...])
    send = send.astype(BF16)
    count = 2 * SEND
    for k, ref in enumerate(send_refs):
        ref[...] = send[k * count : (k + 1) * count]


def plan_kernel(
    meta_ref, cot_ref, slots_ref, placed_ref, back_ref, *, blocks, groups, merged_rows, row_share
):
    tokens = cot_ref.shape[0]
    rows = blocks * merged_rows
    me, expert_index = lax.axis_index("blk"), lax.axis_index("expert")
    member = expert_index // groups
    meta = [meta_ref[k * 16 : (k + 1) * 16].astype(F32) for k in range(blocks)]
    mine = (2 * me + member).astype(F32)
    hits = [jnp.sum((part[:8] == mine).astype(F32), axis=0, keepdims=True) for part in meta]
    hit = jnp.concatenate(hits, axis=0)
    dest = jnp.concatenate([part[9:10] for part in meta], axis=0)
    before = (iota((tokens, tokens), 0) < iota((tokens, tokens), 1)).astype(BF16)
    rank = dot(hit, before)

    def row_of(col):
        inner = col % merged_rows
        return ((inner // row_share) ^ expert_index) * row_share + inner % row_share

    def place_of(col):
        return ((col // merged_rows) ^ me) * merged_rows + row_of(col)

    spread = (iota((128, rows), 0) == row_of(iota((128, rows), 1))).astype(F32)
    own_block = iota((blocks, rows), 1) // merged_rows == iota((blocks, rows), 0)
    dest_row = jnp.sum(jnp.where(own_block, dot(dest, spread), 0.0), axis=0, keepdims=True)
    dest_row = dest_row.astype(jnp.int32) ^ me
    dest_hit = (iota((blocks, rows), 0) == dest_row).astype(F32)
    rows_before = place_of(iota((rows, rows), 0)) < place_of(iota((rows, rows), 1))
    earlier = dot(dest_hit, rows_before.astype(F32))
    slot = jnp.sum(dest_hit * earlier, axis=0, keepdims=True).astype(jnp.int32)
    at_token = (iota((tokens, rows), 0) == slot).astype(F32)
    row_hit = jnp.sum(dest_hit * dot(hit, at_token), axis=0, keepdims=True)
    row_rank = jnp.sum(dest_hit * dot(rank, at_token), axis=0, keepdims=True).astype(jnp.int32)
    slot_id = dest_row * SLOTS + row_rank
    slot_count = slots_ref.shape[0]
    chosen = (iota((slot_count, rows), 0) == slot_id) & (row_hit > 0.5)
    slots_ref[...] = chosen.astype(F32).astype(BF16)
    placed = jnp.where(dest_row == 0, at_token, 0.0).astype(BF16)
    placed_ref[...] = placed
    back_rows = blocks * row_share
    source = iota((back_rows, rows), 0)
    wanted = source // row_share * merged_rows + source % row_share
    row_pick = (iota((back_rows, rows), 1) == wanted).astype(F32).astype(BF16)
    back_ref[...] = dot(dot_nt(row_pick, placed), cot_ref[...]).astype(BF16)


def flat_gain(gain_ref):
    return jnp.concatenate([gain_ref[h : h + 1] for h in range(gain_ref.shape[0])], axis=1)


def attend_kernel(*refs, blocks, share, row_share):
    query_ref, gain_ref, weight_ref = refs[:3]
    near_refs = refs[3 : 3 + blocks]
    merged_ref, meta_ref, *message_refs = refs[3 + blocks : 5 + blocks + share]
    near_weight_ref, sems = refs[5 + blocks + share :]
    chunk = weight_ref.shape[0] // sems.shape[0]
    copies = []
    for i in range(sems.shape[0]):
        mine = pl.ds(i * chunk, chunk)
        copies.append(
            pltpu.make_async_copy(weight_ref.at[mine], near_weight_ref.at[mine], sems.at[i])
        )
        copies[-1].start()
    heads, size, patches = query_ref.shape
    rows, features = merged_ref.shape
    width = weight_ref.shape[1]
    depth = heads * size
    near = [ref[...].astype(F32) for ref in near_refs]
    meta_ref[...] = jnp.concatenate([part[2 * depth :] for part in near], axis=0).astype(BF16)
    key_ids = jnp.concatenate([part[2 * depth + 8 : 2 * depth + 9] for part in near], axis=1)
    eye = iota((patches, patches), 0) == iota((patches, patches), 1)
    own_ids = jnp.sum(jnp.where(eye, key_ids[:, :patches], 0.0), axis=1, keepdims=True)
    same = own_ids == key_ids
    spread = jnp.zeros((patches, features), F32)
    place_row, place_col = iota((size, features), 0), iota((size, features), 1)
    for head in range(heads):
        first = head * size
        keys = jnp.concatenate([part[first : first + size] for part in near], axis=1)
        first = depth + head * size
        values = jnp.concatenate([part[first : first + size] for part in near], axis=1)
        query = query_ref[head].astype(F32).T.astype(BF16)
        scores = dot(query, keys) * (size**-0.5)
        scores = jnp.where(same, scores, -1e30)
        weights = jnp.exp(scores - jnp.max(scores, axis=1, keepdims=True))
        total = jnp.sum(weights, axis=1, keepdims=True)
        attn = dot_nt(weights.astype(BF16), values.astype(BF16)) / total
        place = (place_col % size == place_row) & (place_col // (4 * size) == head)
        spread = spread + dot(attn, place.astype(F32))
    spot = iota((patches, features), 1) // size % 4 == iota((patches, features), 0) % 4
    line = iota((rows, patches), 0)
    line = ((line // row_share) ^ lax.axis_index("expert")) * row_share + line % row_share
    fold = (iota((rows, patches), 1) // 4 == line).astype(F32)
    merged = dot(fold, jnp.where(spot, spread, 0.0))
    merged_ref[...] = merged.astype(BF16)
    local_mean = jnp.sum(merged, axis=1, keepdims=True) / features
    centered = merged - local_mean
    squares = jnp.sum(centered * centered, axis=1, keepdims=True)
    gain = flat_gain(gain_ref)
    gain_high = gain.astype(BF16).astype(F32)
    extra = iota((8, features), 0)
    gain_rows = jnp.where(extra == 0, gain_high, jnp.where(extra == 1, gain - gain_high, 0.0))
    left = jnp.concatenate([centered * gain, gain_rows], axis=0)
    for copy in copies:
        copy.wait()
    product = dot(left, near_weight_ref[...])
    gain_sum = product[rows : rows + 1] + product[rows + 1 : rows + 2]
    piece = width // row_share
    pieces = [gain_sum[:, j * piece : (j + 1) * piece] for j in range(row_share)]
    pieces = jnp.concatenate(pieces, axis=0).astype(BF16)
    scalars = put_scalars([local_mean, squares], rows).astype(BF16)
    for k in range(share):
        mine = slice(k * row_share, (k + 1) * row_share)
        message_refs[k][:, :width] = product[mine].astype(BF16)
        message_refs[k][:, width : width + piece] = pieces
        message_refs[k][:, width + piece :] = scalars[mine]


def merge_kernel(*refs, width, features):
    *message_refs, out_ref = refs
    share, row_share = len(message_refs), out_ref.shape[0]
    piece = width // row_share
    parts = [ref[...].astype(F32) for ref in message_refs]
    scalars = [part[:, width + piece :] for part in parts]
    means = [get_scalar(block, 0) for block in scalars]
    squares = [get_scalar(block, 1) for block in scalars]
    mean = sum(means) / share
    spread = sum(q + features * (m - mean) * (m - mean) for q, m in zip(squares, means))
    inv_std = lax.rsqrt(spread / (share * features) + EPS)
    total = jnp.zeros((row_share, width), F32)
    for part, local in zip(parts, means):
        tail = part[:, width : width + piece]
        gain_sum = jnp.concatenate([tail[j : j + 1] for j in range(row_share)], axis=1)
        total = total + part[:, :width] + (local - mean) * gain_sum
    out_ref[:, :width] = (total * inv_std).astype(BF16)
    out_ref[:, width:] = put_scalars([mean, inv_std], row_share).astype(BF16)


def stack_kernel(_, *refs):
    *part_refs, out_ref = refs
    out_ref[...] = stacked(part_refs)


def stacked(part_refs):
    return jnp.concatenate([ref[...].astype(F32) for ref in part_refs], axis=0).astype(BF16)


def by_chip(own_refs, sibling_ref):
    parts = []
    sibling = sibling_ref[...].astype(F32)
    for k, own_ref in enumerate(own_refs):
        half = own_ref.shape[0] // 2
        parts.append(own_ref[...].astype(F32)[:half])
        parts.append(sibling[k * half : (k + 1) * half])
    return jnp.concatenate(parts, axis=0).astype(BF16)


def other_half_kernel(*refs, count):
    out_ref = refs[-1]
    parts = [ref[...].astype(F32)[ref.shape[0] // 2 :] for ref in refs[:count]]
    out_ref[...] = jnp.concatenate(parts, axis=0).astype(BF16)


def slot_pick(slot_count, send_rows, shift):
    row, col = iota((slot_count, send_rows), 0), iota((slot_count, send_rows), 1)
    place = row % SLOTS
    pick = (col == row // SLOTS * SEND + place + shift) & (place < CAPX)
    return pick.astype(F32)


def early_kernel(down_ref, *refs):
    *early_refs, sibling_ref, text_out, grad_out = refs
    slot_count = text_out.shape[0]
    early = by_chip(early_refs, sibling_ref)
    text_out[...] = dot(slot_pick(slot_count, early.shape[0], 0), early).astype(BF16)
    back_rows = dot(slot_pick(slot_count, early.shape[0], CAPX), early).astype(BF16)
    grad_out[...] = dot_nt(back_rows, down_ref[0])


def forward_kernel(*refs, blocks):
    slots_ref, gain_ref, gate_ref, up_ref, down_ref, text_ref = refs[:6]
    vision_refs = refs[6 : 6 + blocks]
    gate_out, up_out, *down_refs = refs[6 + blocks : -2]
    h_ref, sum_ref = refs[-2:]
    _, hidden, width = gate_ref.shape
    chosen = slots_ref[...]
    is_vision = jnp.sum(chosen.astype(F32), axis=1, keepdims=True) > 0.5
    vision = jnp.concatenate([ref[:, :width] for ref in vision_refs], axis=0)
    inputs = dot(chosen, vision)
    scale = lax.rsqrt(jnp.mean(inputs * inputs, axis=1, keepdims=True) + EPS)
    normed = inputs * scale * gain_ref[...]
    h_ref[...] = jnp.where(is_vision, normed, text_ref[...].astype(F32)).astype(BF16)
    tile = tile_of(hidden)
    for i in range(hidden // tile):
        mine = slice(i * tile, (i + 1) * tile)
        gate_pre = dot_nt(h_ref[...], gate_ref[0, mine])
        up_proj = dot_nt(h_ref[...], up_ref[0, mine])
        gate_out[:, mine] = gate_pre
        up_out[:, mine] = up_proj
        activated = gate_pre * jax.nn.sigmoid(gate_pre) * up_proj
        product = dot(activated, down_ref[0, mine])
        sum_ref[...] = product if i == 0 else sum_ref[...] + product
    count = 2 * SLOTS
    for k, ref in enumerate(down_refs):
        ref[...] = sum_ref[k * count : (k + 1) * count].astype(BF16)


def backward_kernel(
    slots_ref, grad_ref, gate_in, up_in, cot_ref, gate_ref, up_ref, even_ref, odd_ref, sum_ref,
    *, blocks,
):
    hidden = gate_ref.shape[1]
    tile = tile_of(hidden)
    for i in range(hidden // tile):
        mine = slice(i * tile, (i + 1) * tile)
        act_grad = grad_ref[:, mine]
        gate_pre, up_proj = gate_in[:, mine], up_in[:, mine]
        sigmoid = jax.nn.sigmoid(gate_pre)
        gate_grad = act_grad * up_proj * sigmoid * (1.0 + gate_pre * (1.0 - sigmoid))
        up_grad = act_grad * gate_pre * sigmoid
        product = dot(gate_grad, gate_ref[0, mine]) + dot(up_grad, up_ref[0, mine])
        sum_ref[...] = product if i == 0 else sum_ref[...] + product
    grads = dot_tn(slots_ref[...], sum_ref[...].astype(BF16))
    cots = cot_ref[...].astype(F32)
    rows, row_share = grads.shape[0] // blocks, cots.shape[0] // blocks
    parts = ([], [])
    for k in range(blocks):
        parts[k % 2].append(grads[k * rows : (k + 1) * rows])
        parts[k % 2].append(cots[k * row_share : (k + 1) * row_share])
    even_ref[...] = jnp.concatenate(parts[0], axis=0).astype(BF16)
    odd_ref[...] = jnp.concatenate(parts[1], axis=0).astype(BF16)


def tile_of(hidden):
    return 256 if hidden % 256 == 0 else hidden


def halving_order(share):
    order = [0]
    step = share // 2
    while step:
        order = order + [k + step for k in order]
        step //= 2
    return [sum(1 << j for j in range(share.bit_length() - 1) if k >> j & 1) for k in order]


def pair_sum_kernel(own_ref, sibling_ref, *out_refs):
    rows = out_refs[0].shape[0]
    total = own_ref[...].astype(F32) + sibling_ref[...].astype(F32)
    for k, out_ref in enumerate(out_refs):
        out_ref[...] = total[k * rows : (k + 1) * rows].astype(BF16)


def total_of(part_refs):
    total = part_refs[0][...].astype(F32)
    for ref in part_refs[1:]:
        total = total + ref[...].astype(F32)
    return total


def chip_sum_kernel(*refs, count):
    cot_ref, *out_refs = refs[count:]
    total = total_of(refs[:count])
    rows = cot_ref.shape[0]
    for k, out_ref in enumerate(out_refs):
        out_ref[...] = total[k * rows : (k + 1) * rows].astype(BF16)
    cot_ref[...] = total[len(out_refs) * rows :].astype(BF16)


def combine_kernel(comb_ref, *refs):
    *part_refs, sibling_ref, keep_ref, send_ref = refs
    rows = by_chip(part_refs, sibling_ref)
    total = dot_tn(comb_ref[0], rows) + dot_tn(comb_ref[1], rows)
    half = keep_ref.shape[0]
    keep_ref[...] = total[:half]
    send_ref[...] = total[half:].astype(BF16)


def halve_kernel(own_ref, arrived_ref, _, keep_ref, send_ref):
    total = own_ref[...] + arrived_ref[...].astype(F32)
    half = keep_ref.shape[0]
    keep_ref[...] = total[:half]
    send_ref[...] = total[half:].astype(BF16)


def finish_kernel(placed_ref, text_ref, own_ref, arrived_ref, *refs):
    *vision_refs, _, out_ref = refs
    count, width = out_ref.shape
    tokens = placed_ref.shape[0]
    first = lax.axis_index("expert") * count
    pick = iota((count, tokens), 1) == iota((count, tokens), 0) + first
    pick = pick.astype(F32)
    placed = dot(pick, placed_ref[...])
    is_vision = jnp.sum(placed, axis=1, keepdims=True) > 0.5
    vision = jnp.concatenate([ref[:, :width] for ref in vision_refs], axis=0)
    inputs = jnp.where(is_vision, dot(placed, vision), dot(pick, text_ref[...]))
    out_ref[...] = (inputs + own_ref[...] + arrived_ref[...].astype(F32)).astype(BF16)


def lay_kernel(*refs):
    *part_refs, out_ref = refs
    count = part_refs[0].shape[0]
    for k, ref in enumerate(part_refs):
        first = pl.multiple_of((lax.axis_index("expert") ^ k) * count, count)
        out_ref[pl.ds(first, count), :] = ref[...]


def norm_grad_kernel(own_ref, gain_ref, cot_ref, *refs):
    *part_refs, out_ref = refs
    width = out_ref.shape[1]
    hidden = total_of(part_refs)
    cotangent = cot_ref[...].astype(F32)
    inputs = own_ref[:, :width].astype(F32)
    scale = lax.rsqrt(jnp.mean(inputs * inputs, axis=1, keepdims=True) + EPS)
    pulled = hidden * gain_ref[...]
    cross = jnp.mean(pulled * inputs, axis=1, keepdims=True)
    grad = cotangent + scale * pulled - inputs * (scale * scale * scale) * cross
    out_ref[...] = grad.astype(BF16)


def merge_grad_kernel(*refs):
    gain_ref, merged_ref, scalar_ref, weight_ref, *part_refs = refs[:-2]
    out_ref, sums_ref = refs[-2:]
    width = weight_ref.shape[1]
    normed_grad = dot_nt(stacked(part_refs), weight_ref[...]) * flat_gain(gain_ref)
    out_ref[...] = normed_grad
    scalars = scalar_ref[:, width:].astype(F32)
    normed = (merged_ref[...].astype(F32) - get_scalar(scalars, 0)) * get_scalar(scalars, 1)
    first = jnp.sum(normed_grad, axis=1, keepdims=True)
    second = jnp.sum(normed_grad * normed, axis=1, keepdims=True)
    lane = iota(sums_ref.shape, 1)
    sums_ref[...] = jnp.where(lane == 0, first, jnp.where(lane == 1, second, 0.0))


def unfold_kernel(grad_ref, merged_ref, scalar_ref, *refs, size):
    *sums_refs, out_ref = refs
    rows, features = grad_ref.shape
    depth, patches = out_ref.shape
    share = len(sums_refs)
    row_share = rows // share
    sums = sums_refs[0][...]
    for k in range(1, share):
        theirs = [sums_refs[k][(j ^ k) * row_share : ((j ^ k) + 1) * row_share] for j in range(share)]
        sums = sums + jnp.concatenate(theirs, axis=0)
    sums = sums / (share * features)
    lane = iota(sums.shape, 1)
    grad_mean = jnp.sum(jnp.where(lane == 0, sums, 0.0), axis=1, keepdims=True)
    cross_mean = jnp.sum(jnp.where(lane == 1, sums, 0.0), axis=1, keepdims=True)
    scalars = scalar_ref[:, scalar_ref.shape[1] - 128 :].astype(F32)
    inv_std = get_scalar(scalars, 1)
    normed = (merged_ref[...].astype(F32) - get_scalar(scalars, 0)) * inv_std
    grad = inv_std * (grad_ref[...] - grad_mean - normed * cross_mean)
    high = grad.astype(BF16)
    low = (grad - high.astype(F32)).astype(BF16)
    line = iota((patches, rows), 1)
    line = ((line // row_share) ^ lax.axis_index("expert")) * row_share + line % row_share
    unfold = (iota((patches, rows), 0) // 4 == line).astype(F32)
    spot = iota((patches, features), 1) // size % 4 == iota((patches, features), 0) % 4
    row, col = iota((depth, features), 0), iota((depth, features), 1)
    place = (col // (4 * size) == row // size) & (col % size == row % size)
    place = place.astype(F32).astype(BF16)
    out = jnp.zeros((depth, patches), F32)
    for piece in (high, low):
        wide = jnp.where(spot, dot(unfold, piece), 0.0).astype(BF16)
        out = out + dot_nt(place, wide)
    out_ref[...] = out


def whole(memory_space=pltpu.VMEM):
    return pl.BlockSpec(memory_space=memory_space)


def run(kernel, outs, *args, far=(), scratch=(), cost=1.0, vmem=VMEM_BYTES, name=None):
    specs = [whole()] * len(args)
    for place in far:
        specs[place] = whole(pl.ANY)
    return pl.pallas_call(
        kernel,
        out_shape=outs,
        in_specs=specs,
        out_specs=jax.tree.map(lambda _: whole(), outs),
        scratch_shapes=scratch,
        compiler_params=pltpu.CompilerParams(vmem_limit_bytes=vmem),
        cost_estimate=microseconds(cost),
        name=name,
    )(*args)


def to_sibling(parts, deps, name):
    rows, width = parts[0].shape
    half = run(
        functools.partial(other_half_kernel, count=len(parts)),
        shape((len(parts) * rows // 2, width)), *parts, *deps,
        far=range(len(parts), len(parts) + len(deps)), cost=0.3, name=name,
    )
    return swap(half, "blk", 1)


def microseconds(time):
    return pl.CostEstimate(flops=0, transcendentals=0, bytes_accessed=int(time * 3e6))


def after(values, deps):
    count = len(values)
    return pl.pallas_call(
        lambda *refs: None,
        out_shape=[shape(value.shape, value.dtype) for value in values],
        in_specs=[whole(pl.ANY)] * (count + len(deps)),
        out_specs=[whole(pl.ANY)] * count,
        input_output_aliases={i: i for i in range(count)},
        compiler_params=pltpu.CompilerParams(vmem_limit_bytes=VMEM_BYTES),
        cost_estimate=microseconds(0.1),
        name="after",
    )(*values, *deps)


def shape(dims, dtype=BF16):
    return jax.ShapeDtypeStruct(dims, dtype)


def swap(value, axis, step):
    count = lax.axis_size(axis)
    return lax.ppermute(value, axis, [(i, i ^ step) for i in range(count)])


def trade(parts, axis):
    return [parts[0]] + [swap(parts[k], axis, k) for k in range(1, len(parts))]


def spread_out(value, axis):
    return trade([value] * lax.axis_size(axis), axis)


def gather_blocks(value, deps=None):
    own = [value] + [swap(value, "blk", k) for k in range(2, lax.axis_size("blk"), 2)]
    if deps is not None:
        own = own[:1] + list(after(own[1:], deps))
    sibling = [swap(part, "blk", 1) for part in own]
    return [part for pair in zip(own, sibling) for part in pair]


def to_chips(parts):
    return [parts[0]] + [swap(parts[k], "blk", 2 * k) for k in range(1, len(parts))]


def body(
    queries, keys, values, image_ids, placement, merge_gain, merge_weight, text, norm_gain,
    w_gate, w_up, w_down, routes, route_gates, cotangent,
):
    blocks = lax.axis_size("blk")
    share = lax.axis_size("expert")
    heads, size, patches = queries.shape
    depth = heads * size
    rows = image_ids.shape[0]
    row_share = rows // share
    tokens, width = text.shape
    part = tokens // share
    all_rows = blocks * rows
    features = heads * 4 * size
    hidden = w_gate.shape[1]
    slot_count = blocks * SLOTS
    groups = share // 2
    routes_t, gates_t, gain_row = routes.T, route_gates.T, norm_gain[None]

    small = [
        keys.reshape(depth, patches), values.reshape(depth, patches),
        image_ids[None], placement.reshape(1, rows), routes_t,
    ]
    local = run(
        pack_kernel, shape((2 * depth + 16, patches)), *small, far=range(5),
        scratch=[pltpu.VMEM(array.shape, array.dtype) for array in small]
        + [pltpu.SemaphoreType.DMA((5,))],
        vmem=PACK_BYTES, name="pack",
    )
    comb, pick, factor = run(
        functools.partial(route_kernel, groups=groups, share=share),
        [
            shape((2, slot_count, tokens)), shape((2, blocks * SEND, tokens)),
            shape((blocks * SEND, 128), F32),
        ],
        routes_t, gates_t, cost=3.0, name="route",
    )
    send = run(
        dispatch_kernel, [shape((2 * SEND, width))] * (blocks // 2),
        pick, factor, text, gain_row, cotangent, cost=2.0, name="dispatch",
    )
    near = gather_blocks(local, send)
    early = to_chips(after(send, near[1:]))

    weight_flat = merge_weight.reshape(features, width)
    message_width = width + width // row_share + 128
    merged, meta, *message = run(
        functools.partial(attend_kernel, blocks=blocks, share=share, row_share=row_share),
        [shape((rows, features)), shape((blocks * 16, patches))] + [shape((row_share, message_width))] * share,
        queries, merge_gain, weight_flat, *near, far=(2,), cost=4.0, vmem=ATTEND_BYTES,
        scratch=[
            pltpu.VMEM((features, width), BF16),
            pltpu.SemaphoreType.DMA((4 if features % 64 == 0 else 1,)),
        ],
        name="attend",
    )

    slots, placed, back_cots = run(
        functools.partial(
            plan_kernel, blocks=blocks, groups=groups, merged_rows=rows, row_share=row_share
        ),
        [
            shape((slot_count, all_rows)), shape((tokens, all_rows)),
            shape((blocks * row_share, width)),
        ],
        meta, cotangent, cost=1.5, name="plan",
    )
    message = trade(message, "expert")
    text_rows, act_grad = run(
        early_kernel, [shape((slot_count, width)), shape((slot_count, hidden), F32)],
        w_down, *early, to_sibling(early, message[1:], "early_half"), cost=3.0, name="early",
    )
    own = run(
        functools.partial(merge_kernel, width=width, features=features),
        shape((row_share, width + 128)), *message, cost=0.2, name="merge",
    )
    block_rows = run(
        stack_kernel, shape((rows, width + 128)), text_rows, *spread_out(own, "expert"),
        far=(0,), cost=0.2, name="stack",
    )
    vision = gather_blocks(block_rows)

    gate_pre, up_proj, *down = run(
        functools.partial(forward_kernel, blocks=blocks),
        [
            shape((slot_count, hidden), F32), shape((slot_count, hidden), F32),
        ] + [shape((2 * SLOTS, width))] * (blocks // 2),
        slots, gain_row, w_gate, w_up, w_down, text_rows, *vision,
        scratch=[pltpu.VMEM((slot_count, width), BF16), pltpu.VMEM((slot_count, width), F32)],
        cost=4.0, name="forward",
    )
    block = rows + row_share
    even, odd = run(
        functools.partial(backward_kernel, blocks=blocks),
        [shape((blocks // 2 * block, width))] * 2,
        slots, act_grad, gate_pre, up_proj, back_cots, w_gate, w_up,
        scratch=[pltpu.VMEM((slot_count, width), F32)],
        cost=4.0, name="backward",
    )
    grads = run(
        pair_sum_kernel, [shape((block, width))] * (blocks // 2), even, swap(odd, "blk", 1),
        cost=0.2, name="pair_sum",
    )
    grads = to_chips(grads)
    returned = to_chips(after(down, grads[1:2]))
    cot_rows, *grads = run(
        functools.partial(chip_sum_kernel, count=blocks // 2),
        [shape((row_share, width))] * (share + 1), *grads, cost=0.2, name="chip_sum",
    )
    grads = trade(grads, "expert")
    vision_grad = run(
        norm_grad_kernel, shape((row_share, width)), own, gain_row, cot_rows, *grads,
        cost=0.3, name="norm_grad",
    )
    normed_grad, sums = run(
        merge_grad_kernel,
        [shape((rows, features), F32), shape((rows, 128), F32)],
        merge_gain, merged, block_rows, weight_flat, *spread_out(vision_grad, "expert"),
        cost=2.5, name="merge_grad",
    )
    sums_own = sums
    sums = spread_out(sums, "expert")

    count = tokens // 2
    kept, sent = run(
        combine_kernel, [shape((count, width), F32), shape((count, width))], comb, *returned,
        to_sibling(returned, grads[:1], "returned_half"), cost=0.5, name="combine",
    )
    step = 1
    while count > part:
        count //= 2
        kept, sent = run(
            halve_kernel, [shape((count, width), F32), shape((count, width))],
            kept, swap(sent, "expert", step), vision_grad, far=(2,), cost=0.3, name="halve",
        )
        step *= 2
    finished = run(
        finish_kernel, shape((part, width)),
        placed, text, kept, swap(sent, "expert", step), *vision, sums_own, far=(4 + blocks,),
        cost=1.0, name="finish",
    )
    laid = {0: finished}
    while step:
        laid.update({k + step: swap(laid[k], "expert", step) for k in list(laid)})
        step //= 2
    llm_out = run(
        lay_kernel, shape((tokens, width)), *[laid[k] for k in sorted(laid)], cost=1.0, name="lay"
    )
    attn_grad = run(
        functools.partial(unfold_kernel, size=size), shape((depth, patches), F32),
        normed_grad, merged, block_rows, *sums, cost=2.0, name="unfold",
    )
    return llm_out, attn_grad.reshape(heads, size, patches)


def solution(mesh):
    return jax.shard_map(
        body,
        mesh=mesh,
        in_specs=(
            P("expert", None, "blk"),
            P("expert", None, "blk"),
            P("expert", None, "blk"),
            P("blk"),
            P("blk", None),
            P("expert", None),
            P("expert", None, None),
            P("blk", None),
            P(),
            P("blk", "expert", None),
            P("blk", "expert", None),
            P("blk", "expert", None),
            P("blk", None),
            P("blk", None),
            P("blk", None),
        ),
        out_specs=(P("blk", None), P("expert", None, "blk")),
        check_vma=False,
    )
```

```python
import functools

import jax
import jax.numpy as jnp
from jax import lax
from jax.experimental import pallas as pl
from jax.experimental.pallas import tpu as pltpu
from jax.sharding import PartitionSpec as P

CAPX = 10
SLOTS = 16
SEND = 24
EPS = 1e-06
VMEM_BYTES = 16 * 1024 * 1024
PACK_BYTES = 60 * 1024 * 1024
ATTEND_BYTES = 58 * 1024 * 1024
F32 = jnp.float32
BF16 = jnp.bfloat16


def iota(shape, dim):
    return lax.broadcasted_iota(jnp.int32, shape, dim)


def dot(a, b):
    return jnp.dot(a.astype(BF16), b.astype(BF16), preferred_element_type=F32)


def dot_nt(a, b):
    return lax.dot_general(a, b, (((1,), (1,)), ((), ())), preferred_element_type=F32)


def dot_tn(a, b):
    return lax.dot_general(a, b, (((0,), (0,)), ((), ())), preferred_element_type=F32)


def three(value):
    first = value.astype(BF16).astype(F32)
    second = (value - first).astype(BF16).astype(F32)
    return first, second, value - first - second


def put_scalars(columns, rows):
    lane = iota((rows, 128), 1)
    out = jnp.zeros((rows, 128), F32)
    place = 0
    for column in columns:
        for piece in three(column):
            out = jnp.where(lane == place, piece, out)
            place += 1
    return out


def get_scalar(block, which):
    lane = iota(block.shape, 1)
    return jnp.sum(jnp.where(lane // 3 == which, block, 0.0), axis=1, keepdims=True)


def bring(far_refs, near_refs, sems):
    copies = [
        pltpu.make_async_copy(far, near, sems.at[i])
        for i, (far, near) in enumerate(zip(far_refs, near_refs))
    ]
    for copy in copies:
        copy.start()
    return copies


def pack_kernel(*refs):
    far_refs, out_ref, near_refs, sems = refs[:5], refs[5], refs[6:11], refs[11]
    for copy in bring(far_refs, near_refs, sems):
        copy.wait()
    keys_ref, values_ref, images_ref, placement_ref, routes_ref = near_refs
    rows = images_ref.shape[1]
    patches = keys_ref.shape[1]
    repeat = (iota((rows, patches), 0) == iota((rows, patches), 1) // 4).astype(F32)
    keep = (iota((rows, patches), 0) == iota((rows, patches), 1)).astype(F32)
    patch_ids = dot(images_ref[...].astype(F32), repeat)
    dest = dot(placement_ref[...].astype(F32), keep)
    line = iota((8, patches), 0)
    rest = jnp.where(line == 0, patch_ids, jnp.where(line == 1, dest, 0.0))
    parts = [keys_ref[...], values_ref[...], routes_ref[...], rest]
    out_ref[...] = jnp.concatenate([part.astype(F32) for part in parts], axis=0).astype(BF16)


def route_kernel(routes_ref, gates_ref, comb_ref, pick_ref, factor_ref, *, groups, share):
    blocks = comb_ref.shape[1] // SLOTS
    tokens = routes_ref.shape[1]
    me, expert_index = lax.axis_index("blk"), lax.axis_index("expert")
    member = expert_index // groups
    before = (iota((tokens, tokens), 0) < iota((tokens, tokens), 1)).astype(BF16)
    pair_of = 2 * (iota((blocks, tokens), 0) ^ me) + member
    out_hit = jnp.zeros((blocks, tokens), F32)
    out_gate = jnp.zeros((blocks, tokens), F32)
    for k in range(routes_ref.shape[0]):
        same = pair_of == routes_ref[k : k + 1, :]
        out_hit = out_hit + same.astype(F32)
        out_gate = out_gate + jnp.where(same, gates_ref[k : k + 1, :], 0.0)
    out_rank = dot(out_hit, before)

    def expand(stride):
        count = blocks * stride
        pick = (iota((count, blocks), 0) // stride == iota((count, blocks), 1)).astype(BF16)
        gate = sum(dot(pick, piece) for piece in three(out_gate))
        return dot(pick, out_hit), dot(pick, out_rank).astype(jnp.int32), gate

    hits, ranks, gates = expand(SLOTS)
    live = jnp.where(ranks == iota(hits.shape, 0) % SLOTS, hits, 0.0)
    weight = live * gates
    high = weight.astype(BF16).astype(F32)
    part = tokens // share
    col = iota((tokens, tokens), 1)
    turned = (col // part * 0).astype(jnp.int32)
    for place, k in enumerate(halving_order(share)):
        turned = jnp.where(col // part == place, k, turned)
    turned = (iota((tokens, tokens), 0) == (turned ^ expert_index) * part + col % part)
    turned = turned.astype(F32)
    comb_ref[0] = dot(high, turned).astype(BF16)
    comb_ref[1] = dot(weight - high, turned).astype(BF16)

    hits, ranks, gates = expand(SEND)
    place = iota(hits.shape, 0) % SEND
    input_pick = jnp.where((place < CAPX) & (ranks == place), hits, 0.0)
    back_pick = jnp.where((place >= CAPX) & (place < 2 * CAPX) & (ranks == place - CAPX), hits, 0.0)
    pick_ref[0] = input_pick.astype(BF16)
    pick_ref[1] = back_pick.astype(BF16)
    factor = jnp.sum(back_pick * gates, axis=1, keepdims=True)
    factor_ref[...] = jnp.broadcast_to(factor, factor_ref.shape)


def dispatch_kernel(pick_ref, factor_ref, text_ref, gain_ref, cot_ref, *send_refs):
    text = text_ref[...].astype(F32)
    scale = lax.rsqrt(jnp.mean(text * text, axis=1, keepdims=True) + EPS)
    h_rows = (text * scale * gain_ref[...]).astype(BF16)
    factor = factor_ref[:, :1]
    send = dot(pick_ref[0], h_rows) + factor * dot(pick_ref[1], cot_ref[...])
    send = send.astype(BF16)
    count = 2 * SEND
    for k, ref in enumerate(send_refs):
        ref[...] = send[k * count : (k + 1) * count]


def plan_kernel(
    meta_ref, cot_ref, slots_ref, placed_ref, back_ref, *, blocks, groups, merged_rows, row_share
):
    tokens = cot_ref.shape[0]
    rows = blocks * merged_rows
    me, expert_index = lax.axis_index("blk"), lax.axis_index("expert")
    member = expert_index // groups
    meta = [meta_ref[k * 16 : (k + 1) * 16].astype(F32) for k in range(blocks)]
    mine = (2 * me + member).astype(F32)
    hits = [jnp.sum((part[:8] == mine).astype(F32), axis=0, keepdims=True) for part in meta]
    hit = jnp.concatenate(hits, axis=0)
    dest = jnp.concatenate([part[9:10] for part in meta], axis=0)
    before = (iota((tokens, tokens), 0) < iota((tokens, tokens), 1)).astype(BF16)
    rank = dot(hit, before)

    def row_of(col):
        inner = col % merged_rows
        return ((inner // row_share) ^ expert_index) * row_share + inner % row_share

    def place_of(col):
        return ((col // merged_rows) ^ me) * merged_rows + row_of(col)

    spread = (iota((128, rows), 0) == row_of(iota((128, rows), 1))).astype(F32)
    own_block = iota((blocks, rows), 1) // merged_rows == iota((blocks, rows), 0)
    dest_row = jnp.sum(jnp.where(own_block, dot(dest, spread), 0.0), axis=0, keepdims=True)
    dest_row = dest_row.astype(jnp.int32) ^ me
    dest_hit = (iota((blocks, rows), 0) == dest_row).astype(F32)
    rows_before = place_of(iota((rows, rows), 0)) < place_of(iota((rows, rows), 1))
    earlier = dot(dest_hit, rows_before.astype(F32))
    slot = jnp.sum(dest_hit * earlier, axis=0, keepdims=True).astype(jnp.int32)
    at_token = (iota((tokens, rows), 0) == slot).astype(F32)
    row_hit = jnp.sum(dest_hit * dot(hit, at_token), axis=0, keepdims=True)
    row_rank = jnp.sum(dest_hit * dot(rank, at_token), axis=0, keepdims=True).astype(jnp.int32)
    slot_id = dest_row * SLOTS + row_rank
    slot_count = slots_ref.shape[0]
    chosen = (iota((slot_count, rows), 0) == slot_id) & (row_hit > 0.5)
    slots_ref[...] = chosen.astype(F32).astype(BF16)
    placed = jnp.where(dest_row == 0, at_token, 0.0).astype(BF16)
    placed_ref[...] = placed
    back_rows = blocks * row_share
    source = iota((back_rows, rows), 0)
    wanted = source // row_share * merged_rows + source % row_share
    row_pick = (iota((back_rows, rows), 1) == wanted).astype(F32).astype(BF16)
    back_ref[...] = dot(dot_nt(row_pick, placed), cot_ref[...]).astype(BF16)


def chunk_cuts(features):
    firsts = list(range(0, max(features - 255, 1), 256))
    if len(firsts) > 1 and features - firsts[-1] < 256:
        firsts.pop()
    return list(zip(firsts, firsts[1:] + [features]))


def flat_gain(gain_ref):
    return jnp.concatenate([gain_ref[h : h + 1] for h in range(gain_ref.shape[0])], axis=1)


def attend_kernel(*refs, blocks, share, row_share):
    query_ref, gain_ref, weight_ref = refs[:3]
    near_refs = refs[3 : 3 + blocks]
    merged_ref, meta_ref, *message_refs = refs[3 + blocks : 5 + blocks + share]
    near_weight_ref, sems = refs[5 + blocks + share :]
    cuts = chunk_cuts(weight_ref.shape[0])
    parts = [pl.ds(first, last - first) for first, last in cuts]
    copies = bring([weight_ref.at[p] for p in parts], [near_weight_ref.at[p] for p in parts], sems)
    heads, size, patches = query_ref.shape
    rows, features = merged_ref.shape
    width = weight_ref.shape[1]
    depth = heads * size
    near = [ref[...].astype(F32) for ref in near_refs]
    meta_ref[...] = jnp.concatenate([part[2 * depth :] for part in near], axis=0).astype(BF16)
    key_ids = jnp.concatenate([part[2 * depth + 8 : 2 * depth + 9] for part in near], axis=1)
    eye = iota((patches, patches), 0) == iota((patches, patches), 1)
    own_ids = jnp.sum(jnp.where(eye, key_ids[:, :patches], 0.0), axis=1, keepdims=True)
    same = own_ids == key_ids
    spread = jnp.zeros((patches, features), F32)
    place_row, place_col = iota((size, features), 0), iota((size, features), 1)
    for head in range(heads):
        first = head * size
        keys = jnp.concatenate([part[first : first + size] for part in near], axis=1)
        first = depth + head * size
        values = jnp.concatenate([part[first : first + size] for part in near], axis=1)
        query = query_ref[head].astype(F32).T.astype(BF16)
        scores = dot(query, keys) * (size**-0.5)
        scores = jnp.where(same, scores, -1e30)
        weights = jnp.exp(scores - jnp.max(scores, axis=1, keepdims=True))
        total = jnp.sum(weights, axis=1, keepdims=True)
        attn = dot_nt(weights.astype(BF16), values.astype(BF16)) / total
        place = (place_col % size == place_row) & (place_col // (4 * size) == head)
        spread = spread + dot(attn, place.astype(F32))
    spot = iota((patches, features), 1) // size % 4 == iota((patches, features), 0) % 4
    line = iota((rows, patches), 0)
    line = ((line // row_share) ^ lax.axis_index("expert")) * row_share + line % row_share
    fold = (iota((rows, patches), 1) // 4 == line).astype(F32)
    merged = dot(fold, jnp.where(spot, spread, 0.0))
    merged_ref[...] = merged.astype(BF16)
    local_mean = jnp.sum(merged, axis=1, keepdims=True) / features
    centered = merged - local_mean
    squares = jnp.sum(centered * centered, axis=1, keepdims=True)
    gain = flat_gain(gain_ref)
    gain_high = gain.astype(BF16).astype(F32)
    extra = iota((8, features), 0)
    gain_rows = jnp.where(extra == 0, gain_high, jnp.where(extra == 1, gain - gain_high, 0.0))
    left = jnp.concatenate([centered * gain, gain_rows], axis=0)
    left = left.astype(BF16)
    product = 0.0
    for copy, (first, last) in zip(copies, cuts):
        copy.wait()
        product = product + dot(left[:, first:last], near_weight_ref[first:last])
    gain_sum = product[rows : rows + 1] + product[rows + 1 : rows + 2]
    piece = width // row_share
    pieces = [gain_sum[:, j * piece : (j + 1) * piece] for j in range(row_share)]
    pieces = jnp.concatenate(pieces, axis=0).astype(BF16)
    scalars = put_scalars([local_mean, squares], rows).astype(BF16)
    for k in range(share):
        mine = slice(k * row_share, (k + 1) * row_share)
        message_refs[k][:, :width] = product[mine].astype(BF16)
        message_refs[k][:, width : width + piece] = pieces
        message_refs[k][:, width + piece :] = scalars[mine]


def merge_kernel(*refs, width, features):
    *message_refs, out_ref, vision_ref, gain_ref = refs
    share, row_share = len(message_refs), out_ref.shape[0]
    piece = width // row_share
    parts = [ref[...].astype(F32) for ref in message_refs]
    scalars = [part[:, width + piece :] for part in parts]
    means = [get_scalar(block, 0) for block in scalars]
    squares = [get_scalar(block, 1) for block in scalars]
    mean = sum(means) / share
    spread = sum(q + features * (m - mean) * (m - mean) for q, m in zip(squares, means))
    inv_std = lax.rsqrt(spread / (share * features) + EPS)
    total = jnp.zeros((row_share, width), F32)
    gain_total = jnp.zeros((1, width), F32)
    for part, local in zip(parts, means):
        tail = part[:, width : width + piece]
        gain_sum = jnp.concatenate([tail[j : j + 1] for j in range(row_share)], axis=1)
        total = total + part[:, :width] + (local - mean) * gain_sum
        gain_total = gain_total + gain_sum
    vision_ref[...] = total * inv_std
    gain_ref[...] = gain_total
    out_ref[:, :width] = (total * inv_std).astype(BF16)
    out_ref[:, width:] = put_scalars([mean, inv_std], row_share).astype(BF16)


def stack_kernel(_, *refs):
    *part_refs, out_ref = refs
    out_ref[...] = stacked(part_refs)


def stacked(part_refs):
    return jnp.concatenate([ref[...].astype(F32) for ref in part_refs], axis=0).astype(BF16)


def by_chip(own_refs, sibling_ref):
    parts = []
    sibling = sibling_ref[...].astype(F32)
    for k, own_ref in enumerate(own_refs):
        half = own_ref.shape[0] // 2
        parts.append(own_ref[...].astype(F32)[:half])
        parts.append(sibling[k * half : (k + 1) * half])
    return jnp.concatenate(parts, axis=0).astype(BF16)


def other_half_kernel(*refs, count):
    out_ref = refs[-1]
    parts = [ref[...].astype(F32)[ref.shape[0] // 2 :] for ref in refs[:count]]
    out_ref[...] = jnp.concatenate(parts, axis=0).astype(BF16)


def slot_pick(slot_count, send_rows, shift):
    row, col = iota((slot_count, send_rows), 0), iota((slot_count, send_rows), 1)
    place = row % SLOTS
    pick = (col == row // SLOTS * SEND + place + shift) & (place < CAPX)
    return pick.astype(F32)


def early_kernel(down_ref, *refs):
    *early_refs, sibling_ref, text_out, grad_out = refs
    slot_count = text_out.shape[0]
    early = by_chip(early_refs, sibling_ref)
    text_out[...] = dot(slot_pick(slot_count, early.shape[0], 0), early).astype(BF16)
    back_rows = dot(slot_pick(slot_count, early.shape[0], CAPX), early).astype(BF16)
    grad_out[...] = dot_nt(back_rows, down_ref[0])


def forward_kernel(*refs, blocks):
    slots_ref, gain_ref, gate_ref, up_ref, down_ref, text_ref = refs[:6]
    vision_refs = refs[6 : 6 + blocks]
    gate_out, up_out, *down_refs = refs[6 + blocks : -2]
    h_ref, sum_ref = refs[-2:]
    _, hidden, width = gate_ref.shape
    chosen = slots_ref[...]
    is_vision = jnp.sum(chosen.astype(F32), axis=1, keepdims=True) > 0.5
    vision = jnp.concatenate([ref[:, :width] for ref in vision_refs], axis=0)
    inputs = dot(chosen, vision)
    scale = lax.rsqrt(jnp.mean(inputs * inputs, axis=1, keepdims=True) + EPS)
    normed = inputs * scale * gain_ref[...]
    h_ref[...] = jnp.where(is_vision, normed, text_ref[...].astype(F32)).astype(BF16)
    tile = tile_of(hidden)
    for i in range(hidden // tile):
        mine = slice(i * tile, (i + 1) * tile)
        gate_pre = dot_nt(h_ref[...], gate_ref[0, mine])
        up_proj = dot_nt(h_ref[...], up_ref[0, mine])
        gate_out[:, mine] = gate_pre
        up_out[:, mine] = up_proj
        activated = gate_pre * jax.nn.sigmoid(gate_pre) * up_proj
        product = dot(activated, down_ref[0, mine])
        sum_ref[...] = product if i == 0 else sum_ref[...] + product
    count = 2 * SLOTS
    for k, ref in enumerate(down_refs):
        ref[...] = sum_ref[k * count : (k + 1) * count].astype(BF16)


def backward_kernel(
    slots_ref, grad_ref, gate_in, up_in, cot_ref, gate_ref, up_ref, even_ref, odd_ref, sum_ref,
    *, blocks,
):
    hidden = gate_ref.shape[1]
    tile = tile_of(hidden)
    for i in range(hidden // tile):
        mine = slice(i * tile, (i + 1) * tile)
        act_grad = grad_ref[:, mine]
        gate_pre, up_proj = gate_in[:, mine], up_in[:, mine]
        sigmoid = jax.nn.sigmoid(gate_pre)
        gate_grad = act_grad * up_proj * sigmoid * (1.0 + gate_pre * (1.0 - sigmoid))
        up_grad = act_grad * gate_pre * sigmoid
        product = dot(gate_grad, gate_ref[0, mine]) + dot(up_grad, up_ref[0, mine])
        sum_ref[...] = product if i == 0 else sum_ref[...] + product
    grads = dot_tn(slots_ref[...], sum_ref[...].astype(BF16))
    cots = cot_ref[...].astype(F32)
    rows, row_share = grads.shape[0] // blocks, cots.shape[0] // blocks
    parts = ([], [])
    for k in range(blocks):
        parts[k % 2].append(grads[k * rows : (k + 1) * rows])
        parts[k % 2].append(cots[k * row_share : (k + 1) * row_share])
    even_ref[...] = jnp.concatenate(parts[0], axis=0).astype(BF16)
    odd_ref[...] = jnp.concatenate(parts[1], axis=0).astype(BF16)


def tile_of(hidden):
    return 256 if hidden % 256 == 0 else hidden


def halving_order(share):
    order = [0]
    step = share // 2
    while step:
        order = order + [k + step for k in order]
        step //= 2
    return [sum(1 << j for j in range(share.bit_length() - 1) if k >> j & 1) for k in order]


def pair_sum_kernel(own_ref, sibling_ref, *refs, count):
    out_refs = refs[-count:]
    rows = out_refs[0].shape[0]
    total = own_ref[...].astype(F32) + sibling_ref[...].astype(F32)
    for k, out_ref in enumerate(out_refs):
        out_ref[...] = total[k * rows : (k + 1) * rows].astype(BF16)


def total_of(part_refs):
    total = part_refs[0][...].astype(F32)
    for ref in part_refs[1:]:
        total = total + ref[...].astype(F32)
    return total


def chip_sum_kernel(*refs, count):
    cot_ref, *out_refs = refs[count + 1 :]
    total = total_of(refs[:count])
    rows = cot_ref.shape[0]
    for k, out_ref in enumerate(out_refs):
        out_ref[...] = total[k * rows : (k + 1) * rows].astype(BF16)
    cot_ref[...] = total[len(out_refs) * rows :].astype(BF16)


def combine_kernel(comb_ref, *refs):
    *part_refs, sibling_ref, keep_ref, send_ref = refs
    rows = by_chip(part_refs, sibling_ref)
    total = dot_tn(comb_ref[0], rows) + dot_tn(comb_ref[1], rows)
    half = keep_ref.shape[0]
    keep_ref[...] = total[:half]
    send_ref[...] = total[half:].astype(BF16)


def halve_kernel(own_ref, arrived_ref, *refs):
    keep_ref, send_ref = refs[-2:]
    total = own_ref[...] + arrived_ref[...].astype(F32)
    half = keep_ref.shape[0]
    keep_ref[...] = total[:half]
    send_ref[...] = total[half:].astype(BF16)


def finish_kernel(placed_ref, text_ref, own_ref, arrived_ref, *refs, blocks):
    vision_refs, out_ref = refs[:blocks], refs[-1]
    count, width = out_ref.shape
    tokens = placed_ref.shape[0]
    first = lax.axis_index("expert") * count
    pick = iota((count, tokens), 1) == iota((count, tokens), 0) + first
    pick = pick.astype(F32)
    placed = dot(pick, placed_ref[...])
    is_vision = jnp.sum(placed, axis=1, keepdims=True) > 0.5
    vision = jnp.concatenate([ref[:, :width] for ref in vision_refs], axis=0)
    inputs = jnp.where(is_vision, dot(placed, vision), dot(pick, text_ref[...]))
    out_ref[...] = (inputs + own_ref[...] + arrived_ref[...].astype(F32)).astype(BF16)


def lay_kernel(*refs):
    *part_refs, out_ref = refs
    count = part_refs[0].shape[0]
    for k, ref in enumerate(part_refs):
        first = pl.multiple_of((lax.axis_index("expert") ^ k) * count, count)
        out_ref[pl.ds(first, count), :] = ref[...]


def norm_grad_kernel(
    own_ref, gain_ref, cot_ref, vision_ref, total_ref, *refs, features
):
    *part_refs, out_ref = refs
    width = gain_ref.shape[1]
    hidden = total_of(part_refs)
    cotangent = cot_ref[...].astype(F32)
    inputs = own_ref[:, :width].astype(F32)
    scale = lax.rsqrt(jnp.mean(inputs * inputs, axis=1, keepdims=True) + EPS)
    pulled = hidden * gain_ref[...]
    cross = jnp.mean(pulled * inputs, axis=1, keepdims=True)
    grad = cotangent + scale * pulled - inputs * (scale * scale * scale) * cross
    grad = grad.astype(BF16)
    out_ref[:, :width] = grad
    grad = grad.astype(F32)
    grad_mean = jnp.sum(grad * total_ref[...], axis=1, keepdims=True) / features
    cross_mean = jnp.sum(grad * vision_ref[...], axis=1, keepdims=True) / features
    out_ref[:, width:] = put_scalars([grad_mean, cross_mean], grad.shape[0]).astype(BF16)


def merge_grad_kernel(*refs, size):
    gain_ref, merged_ref, scalar_ref, weight_ref, *part_refs, out_ref = refs
    rows, features = merged_ref.shape
    width = weight_ref.shape[1]
    depth, patches = out_ref.shape
    row_share = part_refs[0].shape[0]
    parts = stacked(part_refs)
    normed_grad = dot_nt(parts[:, :width], weight_ref[...]) * flat_gain(gain_ref)
    means = parts[:, width:].astype(F32)
    scalars = scalar_ref[:, width:].astype(F32)
    inv_std = get_scalar(scalars, 1)
    normed = (merged_ref[...].astype(F32) - get_scalar(scalars, 0)) * inv_std
    grad = inv_std * (normed_grad - get_scalar(means, 0) - normed * get_scalar(means, 1))
    high = grad.astype(BF16)
    low = (grad - high.astype(F32)).astype(BF16)
    line = iota((patches, rows), 1)
    line = ((line // row_share) ^ lax.axis_index("expert")) * row_share + line % row_share
    unfold = (iota((patches, rows), 0) // 4 == line).astype(F32)
    spot = iota((patches, features), 1) // size % 4 == iota((patches, features), 0) % 4
    row, col = iota((depth, features), 0), iota((depth, features), 1)
    place = (col // (4 * size) == row // size) & (col % size == row % size)
    place = place.astype(F32).astype(BF16)
    out = jnp.zeros((depth, patches), F32)
    for piece in (high, low):
        wide = jnp.where(spot, dot(unfold, piece), 0.0).astype(BF16)
        out = out + dot_nt(place, wide)
    out_ref[...] = out


def whole(memory_space=pltpu.VMEM):
    return pl.BlockSpec(memory_space=memory_space)


def run(kernel, outs, *args, far=(), scratch=(), cost=1.0, vmem=VMEM_BYTES, name=None):
    specs = [whole()] * len(args)
    for place in far:
        specs[place] = whole(pl.ANY)
    return pl.pallas_call(
        kernel,
        out_shape=outs,
        in_specs=specs,
        out_specs=jax.tree.map(lambda _: whole(), outs),
        scratch_shapes=scratch,
        compiler_params=pltpu.CompilerParams(vmem_limit_bytes=vmem),
        cost_estimate=microseconds(cost),
        name=name,
    )(*args)


def to_sibling(parts, deps, name):
    rows, width = parts[0].shape
    half = run(
        functools.partial(other_half_kernel, count=len(parts)),
        shape((len(parts) * rows // 2, width)), *parts, *deps,
        far=range(len(parts), len(parts) + len(deps)), cost=0.3, name=name,
    )
    return swap(half, "blk", 1)


def microseconds(time):
    return pl.CostEstimate(flops=0, transcendentals=0, bytes_accessed=int(time * 3e6))


def after(values, deps):
    count = len(values)
    return pl.pallas_call(
        lambda *refs: None,
        out_shape=[shape(value.shape, value.dtype) for value in values],
        in_specs=[whole(pl.ANY)] * (count + len(deps)),
        out_specs=[whole(pl.ANY)] * count,
        input_output_aliases={i: i for i in range(count)},
        compiler_params=pltpu.CompilerParams(vmem_limit_bytes=VMEM_BYTES),
        cost_estimate=microseconds(0.1),
        name="after",
    )(*values, *deps)


def shape(dims, dtype=BF16):
    return jax.ShapeDtypeStruct(dims, dtype)


def swap(value, axis, step):
    count = lax.axis_size(axis)
    return lax.ppermute(value, axis, [(i, i ^ step) for i in range(count)])


def trade(parts, axis):
    return [parts[0]] + [swap(parts[k], axis, k) for k in range(1, len(parts))]


def spread_out(value, axis):
    return trade([value] * lax.axis_size(axis), axis)


def gather_blocks(value, deps=None):
    own = [value] + [swap(value, "blk", k) for k in range(2, lax.axis_size("blk"), 2)]
    if deps is not None:
        own = own[:1] + list(after(own[1:], deps))
    sibling = [swap(part, "blk", 1) for part in own]
    return [part for pair in zip(own, sibling) for part in pair]


def to_chips(parts):
    return [parts[0]] + [swap(parts[k], "blk", 2 * k) for k in range(1, len(parts))]


def body(
    queries, keys, values, image_ids, placement, merge_gain, merge_weight, text, norm_gain,
    w_gate, w_up, w_down, routes, route_gates, cotangent,
):
    blocks = lax.axis_size("blk")
    share = lax.axis_size("expert")
    heads, size, patches = queries.shape
    depth = heads * size
    rows = image_ids.shape[0]
    row_share = rows // share
    tokens, width = text.shape
    part = tokens // share
    all_rows = blocks * rows
    features = heads * 4 * size
    hidden = w_gate.shape[1]
    slot_count = blocks * SLOTS
    groups = share // 2
    routes_t, gates_t, gain_row = routes.T, route_gates.T, norm_gain[None]

    small = [
        keys.reshape(depth, patches), values.reshape(depth, patches),
        image_ids[None], placement.reshape(1, rows), routes_t,
    ]
    local = run(
        pack_kernel, shape((2 * depth + 16, patches)), *small, far=range(5),
        scratch=[pltpu.VMEM(array.shape, array.dtype) for array in small]
        + [pltpu.SemaphoreType.DMA((5,))],
        vmem=PACK_BYTES, name="pack",
    )
    comb, pick, factor = run(
        functools.partial(route_kernel, groups=groups, share=share),
        [
            shape((2, slot_count, tokens)), shape((2, blocks * SEND, tokens)),
            shape((blocks * SEND, 128), F32),
        ],
        routes_t, gates_t, cost=3.0, name="route",
    )
    send = run(
        dispatch_kernel, [shape((2 * SEND, width))] * (blocks // 2),
        pick, factor, text, gain_row, cotangent, cost=2.0, name="dispatch",
    )
    near = gather_blocks(local, send)
    early = to_chips(after(send, near[1:]))

    weight_flat = merge_weight.reshape(features, width)
    message_width = width + width // row_share + 128
    merged, meta, *message = run(
        functools.partial(attend_kernel, blocks=blocks, share=share, row_share=row_share),
        [shape((rows, features)), shape((blocks * 16, patches))] + [shape((row_share, message_width))] * share,
        queries, merge_gain, weight_flat, *near, far=(2,), cost=4.0, vmem=ATTEND_BYTES,
        scratch=[
            pltpu.VMEM((features, width), BF16),
            pltpu.SemaphoreType.DMA((len(chunk_cuts(features)),)),
        ],
        name="attend",
    )

    slots, placed, back_cots = run(
        functools.partial(
            plan_kernel, blocks=blocks, groups=groups, merged_rows=rows, row_share=row_share
        ),
        [
            shape((slot_count, all_rows)), shape((tokens, all_rows)),
            shape((blocks * row_share, width)),
        ],
        meta, cotangent, cost=1.5, name="plan",
    )
    message = trade(message, "expert")
    text_rows, act_grad = run(
        early_kernel, [shape((slot_count, width)), shape((slot_count, hidden), F32)],
        w_down, *early, to_sibling(early, message[1:], "early_half"), cost=3.0, name="early",
    )
    own, vision_exact, gain_total = run(
        functools.partial(merge_kernel, width=width, features=features),
        [
            shape((row_share, width + 128)), shape((row_share, width), F32),
            shape((1, width), F32),
        ],
        *message, cost=0.2, name="merge",
    )
    block_rows = run(
        stack_kernel, shape((rows, width + 128)), text_rows, *spread_out(own, "expert"),
        far=(0,), cost=0.2, name="stack",
    )
    vision = gather_blocks(block_rows)

    gate_pre, up_proj, *down = run(
        functools.partial(forward_kernel, blocks=blocks),
        [
            shape((slot_count, hidden), F32), shape((slot_count, hidden), F32),
        ] + [shape((2 * SLOTS, width))] * (blocks // 2),
        slots, gain_row, w_gate, w_up, w_down, text_rows, *vision,
        scratch=[pltpu.VMEM((slot_count, width), BF16), pltpu.VMEM((slot_count, width), F32)],
        cost=4.0, name="forward",
    )
    returned = to_chips(down)
    block = rows + row_share
    even, odd = run(
        functools.partial(backward_kernel, blocks=blocks),
        [shape((blocks // 2 * block, width))] * 2,
        slots, act_grad, gate_pre, up_proj, back_cots, w_gate, w_up,
        scratch=[pltpu.VMEM((slot_count, width), F32)],
        cost=4.0, name="backward",
    )
    grads = run(
        functools.partial(pair_sum_kernel, count=blocks // 2),
        [shape((block, width))] * (blocks // 2), even, swap(odd, "blk", 1), *returned[1:],
        far=range(2, 1 + blocks // 2), cost=0.2, name="pair_sum",
    )
    grads = to_chips(grads)
    count = tokens // 2
    kept, sent = run(
        combine_kernel, [shape((count, width), F32), shape((count, width))], comb, *returned,
        to_sibling(returned, grads[:1], "returned_half"), cost=0.5, name="combine",
    )
    first_sent, step = sent, 1
    while count > part:
        count //= 2
        kept, sent = run(
            halve_kernel, [shape((count, width), F32), shape((count, width))],
            kept, swap(sent, "expert", step), *grads[1:], far=range(2, 1 + blocks // 2), cost=0.3,
            name="halve",
        )
        step *= 2
    cot_rows, *grads = run(
        functools.partial(chip_sum_kernel, count=blocks // 2),
        [shape((row_share, width))] * (share + 1), *grads, first_sent, far=(blocks // 2,), cost=0.2,
        name="chip_sum",
    )
    grads = trade(grads, "expert")
    vision_grad = run(
        functools.partial(norm_grad_kernel, features=share * features),
        shape((row_share, width + 128)),
        own, gain_row, cot_rows, vision_exact, gain_total, *grads, cost=0.3, name="norm_grad",
    )
    vision_grads = spread_out(vision_grad, "expert")
    attn_grad = run(
        functools.partial(merge_grad_kernel, size=size), shape((depth, patches), F32),
        merge_gain, merged, block_rows, weight_flat, *vision_grads, cost=4.0, name="merge_grad",
    )

    finished = run(
        functools.partial(finish_kernel, blocks=blocks), shape((part, width)),
        placed, text, kept, swap(sent, "expert", step), *vision, *grads[1:],
        far=range(4 + blocks, 3 + blocks + share),
        cost=1.0, name="finish",
    )
    laid = {0: finished}
    while step:
        far_ones = [k for k in laid if k]
        if far_ones:
            laid.update(zip(far_ones, after([laid[k] for k in far_ones], vision_grads[1:])))
        laid.update({k + step: swap(laid[k], "expert", step) for k in list(laid)})
        step //= 2
    llm_out = run(
        lay_kernel, shape((tokens, width)), *[laid[k] for k in sorted(laid)], cost=1.0, name="lay"
    )
    return llm_out, attn_grad.reshape(heads, size, patches)


def solution(mesh):
    return jax.shard_map(
        body,
        mesh=mesh,
        in_specs=(
            P("expert", None, "blk"),
            P("expert", None, "blk"),
            P("expert", None, "blk"),
            P("blk"),
            P("blk", None),
            P("expert", None),
            P("expert", None, None),
            P("blk", None),
            P(),
            P("blk", "expert", None),
            P("blk", "expert", None),
            P("blk", "expert", None),
            P("blk", None),
            P("blk", None),
            P("blk", None),
        ),
        out_specs=(P("blk", None), P("expert", None, "blk")),
        check_vma=False,
    )
```

```python
import functools

import jax
import jax.numpy as jnp
from jax import lax
from jax.experimental import pallas as pl
from jax.experimental.pallas import tpu as pltpu
from jax.sharding import PartitionSpec as P

CAPX = 10
SLOTS = 16
SEND = 24
EPS = 1e-06
VMEM_BYTES = 16 * 1024 * 1024
PACK_BYTES = 60 * 1024 * 1024
F32 = jnp.float32
BF16 = jnp.bfloat16


def iota(shape, dim):
    return lax.broadcasted_iota(jnp.int32, shape, dim)


def dot(a, b):
    return jnp.dot(a.astype(BF16), b.astype(BF16), preferred_element_type=F32)


def dot_nt(a, b):
    return lax.dot_general(a, b, (((1,), (1,)), ((), ())), preferred_element_type=F32)


def dot_tn(a, b):
    return lax.dot_general(a, b, (((0,), (0,)), ((), ())), preferred_element_type=F32)


def three(value):
    first = value.astype(BF16).astype(F32)
    second = (value - first).astype(BF16).astype(F32)
    return first, second, value - first - second


def put_scalars(columns, rows):
    lane = iota((rows, 128), 1)
    out = jnp.zeros((rows, 128), F32)
    place = 0
    for column in columns:
        for piece in three(column):
            out = jnp.where(lane == place, piece, out)
            place += 1
    return out


def get_scalar(block, which):
    lane = iota(block.shape, 1)
    return jnp.sum(jnp.where(lane // 3 == which, block, 0.0), axis=1, keepdims=True)


def bring(far_refs, near_refs, sems):
    copies = [
        pltpu.make_async_copy(far, near, sems.at[i])
        for i, (far, near) in enumerate(zip(far_refs, near_refs))
    ]
    for copy in copies:
        copy.start()
    return copies


def pack_kernel(*refs):
    far_refs, out_ref, near_refs, sems = refs[:5], refs[5], refs[6:11], refs[11]
    for copy in bring(far_refs, near_refs, sems):
        copy.wait()
    keys_ref, values_ref, images_ref, placement_ref, routes_ref = near_refs
    rows = images_ref.shape[1]
    patches = keys_ref.shape[1]
    repeat = (iota((rows, patches), 0) == iota((rows, patches), 1) // 4).astype(F32)
    keep = (iota((rows, patches), 0) == iota((rows, patches), 1)).astype(F32)
    patch_ids = dot(images_ref[...].astype(F32), repeat)
    dest = dot(placement_ref[...].astype(F32), keep)
    line = iota((8, patches), 0)
    rest = jnp.where(line == 0, patch_ids, jnp.where(line == 1, dest, 0.0))
    parts = [keys_ref[...], values_ref[...], routes_ref[...], rest]
    out_ref[...] = jnp.concatenate([part.astype(F32) for part in parts], axis=0).astype(BF16)


def route_kernel(routes_ref, gates_ref, comb_ref, pick_ref, factor_ref, *, groups, share):
    blocks = comb_ref.shape[1] // SLOTS
    tokens = routes_ref.shape[1]
    me, expert_index = lax.axis_index("blk"), lax.axis_index("expert")
    member = expert_index // groups
    before = (iota((tokens, tokens), 0) < iota((tokens, tokens), 1)).astype(BF16)
    pair_of = 2 * (iota((blocks, tokens), 0) ^ me) + member
    out_hit = jnp.zeros((blocks, tokens), F32)
    out_gate = jnp.zeros((blocks, tokens), F32)
    for k in range(routes_ref.shape[0]):
        same = pair_of == routes_ref[k : k + 1, :]
        out_hit = out_hit + same.astype(F32)
        out_gate = out_gate + jnp.where(same, gates_ref[k : k + 1, :], 0.0)
    out_rank = dot(out_hit, before)

    def expand(stride):
        count = blocks * stride
        pick = (iota((count, blocks), 0) // stride == iota((count, blocks), 1)).astype(BF16)
        gate = sum(dot(pick, piece) for piece in three(out_gate))
        return dot(pick, out_hit), dot(pick, out_rank).astype(jnp.int32), gate

    hits, ranks, gates = expand(SLOTS)
    live = jnp.where(ranks == iota(hits.shape, 0) % SLOTS, hits, 0.0)
    weight = live * gates
    high = weight.astype(BF16).astype(F32)
    part = tokens // share
    col = iota((tokens, tokens), 1)
    turned = (col // part * 0).astype(jnp.int32)
    for place, k in enumerate(halving_order(share)):
        turned = jnp.where(col // part == place, k, turned)
    turned = (iota((tokens, tokens), 0) == (turned ^ expert_index) * part + col % part)
    turned = turned.astype(F32)
    comb_ref[0] = dot(high, turned).astype(BF16)
    comb_ref[1] = dot(weight - high, turned).astype(BF16)

    hits, ranks, gates = expand(SEND)
    place = iota(hits.shape, 0) % SEND
    input_pick = jnp.where((place < CAPX) & (ranks == place), hits, 0.0)
    back_pick = jnp.where((place >= CAPX) & (place < 2 * CAPX) & (ranks == place - CAPX), hits, 0.0)
    pick_ref[0] = input_pick.astype(BF16)
    pick_ref[1] = back_pick.astype(BF16)
    factor = jnp.sum(back_pick * gates, axis=1, keepdims=True)
    factor_ref[...] = jnp.broadcast_to(factor, factor_ref.shape)


def dispatch_kernel(pick_ref, factor_ref, text_ref, gain_ref, cot_ref, *send_refs):
    text = text_ref[...].astype(F32)
    scale = lax.rsqrt(jnp.mean(text * text, axis=1, keepdims=True) + EPS)
    h_rows = (text * scale * gain_ref[...]).astype(BF16)
    factor = factor_ref[:, :1]
    send = dot(pick_ref[0], h_rows) + factor * dot(pick_ref[1], cot_ref[...])
    send = send.astype(BF16)
    count = 2 * SEND
    for k, ref in enumerate(send_refs):
        ref[...] = send[k * count : (k + 1) * count]


def plan_kernel(
    meta_ref, cot_ref, slots_ref, placed_ref, back_ref, *, blocks, groups, merged_rows, row_share
):
    tokens = cot_ref.shape[0]
    rows = blocks * merged_rows
    me, expert_index = lax.axis_index("blk"), lax.axis_index("expert")
    member = expert_index // groups
    meta = [meta_ref[k * 16 : (k + 1) * 16].astype(F32) for k in range(blocks)]
    mine = (2 * me + member).astype(F32)
    hits = [jnp.sum((part[:8] == mine).astype(F32), axis=0, keepdims=True) for part in meta]
    hit = jnp.concatenate(hits, axis=0)
    dest = jnp.concatenate([part[9:10] for part in meta], axis=0)
    before = (iota((tokens, tokens), 0) < iota((tokens, tokens), 1)).astype(BF16)
    rank = dot(hit, before)

    def row_of(col):
        inner = col % merged_rows
        return ((inner // row_share) ^ expert_index) * row_share + inner % row_share

    def place_of(col):
        return ((col // merged_rows) ^ me) * merged_rows + row_of(col)

    spread = (iota((128, rows), 0) == row_of(iota((128, rows), 1))).astype(F32)
    own_block = iota((blocks, rows), 1) // merged_rows == iota((blocks, rows), 0)
    dest_row = jnp.sum(jnp.where(own_block, dot(dest, spread), 0.0), axis=0, keepdims=True)
    dest_row = dest_row.astype(jnp.int32) ^ me
    dest_hit = (iota((blocks, rows), 0) == dest_row).astype(F32)
    rows_before = place_of(iota((rows, rows), 0)) < place_of(iota((rows, rows), 1))
    earlier = dot(dest_hit, rows_before.astype(F32))
    slot = jnp.sum(dest_hit * earlier, axis=0, keepdims=True).astype(jnp.int32)
    at_token = (iota((tokens, rows), 0) == slot).astype(F32)
    row_hit = jnp.sum(dest_hit * dot(hit, at_token), axis=0, keepdims=True)
    row_rank = jnp.sum(dest_hit * dot(rank, at_token), axis=0, keepdims=True).astype(jnp.int32)
    slot_id = dest_row * SLOTS + row_rank
    slot_count = slots_ref.shape[0]
    chosen = (iota((slot_count, rows), 0) == slot_id) & (row_hit > 0.5)
    slots_ref[...] = chosen.astype(F32).astype(BF16)
    placed = jnp.where(dest_row == 0, at_token, 0.0).astype(BF16)
    placed_ref[...] = placed
    back_rows = blocks * row_share
    source = iota((back_rows, rows), 0)
    wanted = source // row_share * merged_rows + source % row_share
    row_pick = (iota((back_rows, rows), 1) == wanted).astype(F32).astype(BF16)
    back_ref[...] = dot(dot_nt(row_pick, placed), cot_ref[...]).astype(BF16)


def flat_gain(gain_ref):
    return jnp.concatenate([gain_ref[h : h + 1] for h in range(gain_ref.shape[0])], axis=1)


def attend_kernel(*refs, blocks, row_share):
    query_ref, gain_ref = refs[:2]
    near_refs = refs[2 : 2 + blocks]
    merged_ref, meta_ref, left_ref, scalar_ref = refs[2 + blocks :]
    heads, size, patches = query_ref.shape
    rows, features = merged_ref.shape
    depth = heads * size
    near = [ref[...].astype(F32) for ref in near_refs]
    meta_ref[...] = jnp.concatenate([part[2 * depth :] for part in near], axis=0).astype(BF16)
    key_ids = jnp.concatenate([part[2 * depth + 8 : 2 * depth + 9] for part in near], axis=1)
    eye = iota((patches, patches), 0) == iota((patches, patches), 1)
    own_ids = jnp.sum(jnp.where(eye, key_ids[:, :patches], 0.0), axis=1, keepdims=True)
    same = own_ids == key_ids
    spread = jnp.zeros((patches, features), F32)
    place_row, place_col = iota((size, features), 0), iota((size, features), 1)
    for head in range(heads):
        first = head * size
        keys = jnp.concatenate([part[first : first + size] for part in near], axis=1)
        first = depth + head * size
        values = jnp.concatenate([part[first : first + size] for part in near], axis=1)
        query = query_ref[head].astype(F32).T.astype(BF16)
        scores = dot(query, keys) * (size**-0.5)
        scores = jnp.where(same, scores, -1e30)
        weights = jnp.exp(scores - jnp.max(scores, axis=1, keepdims=True))
        total = jnp.sum(weights, axis=1, keepdims=True)
        attn = dot_nt(weights.astype(BF16), values.astype(BF16)) / total
        place = (place_col % size == place_row) & (place_col // (4 * size) == head)
        spread = spread + dot(attn, place.astype(F32))
    spot = iota((patches, features), 1) // size % 4 == iota((patches, features), 0) % 4
    line = iota((rows, patches), 0)
    line = ((line // row_share) ^ lax.axis_index("expert")) * row_share + line % row_share
    fold = (iota((rows, patches), 1) // 4 == line).astype(F32)
    merged = dot(fold, jnp.where(spot, spread, 0.0))
    merged_ref[...] = merged.astype(BF16)
    local_mean = jnp.sum(merged, axis=1, keepdims=True) / features
    centered = merged - local_mean
    squares = jnp.sum(centered * centered, axis=1, keepdims=True)
    gain = flat_gain(gain_ref)
    gain_high = gain.astype(BF16).astype(F32)
    extra = iota((16, features), 0)
    gain_rows = jnp.where(extra == 0, gain_high, jnp.where(extra == 1, gain - gain_high, 0.0))
    left_ref[...] = jnp.concatenate([centered * gain, gain_rows], axis=0).astype(BF16)
    scalar_ref[...] = put_scalars([local_mean, squares], rows)


def project_kernel(left_ref, scalar_ref, weight_ref, _, *message_refs):
    rows = scalar_ref.shape[0]
    width = weight_ref.shape[1]
    row_share = rows // len(message_refs)
    product = dot(left_ref[...], weight_ref[...])
    gain_sum = product[rows : rows + 1] + product[rows + 1 : rows + 2]
    piece = width // row_share
    pieces = [gain_sum[:, j * piece : (j + 1) * piece] for j in range(row_share)]
    pieces = jnp.concatenate(pieces, axis=0).astype(BF16)
    scalars = scalar_ref[...].astype(BF16)
    for k, message_ref in enumerate(message_refs):
        mine = slice(k * row_share, (k + 1) * row_share)
        message_ref[:, :width] = product[mine].astype(BF16)
        message_ref[:, width : width + piece] = pieces
        message_ref[:, width + piece :] = scalars[mine]


def merge_kernel(_, *refs, width, features):
    *message_refs, out_ref, vision_ref, gain_ref = refs
    share, row_share = len(message_refs), out_ref.shape[0]
    piece = width // row_share
    parts = [ref[...].astype(F32) for ref in message_refs]
    scalars = [part[:, width + piece :] for part in parts]
    means = [get_scalar(block, 0) for block in scalars]
    squares = [get_scalar(block, 1) for block in scalars]
    mean = sum(means) / share
    spread = sum(q + features * (m - mean) * (m - mean) for q, m in zip(squares, means))
    inv_std = lax.rsqrt(spread / (share * features) + EPS)
    total = jnp.zeros((row_share, width), F32)
    gain_total = jnp.zeros((1, width), F32)
    for part, local in zip(parts, means):
        tail = part[:, width : width + piece]
        gain_sum = jnp.concatenate([tail[j : j + 1] for j in range(row_share)], axis=1)
        total = total + part[:, :width] + (local - mean) * gain_sum
        gain_total = gain_total + gain_sum
    vision_ref[...] = total * inv_std
    gain_ref[...] = gain_total
    out_ref[:, :width] = (total * inv_std).astype(BF16)
    out_ref[:, width:] = put_scalars([mean, inv_std], row_share).astype(BF16)


def stack_kernel(*refs):
    *part_refs, out_ref = refs
    out_ref[...] = stacked(part_refs)


def stacked(part_refs):
    return jnp.concatenate([ref[...].astype(F32) for ref in part_refs], axis=0).astype(BF16)


def by_chip(own_refs, sibling_ref):
    parts = []
    sibling = sibling_ref[...].astype(F32)
    for k, own_ref in enumerate(own_refs):
        half = own_ref.shape[0] // 2
        parts.append(own_ref[...].astype(F32)[:half])
        parts.append(sibling[k * half : (k + 1) * half])
    return jnp.concatenate(parts, axis=0).astype(BF16)


def other_half_kernel(*refs, count):
    out_ref = refs[-1]
    parts = [ref[...].astype(F32)[ref.shape[0] // 2 :] for ref in refs[:count]]
    out_ref[...] = jnp.concatenate(parts, axis=0).astype(BF16)


def slot_pick(slot_count, send_rows, shift):
    row, col = iota((slot_count, send_rows), 0), iota((slot_count, send_rows), 1)
    place = row % SLOTS
    pick = (col == row // SLOTS * SEND + place + shift) & (place < CAPX)
    return pick.astype(F32)


def early_kernel(down_ref, *refs):
    *early_refs, sibling_ref, text_out, grad_out = refs
    slot_count = text_out.shape[0]
    early = by_chip(early_refs, sibling_ref)
    text_out[...] = dot(slot_pick(slot_count, early.shape[0], 0), early).astype(BF16)
    back_rows = dot(slot_pick(slot_count, early.shape[0], CAPX), early).astype(BF16)
    grad_out[...] = dot_nt(back_rows, down_ref[0])


def forward_kernel(*refs, blocks):
    slots_ref, gain_ref, gate_ref, up_ref, down_ref, text_ref = refs[:6]
    vision_refs = refs[6 : 6 + blocks]
    gate_out, up_out, *down_refs = refs[6 + blocks : -2]
    h_ref, sum_ref = refs[-2:]
    _, hidden, width = gate_ref.shape
    chosen = slots_ref[...]
    is_vision = jnp.sum(chosen.astype(F32), axis=1, keepdims=True) > 0.5
    vision = jnp.concatenate([ref[:, :width] for ref in vision_refs], axis=0)
    inputs = dot(chosen, vision)
    scale = lax.rsqrt(jnp.mean(inputs * inputs, axis=1, keepdims=True) + EPS)
    normed = inputs * scale * gain_ref[...]
    h_ref[...] = jnp.where(is_vision, normed, text_ref[...].astype(F32)).astype(BF16)
    tile = tile_of(hidden)
    for i in range(hidden // tile):
        mine = slice(i * tile, (i + 1) * tile)
        gate_pre = dot_nt(h_ref[...], gate_ref[0, mine])
        up_proj = dot_nt(h_ref[...], up_ref[0, mine])
        gate_out[:, mine] = gate_pre
        up_out[:, mine] = up_proj
        activated = gate_pre * jax.nn.sigmoid(gate_pre) * up_proj
        product = dot(activated, down_ref[0, mine])
        sum_ref[...] = product if i == 0 else sum_ref[...] + product
    count = 2 * SLOTS
    for k, ref in enumerate(down_refs):
        ref[...] = sum_ref[k * count : (k + 1) * count].astype(BF16)


def backward_kernel(
    slots_ref, grad_ref, gate_in, up_in, cot_ref, gate_ref, up_ref, even_ref, odd_ref, sum_ref,
    *, blocks,
):
    hidden = gate_ref.shape[1]
    tile = tile_of(hidden)
    for i in range(hidden // tile):
        mine = slice(i * tile, (i + 1) * tile)
        act_grad = grad_ref[:, mine]
        gate_pre, up_proj = gate_in[:, mine], up_in[:, mine]
        sigmoid = jax.nn.sigmoid(gate_pre)
        gate_grad = act_grad * up_proj * sigmoid * (1.0 + gate_pre * (1.0 - sigmoid))
        up_grad = act_grad * gate_pre * sigmoid
        product = dot(gate_grad, gate_ref[0, mine]) + dot(up_grad, up_ref[0, mine])
        sum_ref[...] = product if i == 0 else sum_ref[...] + product
    grads = dot_tn(slots_ref[...], sum_ref[...].astype(BF16))
    cots = cot_ref[...].astype(F32)
    rows, row_share = grads.shape[0] // blocks, cots.shape[0] // blocks
    parts = ([], [])
    for k in range(blocks):
        parts[k % 2].append(grads[k * rows : (k + 1) * rows])
        parts[k % 2].append(cots[k * row_share : (k + 1) * row_share])
    even_ref[...] = jnp.concatenate(parts[0], axis=0).astype(BF16)
    odd_ref[...] = jnp.concatenate(parts[1], axis=0).astype(BF16)


def tile_of(hidden):
    return 256 if hidden % 256 == 0 else hidden


def halving_order(share):
    order = [0]
    step = share // 2
    while step:
        order = order + [k + step for k in order]
        step //= 2
    return [sum(1 << j for j in range(share.bit_length() - 1) if k >> j & 1) for k in order]


def pair_sum_kernel(own_ref, sibling_ref, *out_refs):
    rows = out_refs[0].shape[0]
    total = own_ref[...].astype(F32) + sibling_ref[...].astype(F32)
    for k, out_ref in enumerate(out_refs):
        out_ref[...] = total[k * rows : (k + 1) * rows].astype(BF16)


def total_of(part_refs):
    total = part_refs[0][...].astype(F32)
    for ref in part_refs[1:]:
        total = total + ref[...].astype(F32)
    return total


def chip_sum_kernel(*refs, count):
    cot_ref, *out_refs = refs[count + 1 :]
    total = total_of(refs[:count])
    rows = cot_ref.shape[0]
    for k, out_ref in enumerate(out_refs):
        out_ref[...] = total[k * rows : (k + 1) * rows].astype(BF16)
    cot_ref[...] = total[len(out_refs) * rows :].astype(BF16)


def quarters(total, out_refs):
    count = out_refs[0].shape[0]
    for k, ref in enumerate(out_refs):
        ref[...] = total[k * count : (k + 1) * count].astype(ref.dtype)


def combine_kernel(comb_ref, *refs):
    *part_refs, sibling_ref = refs[:-4]
    rows = by_chip(part_refs, sibling_ref)
    quarters(dot_tn(comb_ref[0], rows) + dot_tn(comb_ref[1], rows), refs[-4:])


def halve_kernel(*refs):
    low, high, arrived_low, arrived_high = [ref[...].astype(F32) for ref in refs[:4]]
    quarters(jnp.concatenate([low + arrived_low, high + arrived_high], axis=0), refs[4:])


def last_halve_kernel(high_ref, arrived_ref, *refs):
    refs[-1][...] = (high_ref[...] + arrived_ref[...].astype(F32)).astype(BF16)


def finish_kernel(placed_ref, text_ref, own_ref, arrived_ref, second_ref, *refs, blocks):
    vision_refs, out_ref = refs[:blocks], refs[-1]
    count, width = out_ref.shape
    tokens = placed_ref.shape[0]
    first = lax.axis_index("expert") * count
    pick = iota((count, tokens), 1) == iota((count, tokens), 0) + first
    pick = pick.astype(F32)
    placed = dot(pick, placed_ref[...])
    is_vision = jnp.sum(placed, axis=1, keepdims=True) > 0.5
    vision = jnp.concatenate([ref[:, :width] for ref in vision_refs], axis=0)
    inputs = jnp.where(is_vision, dot(placed, vision), dot(pick, text_ref[...]))
    arrived = arrived_ref[...].astype(F32) + second_ref[...].astype(F32)
    out_ref[...] = (inputs + own_ref[...] + arrived).astype(BF16)


def lay_kernel(*refs):
    *part_refs, out_ref = refs
    count = part_refs[0].shape[0]
    for k, ref in enumerate(part_refs):
        first = pl.multiple_of((lax.axis_index("expert") ^ k) * count, count)
        out_ref[pl.ds(first, count), :] = ref[...]


def norm_grad_kernel(
    own_ref, gain_ref, cot_ref, vision_ref, total_ref, *refs, features
):
    *part_refs, out_ref = refs
    width = gain_ref.shape[1]
    hidden = total_of(part_refs)
    cotangent = cot_ref[...].astype(F32)
    inputs = own_ref[:, :width].astype(F32)
    scale = lax.rsqrt(jnp.mean(inputs * inputs, axis=1, keepdims=True) + EPS)
    pulled = hidden * gain_ref[...]
    cross = jnp.mean(pulled * inputs, axis=1, keepdims=True)
    grad = cotangent + scale * pulled - inputs * (scale * scale * scale) * cross
    grad = grad.astype(BF16)
    out_ref[:, :width] = grad
    grad = grad.astype(F32)
    grad_mean = jnp.sum(grad * total_ref[...], axis=1, keepdims=True) / features
    cross_mean = jnp.sum(grad * vision_ref[...], axis=1, keepdims=True) / features
    out_ref[:, width:] = put_scalars([grad_mean, cross_mean], grad.shape[0]).astype(BF16)


def merge_grad_kernel(*refs, size):
    gain_ref, merged_ref, scalar_ref, weight_ref, *part_refs, out_ref = refs
    rows, features = merged_ref.shape
    width = weight_ref.shape[1]
    depth, patches = out_ref.shape
    row_share = part_refs[0].shape[0]
    parts = stacked(part_refs)
    normed_grad = dot_nt(parts[:, :width], weight_ref[...]) * flat_gain(gain_ref)
    means = parts[:, width:].astype(F32)
    scalars = scalar_ref[:, width:].astype(F32)
    inv_std = get_scalar(scalars, 1)
    normed = (merged_ref[...].astype(F32) - get_scalar(scalars, 0)) * inv_std
    grad = inv_std * (normed_grad - get_scalar(means, 0) - normed * get_scalar(means, 1))
    high = grad.astype(BF16)
    low = (grad - high.astype(F32)).astype(BF16)
    line = iota((patches, rows), 1)
    line = ((line // row_share) ^ lax.axis_index("expert")) * row_share + line % row_share
    unfold = (iota((patches, rows), 0) // 4 == line).astype(F32)
    spot = iota((patches, features), 1) // size % 4 == iota((patches, features), 0) % 4
    row, col = iota((depth, features), 0), iota((depth, features), 1)
    place = (col // (4 * size) == row // size) & (col % size == row % size)
    place = place.astype(F32).astype(BF16)
    out = jnp.zeros((depth, patches), F32)
    for piece in (high, low):
        wide = jnp.where(spot, dot(unfold, piece), 0.0).astype(BF16)
        out = out + dot_nt(place, wide)
    out_ref[...] = out


def whole(memory_space=pltpu.VMEM):
    return pl.BlockSpec(memory_space=memory_space)


def run(kernel, outs, *args, far=(), scratch=(), cost=1.0, vmem=VMEM_BYTES, name=None):
    specs = [whole()] * len(args)
    for place in far:
        specs[place] = whole(pl.ANY)
    return pl.pallas_call(
        kernel,
        out_shape=outs,
        in_specs=specs,
        out_specs=jax.tree.map(lambda _: whole(), outs),
        scratch_shapes=scratch,
        compiler_params=pltpu.CompilerParams(vmem_limit_bytes=vmem),
        cost_estimate=microseconds(cost),
        name=name,
    )(*args)


def to_sibling(parts, deps, name):
    rows, width = parts[0].shape
    half = run(
        functools.partial(other_half_kernel, count=len(parts)),
        shape((len(parts) * rows // 2, width)), *parts, *deps,
        far=range(len(parts), len(parts) + len(deps)), cost=0.3, name=name,
    )
    return swap(half, "blk", 1)


def microseconds(time):
    return pl.CostEstimate(flops=0, transcendentals=0, bytes_accessed=int(time * 3e6))


def after(values, deps):
    count = len(values)
    return pl.pallas_call(
        lambda *refs: None,
        out_shape=[shape(value.shape, value.dtype) for value in values],
        in_specs=[whole(pl.ANY)] * (count + len(deps)),
        out_specs=[whole(pl.ANY)] * count,
        input_output_aliases={i: i for i in range(count)},
        compiler_params=pltpu.CompilerParams(vmem_limit_bytes=VMEM_BYTES),
        cost_estimate=microseconds(0.1),
        name="after",
    )(*values, *deps)


def shape(dims, dtype=BF16):
    return jax.ShapeDtypeStruct(dims, dtype)


def swap(value, axis, step):
    count = lax.axis_size(axis)
    return lax.ppermute(value, axis, [(i, i ^ step) for i in range(count)])


def trade(parts, axis):
    return [parts[0]] + [swap(parts[k], axis, k) for k in range(1, len(parts))]


def spread_out(value, axis):
    return trade([value] * lax.axis_size(axis), axis)


def gather_blocks(value, deps=None):
    own = [value] + [swap(value, "blk", k) for k in range(2, lax.axis_size("blk"), 2)]
    if deps is not None:
        own = own[:1] + list(after(own[1:], deps))
    sibling = [swap(part, "blk", 1) for part in own]
    return [part for pair in zip(own, sibling) for part in pair]


def to_chips(parts):
    return [parts[0]] + [swap(parts[k], "blk", 2 * k) for k in range(1, len(parts))]


def body(
    queries, keys, values, image_ids, placement, merge_gain, merge_weight, text, norm_gain,
    w_gate, w_up, w_down, routes, route_gates, cotangent,
):
    blocks = lax.axis_size("blk")
    share = lax.axis_size("expert")
    heads, size, patches = queries.shape
    depth = heads * size
    rows = image_ids.shape[0]
    row_share = rows // share
    tokens, width = text.shape
    part = tokens // share
    all_rows = blocks * rows
    features = heads * 4 * size
    hidden = w_gate.shape[1]
    slot_count = blocks * SLOTS
    groups = share // 2
    routes_t, gates_t, gain_row = routes.T, route_gates.T, norm_gain[None]

    small = [
        keys.reshape(depth, patches), values.reshape(depth, patches),
        image_ids[None], placement.reshape(1, rows), routes_t,
    ]
    local = run(
        pack_kernel, shape((2 * depth + 16, patches)), *small, far=range(5),
        scratch=[pltpu.VMEM(array.shape, array.dtype) for array in small]
        + [pltpu.SemaphoreType.DMA((5,))],
        vmem=PACK_BYTES, name="pack",
    )
    comb, pick, factor = run(
        functools.partial(route_kernel, groups=groups, share=share),
        [
            shape((2, slot_count, tokens)), shape((2, blocks * SEND, tokens)),
            shape((blocks * SEND, 128), F32),
        ],
        routes_t, gates_t, cost=3.0, name="route",
    )
    send = run(
        dispatch_kernel, [shape((2 * SEND, width))] * (blocks // 2),
        pick, factor, text, gain_row, cotangent, cost=2.0, name="dispatch",
    )
    near = gather_blocks(local, send)
    early = to_chips(after(send, near[1:]))

    weight_flat = merge_weight.reshape(features, width)
    message_width = width + width // row_share + 128
    merged, meta, left, local_scalars = run(
        functools.partial(attend_kernel, blocks=blocks, row_share=row_share),
        [
            shape((rows, features)), shape((blocks * 16, patches)), shape((rows + 16, features)),
            shape((rows, 128), F32),
        ],
        queries, merge_gain, *near, cost=3.0, name="attend",
    )
    message = run(
        project_kernel, [shape((row_share, message_width))] * share,
        left, local_scalars, weight_flat, early[1], far=(3,), cost=2.0, name="project",
    )
    slots, placed, back_cots = run(
        functools.partial(
            plan_kernel, blocks=blocks, groups=groups, merged_rows=rows, row_share=row_share
        ),
        [
            shape((slot_count, all_rows)), shape((tokens, all_rows)),
            shape((blocks * row_share, width)),
        ],
        meta, cotangent, cost=1.5, name="plan",
    )
    message = trade(message, "expert")
    early = early[:1] + list(after(early[1:], message[1:]))
    own, vision_exact, gain_total = run(
        functools.partial(merge_kernel, width=width, features=features),
        [
            shape((row_share, width + 128)), shape((row_share, width), F32),
            shape((1, width), F32),
        ],
        early[1], *message, far=(0,), cost=0.2, name="merge",
    )
    owns = spread_out(own, "expert")
    block_rows = run(
        stack_kernel, shape((rows, width + 128)), *owns, cost=0.2, name="stack",
    )
    vision = gather_blocks(block_rows)
    text_rows, act_grad = run(
        early_kernel, [shape((slot_count, width)), shape((slot_count, hidden), F32)],
        w_down, *early, to_sibling(early, owns[1:], "early_half"), cost=3.0, name="early",
    )

    gate_pre, up_proj, *down = run(
        functools.partial(forward_kernel, blocks=blocks),
        [
            shape((slot_count, hidden), F32), shape((slot_count, hidden), F32),
        ] + [shape((2 * SLOTS, width))] * (blocks // 2),
        slots, gain_row, w_gate, w_up, w_down, text_rows, *vision,
        scratch=[pltpu.VMEM((slot_count, width), BF16), pltpu.VMEM((slot_count, width), F32)],
        cost=4.0, name="forward",
    )
    returned = to_chips(down)
    block = rows + row_share
    even, odd = run(
        functools.partial(backward_kernel, blocks=blocks),
        [shape((blocks // 2 * block, width))] * 2,
        slots, act_grad, gate_pre, up_proj, back_cots, w_gate, w_up,
        scratch=[pltpu.VMEM((slot_count, width), F32)],
        cost=4.0, name="backward",
    )
    grads = run(
        pair_sum_kernel, [shape((block, width))] * (blocks // 2), even, swap(odd, "blk", 1),
        cost=0.2, name="pair_sum",
    )
    grads = to_chips(grads)
    count = tokens // 4
    pieces = [shape((count, width), F32)] * 2 + [shape((count, width))] * 2
    low, high, sent_low, sent_high = run(
        combine_kernel, pieces, comb, *returned,
        to_sibling(returned, grads[:1], "returned_half"), cost=0.5, name="combine",
    )
    first_sent, step = sent_low, 1
    arrived_high = swap(sent_high, "expert", step)
    arrived_low = swap(sent_low, "expert", step)
    while count > part:
        count //= 2
        step *= 2
        pieces = [shape((count, width), F32)] * 2 + [shape((count, width))] * 2
        low, high, sent_low, sent_high = run(
            halve_kernel, pieces, low, high, arrived_low, arrived_high, cost=0.3, name="halve"
        )
        arrived_high = swap(sent_high, "expert", step)
        arrived_low = swap(sent_low, "expert", step)
    step *= 2
    chips = len(grads) - 1
    sent = run(
        last_halve_kernel, shape((part, width)), high, arrived_high, *grads[1:],
        far=range(2, 2 + chips), cost=0.3, name="last_halve",
    )
    cot_rows, *grads = run(
        functools.partial(chip_sum_kernel, count=blocks // 2),
        [shape((row_share, width))] * (share + 1), *grads, first_sent, far=(blocks // 2,), cost=0.2,
        name="chip_sum",
    )
    grads = trade(grads, "expert")
    vision_grad = run(
        functools.partial(norm_grad_kernel, features=share * features),
        shape((row_share, width + 128)),
        own, gain_row, cot_rows, vision_exact, gain_total, *grads, cost=0.3, name="norm_grad",
    )
    vision_grads = spread_out(vision_grad, "expert")
    attn_grad = run(
        functools.partial(merge_grad_kernel, size=size), shape((depth, patches), F32),
        merge_gain, merged, block_rows, weight_flat, *vision_grads, cost=4.0, name="merge_grad",
    )

    finished = run(
        functools.partial(finish_kernel, blocks=blocks), shape((part, width)),
        placed, text, low, arrived_low, swap(sent, "expert", step), *vision, *grads[1:],
        far=range(5 + blocks, 4 + blocks + share),
        cost=1.0, name="finish",
    )
    laid = {0: finished}
    while step:
        far_ones = [k for k in laid if k]
        if far_ones:
            laid.update(zip(far_ones, after([laid[k] for k in far_ones], vision_grads[1:])))
        laid.update({k + step: swap(laid[k], "expert", step) for k in list(laid)})
        step //= 2
    llm_out = run(
        lay_kernel, shape((tokens, width)), *[laid[k] for k in sorted(laid)], cost=1.0, name="lay"
    )
    return llm_out, attn_grad.reshape(heads, size, patches)


def solution(mesh):
    return jax.shard_map(
        body,
        mesh=mesh,
        in_specs=(
            P("expert", None, "blk"),
            P("expert", None, "blk"),
            P("expert", None, "blk"),
            P("blk"),
            P("blk", None),
            P("expert", None),
            P("expert", None, None),
            P("blk", None),
            P(),
            P("blk", "expert", None),
            P("blk", "expert", None),
            P("blk", "expert", None),
            P("blk", None),
            P("blk", None),
            P("blk", None),
        ),
        out_specs=(P("blk", None), P("expert", None, "blk")),
        check_vma=False,
    )
```

```python
import functools

import jax
import jax.numpy as jnp
from jax import lax
from jax.experimental import pallas as pl
from jax.experimental.pallas import tpu as pltpu
from jax.sharding import PartitionSpec as P

CAPX = 10
SLOTS = 16
SEND = 24
EPS = 1e-06
VMEM_BYTES = 16 * 1024 * 1024
PACK_BYTES = 60 * 1024 * 1024
F32 = jnp.float32
BF16 = jnp.bfloat16


def iota(shape, dim):
    return lax.broadcasted_iota(jnp.int32, shape, dim)


def dot(a, b):
    return jnp.dot(a.astype(BF16), b.astype(BF16), preferred_element_type=F32)


def dot_nt(a, b):
    return lax.dot_general(a, b, (((1,), (1,)), ((), ())), preferred_element_type=F32)


def dot_tn(a, b):
    return lax.dot_general(a, b, (((0,), (0,)), ((), ())), preferred_element_type=F32)


def three(value):
    first = value.astype(BF16).astype(F32)
    second = (value - first).astype(BF16).astype(F32)
    return first, second, value - first - second


def put_scalars(columns, rows):
    lane = iota((rows, 128), 1)
    out = jnp.zeros((rows, 128), F32)
    place = 0
    for column in columns:
        for piece in three(column):
            out = jnp.where(lane == place, piece, out)
            place += 1
    return out


def get_scalar(block, which):
    lane = iota(block.shape, 1)
    return jnp.sum(jnp.where(lane // 3 == which, block, 0.0), axis=1, keepdims=True)


def bring(far_refs, near_refs, sems):
    copies = [
        pltpu.make_async_copy(far, near, sems.at[i])
        for i, (far, near) in enumerate(zip(far_refs, near_refs))
    ]
    for copy in copies:
        copy.start()
    return copies


def pack_kernel(*refs):
    far_refs, out_ref, near_refs, sems = refs[:5], refs[5], refs[6:11], refs[11]
    for copy in bring(far_refs, near_refs, sems):
        copy.wait()
    out_ref[...] = packed(*near_refs).astype(BF16)


def packed(keys_ref, values_ref, images_ref, placement_ref, routes_ref):
    rows = images_ref.shape[1]
    patches = keys_ref.shape[1]
    repeat = (iota((rows, patches), 0) == iota((rows, patches), 1) // 4).astype(F32)
    keep = (iota((rows, patches), 0) == iota((rows, patches), 1)).astype(F32)
    patch_ids = dot(images_ref[...].astype(F32), repeat)
    dest = dot(placement_ref[...].astype(F32), keep)
    line = iota((8, patches), 0)
    rest = jnp.where(line == 0, patch_ids, jnp.where(line == 1, dest, 0.0))
    parts = [keys_ref[...], values_ref[...], routes_ref[...], rest]
    return jnp.concatenate([part.astype(F32) for part in parts], axis=0)


def route_kernel(routes_ref, gates_ref, comb_ref, pick_ref, factor_ref, *, groups, share):
    blocks = comb_ref.shape[1] // SLOTS
    tokens = routes_ref.shape[1]
    me, expert_index = lax.axis_index("blk"), lax.axis_index("expert")
    member = expert_index // groups
    before = (iota((tokens, tokens), 0) < iota((tokens, tokens), 1)).astype(BF16)
    pair_of = 2 * (iota((blocks, tokens), 0) ^ me) + member
    out_hit = jnp.zeros((blocks, tokens), F32)
    out_gate = jnp.zeros((blocks, tokens), F32)
    for k in range(routes_ref.shape[0]):
        same = pair_of == routes_ref[k : k + 1, :]
        out_hit = out_hit + same.astype(F32)
        out_gate = out_gate + jnp.where(same, gates_ref[k : k + 1, :], 0.0)
    out_rank = dot(out_hit, before)

    def expand(stride):
        count = blocks * stride
        pick = (iota((count, blocks), 0) // stride == iota((count, blocks), 1)).astype(BF16)
        gate = sum(dot(pick, piece) for piece in three(out_gate))
        return dot(pick, out_hit), dot(pick, out_rank).astype(jnp.int32), gate

    hits, ranks, gates = expand(SLOTS)
    live = jnp.where(ranks == iota(hits.shape, 0) % SLOTS, hits, 0.0)
    weight = live * gates
    high = weight.astype(BF16).astype(F32)
    part = tokens // share
    col = iota((tokens, tokens), 1)
    turned = (col // part * 0).astype(jnp.int32)
    for place, k in enumerate(halving_order(share)):
        turned = jnp.where(col // part == place, k, turned)
    turned = (iota((tokens, tokens), 0) == (turned ^ expert_index) * part + col % part)
    turned = turned.astype(F32)
    comb_ref[0] = dot(high, turned).astype(BF16)
    comb_ref[1] = dot(weight - high, turned).astype(BF16)

    hits, ranks, gates = expand(SEND)
    place = iota(hits.shape, 0) % SEND
    input_pick = jnp.where((place < CAPX) & (ranks == place), hits, 0.0)
    back_pick = jnp.where((place >= CAPX) & (place < 2 * CAPX) & (ranks == place - CAPX), hits, 0.0)
    pick_ref[0] = input_pick.astype(BF16)
    pick_ref[1] = back_pick.astype(BF16)
    factor = jnp.sum(back_pick * gates, axis=1, keepdims=True)
    factor_ref[...] = jnp.broadcast_to(factor, factor_ref.shape)


def dispatch_kernel(pick_ref, factor_ref, text_ref, gain_ref, cot_ref, *send_refs):
    text = text_ref[...].astype(F32)
    scale = lax.rsqrt(jnp.mean(text * text, axis=1, keepdims=True) + EPS)
    h_rows = (text * scale * gain_ref[...]).astype(BF16)
    factor = factor_ref[:, :1]
    send = dot(pick_ref[0], h_rows) + factor * dot(pick_ref[1], cot_ref[...])
    send = send.astype(BF16)
    count = 2 * SEND
    for k, ref in enumerate(send_refs):
        ref[...] = send[k * count : (k + 1) * count]


def plan_kernel(
    meta_ref, cot_ref, slots_ref, placed_ref, back_ref, *, blocks, groups, merged_rows, row_share
):
    tokens = cot_ref.shape[0]
    rows = blocks * merged_rows
    me, expert_index = lax.axis_index("blk"), lax.axis_index("expert")
    member = expert_index // groups
    meta = [meta_ref[k * 16 : (k + 1) * 16].astype(F32) for k in range(blocks)]
    mine = (2 * me + member).astype(F32)
    hits = [jnp.sum((part[:8] == mine).astype(F32), axis=0, keepdims=True) for part in meta]
    hit = jnp.concatenate(hits, axis=0)
    dest = jnp.concatenate([part[9:10] for part in meta], axis=0)
    before = (iota((tokens, tokens), 0) < iota((tokens, tokens), 1)).astype(BF16)
    rank = dot(hit, before)

    def row_of(col):
        inner = col % merged_rows
        return ((inner // row_share) ^ expert_index) * row_share + inner % row_share

    def place_of(col):
        return ((col // merged_rows) ^ me) * merged_rows + row_of(col)

    spread = (iota((128, rows), 0) == row_of(iota((128, rows), 1))).astype(F32)
    own_block = iota((blocks, rows), 1) // merged_rows == iota((blocks, rows), 0)
    dest_row = jnp.sum(jnp.where(own_block, dot(dest, spread), 0.0), axis=0, keepdims=True)
    dest_row = dest_row.astype(jnp.int32) ^ me
    dest_hit = (iota((blocks, rows), 0) == dest_row).astype(F32)
    rows_before = place_of(iota((rows, rows), 0)) < place_of(iota((rows, rows), 1))
    earlier = dot(dest_hit, rows_before.astype(F32))
    slot = jnp.sum(dest_hit * earlier, axis=0, keepdims=True).astype(jnp.int32)
    at_token = (iota((tokens, rows), 0) == slot).astype(F32)
    row_hit = jnp.sum(dest_hit * dot(hit, at_token), axis=0, keepdims=True)
    row_rank = jnp.sum(dest_hit * dot(rank, at_token), axis=0, keepdims=True).astype(jnp.int32)
    slot_id = dest_row * SLOTS + row_rank
    slot_count = slots_ref.shape[0]
    chosen = (iota((slot_count, rows), 0) == slot_id) & (row_hit > 0.5)
    slots_ref[...] = chosen.astype(F32).astype(BF16)
    placed = jnp.where(dest_row == 0, at_token, 0.0).astype(BF16)
    placed_ref[...] = placed
    back_rows = blocks * row_share
    source = iota((back_rows, rows), 0)
    wanted = source // row_share * merged_rows + source % row_share
    row_pick = (iota((back_rows, rows), 1) == wanted).astype(F32).astype(BF16)
    back_ref[...] = dot(dot_nt(row_pick, placed), cot_ref[...]).astype(BF16)


def flat_gain(gain_ref):
    return jnp.concatenate([gain_ref[h : h + 1] for h in range(gain_ref.shape[0])], axis=1)


def attend_kernel(*refs, blocks, row_share):
    query_ref, gain_ref = refs[:2]
    near_refs = refs[7 : 6 + blocks]
    merged_ref, meta_ref, left_ref, scalar_ref = refs[6 + blocks :]
    heads, size, patches = query_ref.shape
    rows, features = merged_ref.shape
    depth = heads * size
    near = [packed(*refs[2:7])] + [ref[...].astype(F32) for ref in near_refs]
    meta_ref[...] = jnp.concatenate([part[2 * depth :] for part in near], axis=0).astype(BF16)
    key_ids = jnp.concatenate([part[2 * depth + 8 : 2 * depth + 9] for part in near], axis=1)
    eye = iota((patches, patches), 0) == iota((patches, patches), 1)
    own_ids = jnp.sum(jnp.where(eye, key_ids[:, :patches], 0.0), axis=1, keepdims=True)
    same = own_ids == key_ids
    spread = jnp.zeros((patches, features), F32)
    place_row, place_col = iota((size, features), 0), iota((size, features), 1)
    for head in range(heads):
        first = head * size
        keys = jnp.concatenate([part[first : first + size] for part in near], axis=1)
        first = depth + head * size
        values = jnp.concatenate([part[first : first + size] for part in near], axis=1)
        query = query_ref[head].astype(F32).T.astype(BF16)
        scores = dot(query, keys) * (size**-0.5)
        scores = jnp.where(same, scores, -1e30)
        weights = jnp.exp(scores - jnp.max(scores, axis=1, keepdims=True))
        total = jnp.sum(weights, axis=1, keepdims=True)
        attn = dot_nt(weights.astype(BF16), values.astype(BF16)) / total
        place = (place_col % size == place_row) & (place_col // (4 * size) == head)
        spread = spread + dot(attn, place.astype(F32))
    spot = iota((patches, features), 1) // size % 4 == iota((patches, features), 0) % 4
    line = iota((rows, patches), 0)
    line = ((line // row_share) ^ lax.axis_index("expert")) * row_share + line % row_share
    fold = (iota((rows, patches), 1) // 4 == line).astype(F32)
    merged = dot(fold, jnp.where(spot, spread, 0.0))
    merged_ref[...] = merged.astype(BF16)
    local_mean = jnp.sum(merged, axis=1, keepdims=True) / features
    centered = merged - local_mean
    squares = jnp.sum(centered * centered, axis=1, keepdims=True)
    gain = flat_gain(gain_ref)
    gain_high = gain.astype(BF16).astype(F32)
    extra = iota((16, features), 0)
    gain_rows = jnp.where(extra == 0, gain_high, jnp.where(extra == 1, gain - gain_high, 0.0))
    left_ref[...] = jnp.concatenate([centered * gain, gain_rows], axis=0).astype(BF16)
    scalar_ref[...] = put_scalars([local_mean, squares], rows)


def project_kernel(left_ref, scalar_ref, weight_ref, _, *message_refs):
    rows = scalar_ref.shape[0]
    width = weight_ref.shape[1]
    row_share = rows // len(message_refs)
    product = dot(left_ref[...], weight_ref[...])
    gain_sum = product[rows : rows + 1] + product[rows + 1 : rows + 2]
    piece = width // row_share
    pieces = [gain_sum[:, j * piece : (j + 1) * piece] for j in range(row_share)]
    pieces = jnp.concatenate(pieces, axis=0).astype(BF16)
    scalars = scalar_ref[...].astype(BF16)
    for k, message_ref in enumerate(message_refs):
        mine = slice(k * row_share, (k + 1) * row_share)
        message_ref[:, :width] = product[mine].astype(BF16)
        message_ref[:, width : width + piece] = pieces
        message_ref[:, width + piece :] = scalars[mine]


def merge_kernel(_, *refs, width, features):
    *message_refs, out_ref, vision_ref, gain_ref = refs
    share, row_share = len(message_refs), out_ref.shape[0]
    piece = width // row_share
    parts = [ref[...].astype(F32) for ref in message_refs]
    scalars = [part[:, width + piece :] for part in parts]
    means = [get_scalar(block, 0) for block in scalars]
    squares = [get_scalar(block, 1) for block in scalars]
    mean = sum(means) / share
    spread = sum(q + features * (m - mean) * (m - mean) for q, m in zip(squares, means))
    inv_std = lax.rsqrt(spread / (share * features) + EPS)
    total = jnp.zeros((row_share, width), F32)
    gain_total = jnp.zeros((1, width), F32)
    for part, local in zip(parts, means):
        tail = part[:, width : width + piece]
        gain_sum = jnp.concatenate([tail[j : j + 1] for j in range(row_share)], axis=1)
        total = total + part[:, :width] + (local - mean) * gain_sum
        gain_total = gain_total + gain_sum
    vision_ref[...] = total * inv_std
    gain_ref[...] = gain_total
    out_ref[:, :width] = (total * inv_std).astype(BF16)
    out_ref[:, width:] = put_scalars([mean, inv_std], row_share).astype(BF16)


def stack_kernel(*refs):
    *part_refs, out_ref = refs
    out_ref[...] = stacked(part_refs)


def stacked(part_refs):
    return jnp.concatenate([ref[...].astype(F32) for ref in part_refs], axis=0).astype(BF16)


def by_chip(own_refs, sibling_ref):
    parts = []
    sibling = sibling_ref[...].astype(F32)
    for k, own_ref in enumerate(own_refs):
        half = own_ref.shape[0] // 2
        parts.append(own_ref[...].astype(F32)[:half])
        parts.append(sibling[k * half : (k + 1) * half])
    return jnp.concatenate(parts, axis=0).astype(BF16)


def other_half_kernel(*refs, count):
    out_ref = refs[-1]
    parts = [ref[...].astype(F32)[ref.shape[0] // 2 :] for ref in refs[:count]]
    out_ref[...] = jnp.concatenate(parts, axis=0).astype(BF16)


def slot_pick(slot_count, send_rows, shift):
    row, col = iota((slot_count, send_rows), 0), iota((slot_count, send_rows), 1)
    place = row % SLOTS
    pick = (col == row // SLOTS * SEND + place + shift) & (place < CAPX)
    return pick.astype(F32)


def early_kernel(down_ref, *refs):
    *early_refs, sibling_ref, text_out, grad_out = refs
    slot_count = text_out.shape[0]
    early = by_chip(early_refs, sibling_ref)
    text_out[...] = dot(slot_pick(slot_count, early.shape[0], 0), early).astype(BF16)
    back_rows = dot(slot_pick(slot_count, early.shape[0], CAPX), early).astype(BF16)
    grad_out[...] = dot_nt(back_rows, down_ref[0])


def forward_kernel(*refs, blocks):
    slots_ref, gain_ref, gate_ref, up_ref, down_ref, text_ref = refs[:6]
    vision_refs = refs[6 : 6 + blocks]
    gate_out, up_out, *down_refs = refs[6 + blocks : -2]
    h_ref, sum_ref = refs[-2:]
    _, hidden, width = gate_ref.shape
    chosen = slots_ref[...]
    is_vision = jnp.sum(chosen.astype(F32), axis=1, keepdims=True) > 0.5
    vision = jnp.concatenate([ref[:, :width] for ref in vision_refs], axis=0)
    inputs = dot(chosen, vision)
    scale = lax.rsqrt(jnp.mean(inputs * inputs, axis=1, keepdims=True) + EPS)
    normed = inputs * scale * gain_ref[...]
    h_ref[...] = jnp.where(is_vision, normed, text_ref[...].astype(F32)).astype(BF16)
    tile = tile_of(hidden)
    for i in range(hidden // tile):
        mine = slice(i * tile, (i + 1) * tile)
        gate_pre = dot_nt(h_ref[...], gate_ref[0, mine])
        up_proj = dot_nt(h_ref[...], up_ref[0, mine])
        gate_out[:, mine] = gate_pre
        up_out[:, mine] = up_proj
        activated = gate_pre * jax.nn.sigmoid(gate_pre) * up_proj
        product = dot(activated, down_ref[0, mine])
        sum_ref[...] = product if i == 0 else sum_ref[...] + product
    count = 2 * SLOTS
    for k, ref in enumerate(down_refs):
        ref[...] = sum_ref[k * count : (k + 1) * count].astype(BF16)


def backward_kernel(
    slots_ref, grad_ref, gate_in, up_in, cot_ref, gate_ref, up_ref, even_ref, odd_ref, sum_ref,
    *, blocks,
):
    hidden = gate_ref.shape[1]
    tile = tile_of(hidden)
    for i in range(hidden // tile):
        mine = slice(i * tile, (i + 1) * tile)
        act_grad = grad_ref[:, mine]
        gate_pre, up_proj = gate_in[:, mine], up_in[:, mine]
        sigmoid = jax.nn.sigmoid(gate_pre)
        gate_grad = act_grad * up_proj * sigmoid * (1.0 + gate_pre * (1.0 - sigmoid))
        up_grad = act_grad * gate_pre * sigmoid
        product = dot(gate_grad, gate_ref[0, mine]) + dot(up_grad, up_ref[0, mine])
        sum_ref[...] = product if i == 0 else sum_ref[...] + product
    grads = dot_tn(slots_ref[...], sum_ref[...].astype(BF16))
    cots = cot_ref[...].astype(F32)
    rows, row_share = grads.shape[0] // blocks, cots.shape[0] // blocks
    parts = ([], [])
    for k in range(blocks):
        parts[k % 2].append(grads[k * rows : (k + 1) * rows])
        parts[k % 2].append(cots[k * row_share : (k + 1) * row_share])
    even_ref[...] = jnp.concatenate(parts[0], axis=0).astype(BF16)
    odd_ref[...] = jnp.concatenate(parts[1], axis=0).astype(BF16)


def tile_of(hidden):
    return 256 if hidden % 256 == 0 else hidden


def halving_order(share):
    order = [0]
    step = share // 2
    while step:
        order = order + [k + step for k in order]
        step //= 2
    return [sum(1 << j for j in range(share.bit_length() - 1) if k >> j & 1) for k in order]


def pair_sum_kernel(own_ref, sibling_ref, *out_refs):
    rows = out_refs[0].shape[0]
    total = own_ref[...].astype(F32) + sibling_ref[...].astype(F32)
    for k, out_ref in enumerate(out_refs):
        out_ref[...] = total[k * rows : (k + 1) * rows].astype(BF16)


def total_of(part_refs):
    total = part_refs[0][...].astype(F32)
    for ref in part_refs[1:]:
        total = total + ref[...].astype(F32)
    return total


def chip_sum_kernel(*refs, count):
    cot_ref, *out_refs = refs[count + 1 :]
    total = total_of(refs[:count])
    rows = cot_ref.shape[0]
    for k, out_ref in enumerate(out_refs):
        out_ref[...] = total[k * rows : (k + 1) * rows].astype(BF16)
    cot_ref[...] = total[len(out_refs) * rows :].astype(BF16)


def quarters(total, out_refs):
    count = out_refs[0].shape[0]
    for k, ref in enumerate(out_refs):
        ref[...] = total[k * count : (k + 1) * count].astype(ref.dtype)


def combine_kernel(comb_ref, *refs):
    *part_refs, sibling_ref = refs[:-4]
    rows = by_chip(part_refs, sibling_ref)
    quarters(dot_tn(comb_ref[0], rows) + dot_tn(comb_ref[1], rows), refs[-4:])


def halve_kernel(*refs):
    low, high, arrived_low, arrived_high = [ref[...].astype(F32) for ref in refs[:4]]
    quarters(jnp.concatenate([low + arrived_low, high + arrived_high], axis=0), refs[4:])


def last_halve_kernel(high_ref, arrived_ref, *refs):
    refs[-1][...] = (high_ref[...] + arrived_ref[...].astype(F32)).astype(BF16)


def finish_kernel(placed_ref, text_ref, own_ref, arrived_ref, second_ref, *refs, blocks):
    vision_refs, out_ref = refs[:blocks], refs[-1]
    count, width = out_ref.shape
    tokens = placed_ref.shape[0]
    first = lax.axis_index("expert") * count
    pick = iota((count, tokens), 1) == iota((count, tokens), 0) + first
    pick = pick.astype(F32)
    placed = dot(pick, placed_ref[...])
    is_vision = jnp.sum(placed, axis=1, keepdims=True) > 0.5
    vision = jnp.concatenate([ref[:, :width] for ref in vision_refs], axis=0)
    inputs = jnp.where(is_vision, dot(placed, vision), dot(pick, text_ref[...]))
    arrived = arrived_ref[...].astype(F32) + second_ref[...].astype(F32)
    out_ref[...] = (inputs + own_ref[...] + arrived).astype(BF16)


def lay_kernel(*refs):
    *part_refs, out_ref = refs
    count = part_refs[0].shape[0]
    for k, ref in enumerate(part_refs):
        first = pl.multiple_of((lax.axis_index("expert") ^ k) * count, count)
        out_ref[pl.ds(first, count), :] = ref[...]


def norm_grad_kernel(
    own_ref, gain_ref, cot_ref, vision_ref, total_ref, *refs, features
):
    *part_refs, out_ref = refs
    width = gain_ref.shape[1]
    hidden = total_of(part_refs)
    cotangent = cot_ref[...].astype(F32)
    inputs = own_ref[:, :width].astype(F32)
    scale = lax.rsqrt(jnp.mean(inputs * inputs, axis=1, keepdims=True) + EPS)
    pulled = hidden * gain_ref[...]
    cross = jnp.mean(pulled * inputs, axis=1, keepdims=True)
    grad = cotangent + scale * pulled - inputs * (scale * scale * scale) * cross
    grad = grad.astype(BF16)
    out_ref[:, :width] = grad
    grad = grad.astype(F32)
    grad_mean = jnp.sum(grad * total_ref[...], axis=1, keepdims=True) / features
    cross_mean = jnp.sum(grad * vision_ref[...], axis=1, keepdims=True) / features
    out_ref[:, width:] = put_scalars([grad_mean, cross_mean], grad.shape[0]).astype(BF16)


def merge_grad_kernel(*refs, size):
    gain_ref, merged_ref, scalar_ref, weight_ref, *part_refs, out_ref = refs
    rows, features = merged_ref.shape
    width = weight_ref.shape[1]
    depth, patches = out_ref.shape
    row_share = part_refs[0].shape[0]
    parts = stacked(part_refs)
    normed_grad = dot_nt(parts[:, :width], weight_ref[...]) * flat_gain(gain_ref)
    means = parts[:, width:].astype(F32)
    scalars = scalar_ref[:, width:].astype(F32)
    inv_std = get_scalar(scalars, 1)
    normed = (merged_ref[...].astype(F32) - get_scalar(scalars, 0)) * inv_std
    grad = inv_std * (normed_grad - get_scalar(means, 0) - normed * get_scalar(means, 1))
    high = grad.astype(BF16)
    low = (grad - high.astype(F32)).astype(BF16)
    line = iota((patches, rows), 1)
    line = ((line // row_share) ^ lax.axis_index("expert")) * row_share + line % row_share
    unfold = (iota((patches, rows), 0) // 4 == line).astype(F32)
    spot = iota((patches, features), 1) // size % 4 == iota((patches, features), 0) % 4
    row, col = iota((depth, features), 0), iota((depth, features), 1)
    place = (col // (4 * size) == row // size) & (col % size == row % size)
    place = place.astype(F32).astype(BF16)
    out = jnp.zeros((depth, patches), F32)
    for piece in (high, low):
        wide = jnp.where(spot, dot(unfold, piece), 0.0).astype(BF16)
        out = out + dot_nt(place, wide)
    out_ref[...] = out


def whole(memory_space=pltpu.VMEM):
    return pl.BlockSpec(memory_space=memory_space)


def run(kernel, outs, *args, far=(), scratch=(), cost=1.0, vmem=VMEM_BYTES, name=None):
    specs = [whole()] * len(args)
    for place in far:
        specs[place] = whole(pl.ANY)
    return pl.pallas_call(
        kernel,
        out_shape=outs,
        in_specs=specs,
        out_specs=jax.tree.map(lambda _: whole(), outs),
        scratch_shapes=scratch,
        compiler_params=pltpu.CompilerParams(vmem_limit_bytes=vmem),
        cost_estimate=microseconds(cost),
        name=name,
    )(*args)


def to_sibling(parts, deps, name):
    rows, width = parts[0].shape
    half = run(
        functools.partial(other_half_kernel, count=len(parts)),
        shape((len(parts) * rows // 2, width)), *parts, *deps,
        far=range(len(parts), len(parts) + len(deps)), cost=0.01, name=name,
    )
    return swap(half, "blk", 1)


def microseconds(time):
    return pl.CostEstimate(flops=0, transcendentals=0, bytes_accessed=int(time * 3e6))


def after(values, deps):
    count = len(values)
    return pl.pallas_call(
        lambda *refs: None,
        out_shape=[shape(value.shape, value.dtype) for value in values],
        in_specs=[whole(pl.ANY)] * (count + len(deps)),
        out_specs=[whole(pl.ANY)] * count,
        input_output_aliases={i: i for i in range(count)},
        compiler_params=pltpu.CompilerParams(vmem_limit_bytes=VMEM_BYTES),
        cost_estimate=microseconds(0.1),
        name="after",
    )(*values, *deps)


def shape(dims, dtype=BF16):
    return jax.ShapeDtypeStruct(dims, dtype)


def swap(value, axis, step):
    count = lax.axis_size(axis)
    return lax.ppermute(value, axis, [(i, i ^ step) for i in range(count)])


def trade(parts, axis):
    return [parts[0]] + [swap(parts[k], axis, k) for k in range(1, len(parts))]


def spread_out(value, axis):
    return trade([value] * lax.axis_size(axis), axis)


def gather_blocks(value, deps=None):
    own = [value] + [swap(value, "blk", k) for k in range(2, lax.axis_size("blk"), 2)]
    if deps is not None:
        own = own[:1] + list(after(own[1:], deps))
    sibling = [swap(part, "blk", 1) for part in own]
    return [part for pair in zip(own, sibling) for part in pair]


def to_chips(parts):
    return [parts[0]] + [swap(parts[k], "blk", 2 * k) for k in range(1, len(parts))]


def body(
    queries, keys, values, image_ids, placement, merge_gain, merge_weight, text, norm_gain,
    w_gate, w_up, w_down, routes, route_gates, cotangent,
):
    blocks = lax.axis_size("blk")
    share = lax.axis_size("expert")
    heads, size, patches = queries.shape
    depth = heads * size
    rows = image_ids.shape[0]
    row_share = rows // share
    tokens, width = text.shape
    part = tokens // share
    all_rows = blocks * rows
    features = heads * 4 * size
    hidden = w_gate.shape[1]
    slot_count = blocks * SLOTS
    groups = share // 2
    routes_t, gates_t, gain_row = routes.T, route_gates.T, norm_gain[None]

    small = [
        keys.reshape(depth, patches), values.reshape(depth, patches),
        image_ids[None], placement.reshape(1, rows), routes_t,
    ]
    local = run(
        pack_kernel, shape((2 * depth + 16, patches)), *small, far=range(5),
        scratch=[pltpu.VMEM(array.shape, array.dtype) for array in small]
        + [pltpu.SemaphoreType.DMA((5,))],
        vmem=PACK_BYTES, name="pack",
    )
    comb, pick, factor = run(
        functools.partial(route_kernel, groups=groups, share=share),
        [
            shape((2, slot_count, tokens)), shape((2, blocks * SEND, tokens)),
            shape((blocks * SEND, 128), F32),
        ],
        routes_t, gates_t, cost=3.0, name="route",
    )
    send = run(
        dispatch_kernel, [shape((2 * SEND, width))] * (blocks // 2),
        pick, factor, text, gain_row, cotangent, cost=2.0, name="dispatch",
    )
    near = gather_blocks(local, send)
    early = to_chips(after(send, near[2::2]))

    weight_flat = merge_weight.reshape(features, width)
    message_width = width + width // row_share + 128
    merged, meta, left, local_scalars = run(
        functools.partial(attend_kernel, blocks=blocks, row_share=row_share),
        [
            shape((rows, features)), shape((blocks * 16, patches)), shape((rows + 16, features)),
            shape((rows, 128), F32),
        ],
        queries, merge_gain, *small, *near[1:], cost=3.0, name="attend",
    )
    message = run(
        project_kernel, [shape((row_share, message_width))] * share,
        left, local_scalars, weight_flat, early[1], far=(3,), cost=2.0, name="project",
    )
    slots, placed, back_cots = run(
        functools.partial(
            plan_kernel, blocks=blocks, groups=groups, merged_rows=rows, row_share=row_share
        ),
        [
            shape((slot_count, all_rows)), shape((tokens, all_rows)),
            shape((blocks * row_share, width)),
        ],
        meta, cotangent, cost=1.5, name="plan",
    )
    message = trade(message, "expert")
    early = early[:1] + list(after(early[1:], message[1:]))
    own, vision_exact, gain_total = run(
        functools.partial(merge_kernel, width=width, features=features),
        [
            shape((row_share, width + 128)), shape((row_share, width), F32),
            shape((1, width), F32),
        ],
        early[1], *message, far=(0,), cost=0.2, name="merge",
    )
    owns = spread_out(own, "expert")
    block_rows = run(
        stack_kernel, shape((rows, width + 128)), *owns, cost=0.2, name="stack",
    )
    text_rows, act_grad = run(
        early_kernel, [shape((slot_count, width)), shape((slot_count, hidden), F32)],
        w_down, *early, to_sibling(early, owns[1:], "early_half"), cost=3.0, name="early",
    )

    vision = gather_blocks(block_rows, [text_rows, slots])
    gate_pre, up_proj, *down = run(
        functools.partial(forward_kernel, blocks=blocks),
        [
            shape((slot_count, hidden), F32), shape((slot_count, hidden), F32),
        ] + [shape((2 * SLOTS, width))] * (blocks // 2),
        slots, gain_row, w_gate, w_up, w_down, text_rows, *vision,
        scratch=[pltpu.VMEM((slot_count, width), BF16), pltpu.VMEM((slot_count, width), F32)],
        cost=4.0, name="forward",
    )
    returned = to_chips(down)
    block = rows + row_share
    even, odd = run(
        functools.partial(backward_kernel, blocks=blocks),
        [shape((blocks // 2 * block, width))] * 2,
        slots, act_grad, gate_pre, up_proj, back_cots, w_gate, w_up,
        scratch=[pltpu.VMEM((slot_count, width), F32)],
        cost=4.0, name="backward",
    )
    grads = run(
        pair_sum_kernel, [shape((block, width))] * (blocks // 2), even, swap(odd, "blk", 1),
        cost=0.2, name="pair_sum",
    )
    grads = to_chips(grads)
    count = tokens // 4
    pieces = [shape((count, width), F32)] * 2 + [shape((count, width))] * 2
    low, high, sent_low, sent_high = run(
        combine_kernel, pieces, comb, *returned,
        to_sibling(returned, grads[:1], "returned_half"), cost=0.01, name="combine",
    )
    first_sent, step = sent_low, 1
    arrived_high = swap(sent_high, "expert", step)
    arrived_low = swap(sent_low, "expert", step)
    while count > part:
        count //= 2
        step *= 2
        pieces = [shape((count, width), F32)] * 2 + [shape((count, width))] * 2
        low, high, sent_low, sent_high = run(
            halve_kernel, pieces, low, high, arrived_low, arrived_high, cost=0.3, name="halve"
        )
        arrived_high = swap(sent_high, "expert", step)
        arrived_low = swap(sent_low, "expert", step)
    step *= 2
    chips = len(grads) - 1
    sent = run(
        last_halve_kernel, shape((part, width)), high, arrived_high, *grads[1:],
        far=range(2, 2 + chips), cost=0.3, name="last_halve",
    )
    cot_rows, *grads = run(
        functools.partial(chip_sum_kernel, count=blocks // 2),
        [shape((row_share, width))] * (share + 1), *grads, first_sent, far=(blocks // 2,), cost=0.2,
        name="chip_sum",
    )
    grads = trade(grads, "expert")
    vision_grad = run(
        functools.partial(norm_grad_kernel, features=share * features),
        shape((row_share, width + 128)),
        own, gain_row, cot_rows, vision_exact, gain_total, *grads, cost=0.3, name="norm_grad",
    )
    vision_grads = spread_out(vision_grad, "expert")
    attn_grad = run(
        functools.partial(merge_grad_kernel, size=size), shape((depth, patches), F32),
        merge_gain, merged, block_rows, weight_flat, *vision_grads, cost=4.0, name="merge_grad",
    )

    finished = run(
        functools.partial(finish_kernel, blocks=blocks), shape((part, width)),
        placed, text, low, arrived_low, swap(sent, "expert", step), *vision, *grads[1:],
        far=range(5 + blocks, 4 + blocks + share),
        cost=1.0, name="finish",
    )
    laid = {0: finished}
    while step:
        far_ones = [k for k in laid if k]
        if far_ones:
            laid.update(zip(far_ones, after([laid[k] for k in far_ones], vision_grads[1:])))
        laid.update({k + step: swap(laid[k], "expert", step) for k in list(laid)})
        step //= 2
    llm_out = run(
        lay_kernel, shape((tokens, width)), *[laid[k] for k in sorted(laid)], cost=1.0, name="lay"
    )
    return llm_out, attn_grad.reshape(heads, size, patches)


def solution(mesh):
    return jax.shard_map(
        body,
        mesh=mesh,
        in_specs=(
            P("expert", None, "blk"),
            P("expert", None, "blk"),
            P("expert", None, "blk"),
            P("blk"),
            P("blk", None),
            P("expert", None),
            P("expert", None, None),
            P("blk", None),
            P(),
            P("blk", "expert", None),
            P("blk", "expert", None),
            P("blk", "expert", None),
            P("blk", None),
            P("blk", None),
            P("blk", None),
        ),
        out_specs=(P("blk", None), P("expert", None, "blk")),
        check_vma=False,
    )
```

```python
import functools

import jax
import jax.numpy as jnp
from jax import lax
from jax.experimental import pallas as pl
from jax.experimental.pallas import tpu as pltpu
from jax.sharding import PartitionSpec as P

CAPX = 10
SLOTS = 12
SEND = 24
EPS = 1e-06
VMEM_BYTES = 16 * 1024 * 1024
PACK_BYTES = 60 * 1024 * 1024
F32 = jnp.float32
BF16 = jnp.bfloat16


def iota(shape, dim):
    return lax.broadcasted_iota(jnp.int32, shape, dim)


def dot(a, b):
    return jnp.dot(a.astype(BF16), b.astype(BF16), preferred_element_type=F32)


def dot_nt(a, b):
    return lax.dot_general(a, b, (((1,), (1,)), ((), ())), preferred_element_type=F32)


def dot_tn(a, b):
    return lax.dot_general(a, b, (((0,), (0,)), ((), ())), preferred_element_type=F32)


def three(value):
    first = value.astype(BF16).astype(F32)
    second = (value - first).astype(BF16).astype(F32)
    return first, second, value - first - second


def put_scalars(columns, rows):
    lane = iota((rows, 128), 1)
    out = jnp.zeros((rows, 128), F32)
    place = 0
    for column in columns:
        for piece in three(column):
            out = jnp.where(lane == place, piece, out)
            place += 1
    return out


def get_scalar(block, which):
    lane = iota(block.shape, 1)
    return jnp.sum(jnp.where(lane // 3 == which, block, 0.0), axis=1, keepdims=True)


def bring(far_refs, near_refs, sems):
    copies = [
        pltpu.make_async_copy(far, near, sems.at[i])
        for i, (far, near) in enumerate(zip(far_refs, near_refs))
    ]
    for copy in copies:
        copy.start()
    return copies


def pack_kernel(*refs):
    far_refs, out_ref, near_refs, sems = refs[:5], refs[5], refs[6:11], refs[11]
    for copy in bring(far_refs, near_refs, sems):
        copy.wait()
    out_ref[...] = packed(*near_refs).astype(BF16)


def packed(keys_ref, values_ref, images_ref, placement_ref, routes_ref):
    rows = images_ref.shape[1]
    patches = keys_ref.shape[1]
    repeat = (iota((rows, patches), 0) == iota((rows, patches), 1) // 4).astype(F32)
    keep = (iota((rows, patches), 0) == iota((rows, patches), 1)).astype(F32)
    patch_ids = dot(images_ref[...].astype(F32), repeat)
    dest = dot(placement_ref[...].astype(F32), keep)
    line = iota((8, patches), 0)
    rest = jnp.where(line == 0, patch_ids, jnp.where(line == 1, dest, 0.0))
    parts = [keys_ref[...], values_ref[...], routes_ref[...], rest]
    return jnp.concatenate([part.astype(F32) for part in parts], axis=0)


def route_kernel(routes_ref, gates_ref, comb_ref, pick_ref, factor_ref, *, groups, share):
    blocks = comb_ref.shape[1] // SLOTS
    tokens = routes_ref.shape[1]
    me, expert_index = lax.axis_index("blk"), lax.axis_index("expert")
    member = expert_index // groups
    before = (iota((tokens, tokens), 0) < iota((tokens, tokens), 1)).astype(BF16)
    pair_of = 2 * (iota((blocks, tokens), 0) ^ me) + member
    out_hit = jnp.zeros((blocks, tokens), F32)
    out_gate = jnp.zeros((blocks, tokens), F32)
    for k in range(routes_ref.shape[0]):
        same = pair_of == routes_ref[k : k + 1, :]
        out_hit = out_hit + same.astype(F32)
        out_gate = out_gate + jnp.where(same, gates_ref[k : k + 1, :], 0.0)
    out_rank = dot(out_hit, before)

    def expand(stride):
        count = blocks * stride
        pick = (iota((count, blocks), 0) // stride == iota((count, blocks), 1)).astype(BF16)
        gate = sum(dot(pick, piece) for piece in three(out_gate))
        return dot(pick, out_hit), dot(pick, out_rank).astype(jnp.int32), gate

    hits, ranks, gates = expand(SLOTS)
    live = jnp.where(ranks == iota(hits.shape, 0) % SLOTS, hits, 0.0)
    weight = live * gates
    high = weight.astype(BF16).astype(F32)
    part = tokens // share
    col = iota((tokens, tokens), 1)
    turned = (col // part * 0).astype(jnp.int32)
    for place, k in enumerate(halving_order(share)):
        turned = jnp.where(col // part == place, k, turned)
    turned = (iota((tokens, tokens), 0) == (turned ^ expert_index) * part + col % part)
    turned = turned.astype(F32)
    comb_ref[0] = dot(high, turned).astype(BF16)
    comb_ref[1] = dot(weight - high, turned).astype(BF16)

    hits, ranks, gates = expand(SEND)
    place = iota(hits.shape, 0) % SEND
    input_pick = jnp.where((place < CAPX) & (ranks == place), hits, 0.0)
    back_pick = jnp.where((place >= CAPX) & (place < 2 * CAPX) & (ranks == place - CAPX), hits, 0.0)
    pick_ref[0] = input_pick.astype(BF16)
    pick_ref[1] = back_pick.astype(BF16)
    factor = jnp.sum(back_pick * gates, axis=1, keepdims=True)
    factor_ref[...] = jnp.broadcast_to(factor, factor_ref.shape)


def dispatch_kernel(pick_ref, factor_ref, text_ref, gain_ref, cot_ref, *send_refs):
    text = text_ref[...].astype(F32)
    scale = lax.rsqrt(jnp.mean(text * text, axis=1, keepdims=True) + EPS)
    h_rows = (text * scale * gain_ref[...]).astype(BF16)
    factor = factor_ref[:, :1]
    send = dot(pick_ref[0], h_rows) + factor * dot(pick_ref[1], cot_ref[...])
    send = send.astype(BF16)
    count = 2 * SEND
    for k, ref in enumerate(send_refs):
        ref[...] = send[k * count : (k + 1) * count]


def plan_kernel(
    meta_ref, cot_ref, slots_ref, placed_ref, back_ref, *, blocks, groups, merged_rows, row_share
):
    tokens = cot_ref.shape[0]
    rows = blocks * merged_rows
    me, expert_index = lax.axis_index("blk"), lax.axis_index("expert")
    member = expert_index // groups
    meta = [meta_ref[k * 16 : (k + 1) * 16].astype(F32) for k in range(blocks)]
    mine = (2 * me + member).astype(F32)
    hits = [jnp.sum((part[:8] == mine).astype(F32), axis=0, keepdims=True) for part in meta]
    hit = jnp.concatenate(hits, axis=0)
    dest = jnp.concatenate([part[9:10] for part in meta], axis=0)
    before = (iota((tokens, tokens), 0) < iota((tokens, tokens), 1)).astype(BF16)
    rank = dot(hit, before)

    def row_of(col):
        inner = col % merged_rows
        return ((inner // row_share) ^ expert_index) * row_share + inner % row_share

    def place_of(col):
        return ((col // merged_rows) ^ me) * merged_rows + row_of(col)

    spread = (iota((128, rows), 0) == row_of(iota((128, rows), 1))).astype(F32)
    own_block = iota((blocks, rows), 1) // merged_rows == iota((blocks, rows), 0)
    dest_row = jnp.sum(jnp.where(own_block, dot(dest, spread), 0.0), axis=0, keepdims=True)
    dest_row = dest_row.astype(jnp.int32) ^ me
    dest_hit = (iota((blocks, rows), 0) == dest_row).astype(F32)
    rows_before = place_of(iota((rows, rows), 0)) < place_of(iota((rows, rows), 1))
    earlier = dot(dest_hit, rows_before.astype(F32))
    slot = jnp.sum(dest_hit * earlier, axis=0, keepdims=True).astype(jnp.int32)
    at_token = (iota((tokens, rows), 0) == slot).astype(F32)
    row_hit = jnp.sum(dest_hit * dot(hit, at_token), axis=0, keepdims=True)
    row_rank = jnp.sum(dest_hit * dot(rank, at_token), axis=0, keepdims=True).astype(jnp.int32)
    slot_id = dest_row * SLOTS + row_rank
    slot_count = slots_ref.shape[0]
    chosen = (iota((slot_count, rows), 0) == slot_id) & (row_hit > 0.5)
    slots_ref[...] = chosen.astype(F32).astype(BF16)
    placed = jnp.where(dest_row == 0, at_token, 0.0).astype(BF16)
    placed_ref[...] = placed
    back_rows = blocks * row_share
    source = iota((back_rows, rows), 0)
    wanted = source // row_share * merged_rows + source % row_share
    row_pick = (iota((back_rows, rows), 1) == wanted).astype(F32).astype(BF16)
    back_ref[...] = dot(dot_nt(row_pick, placed), cot_ref[...]).astype(BF16)


def flat_gain(gain_ref):
    return jnp.concatenate([gain_ref[h : h + 1] for h in range(gain_ref.shape[0])], axis=1)


def attend_kernel(*refs, blocks, row_share):
    query_ref, gain_ref = refs[:2]
    near_refs = refs[7 : 6 + blocks]
    merged_ref, meta_ref, left_ref, scalar_ref = refs[6 + blocks :]
    heads, size, patches = query_ref.shape
    rows, features = merged_ref.shape
    depth = heads * size
    near = [packed(*refs[2:7])] + [ref[...].astype(F32) for ref in near_refs]
    meta_ref[...] = jnp.concatenate([part[2 * depth :] for part in near], axis=0).astype(BF16)
    key_ids = jnp.concatenate([part[2 * depth + 8 : 2 * depth + 9] for part in near], axis=1)
    eye = iota((patches, patches), 0) == iota((patches, patches), 1)
    own_ids = jnp.sum(jnp.where(eye, key_ids[:, :patches], 0.0), axis=1, keepdims=True)
    same = own_ids == key_ids
    spread = jnp.zeros((patches, features), F32)
    place_row, place_col = iota((size, features), 0), iota((size, features), 1)
    for head in range(heads):
        first = head * size
        keys = jnp.concatenate([part[first : first + size] for part in near], axis=1)
        first = depth + head * size
        values = jnp.concatenate([part[first : first + size] for part in near], axis=1)
        query = query_ref[head].astype(F32).T.astype(BF16)
        scores = dot(query, keys) * (size**-0.5)
        scores = jnp.where(same, scores, -1e30)
        weights = jnp.exp(scores - jnp.max(scores, axis=1, keepdims=True))
        total = jnp.sum(weights, axis=1, keepdims=True)
        attn = dot_nt(weights.astype(BF16), values.astype(BF16)) / total
        place = (place_col % size == place_row) & (place_col // (4 * size) == head)
        spread = spread + dot(attn, place.astype(F32))
    spot = iota((patches, features), 1) // size % 4 == iota((patches, features), 0) % 4
    line = iota((rows, patches), 0)
    line = ((line // row_share) ^ lax.axis_index("expert")) * row_share + line % row_share
    fold = (iota((rows, patches), 1) // 4 == line).astype(F32)
    merged = dot(fold, jnp.where(spot, spread, 0.0))
    merged_ref[...] = merged.astype(BF16)
    local_mean = jnp.sum(merged, axis=1, keepdims=True) / features
    centered = merged - local_mean
    squares = jnp.sum(centered * centered, axis=1, keepdims=True)
    gain = flat_gain(gain_ref)
    gain_high = gain.astype(BF16).astype(F32)
    extra = iota((16, features), 0)
    gain_rows = jnp.where(extra == 0, gain_high, jnp.where(extra == 1, gain - gain_high, 0.0))
    left_ref[...] = jnp.concatenate([centered * gain, gain_rows], axis=0).astype(BF16)
    scalar_ref[...] = put_scalars([local_mean, squares], rows)


def project_kernel(left_ref, scalar_ref, weight_ref, _, *message_refs):
    rows = scalar_ref.shape[0]
    width = weight_ref.shape[1]
    row_share = rows // len(message_refs)
    product = dot(left_ref[...], weight_ref[...])
    gain_sum = product[rows : rows + 1] + product[rows + 1 : rows + 2]
    piece = width // row_share
    pieces = [gain_sum[:, j * piece : (j + 1) * piece] for j in range(row_share)]
    pieces = jnp.concatenate(pieces, axis=0).astype(BF16)
    scalars = scalar_ref[...].astype(BF16)
    for k, message_ref in enumerate(message_refs):
        mine = slice(k * row_share, (k + 1) * row_share)
        message_ref[:, :width] = product[mine].astype(BF16)
        message_ref[:, width : width + piece] = pieces
        message_ref[:, width + piece :] = scalars[mine]


def merge_kernel(_, *refs, width, features):
    *message_refs, out_ref, vision_ref, gain_ref = refs
    share, row_share = len(message_refs), out_ref.shape[0]
    piece = width // row_share
    parts = [ref[...].astype(F32) for ref in message_refs]
    scalars = [part[:, width + piece :] for part in parts]
    means = [get_scalar(block, 0) for block in scalars]
    squares = [get_scalar(block, 1) for block in scalars]
    mean = sum(means) / share
    spread = sum(q + features * (m - mean) * (m - mean) for q, m in zip(squares, means))
    inv_std = lax.rsqrt(spread / (share * features) + EPS)
    total = jnp.zeros((row_share, width), F32)
    gain_total = jnp.zeros((1, width), F32)
    for part, local in zip(parts, means):
        tail = part[:, width : width + piece]
        gain_sum = jnp.concatenate([tail[j : j + 1] for j in range(row_share)], axis=1)
        total = total + part[:, :width] + (local - mean) * gain_sum
        gain_total = gain_total + gain_sum
    vision_ref[...] = total * inv_std
    gain_ref[...] = gain_total
    out_ref[:, :width] = (total * inv_std).astype(BF16)
    out_ref[:, width:] = put_scalars([mean, inv_std], row_share).astype(BF16)


def stack_kernel(*refs):
    *part_refs, out_ref = refs
    out_ref[...] = stacked(part_refs)


def stacked(part_refs):
    return jnp.concatenate([ref[...].astype(F32) for ref in part_refs], axis=0).astype(BF16)


def by_chip(own_refs, sibling_ref):
    parts = []
    sibling = sibling_ref[...].astype(F32)
    for k, own_ref in enumerate(own_refs):
        half = own_ref.shape[0] // 2
        parts.append(own_ref[...].astype(F32)[:half])
        parts.append(sibling[k * half : (k + 1) * half])
    return jnp.concatenate(parts, axis=0).astype(BF16)


def other_half_kernel(*refs, count):
    out_ref = refs[-1]
    parts = [ref[...].astype(F32)[ref.shape[0] // 2 :] for ref in refs[:count]]
    out_ref[...] = jnp.concatenate(parts, axis=0).astype(BF16)


def slot_pick(slot_count, send_rows, shift):
    row, col = iota((slot_count, send_rows), 0), iota((slot_count, send_rows), 1)
    place = row % SLOTS
    pick = (col == row // SLOTS * SEND + place + shift) & (place < CAPX)
    return pick.astype(F32)


def early_kernel(down_ref, *refs):
    *early_refs, sibling_ref, text_out, grad_out = refs
    slot_count = text_out.shape[0]
    early = by_chip(early_refs, sibling_ref)
    text_out[...] = dot(slot_pick(slot_count, early.shape[0], 0), early).astype(BF16)
    back_rows = dot(slot_pick(slot_count, early.shape[0], CAPX), early).astype(BF16)
    grad_out[...] = dot_nt(back_rows, down_ref[0])


def forward_kernel(*refs, blocks):
    slots_ref, gain_ref, gate_ref, up_ref, down_ref, text_ref = refs[:6]
    vision_refs = refs[6 : 6 + blocks]
    gate_out, up_out, *down_refs = refs[6 + blocks : -2]
    h_ref, sum_ref = refs[-2:]
    _, hidden, width = gate_ref.shape
    chosen = slots_ref[...]
    is_vision = jnp.sum(chosen.astype(F32), axis=1, keepdims=True) > 0.5
    vision = jnp.concatenate([ref[:, :width] for ref in vision_refs], axis=0)
    inputs = dot(chosen, vision)
    scale = lax.rsqrt(jnp.mean(inputs * inputs, axis=1, keepdims=True) + EPS)
    normed = inputs * scale * gain_ref[...]
    h_ref[...] = jnp.where(is_vision, normed, text_ref[...].astype(F32)).astype(BF16)
    tile = tile_of(hidden)
    for i in range(hidden // tile):
        mine = slice(i * tile, (i + 1) * tile)
        gate_pre = dot_nt(h_ref[...], gate_ref[0, mine])
        up_proj = dot_nt(h_ref[...], up_ref[0, mine])
        gate_out[:, mine] = gate_pre
        up_out[:, mine] = up_proj
        activated = gate_pre * jax.nn.sigmoid(gate_pre) * up_proj
        product = dot(activated, down_ref[0, mine])
        sum_ref[...] = product if i == 0 else sum_ref[...] + product
    count = 2 * SLOTS
    for k, ref in enumerate(down_refs):
        ref[...] = sum_ref[k * count : (k + 1) * count].astype(BF16)


def backward_kernel(
    slots_ref, grad_ref, gate_in, up_in, cot_ref, gate_ref, up_ref, even_ref, odd_ref, sum_ref,
    *, blocks,
):
    hidden = gate_ref.shape[1]
    tile = tile_of(hidden)
    for i in range(hidden // tile):
        mine = slice(i * tile, (i + 1) * tile)
        act_grad = grad_ref[:, mine]
        gate_pre, up_proj = gate_in[:, mine], up_in[:, mine]
        sigmoid = jax.nn.sigmoid(gate_pre)
        gate_grad = act_grad * up_proj * sigmoid * (1.0 + gate_pre * (1.0 - sigmoid))
        up_grad = act_grad * gate_pre * sigmoid
        product = dot(gate_grad, gate_ref[0, mine]) + dot(up_grad, up_ref[0, mine])
        sum_ref[...] = product if i == 0 else sum_ref[...] + product
    grads = dot_tn(slots_ref[...], sum_ref[...].astype(BF16))
    cots = cot_ref[...].astype(F32)
    rows, row_share = grads.shape[0] // blocks, cots.shape[0] // blocks
    parts = ([], [])
    for k in range(blocks):
        parts[k % 2].append(grads[k * rows : (k + 1) * rows])
        parts[k % 2].append(cots[k * row_share : (k + 1) * row_share])
    even_ref[...] = jnp.concatenate(parts[0], axis=0).astype(BF16)
    odd_ref[...] = jnp.concatenate(parts[1], axis=0).astype(BF16)


def tile_of(hidden):
    return 256 if hidden % 256 == 0 else hidden


def halving_order(share):
    order = [0]
    step = share // 2
    while step:
        order = order + [k + step for k in order]
        step //= 2
    return [sum(1 << j for j in range(share.bit_length() - 1) if k >> j & 1) for k in order]


def pair_sum_kernel(own_ref, sibling_ref, *out_refs):
    rows = out_refs[0].shape[0]
    total = own_ref[...].astype(F32) + sibling_ref[...].astype(F32)
    for k, out_ref in enumerate(out_refs):
        out_ref[...] = total[k * rows : (k + 1) * rows].astype(BF16)


def total_of(part_refs):
    total = part_refs[0][...].astype(F32)
    for ref in part_refs[1:]:
        total = total + ref[...].astype(F32)
    return total


def chip_sum_kernel(*refs, count):
    cot_ref, *out_refs = refs[count + 1 :]
    total = total_of(refs[:count])
    rows = cot_ref.shape[0]
    for k, out_ref in enumerate(out_refs):
        out_ref[...] = total[k * rows : (k + 1) * rows].astype(BF16)
    cot_ref[...] = total[len(out_refs) * rows :].astype(BF16)


def quarters(total, out_refs):
    count = out_refs[0].shape[0]
    for k, ref in enumerate(out_refs):
        ref[...] = total[k * count : (k + 1) * count].astype(ref.dtype)


def combine_kernel(comb_ref, *refs):
    *part_refs, sibling_ref = refs[:-4]
    rows = by_chip(part_refs, sibling_ref)
    quarters(dot_tn(comb_ref[0], rows) + dot_tn(comb_ref[1], rows), refs[-4:])


def halve_kernel(*refs):
    low, high, arrived_low, arrived_high = [ref[...].astype(F32) for ref in refs[:4]]
    quarters(jnp.concatenate([low + arrived_low, high + arrived_high], axis=0), refs[4:])


def add_kernel(own_ref, arrived_ref, *refs):
    refs[-1][...] = (own_ref[...] + arrived_ref[...].astype(F32)).astype(BF16)


def finish_kernel(placed_ref, text_ref, own_ref, arrived_ref, *refs, blocks, turn):
    vision_refs, out_ref = refs[:blocks], refs[-1]
    count, width = out_ref.shape
    tokens = placed_ref.shape[0]
    first = (lax.axis_index("expert") ^ turn) * count
    pick = iota((count, tokens), 1) == iota((count, tokens), 0) + first
    pick = pick.astype(F32)
    placed = dot(pick, placed_ref[...])
    is_vision = jnp.sum(placed, axis=1, keepdims=True) > 0.5
    vision = jnp.concatenate([ref[:, :width] for ref in vision_refs], axis=0)
    inputs = jnp.where(is_vision, dot(placed, vision), dot(pick, text_ref[...]))
    out_ref[...] = (inputs + (own_ref[...].astype(F32) + arrived_ref[...].astype(F32))).astype(BF16)


def lay_kernel(*refs):
    *part_refs, out_ref = refs
    count = part_refs[0].shape[0]
    for k, ref in enumerate(part_refs):
        first = pl.multiple_of((lax.axis_index("expert") ^ k) * count, count)
        out_ref[pl.ds(first, count), :] = ref[...]


def norm_grad_kernel(
    own_ref, gain_ref, cot_ref, vision_ref, total_ref, *refs, features
):
    *part_refs, out_ref = refs
    width = gain_ref.shape[1]
    hidden = total_of(part_refs)
    cotangent = cot_ref[...].astype(F32)
    inputs = own_ref[:, :width].astype(F32)
    scale = lax.rsqrt(jnp.mean(inputs * inputs, axis=1, keepdims=True) + EPS)
    pulled = hidden * gain_ref[...]
    cross = jnp.mean(pulled * inputs, axis=1, keepdims=True)
    grad = cotangent + scale * pulled - inputs * (scale * scale * scale) * cross
    grad = grad.astype(BF16)
    out_ref[:, :width] = grad
    grad = grad.astype(F32)
    grad_mean = jnp.sum(grad * total_ref[...], axis=1, keepdims=True) / features
    cross_mean = jnp.sum(grad * vision_ref[...], axis=1, keepdims=True) / features
    out_ref[:, width:] = put_scalars([grad_mean, cross_mean], grad.shape[0]).astype(BF16)


def merge_grad_kernel(*refs, size):
    gain_ref, merged_ref, scalar_ref, weight_ref, *part_refs, out_ref = refs
    rows, features = merged_ref.shape
    width = weight_ref.shape[1]
    depth, patches = out_ref.shape
    row_share = part_refs[0].shape[0]
    parts = stacked(part_refs)
    normed_grad = dot_nt(parts[:, :width], weight_ref[...]) * flat_gain(gain_ref)
    means = parts[:, width:].astype(F32)
    scalars = scalar_ref[:, width:].astype(F32)
    inv_std = get_scalar(scalars, 1)
    normed = (merged_ref[...].astype(F32) - get_scalar(scalars, 0)) * inv_std
    grad = inv_std * (normed_grad - get_scalar(means, 0) - normed * get_scalar(means, 1))
    high = grad.astype(BF16)
    low = (grad - high.astype(F32)).astype(BF16)
    line = iota((patches, rows), 1)
    line = ((line // row_share) ^ lax.axis_index("expert")) * row_share + line % row_share
    unfold = (iota((patches, rows), 0) // 4 == line).astype(F32)
    spot = iota((patches, features), 1) // size % 4 == iota((patches, features), 0) % 4
    row, col = iota((depth, features), 0), iota((depth, features), 1)
    place = (col // (4 * size) == row // size) & (col % size == row % size)
    place = place.astype(F32).astype(BF16)
    out = jnp.zeros((depth, patches), F32)
    for piece in (high, low):
        wide = jnp.where(spot, dot(unfold, piece), 0.0).astype(BF16)
        out = out + dot_nt(place, wide)
    out_ref[...] = out


def whole(memory_space=pltpu.VMEM):
    return pl.BlockSpec(memory_space=memory_space)


def run(kernel, outs, *args, far=(), scratch=(), cost=1.0, vmem=VMEM_BYTES, name=None):
    specs = [whole()] * len(args)
    for place in far:
        specs[place] = whole(pl.ANY)
    return pl.pallas_call(
        kernel,
        out_shape=outs,
        in_specs=specs,
        out_specs=jax.tree.map(lambda _: whole(), outs),
        scratch_shapes=scratch,
        compiler_params=pltpu.CompilerParams(vmem_limit_bytes=vmem),
        cost_estimate=microseconds(cost),
        name=name,
    )(*args)


def to_sibling(parts, deps, name):
    rows, width = parts[0].shape
    half = run(
        functools.partial(other_half_kernel, count=len(parts)),
        shape((len(parts) * rows // 2, width)), *parts, *deps,
        far=range(len(parts), len(parts) + len(deps)), cost=0.01, name=name,
    )
    return swap(half, "blk", 1)


def microseconds(time):
    return pl.CostEstimate(flops=0, transcendentals=0, bytes_accessed=int(time * 3e6))


def after(values, deps):
    count = len(values)
    return pl.pallas_call(
        lambda *refs: None,
        out_shape=[shape(value.shape, value.dtype) for value in values],
        in_specs=[whole(pl.ANY)] * (count + len(deps)),
        out_specs=[whole(pl.ANY)] * count,
        input_output_aliases={i: i for i in range(count)},
        compiler_params=pltpu.CompilerParams(vmem_limit_bytes=VMEM_BYTES),
        cost_estimate=microseconds(0.1),
        name="after",
    )(*values, *deps)


def shape(dims, dtype=BF16):
    return jax.ShapeDtypeStruct(dims, dtype)


def swap(value, axis, step):
    count = lax.axis_size(axis)
    return lax.ppermute(value, axis, [(i, i ^ step) for i in range(count)])


def trade(parts, axis):
    return [parts[0]] + [swap(parts[k], axis, k) for k in range(1, len(parts))]


def spread_out(value, axis):
    return trade([value] * lax.axis_size(axis), axis)


def gather_blocks(value, deps=None):
    own = [value] + [swap(value, "blk", k) for k in range(2, lax.axis_size("blk"), 2)]
    if deps is not None:
        own = own[:1] + list(after(own[1:], deps))
    sibling = [swap(part, "blk", 1) for part in own]
    return [part for pair in zip(own, sibling) for part in pair]


def to_chips(parts):
    return [parts[0]] + [swap(parts[k], "blk", 2 * k) for k in range(1, len(parts))]


def body(
    queries, keys, values, image_ids, placement, merge_gain, merge_weight, text, norm_gain,
    w_gate, w_up, w_down, routes, route_gates, cotangent,
):
    blocks = lax.axis_size("blk")
    share = lax.axis_size("expert")
    heads, size, patches = queries.shape
    depth = heads * size
    rows = image_ids.shape[0]
    row_share = rows // share
    tokens, width = text.shape
    part = tokens // share
    all_rows = blocks * rows
    features = heads * 4 * size
    hidden = w_gate.shape[1]
    slot_count = blocks * SLOTS
    groups = share // 2
    routes_t, gates_t, gain_row = routes.T, route_gates.T, norm_gain[None]

    small = [
        keys.reshape(depth, patches), values.reshape(depth, patches),
        image_ids[None], placement.reshape(1, rows), routes_t,
    ]
    local = run(
        pack_kernel, shape((2 * depth + 16, patches)), *small, far=range(5),
        scratch=[pltpu.VMEM(array.shape, array.dtype) for array in small]
        + [pltpu.SemaphoreType.DMA((5,))],
        vmem=PACK_BYTES, name="pack",
    )
    comb, pick, factor = run(
        functools.partial(route_kernel, groups=groups, share=share),
        [
            shape((2, slot_count, tokens)), shape((2, blocks * SEND, tokens)),
            shape((blocks * SEND, 128), F32),
        ],
        routes_t, gates_t, cost=3.0, name="route",
    )
    send = run(
        dispatch_kernel, [shape((2 * SEND, width))] * (blocks // 2),
        pick, factor, text, gain_row, cotangent, cost=2.0, name="dispatch",
    )
    near = gather_blocks(local, send)
    early = to_chips(after(send, near[2::2]))

    weight_flat = merge_weight.reshape(features, width)
    message_width = width + width // row_share + 128
    merged, meta, left, local_scalars = run(
        functools.partial(attend_kernel, blocks=blocks, row_share=row_share),
        [
            shape((rows, features)), shape((blocks * 16, patches)), shape((rows + 16, features)),
            shape((rows, 128), F32),
        ],
        queries, merge_gain, *small, *near[1:], cost=3.0, name="attend",
    )
    message = run(
        project_kernel, [shape((row_share, message_width))] * share,
        left, local_scalars, weight_flat, early[1], far=(3,), cost=2.0, name="project",
    )
    slots, placed, back_cots = run(
        functools.partial(
            plan_kernel, blocks=blocks, groups=groups, merged_rows=rows, row_share=row_share
        ),
        [
            shape((slot_count, all_rows)), shape((tokens, all_rows)),
            shape((blocks * row_share, width)),
        ],
        meta, cotangent, cost=1.5, name="plan",
    )
    message = trade(message, "expert")
    early = early[:1] + list(after(early[1:], message[1:]))
    own, vision_exact, gain_total = run(
        functools.partial(merge_kernel, width=width, features=features),
        [
            shape((row_share, width + 128)), shape((row_share, width), F32),
            shape((1, width), F32),
        ],
        early[1], *message, far=(0,), cost=0.2, name="merge",
    )
    owns = spread_out(own, "expert")
    block_rows = run(
        stack_kernel, shape((rows, width + 128)), *owns, cost=0.2, name="stack",
    )
    text_rows, act_grad = run(
        early_kernel, [shape((slot_count, width)), shape((slot_count, hidden), F32)],
        w_down, *early, to_sibling(early, owns[1:], "early_half"), cost=3.0, name="early",
    )

    vision = gather_blocks(block_rows, [text_rows, slots])
    gate_pre, up_proj, *down = run(
        functools.partial(forward_kernel, blocks=blocks),
        [
            shape((slot_count, hidden), F32), shape((slot_count, hidden), F32),
        ] + [shape((2 * SLOTS, width))] * (blocks // 2),
        slots, gain_row, w_gate, w_up, w_down, text_rows, *vision,
        scratch=[pltpu.VMEM((slot_count, width), BF16), pltpu.VMEM((slot_count, width), F32)],
        cost=4.0, name="forward",
    )
    returned = to_chips(down)
    block = rows + row_share
    even, odd = run(
        functools.partial(backward_kernel, blocks=blocks),
        [shape((blocks // 2 * block, width))] * 2,
        slots, act_grad, gate_pre, up_proj, back_cots, w_gate, w_up,
        scratch=[pltpu.VMEM((slot_count, width), F32)],
        cost=4.0, name="backward",
    )
    grads = run(
        pair_sum_kernel, [shape((block, width))] * (blocks // 2), even, swap(odd, "blk", 1),
        cost=0.2, name="pair_sum",
    )
    grads = to_chips(grads)
    count = tokens // 4
    pieces = [shape((count, width), F32)] * 2 + [shape((count, width))] * 2
    low, high, sent_low, sent_high = run(
        combine_kernel, pieces, comb, *returned,
        to_sibling(returned, grads[:1], "returned_half"), cost=0.01, name="combine",
    )
    first_sent, step = sent_low, 1
    arrived_high = swap(sent_high, "expert", step)
    arrived_low = swap(sent_low, "expert", step)
    while count > part:
        count //= 2
        step *= 2
        pieces = [shape((count, width), F32)] * 2 + [shape((count, width))] * 2
        low, high, sent_low, sent_high = run(
            halve_kernel, pieces, low, high, arrived_low, arrived_high, cost=0.3, name="halve"
        )
        arrived_high = swap(sent_high, "expert", step)
        arrived_low = swap(sent_low, "expert", step)
    step *= 2
    chips = len(grads) - 1

    def add(own_part, arrived, name):
        return run(
            add_kernel, shape((part, width)), own_part, arrived, *grads[1:],
            far=range(2, 2 + chips), cost=0.3, name=name,
        )

    sums = [add(low, arrived_low, "add_low"), add(high, arrived_high, "add_high")]
    others = [swap(value, "expert", step) for value in sums][::-1]
    cot_rows, *grads = run(
        functools.partial(chip_sum_kernel, count=blocks // 2),
        [shape((row_share, width))] * (share + 1), *grads, first_sent, far=(blocks // 2,), cost=0.2,
        name="chip_sum",
    )
    grads = trade(grads, "expert")
    vision_grad = run(
        functools.partial(norm_grad_kernel, features=share * features),
        shape((row_share, width + 128)),
        own, gain_row, cot_rows, vision_exact, gain_total, *grads, cost=0.3, name="norm_grad",
    )
    vision_grads = spread_out(vision_grad, "expert")
    attn_grad = run(
        functools.partial(merge_grad_kernel, size=size), shape((depth, patches), F32),
        merge_gain, merged, block_rows, weight_flat, *vision_grads, cost=4.0, name="merge_grad",
    )

    laid = {}
    for turn, value, other, gate in zip((0, step), sums, others, (grads, vision_grads)):
        laid[turn] = run(
            functools.partial(finish_kernel, blocks=blocks, turn=turn), shape((part, width)),
            placed, text, value, other, *vision, *gate[1:],
            far=range(4 + blocks, 3 + blocks + share), cost=1.0, name="finish",
        )
    while step > 1:
        step //= 2
        laid.update({k + step: swap(laid[k], "expert", step) for k in list(laid)})
    llm_out = run(
        lay_kernel, shape((tokens, width)), *[laid[k] for k in sorted(laid)], cost=1.0, name="lay"
    )
    return llm_out, attn_grad.reshape(heads, size, patches)


def solution(mesh):
    return jax.shard_map(
        body,
        mesh=mesh,
        in_specs=(
            P("expert", None, "blk"),
            P("expert", None, "blk"),
            P("expert", None, "blk"),
            P("blk"),
            P("blk", None),
            P("expert", None),
            P("expert", None, None),
            P("blk", None),
            P(),
            P("blk", "expert", None),
            P("blk", "expert", None),
            P("blk", "expert", None),
            P("blk", None),
            P("blk", None),
            P("blk", None),
        ),
        out_specs=(P("blk", None), P("expert", None, "blk")),
        check_vma=False,
    )
```

```python
import functools

import jax
import jax.numpy as jnp
from jax import lax
from jax.experimental import pallas as pl
from jax.experimental.pallas import tpu as pltpu
from jax.sharding import PartitionSpec as P

CAPX = 10
SLOTS = 12
SEND = 24
EPS = 1e-06
VMEM_BYTES = 16 * 1024 * 1024
PACK_BYTES = 60 * 1024 * 1024
F32 = jnp.float32
BF16 = jnp.bfloat16


def iota(shape, dim):
    return lax.broadcasted_iota(jnp.int32, shape, dim)


def dot(a, b):
    return jnp.dot(a.astype(BF16), b.astype(BF16), preferred_element_type=F32)


def dot_nt(a, b):
    return lax.dot_general(a, b, (((1,), (1,)), ((), ())), preferred_element_type=F32)


def dot_tn(a, b):
    return lax.dot_general(a, b, (((0,), (0,)), ((), ())), preferred_element_type=F32)


def three(value):
    first = value.astype(BF16).astype(F32)
    second = (value - first).astype(BF16).astype(F32)
    return first, second, value - first - second


def put_scalars(columns, rows):
    lane = iota((rows, 128), 1)
    out = jnp.zeros((rows, 128), F32)
    place = 0
    for column in columns:
        for piece in three(column):
            out = jnp.where(lane == place, piece, out)
            place += 1
    return out


def get_scalar(block, which):
    lane = iota(block.shape, 1)
    return jnp.sum(jnp.where(lane // 3 == which, block, 0.0), axis=1, keepdims=True)


def bring(far_refs, near_refs, sems):
    copies = [
        pltpu.make_async_copy(far, near, sems.at[i])
        for i, (far, near) in enumerate(zip(far_refs, near_refs))
    ]
    for copy in copies:
        copy.start()
    return copies


def pack_kernel(*refs):
    far_refs, out_ref, near_refs, sems = refs[:5], refs[5], refs[6:11], refs[11]
    for copy in bring(far_refs, near_refs, sems):
        copy.wait()
    out_ref[...] = packed(*near_refs).astype(BF16)


def packed(keys_ref, values_ref, images_ref, placement_ref, routes_ref):
    rows = images_ref.shape[1]
    patches = keys_ref.shape[1]
    repeat = (iota((rows, patches), 0) == iota((rows, patches), 1) // 4).astype(F32)
    keep = (iota((rows, patches), 0) == iota((rows, patches), 1)).astype(F32)
    patch_ids = dot(images_ref[...].astype(F32), repeat)
    dest = dot(placement_ref[...].astype(F32), keep)
    line = iota((8, patches), 0)
    rest = jnp.where(line == 0, patch_ids, jnp.where(line == 1, dest, 0.0))
    parts = [keys_ref[...], values_ref[...], routes_ref[...], rest]
    return jnp.concatenate([part.astype(F32) for part in parts], axis=0)


def route_kernel(routes_ref, gates_ref, comb_ref, pick_ref, factor_ref, *, groups, share):
    blocks = comb_ref.shape[1] // SLOTS
    tokens = routes_ref.shape[1]
    me, expert_index = lax.axis_index("blk"), lax.axis_index("expert")
    member = expert_index // groups
    before = (iota((tokens, tokens), 0) < iota((tokens, tokens), 1)).astype(BF16)
    pair_of = 2 * (iota((blocks, tokens), 0) ^ me) + member
    out_hit = jnp.zeros((blocks, tokens), F32)
    out_gate = jnp.zeros((blocks, tokens), F32)
    for k in range(routes_ref.shape[0]):
        same = pair_of == routes_ref[k : k + 1, :]
        out_hit = out_hit + same.astype(F32)
        out_gate = out_gate + jnp.where(same, gates_ref[k : k + 1, :], 0.0)
    out_rank = dot(out_hit, before)

    def expand(stride):
        count = blocks * stride
        pick = (iota((count, blocks), 0) // stride == iota((count, blocks), 1)).astype(BF16)
        gate = sum(dot(pick, piece) for piece in three(out_gate))
        return dot(pick, out_hit), dot(pick, out_rank).astype(jnp.int32), gate

    hits, ranks, gates = expand(SLOTS)
    live = jnp.where(ranks == iota(hits.shape, 0) % SLOTS, hits, 0.0)
    weight = live * gates
    high = weight.astype(BF16).astype(F32)
    part = tokens // share
    col = iota((tokens, tokens), 1)
    turned = (col // part * 0).astype(jnp.int32)
    for place, k in enumerate(halving_order(share)):
        turned = jnp.where(col // part == place, k, turned)
    turned = (iota((tokens, tokens), 0) == (turned ^ expert_index) * part + col % part)
    turned = turned.astype(F32)
    comb_ref[0] = dot(high, turned).astype(BF16)
    comb_ref[1] = dot(weight - high, turned).astype(BF16)

    hits, ranks, gates = expand(SEND)
    place = iota(hits.shape, 0) % SEND
    input_pick = jnp.where((place < CAPX) & (ranks == place), hits, 0.0)
    back_pick = jnp.where((place >= CAPX) & (place < 2 * CAPX) & (ranks == place - CAPX), hits, 0.0)
    pick_ref[0] = input_pick.astype(BF16)
    pick_ref[1] = back_pick.astype(BF16)
    factor = jnp.sum(back_pick * gates, axis=1, keepdims=True)
    factor_ref[...] = jnp.broadcast_to(factor, factor_ref.shape)


def dispatch_kernel(pick_ref, factor_ref, text_ref, gain_ref, cot_ref, *send_refs):
    text = text_ref[...].astype(F32)
    scale = lax.rsqrt(jnp.mean(text * text, axis=1, keepdims=True) + EPS)
    h_rows = (text * scale * gain_ref[...]).astype(BF16)
    factor = factor_ref[:, :1]
    send = dot(pick_ref[0], h_rows) + factor * dot(pick_ref[1], cot_ref[...])
    send = send.astype(BF16)
    count = 2 * SEND
    for k, ref in enumerate(send_refs):
        ref[...] = send[k * count : (k + 1) * count]


def plan_kernel(
    meta_ref, cot_ref, slots_ref, placed_ref, back_ref, *, blocks, groups, merged_rows, row_share
):
    tokens = cot_ref.shape[0]
    rows = blocks * merged_rows
    me, expert_index = lax.axis_index("blk"), lax.axis_index("expert")
    member = expert_index // groups
    meta = [meta_ref[k * 16 : (k + 1) * 16].astype(F32) for k in range(blocks)]
    mine = (2 * me + member).astype(F32)
    hits = [jnp.sum((part[:8] == mine).astype(F32), axis=0, keepdims=True) for part in meta]
    hit = jnp.concatenate(hits, axis=0)
    dest = jnp.concatenate([part[9:10] for part in meta], axis=0)
    before = (iota((tokens, tokens), 0) < iota((tokens, tokens), 1)).astype(BF16)
    rank = dot(hit, before)

    def row_of(col):
        inner = col % merged_rows
        return ((inner // row_share) ^ expert_index) * row_share + inner % row_share

    def place_of(col):
        return ((col // merged_rows) ^ me) * merged_rows + row_of(col)

    spread = (iota((128, rows), 0) == row_of(iota((128, rows), 1))).astype(F32)
    own_block = iota((blocks, rows), 1) // merged_rows == iota((blocks, rows), 0)
    dest_row = jnp.sum(jnp.where(own_block, dot(dest, spread), 0.0), axis=0, keepdims=True)
    dest_row = dest_row.astype(jnp.int32) ^ me
    dest_hit = (iota((blocks, rows), 0) == dest_row).astype(F32)
    rows_before = place_of(iota((rows, rows), 0)) < place_of(iota((rows, rows), 1))
    earlier = dot(dest_hit, rows_before.astype(F32))
    slot = jnp.sum(dest_hit * earlier, axis=0, keepdims=True).astype(jnp.int32)
    at_token = (iota((tokens, rows), 0) == slot).astype(F32)
    row_hit = jnp.sum(dest_hit * dot(hit, at_token), axis=0, keepdims=True)
    row_rank = jnp.sum(dest_hit * dot(rank, at_token), axis=0, keepdims=True).astype(jnp.int32)
    slot_id = dest_row * SLOTS + row_rank
    slot_count = slots_ref.shape[0]
    chosen = (iota((slot_count, rows), 0) == slot_id) & (row_hit > 0.5)
    slots_ref[...] = chosen.astype(F32).astype(BF16)
    placed = jnp.where(dest_row == 0, at_token, 0.0).astype(BF16)
    placed_ref[...] = placed
    back_rows = blocks * row_share
    source = iota((back_rows, rows), 0)
    wanted = source // row_share * merged_rows + source % row_share
    row_pick = (iota((back_rows, rows), 1) == wanted).astype(F32).astype(BF16)
    back_ref[...] = dot(dot_nt(row_pick, placed), cot_ref[...]).astype(BF16)


def flat_gain(gain_ref):
    return jnp.concatenate([gain_ref[h : h + 1] for h in range(gain_ref.shape[0])], axis=1)


def attend_kernel(*refs, blocks, row_share):
    query_ref, gain_ref = refs[:2]
    near_refs = refs[7 : 6 + blocks]
    merged_ref, meta_ref, left_ref, scalar_ref = refs[6 + blocks :]
    heads, size, patches = query_ref.shape
    rows, features = merged_ref.shape
    depth = heads * size
    near = [packed(*refs[2:7])] + [ref[...].astype(F32) for ref in near_refs]
    meta_ref[...] = jnp.concatenate([part[2 * depth :] for part in near], axis=0).astype(BF16)
    key_ids = jnp.concatenate([part[2 * depth + 8 : 2 * depth + 9] for part in near], axis=1)
    eye = iota((patches, patches), 0) == iota((patches, patches), 1)
    own_ids = jnp.sum(jnp.where(eye, key_ids[:, :patches], 0.0), axis=1, keepdims=True)
    same = own_ids == key_ids
    spread = jnp.zeros((patches, features), F32)
    place_row, place_col = iota((size, features), 0), iota((size, features), 1)
    for head in range(heads):
        first = head * size
        keys = jnp.concatenate([part[first : first + size] for part in near], axis=1)
        first = depth + head * size
        values = jnp.concatenate([part[first : first + size] for part in near], axis=1)
        query = query_ref[head].astype(F32).T.astype(BF16)
        scores = dot(query, keys) * (size**-0.5)
        scores = jnp.where(same, scores, -1e30)
        weights = jnp.exp(scores - jnp.max(scores, axis=1, keepdims=True))
        total = jnp.sum(weights, axis=1, keepdims=True)
        attn = dot_nt(weights.astype(BF16), values.astype(BF16)) / total
        place = (place_col % size == place_row) & (place_col // (4 * size) == head)
        spread = spread + dot(attn, place.astype(F32))
    spot = iota((patches, features), 1) // size % 4 == iota((patches, features), 0) % 4
    line = iota((rows, patches), 0)
    line = ((line // row_share) ^ lax.axis_index("expert")) * row_share + line % row_share
    fold = (iota((rows, patches), 1) // 4 == line).astype(F32)
    merged = dot(fold, jnp.where(spot, spread, 0.0))
    merged_ref[...] = merged.astype(BF16)
    local_mean = jnp.sum(merged, axis=1, keepdims=True) / features
    centered = merged - local_mean
    squares = jnp.sum(centered * centered, axis=1, keepdims=True)
    gain = flat_gain(gain_ref)
    gain_high = gain.astype(BF16).astype(F32)
    extra = iota((16, features), 0)
    gain_rows = jnp.where(extra == 0, gain_high, jnp.where(extra == 1, gain - gain_high, 0.0))
    left_ref[...] = jnp.concatenate([centered * gain, gain_rows], axis=0).astype(BF16)
    scalar_ref[...] = put_scalars([local_mean, squares], rows)


def project_kernel(left_ref, scalar_ref, weight_ref, _, *message_refs):
    rows = scalar_ref.shape[0]
    width = weight_ref.shape[1]
    row_share = rows // len(message_refs)
    product = dot(left_ref[...], weight_ref[...])
    gain_sum = product[rows : rows + 1] + product[rows + 1 : rows + 2]
    piece = width // row_share
    pieces = [gain_sum[:, j * piece : (j + 1) * piece] for j in range(row_share)]
    pieces = jnp.concatenate(pieces, axis=0).astype(BF16)
    scalars = scalar_ref[...].astype(BF16)
    for k, message_ref in enumerate(message_refs):
        mine = slice(k * row_share, (k + 1) * row_share)
        message_ref[:, :width] = product[mine].astype(BF16)
        message_ref[:, width : width + piece] = pieces
        message_ref[:, width + piece :] = scalars[mine]


def merge_kernel(_, *refs, width, features):
    *message_refs, out_ref, vision_ref, gain_ref = refs
    share, row_share = len(message_refs), out_ref.shape[0]
    piece = width // row_share
    parts = [ref[...].astype(F32) for ref in message_refs]
    scalars = [part[:, width + piece :] for part in parts]
    means = [get_scalar(block, 0) for block in scalars]
    squares = [get_scalar(block, 1) for block in scalars]
    mean = sum(means) / share
    spread = sum(q + features * (m - mean) * (m - mean) for q, m in zip(squares, means))
    inv_std = lax.rsqrt(spread / (share * features) + EPS)
    total = jnp.zeros((row_share, width), F32)
    gain_total = jnp.zeros((1, width), F32)
    for part, local in zip(parts, means):
        tail = part[:, width : width + piece]
        gain_sum = jnp.concatenate([tail[j : j + 1] for j in range(row_share)], axis=1)
        total = total + part[:, :width] + (local - mean) * gain_sum
        gain_total = gain_total + gain_sum
    vision_ref[...] = total * inv_std
    gain_ref[...] = gain_total
    out_ref[:, :width] = (total * inv_std).astype(BF16)
    out_ref[:, width:] = put_scalars([mean, inv_std], row_share).astype(BF16)


def stack_kernel(*refs):
    *part_refs, out_ref = refs
    out_ref[...] = stacked(part_refs)


def stacked(part_refs):
    return jnp.concatenate([ref[...].astype(F32) for ref in part_refs], axis=0).astype(BF16)


def by_chip(own_refs, sibling_ref):
    parts = []
    sibling = sibling_ref[...].astype(F32)
    for k, own_ref in enumerate(own_refs):
        half = own_ref.shape[0] // 2
        parts.append(own_ref[...].astype(F32)[:half])
        parts.append(sibling[k * half : (k + 1) * half])
    return jnp.concatenate(parts, axis=0).astype(BF16)


def other_half_kernel(*refs, count):
    out_ref = refs[-1]
    parts = [ref[...].astype(F32)[ref.shape[0] // 2 :] for ref in refs[:count]]
    out_ref[...] = jnp.concatenate(parts, axis=0).astype(BF16)


def slot_pick(slot_count, send_rows, shift):
    row, col = iota((slot_count, send_rows), 0), iota((slot_count, send_rows), 1)
    place = row % SLOTS
    pick = (col == row // SLOTS * SEND + place + shift) & (place < CAPX)
    return pick.astype(F32)


def early_kernel(down_ref, *refs):
    *early_refs, sibling_ref, text_out, grad_out = refs
    slot_count = text_out.shape[0]
    early = by_chip(early_refs, sibling_ref)
    text_out[...] = dot(slot_pick(slot_count, early.shape[0], 0), early).astype(BF16)
    back_rows = dot(slot_pick(slot_count, early.shape[0], CAPX), early).astype(BF16)
    grad_out[...] = dot_nt(back_rows, down_ref[0])


def forward_kernel(*refs, blocks):
    slots_ref, gain_ref, gate_ref, up_ref, down_ref, text_ref = refs[:6]
    vision_refs = refs[6 : 6 + blocks]
    gate_out, up_out, *down_refs = refs[6 + blocks : -2]
    h_ref, sum_ref = refs[-2:]
    _, hidden, width = gate_ref.shape
    chosen = slots_ref[...]
    is_vision = jnp.sum(chosen.astype(F32), axis=1, keepdims=True) > 0.5
    vision = jnp.concatenate([ref[:, :width] for ref in vision_refs], axis=0)
    inputs = dot(chosen, vision)
    scale = lax.rsqrt(jnp.mean(inputs * inputs, axis=1, keepdims=True) + EPS)
    normed = inputs * scale * gain_ref[...]
    h_ref[...] = jnp.where(is_vision, normed, text_ref[...].astype(F32)).astype(BF16)
    tile = tile_of(hidden)
    for i in range(hidden // tile):
        mine = slice(i * tile, (i + 1) * tile)
        gate_pre = dot_nt(h_ref[...], gate_ref[0, mine])
        up_proj = dot_nt(h_ref[...], up_ref[0, mine])
        gate_out[:, mine] = gate_pre
        up_out[:, mine] = up_proj
        activated = gate_pre * jax.nn.sigmoid(gate_pre) * up_proj
        product = dot(activated, down_ref[0, mine])
        sum_ref[...] = product if i == 0 else sum_ref[...] + product
    count = 2 * SLOTS
    for k, ref in enumerate(down_refs):
        ref[...] = sum_ref[k * count : (k + 1) * count].astype(BF16)


def backward_kernel(
    slots_ref, grad_ref, gate_in, up_in, cot_ref, gate_ref, up_ref, even_ref, odd_ref, sum_ref,
    *, blocks,
):
    hidden = gate_ref.shape[1]
    tile = tile_of(hidden)
    for i in range(hidden // tile):
        mine = slice(i * tile, (i + 1) * tile)
        act_grad = grad_ref[:, mine]
        gate_pre, up_proj = gate_in[:, mine], up_in[:, mine]
        sigmoid = jax.nn.sigmoid(gate_pre)
        gate_grad = act_grad * up_proj * sigmoid * (1.0 + gate_pre * (1.0 - sigmoid))
        up_grad = act_grad * gate_pre * sigmoid
        product = dot(gate_grad, gate_ref[0, mine]) + dot(up_grad, up_ref[0, mine])
        sum_ref[...] = product if i == 0 else sum_ref[...] + product
    grads = dot_tn(slots_ref[...], sum_ref[...].astype(BF16))
    cots = cot_ref[...].astype(F32)
    rows, row_share = grads.shape[0] // blocks, cots.shape[0] // blocks
    parts = ([], [])
    for k in range(blocks):
        parts[k % 2].append(grads[k * rows : (k + 1) * rows])
        parts[k % 2].append(cots[k * row_share : (k + 1) * row_share])
    even_ref[...] = jnp.concatenate(parts[0], axis=0).astype(BF16)
    odd_ref[...] = jnp.concatenate(parts[1], axis=0).astype(BF16)


def tile_of(hidden):
    return 256 if hidden % 256 == 0 else hidden


def halving_order(share):
    order = [0]
    step = share // 2
    while step:
        order = order + [k + step for k in order]
        step //= 2
    return [sum(1 << j for j in range(share.bit_length() - 1) if k >> j & 1) for k in order]


def pair_sum_kernel(own_ref, sibling_ref, *out_refs):
    rows = out_refs[0].shape[0]
    total = own_ref[...].astype(F32) + sibling_ref[...].astype(F32)
    for k, out_ref in enumerate(out_refs):
        out_ref[...] = total[k * rows : (k + 1) * rows].astype(BF16)


def total_of(part_refs):
    total = part_refs[0][...].astype(F32)
    for ref in part_refs[1:]:
        total = total + ref[...].astype(F32)
    return total


def chip_sum_kernel(*refs, count):
    cot_ref, *out_refs = refs[count + 1 :]
    total = total_of(refs[:count])
    rows = cot_ref.shape[0]
    for k, out_ref in enumerate(out_refs):
        out_ref[...] = total[k * rows : (k + 1) * rows].astype(BF16)
    cot_ref[...] = total[len(out_refs) * rows :].astype(BF16)


def quarters(total, out_refs):
    count = out_refs[0].shape[0]
    for k, ref in enumerate(out_refs):
        ref[...] = total[k * count : (k + 1) * count].astype(ref.dtype)


def combine_kernel(comb_ref, *refs):
    *part_refs, sibling_ref = refs[:-4]
    rows = by_chip(part_refs, sibling_ref)
    quarters(dot_tn(comb_ref[0], rows) + dot_tn(comb_ref[1], rows), refs[-4:])


def halve_kernel(*refs):
    low, high, arrived_low, arrived_high = [ref[...].astype(F32) for ref in refs[:4]]
    quarters(jnp.concatenate([low + arrived_low, high + arrived_high], axis=0), refs[4:])


def add_kernel(own_ref, arrived_ref, *refs):
    refs[-1][...] = (own_ref[...] + arrived_ref[...].astype(F32)).astype(BF16)


def finish_kernel(placed_ref, text_ref, own_ref, arrived_ref, *refs, blocks, turn):
    vision_refs, out_ref = refs[:blocks], refs[-1]
    count, width = out_ref.shape
    tokens = placed_ref.shape[0]
    first = (lax.axis_index("expert") ^ turn) * count
    pick = iota((count, tokens), 1) == iota((count, tokens), 0) + first
    pick = pick.astype(F32)
    placed = dot(pick, placed_ref[...])
    is_vision = jnp.sum(placed, axis=1, keepdims=True) > 0.5
    vision = jnp.concatenate([ref[:, :width] for ref in vision_refs], axis=0)
    inputs = jnp.where(is_vision, dot(placed, vision), dot(pick, text_ref[...]))
    out_ref[...] = (inputs + (own_ref[...].astype(F32) + arrived_ref[...].astype(F32))).astype(BF16)


def lay_kernel(*refs):
    *part_refs, out_ref = refs
    count = part_refs[0].shape[0]
    for k, ref in enumerate(part_refs):
        first = pl.multiple_of((lax.axis_index("expert") ^ k) * count, count)
        out_ref[pl.ds(first, count), :] = ref[...]


def norm_grad_kernel(
    own_ref, gain_ref, cot_ref, vision_ref, total_ref, *refs, features
):
    *part_refs, out_ref = refs
    width = gain_ref.shape[1]
    hidden = total_of(part_refs)
    cotangent = cot_ref[...].astype(F32)
    inputs = own_ref[:, :width].astype(F32)
    scale = lax.rsqrt(jnp.mean(inputs * inputs, axis=1, keepdims=True) + EPS)
    pulled = hidden * gain_ref[...]
    cross = jnp.mean(pulled * inputs, axis=1, keepdims=True)
    grad = cotangent + scale * pulled - inputs * (scale * scale * scale) * cross
    grad = grad.astype(BF16)
    out_ref[:, :width] = grad
    grad = grad.astype(F32)
    grad_mean = jnp.sum(grad * total_ref[...], axis=1, keepdims=True) / features
    cross_mean = jnp.sum(grad * vision_ref[...], axis=1, keepdims=True) / features
    out_ref[:, width:] = put_scalars([grad_mean, cross_mean], grad.shape[0]).astype(BF16)


def merge_grad_kernel(*refs, size):
    gain_ref, merged_ref, scalar_ref, weight_ref, *part_refs, out_ref = refs
    rows, features = merged_ref.shape
    width = weight_ref.shape[1]
    depth, patches = out_ref.shape
    row_share = part_refs[0].shape[0]
    parts = stacked(part_refs)
    normed_grad = dot_nt(parts[:, :width], weight_ref[...]) * flat_gain(gain_ref)
    means = parts[:, width:].astype(F32)
    scalars = scalar_ref[:, width:].astype(F32)
    inv_std = get_scalar(scalars, 1)
    normed = (merged_ref[...].astype(F32) - get_scalar(scalars, 0)) * inv_std
    grad = inv_std * (normed_grad - get_scalar(means, 0) - normed * get_scalar(means, 1))
    high = grad.astype(BF16)
    low = (grad - high.astype(F32)).astype(BF16)
    line = iota((patches, rows), 1)
    line = ((line // row_share) ^ lax.axis_index("expert")) * row_share + line % row_share
    unfold = (iota((patches, rows), 0) // 4 == line).astype(F32)
    spot = iota((patches, features), 1) // size % 4 == iota((patches, features), 0) % 4
    row, col = iota((depth, features), 0), iota((depth, features), 1)
    place = (col // (4 * size) == row // size) & (col % size == row % size)
    place = place.astype(F32).astype(BF16)
    out = jnp.zeros((depth, patches), F32)
    for piece in (high, low):
        wide = jnp.where(spot, dot(unfold, piece), 0.0).astype(BF16)
        out = out + dot_nt(place, wide)
    out_ref[...] = out


def whole(memory_space=pltpu.VMEM):
    return pl.BlockSpec(memory_space=memory_space)


def run(kernel, outs, *args, far=(), scratch=(), cost=1.0, vmem=VMEM_BYTES, name=None):
    specs = [whole()] * len(args)
    for place in far:
        specs[place] = whole(pl.ANY)
    return pl.pallas_call(
        kernel,
        out_shape=outs,
        in_specs=specs,
        out_specs=jax.tree.map(lambda _: whole(), outs),
        scratch_shapes=scratch,
        compiler_params=pltpu.CompilerParams(vmem_limit_bytes=vmem),
        cost_estimate=microseconds(cost),
        name=name,
    )(*args)


def to_sibling(parts, deps, name):
    rows, width = parts[0].shape
    half = run(
        functools.partial(other_half_kernel, count=len(parts)),
        shape((len(parts) * rows // 2, width)), *parts, *deps,
        far=range(len(parts), len(parts) + len(deps)), cost=0.01, name=name,
    )
    return swap(half, "blk", 1)


def microseconds(time):
    return pl.CostEstimate(flops=0, transcendentals=0, bytes_accessed=int(time * 3e6))


def after(values, deps):
    count = len(values)
    return pl.pallas_call(
        lambda *refs: None,
        out_shape=[shape(value.shape, value.dtype) for value in values],
        in_specs=[whole(pl.ANY)] * (count + len(deps)),
        out_specs=[whole(pl.ANY)] * count,
        input_output_aliases={i: i for i in range(count)},
        compiler_params=pltpu.CompilerParams(vmem_limit_bytes=VMEM_BYTES),
        cost_estimate=microseconds(0.1),
        name="after",
    )(*values, *deps)


def shape(dims, dtype=BF16):
    return jax.ShapeDtypeStruct(dims, dtype)


def swap(value, axis, step):
    count = lax.axis_size(axis)
    return lax.ppermute(value, axis, [(i, i ^ step) for i in range(count)])


def trade(parts, axis):
    return [parts[0]] + [swap(parts[k], axis, k) for k in range(1, len(parts))]


def spread_out(value, axis):
    return trade([value] * lax.axis_size(axis), axis)


def gather_blocks(value, deps=None):
    own = [value] + [swap(value, "blk", k) for k in range(2, lax.axis_size("blk"), 2)]
    if deps is not None:
        own = own[:1] + list(after(own[1:], deps))
    sibling = [swap(part, "blk", 1) for part in own]
    return [part for pair in zip(own, sibling) for part in pair]


def to_chips(parts):
    return [parts[0]] + [swap(parts[k], "blk", 2 * k) for k in range(1, len(parts))]


def body(
    queries, keys, values, image_ids, placement, merge_gain, merge_weight, text, norm_gain,
    w_gate, w_up, w_down, routes, route_gates, cotangent,
):
    blocks = lax.axis_size("blk")
    share = lax.axis_size("expert")
    heads, size, patches = queries.shape
    depth = heads * size
    rows = image_ids.shape[0]
    row_share = rows // share
    tokens, width = text.shape
    part = tokens // share
    all_rows = blocks * rows
    features = heads * 4 * size
    hidden = w_gate.shape[1]
    slot_count = blocks * SLOTS
    groups = share // 2
    routes_t, gates_t, gain_row = routes.T, route_gates.T, norm_gain[None]

    small = [
        keys.reshape(depth, patches), values.reshape(depth, patches),
        image_ids[None], placement.reshape(1, rows), routes_t,
    ]
    local = run(
        pack_kernel, shape((2 * depth + 16, patches)), *small, far=range(5),
        scratch=[pltpu.VMEM(array.shape, array.dtype) for array in small]
        + [pltpu.SemaphoreType.DMA((5,))],
        vmem=PACK_BYTES, name="pack",
    )
    comb, pick, factor = run(
        functools.partial(route_kernel, groups=groups, share=share),
        [
            shape((2, slot_count, tokens)), shape((2, blocks * SEND, tokens)),
            shape((blocks * SEND, 128), F32),
        ],
        routes_t, gates_t, cost=3.0, name="route",
    )
    send = run(
        dispatch_kernel, [shape((2 * SEND, width))] * (blocks // 2),
        pick, factor, text, gain_row, cotangent, cost=2.0, name="dispatch",
    )
    near = gather_blocks(local, send)
    early = to_chips(after(send, near[2::2]))

    weight_flat = merge_weight.reshape(features, width)
    message_width = width + width // row_share + 128
    merged, meta, left, local_scalars = run(
        functools.partial(attend_kernel, blocks=blocks, row_share=row_share),
        [
            shape((rows, features)), shape((blocks * 16, patches)), shape((rows + 16, features)),
            shape((rows, 128), F32),
        ],
        queries, merge_gain, *small, *near[1:], cost=3.0, name="attend",
    )
    message = run(
        project_kernel, [shape((row_share, message_width))] * share,
        left, local_scalars, weight_flat, early[1], far=(3,), cost=2.0, name="project",
    )
    slots, placed, back_cots = run(
        functools.partial(
            plan_kernel, blocks=blocks, groups=groups, merged_rows=rows, row_share=row_share
        ),
        [
            shape((slot_count, all_rows)), shape((tokens, all_rows)),
            shape((blocks * row_share, width)),
        ],
        meta, cotangent, cost=1.5, name="plan",
    )
    message = trade(message, "expert")
    early = early[:1] + list(after(early[1:], message[1:]))
    own, vision_exact, gain_total = run(
        functools.partial(merge_kernel, width=width, features=features),
        [
            shape((row_share, width + 128)), shape((row_share, width), F32),
            shape((1, width), F32),
        ],
        early[1], *message, far=(0,), cost=0.2, name="merge",
    )
    owns = spread_out(own, "expert")
    block_rows = run(
        stack_kernel, shape((rows, width + 128)), *owns, cost=0.2, name="stack",
    )
    text_rows, act_grad = run(
        early_kernel, [shape((slot_count, width)), shape((slot_count, hidden), F32)],
        w_down, *early, to_sibling(early, owns[1:], "early_half"), cost=3.0, name="early",
    )

    vision = gather_blocks(block_rows, [text_rows, slots])
    gate_pre, up_proj, *down = run(
        functools.partial(forward_kernel, blocks=blocks),
        [
            shape((slot_count, hidden), F32), shape((slot_count, hidden), F32),
        ] + [shape((2 * SLOTS, width))] * (blocks // 2),
        slots, gain_row, w_gate, w_up, w_down, text_rows, *vision,
        scratch=[pltpu.VMEM((slot_count, width), BF16), pltpu.VMEM((slot_count, width), F32)],
        cost=4.0, name="forward",
    )
    returned = to_chips(down)
    block = rows + row_share
    even, odd = run(
        functools.partial(backward_kernel, blocks=blocks),
        [shape((blocks // 2 * block, width))] * 2,
        slots, act_grad, gate_pre, up_proj, back_cots, w_gate, w_up,
        scratch=[pltpu.VMEM((slot_count, width), F32)],
        cost=4.0, name="backward",
    )
    grads = run(
        pair_sum_kernel, [shape((block, width))] * (blocks // 2), even, swap(odd, "blk", 1),
        cost=0.2, name="pair_sum",
    )
    grads = to_chips(grads)
    count = tokens // 4
    pieces = [shape((count, width), F32)] * 2 + [shape((count, width))] * 2
    low, high, sent_low, sent_high = run(
        combine_kernel, pieces, comb, *returned,
        to_sibling(returned, grads[:1], "returned_half"), cost=0.01, name="combine",
    )
    first_sent, step = sent_low, 1
    arrived_high = swap(sent_high, "expert", step)
    arrived_low = swap(sent_low, "expert", step)
    while count > part:
        count //= 2
        step *= 2
        pieces = [shape((count, width), F32)] * 2 + [shape((count, width))] * 2
        low, high, sent_low, sent_high = run(
            halve_kernel, pieces, low, high, arrived_low, arrived_high, cost=0.3, name="halve"
        )
        arrived_high = swap(sent_high, "expert", step)
        arrived_low = swap(sent_low, "expert", step)
    step *= 2

    def add(own_part, arrived, gate, name):
        return run(
            add_kernel, shape((part, width)), own_part, arrived, *gate,
            far=range(2, 2 + len(gate)), cost=0.3, name=name,
        )

    sum_high = add(high, arrived_high, grads[1:], "add_high")
    cot_rows, *grads = run(
        functools.partial(chip_sum_kernel, count=blocks // 2),
        [shape((row_share, width))] * (share + 1), *grads, first_sent, far=(blocks // 2,), cost=0.2,
        name="chip_sum",
    )
    grads = trade(grads, "expert")
    sums = [add(low, arrived_low, grads[1:], "add_low"), sum_high]
    others = [swap(value, "expert", step) for value in sums][::-1]
    vision_grad = run(
        functools.partial(norm_grad_kernel, features=share * features),
        shape((row_share, width + 128)),
        own, gain_row, cot_rows, vision_exact, gain_total, *grads, cost=0.3, name="norm_grad",
    )
    vision_grads = spread_out(vision_grad, "expert")
    attn_grad = run(
        functools.partial(merge_grad_kernel, size=size), shape((depth, patches), F32),
        merge_gain, merged, block_rows, weight_flat, *vision_grads, cost=4.0, name="merge_grad",
    )

    laid = {}
    for turn, value, other, gate in zip((0, step), sums, others, (grads, vision_grads)):
        laid[turn] = run(
            functools.partial(finish_kernel, blocks=blocks, turn=turn), shape((part, width)),
            placed, text, value, other, *vision, *gate[1:],
            far=range(4 + blocks, 3 + blocks + share), cost=1.0, name="finish",
        )
    while step > 1:
        step //= 2
        laid.update({k + step: swap(laid[k], "expert", step) for k in list(laid)})
    llm_out = run(
        lay_kernel, shape((tokens, width)), *[laid[k] for k in sorted(laid)], cost=1.0, name="lay"
    )
    return llm_out, attn_grad.reshape(heads, size, patches)


def solution(mesh):
    return jax.shard_map(
        body,
        mesh=mesh,
        in_specs=(
            P("expert", None, "blk"),
            P("expert", None, "blk"),
            P("expert", None, "blk"),
            P("blk"),
            P("blk", None),
            P("expert", None),
            P("expert", None, None),
            P("blk", None),
            P(),
            P("blk", "expert", None),
            P("blk", "expert", None),
            P("blk", "expert", None),
            P("blk", None),
            P("blk", None),
            P("blk", None),
        ),
        out_specs=(P("blk", None), P("expert", None, "blk")),
        check_vma=False,
    )
```

```python
import functools

import jax
import jax.numpy as jnp
from jax import lax
from jax.experimental import pallas as pl
from jax.experimental.pallas import tpu as pltpu
from jax.sharding import PartitionSpec as P

CAPX = 10
SLOTS = 12
SEND = 24
EPS = 1e-06
VMEM_BYTES = 16 * 1024 * 1024
PACK_BYTES = 60 * 1024 * 1024
F32 = jnp.float32
BF16 = jnp.bfloat16


def iota(shape, dim):
    return lax.broadcasted_iota(jnp.int32, shape, dim)


def dot(a, b):
    return jnp.dot(a.astype(BF16), b.astype(BF16), preferred_element_type=F32)


def dot_nt(a, b):
    return lax.dot_general(a, b, (((1,), (1,)), ((), ())), preferred_element_type=F32)


def dot_tn(a, b):
    return lax.dot_general(a, b, (((0,), (0,)), ((), ())), preferred_element_type=F32)


def three(value):
    first = value.astype(BF16).astype(F32)
    second = (value - first).astype(BF16).astype(F32)
    return first, second, value - first - second


def put_scalars(columns, rows):
    lane = iota((rows, 128), 1)
    out = jnp.zeros((rows, 128), F32)
    place = 0
    for column in columns:
        for piece in three(column):
            out = jnp.where(lane == place, piece, out)
            place += 1
    return out


def get_scalar(block, which):
    lane = iota(block.shape, 1)
    return jnp.sum(jnp.where(lane // 3 == which, block, 0.0), axis=1, keepdims=True)


def bring(far_refs, near_refs, sems):
    copies = [
        pltpu.make_async_copy(far, near, sems.at[i])
        for i, (far, near) in enumerate(zip(far_refs, near_refs))
    ]
    for copy in copies:
        copy.start()
    return copies


def pack_kernel(*refs):
    far_refs, out_ref, near_refs, sems = refs[:5], refs[5], refs[6:11], refs[11]
    for copy in bring(far_refs, near_refs, sems):
        copy.wait()
    out_ref[...] = packed(*near_refs).astype(BF16)


def packed(keys_ref, values_ref, images_ref, placement_ref, routes_ref):
    rows = images_ref.shape[1]
    patches = keys_ref.shape[1]
    repeat = (iota((rows, patches), 0) == iota((rows, patches), 1) // 4).astype(F32)
    keep = (iota((rows, patches), 0) == iota((rows, patches), 1)).astype(F32)
    patch_ids = dot(images_ref[...].astype(F32), repeat)
    dest = dot(placement_ref[...].astype(F32), keep)
    line = iota((8, patches), 0)
    rest = jnp.where(line == 0, patch_ids, jnp.where(line == 1, dest, 0.0))
    parts = [keys_ref[...], values_ref[...], routes_ref[...], rest]
    return jnp.concatenate([part.astype(F32) for part in parts], axis=0)


def route_kernel(routes_ref, gates_ref, comb_ref, pick_ref, factor_ref, *, groups, share):
    blocks = comb_ref.shape[1] // SLOTS
    tokens = routes_ref.shape[1]
    me, expert_index = lax.axis_index("blk"), lax.axis_index("expert")
    member = expert_index // groups
    before = (iota((tokens, tokens), 0) < iota((tokens, tokens), 1)).astype(BF16)
    pair_of = 2 * (iota((blocks, tokens), 0) ^ me) + member
    out_hit = jnp.zeros((blocks, tokens), F32)
    out_gate = jnp.zeros((blocks, tokens), F32)
    for k in range(routes_ref.shape[0]):
        same = pair_of == routes_ref[k : k + 1, :]
        out_hit = out_hit + same.astype(F32)
        out_gate = out_gate + jnp.where(same, gates_ref[k : k + 1, :], 0.0)
    out_rank = dot(out_hit, before)

    def expand(stride):
        count = blocks * stride
        pick = (iota((count, blocks), 0) // stride == iota((count, blocks), 1)).astype(BF16)
        gate = sum(dot(pick, piece) for piece in three(out_gate))
        return dot(pick, out_hit), dot(pick, out_rank).astype(jnp.int32), gate

    hits, ranks, gates = expand(SLOTS)
    live = jnp.where(ranks == iota(hits.shape, 0) % SLOTS, hits, 0.0)
    weight = live * gates
    high = weight.astype(BF16).astype(F32)
    part = tokens // share
    col = iota((tokens, tokens), 1)
    turned = (col // part * 0).astype(jnp.int32)
    for place, k in enumerate(halving_order(share)):
        turned = jnp.where(col // part == place, k, turned)
    turned = (iota((tokens, tokens), 0) == (turned ^ expert_index) * part + col % part)
    turned = turned.astype(F32)
    comb_ref[0] = dot(high, turned).astype(BF16)
    comb_ref[1] = dot(weight - high, turned).astype(BF16)

    hits, ranks, gates = expand(SEND)
    place = iota(hits.shape, 0) % SEND
    input_pick = jnp.where((place < CAPX) & (ranks == place), hits, 0.0)
    back_pick = jnp.where((place >= CAPX) & (place < 2 * CAPX) & (ranks == place - CAPX), hits, 0.0)
    pick_ref[0] = input_pick.astype(BF16)
    pick_ref[1] = back_pick.astype(BF16)
    factor = jnp.sum(back_pick * gates, axis=1, keepdims=True)
    factor_ref[...] = jnp.broadcast_to(factor, factor_ref.shape)


def dispatch_kernel(pick_ref, factor_ref, text_ref, gain_ref, cot_ref, *send_refs):
    text = text_ref[...].astype(F32)
    scale = lax.rsqrt(jnp.mean(text * text, axis=1, keepdims=True) + EPS)
    h_rows = (text * scale * gain_ref[...]).astype(BF16)
    factor = factor_ref[:, :1]
    send = dot(pick_ref[0], h_rows) + factor * dot(pick_ref[1], cot_ref[...])
    send = send.astype(BF16)
    count = 2 * SEND
    for k, ref in enumerate(send_refs):
        ref[...] = send[k * count : (k + 1) * count]


def plan_kernel(
    meta_ref, cot_ref, slots_ref, placed_ref, back_ref, *, blocks, groups, merged_rows, row_share
):
    tokens = cot_ref.shape[0]
    rows = blocks * merged_rows
    me, expert_index = lax.axis_index("blk"), lax.axis_index("expert")
    member = expert_index // groups
    meta = [meta_ref[k * 16 : (k + 1) * 16].astype(F32) for k in range(blocks)]
    mine = (2 * me + member).astype(F32)
    hits = [jnp.sum((part[:8] == mine).astype(F32), axis=0, keepdims=True) for part in meta]
    hit = jnp.concatenate(hits, axis=0)
    dest = jnp.concatenate([part[9:10] for part in meta], axis=0)
    before = (iota((tokens, tokens), 0) < iota((tokens, tokens), 1)).astype(BF16)
    rank = dot(hit, before)

    def row_of(col):
        inner = col % merged_rows
        return ((inner // row_share) ^ expert_index) * row_share + inner % row_share

    def place_of(col):
        return ((col // merged_rows) ^ me) * merged_rows + row_of(col)

    spread = (iota((128, rows), 0) == row_of(iota((128, rows), 1))).astype(F32)
    own_block = iota((blocks, rows), 1) // merged_rows == iota((blocks, rows), 0)
    dest_row = jnp.sum(jnp.where(own_block, dot(dest, spread), 0.0), axis=0, keepdims=True)
    dest_row = dest_row.astype(jnp.int32) ^ me
    dest_hit = (iota((blocks, rows), 0) == dest_row).astype(F32)
    rows_before = place_of(iota((rows, rows), 0)) < place_of(iota((rows, rows), 1))
    earlier = dot(dest_hit, rows_before.astype(F32))
    slot = jnp.sum(dest_hit * earlier, axis=0, keepdims=True).astype(jnp.int32)
    at_token = (iota((tokens, rows), 0) == slot).astype(F32)
    row_hit = jnp.sum(dest_hit * dot(hit, at_token), axis=0, keepdims=True)
    row_rank = jnp.sum(dest_hit * dot(rank, at_token), axis=0, keepdims=True).astype(jnp.int32)
    slot_id = dest_row * SLOTS + row_rank
    slot_count = slots_ref.shape[0]
    chosen = (iota((slot_count, rows), 0) == slot_id) & (row_hit > 0.5)
    slots_ref[...] = chosen.astype(F32).astype(BF16)
    placed = jnp.where(dest_row == 0, at_token, 0.0).astype(BF16)
    placed_ref[...] = placed
    back_rows = blocks * row_share
    source = iota((back_rows, rows), 0)
    wanted = source // row_share * merged_rows + source % row_share
    row_pick = (iota((back_rows, rows), 1) == wanted).astype(F32).astype(BF16)
    back_ref[...] = dot(dot_nt(row_pick, placed), cot_ref[...]).astype(BF16)


def flat_gain(gain_ref):
    return jnp.concatenate([gain_ref[h : h + 1] for h in range(gain_ref.shape[0])], axis=1)


def attend_kernel(*refs, blocks, row_share):
    query_ref, gain_ref = refs[:2]
    near_refs = refs[7 : 6 + blocks]
    merged_ref, meta_ref, left_ref, scalar_ref = refs[6 + blocks :]
    heads, size, patches = query_ref.shape
    rows, features = merged_ref.shape
    depth = heads * size
    near = [packed(*refs[2:7])] + [ref[...].astype(F32) for ref in near_refs]
    meta_ref[...] = jnp.concatenate([part[2 * depth :] for part in near], axis=0).astype(BF16)
    key_ids = jnp.concatenate([part[2 * depth + 8 : 2 * depth + 9] for part in near], axis=1)
    eye = iota((patches, patches), 0) == iota((patches, patches), 1)
    own_ids = jnp.sum(jnp.where(eye, key_ids[:, :patches], 0.0), axis=1, keepdims=True)
    same = own_ids == key_ids
    spread = jnp.zeros((patches, features), F32)
    place_row, place_col = iota((size, features), 0), iota((size, features), 1)
    for head in range(heads):
        first = head * size
        keys = jnp.concatenate([part[first : first + size] for part in near], axis=1)
        first = depth + head * size
        values = jnp.concatenate([part[first : first + size] for part in near], axis=1)
        query = query_ref[head].astype(F32).T.astype(BF16)
        scores = dot(query, keys) * (size**-0.5)
        scores = jnp.where(same, scores, -1e30)
        weights = jnp.exp(scores - jnp.max(scores, axis=1, keepdims=True))
        total = jnp.sum(weights, axis=1, keepdims=True)
        attn = dot_nt(weights.astype(BF16), values.astype(BF16)) / total
        place = (place_col % size == place_row) & (place_col // (4 * size) == head)
        spread = spread + dot(attn, place.astype(F32))
    spot = iota((patches, features), 1) // size % 4 == iota((patches, features), 0) % 4
    line = iota((rows, patches), 0)
    line = ((line // row_share) ^ lax.axis_index("expert")) * row_share + line % row_share
    fold = (iota((rows, patches), 1) // 4 == line).astype(F32)
    merged = dot(fold, jnp.where(spot, spread, 0.0))
    merged_ref[...] = merged.astype(BF16)
    local_mean = jnp.sum(merged, axis=1, keepdims=True) / features
    centered = merged - local_mean
    squares = jnp.sum(centered * centered, axis=1, keepdims=True)
    gain = flat_gain(gain_ref)
    gain_high = gain.astype(BF16).astype(F32)
    extra = iota((16, features), 0)
    gain_rows = jnp.where(extra == 0, gain_high, jnp.where(extra == 1, gain - gain_high, 0.0))
    left_ref[...] = jnp.concatenate([centered * gain, gain_rows], axis=0).astype(BF16)
    scalar_ref[...] = put_scalars([local_mean, squares], rows)


def project_kernel(left_ref, scalar_ref, weight_ref, _, *message_refs):
    rows = scalar_ref.shape[0]
    width = weight_ref.shape[1]
    row_share = rows // len(message_refs)
    product = dot(left_ref[...], weight_ref[...])
    gain_sum = product[rows : rows + 1] + product[rows + 1 : rows + 2]
    piece = width // row_share
    pieces = [gain_sum[:, j * piece : (j + 1) * piece] for j in range(row_share)]
    pieces = jnp.concatenate(pieces, axis=0).astype(BF16)
    scalars = scalar_ref[...].astype(BF16)
    for k, message_ref in enumerate(message_refs):
        mine = slice(k * row_share, (k + 1) * row_share)
        message_ref[:, :width] = product[mine].astype(BF16)
        message_ref[:, width : width + piece] = pieces
        message_ref[:, width + piece :] = scalars[mine]


def merge_kernel(_, *refs, width, features):
    *message_refs, out_ref, gain_ref = refs
    share, row_share = len(message_refs), out_ref.shape[0]
    piece = width // row_share
    parts = [ref[...].astype(F32) for ref in message_refs]
    scalars = [part[:, width + piece :] for part in parts]
    means = [get_scalar(block, 0) for block in scalars]
    squares = [get_scalar(block, 1) for block in scalars]
    mean = sum(means) / share
    spread = sum(q + features * (m - mean) * (m - mean) for q, m in zip(squares, means))
    inv_std = lax.rsqrt(spread / (share * features) + EPS)
    total = jnp.zeros((row_share, width), F32)
    gain_total = jnp.zeros((1, width), F32)
    for part, local in zip(parts, means):
        tail = part[:, width : width + piece]
        gain_sum = jnp.concatenate([tail[j : j + 1] for j in range(row_share)], axis=1)
        total = total + part[:, :width] + (local - mean) * gain_sum
        gain_total = gain_total + gain_sum
    gain_ref[...] = gain_total
    out_ref[:, :width] = (total * inv_std).astype(BF16)
    out_ref[:, width:] = put_scalars([mean, inv_std], row_share).astype(BF16)


def stack_kernel(*refs):
    *part_refs, out_ref = refs
    out_ref[...] = stacked(part_refs)


def stacked(part_refs):
    return jnp.concatenate([ref[...].astype(F32) for ref in part_refs], axis=0).astype(BF16)


def by_chip(own_refs, sibling_ref):
    parts = []
    sibling = sibling_ref[...].astype(F32)
    for k, own_ref in enumerate(own_refs):
        half = own_ref.shape[0] // 2
        parts.append(own_ref[...].astype(F32)[:half])
        parts.append(sibling[k * half : (k + 1) * half])
    return jnp.concatenate(parts, axis=0).astype(BF16)


def other_half_kernel(*refs, count):
    out_ref = refs[-1]
    parts = [ref[...].astype(F32)[ref.shape[0] // 2 :] for ref in refs[:count]]
    out_ref[...] = jnp.concatenate(parts, axis=0).astype(BF16)


def slot_pick(slot_count, send_rows, shift):
    row, col = iota((slot_count, send_rows), 0), iota((slot_count, send_rows), 1)
    place = row % SLOTS
    pick = (col == row // SLOTS * SEND + place + shift) & (place < CAPX)
    return pick.astype(F32)


def early_kernel(down_ref, *refs):
    *early_refs, sibling_ref, text_out, grad_out = refs
    slot_count = text_out.shape[0]
    early = by_chip(early_refs, sibling_ref)
    text_out[...] = dot(slot_pick(slot_count, early.shape[0], 0), early).astype(BF16)
    back_rows = dot(slot_pick(slot_count, early.shape[0], CAPX), early).astype(BF16)
    grad_out[...] = dot_nt(back_rows, down_ref[0])


def forward_kernel(*refs, blocks):
    slots_ref, gain_ref, gate_ref, up_ref, down_ref, text_ref = refs[:6]
    vision_refs = refs[6 : 6 + blocks]
    gate_out, up_out, *down_refs = refs[6 + blocks : -2]
    h_ref, sum_ref = refs[-2:]
    _, hidden, width = gate_ref.shape
    chosen = slots_ref[...]
    is_vision = jnp.sum(chosen.astype(F32), axis=1, keepdims=True) > 0.5
    vision = jnp.concatenate([ref[:, :width] for ref in vision_refs], axis=0)
    inputs = dot(chosen, vision)
    scale = lax.rsqrt(jnp.mean(inputs * inputs, axis=1, keepdims=True) + EPS)
    normed = inputs * scale * gain_ref[...]
    h_ref[...] = jnp.where(is_vision, normed, text_ref[...].astype(F32)).astype(BF16)
    tile = tile_of(hidden)
    for i in range(hidden // tile):
        mine = slice(i * tile, (i + 1) * tile)
        gate_pre = dot_nt(h_ref[...], gate_ref[0, mine])
        up_proj = dot_nt(h_ref[...], up_ref[0, mine])
        gate_out[:, mine] = gate_pre
        up_out[:, mine] = up_proj
        activated = gate_pre * jax.nn.sigmoid(gate_pre) * up_proj
        product = dot(activated, down_ref[0, mine])
        sum_ref[...] = product if i == 0 else sum_ref[...] + product
    count = 2 * SLOTS
    for k, ref in enumerate(down_refs):
        ref[...] = sum_ref[k * count : (k + 1) * count].astype(BF16)


def backward_kernel(
    slots_ref, grad_ref, gate_in, up_in, cot_ref, gate_ref, up_ref, even_ref, odd_ref, sum_ref,
    *, blocks,
):
    hidden = gate_ref.shape[1]
    tile = tile_of(hidden)
    for i in range(hidden // tile):
        mine = slice(i * tile, (i + 1) * tile)
        act_grad = grad_ref[:, mine]
        gate_pre, up_proj = gate_in[:, mine], up_in[:, mine]
        sigmoid = jax.nn.sigmoid(gate_pre)
        gate_grad = act_grad * up_proj * sigmoid * (1.0 + gate_pre * (1.0 - sigmoid))
        up_grad = act_grad * gate_pre * sigmoid
        product = dot(gate_grad, gate_ref[0, mine]) + dot(up_grad, up_ref[0, mine])
        sum_ref[...] = product if i == 0 else sum_ref[...] + product
    grads = dot_tn(slots_ref[...], sum_ref[...].astype(BF16))
    cots = cot_ref[...].astype(F32)
    rows, row_share = grads.shape[0] // blocks, cots.shape[0] // blocks
    parts = ([], [])
    for k in range(blocks):
        parts[k % 2].append(grads[k * rows : (k + 1) * rows])
        parts[k % 2].append(cots[k * row_share : (k + 1) * row_share])
    even_ref[...] = jnp.concatenate(parts[0], axis=0).astype(BF16)
    odd_ref[...] = jnp.concatenate(parts[1], axis=0).astype(BF16)


def tile_of(hidden):
    return 256 if hidden % 256 == 0 else hidden


def halving_order(share):
    order = [0]
    step = share // 2
    while step:
        order = order + [k + step for k in order]
        step //= 2
    return [sum(1 << j for j in range(share.bit_length() - 1) if k >> j & 1) for k in order]


def pair_sum_kernel(own_ref, sibling_ref, *out_refs):
    rows = out_refs[0].shape[0]
    total = own_ref[...].astype(F32) + sibling_ref[...].astype(F32)
    for k, out_ref in enumerate(out_refs):
        out_ref[...] = total[k * rows : (k + 1) * rows].astype(BF16)


def total_of(part_refs):
    total = part_refs[0][...].astype(F32)
    for ref in part_refs[1:]:
        total = total + ref[...].astype(F32)
    return total


def chip_sum_kernel(*refs, count, order):
    cot_ref, keep_ref, send_ref = refs[count + 1 :]
    total = total_of(refs[:count])
    rows = cot_ref.shape[0]
    turned = jnp.concatenate([total[k * rows : (k + 1) * rows] for k in order], axis=0)
    half = turned.shape[0] // 2
    keep_ref[...] = turned[:half]
    send_ref[...] = turned[half:].astype(BF16)
    cot_ref[...] = total[len(order) * rows :].astype(BF16)


def grad_halve_kernel(keep_ref, arrived_ref, *refs):
    quarters(keep_ref[...] + arrived_ref[...].astype(F32), refs)


def grad_join_kernel(keep_ref, arrived_ref, cot_ref, out_ref):
    total = keep_ref[...] + arrived_ref[...].astype(F32)
    out_ref[...] = jnp.concatenate([total, cot_ref[...].astype(F32)], axis=0).astype(BF16)


def quarters(total, out_refs):
    count = out_refs[0].shape[0]
    for k, ref in enumerate(out_refs):
        ref[...] = total[k * count : (k + 1) * count].astype(ref.dtype)


def combine_kernel(comb_ref, *refs):
    *part_refs, sibling_ref = refs[:-4]
    rows = by_chip(part_refs, sibling_ref)
    quarters(dot_tn(comb_ref[0], rows) + dot_tn(comb_ref[1], rows), refs[-4:])


def halve_kernel(*refs):
    low, high, arrived_low, arrived_high = [ref[...].astype(F32) for ref in refs[:4]]
    quarters(jnp.concatenate([low + arrived_low, high + arrived_high], axis=0), refs[4:])


def add_kernel(own_ref, arrived_ref, *refs):
    refs[-1][...] = (own_ref[...] + arrived_ref[...].astype(F32)).astype(BF16)


def finish_kernel(placed_ref, text_ref, own_ref, arrived_ref, *refs, blocks, turn):
    vision_refs, out_ref = refs[:blocks], refs[-1]
    count, width = out_ref.shape
    tokens = placed_ref.shape[0]
    first = (lax.axis_index("expert") ^ turn) * count
    pick = iota((count, tokens), 1) == iota((count, tokens), 0) + first
    pick = pick.astype(F32)
    placed = dot(pick, placed_ref[...])
    is_vision = jnp.sum(placed, axis=1, keepdims=True) > 0.5
    vision = jnp.concatenate([ref[:, :width] for ref in vision_refs], axis=0)
    inputs = jnp.where(is_vision, dot(placed, vision), dot(pick, text_ref[...]))
    out_ref[...] = (inputs + (own_ref[...].astype(F32) + arrived_ref[...].astype(F32))).astype(BF16)


def lay_kernel(*refs):
    *part_refs, out_ref = refs
    count = part_refs[0].shape[0]
    for k, ref in enumerate(part_refs):
        first = pl.multiple_of((lax.axis_index("expert") ^ k) * count, count)
        out_ref[pl.ds(first, count), :] = ref[...]


def norm_grad_kernel(
    joined_ref, other_ref, rows_ref, gain_ref, total_ref, out_ref, *, features
):
    width = gain_ref.shape[1]
    count = out_ref.shape[0] // 2
    far = rows_ref.shape[0] // 2
    joined, other = joined_ref[...].astype(F32), other_ref[...].astype(F32)
    turned = jnp.concatenate([other[count : 2 * count], other[:count]], axis=0)
    hidden = joined[: 2 * count] + turned
    cotangent = jnp.concatenate([joined[2 * count :], other[2 * count :]], axis=0)
    rows = rows_ref[:, :width].astype(F32)
    inputs = jnp.concatenate([rows[:count], rows[far : far + count]], axis=0)
    scale = lax.rsqrt(jnp.mean(inputs * inputs, axis=1, keepdims=True) + EPS)
    pulled = hidden * gain_ref[...]
    cross = jnp.mean(pulled * inputs, axis=1, keepdims=True)
    grad = cotangent + scale * pulled - inputs * (scale * scale * scale) * cross
    grad = grad.astype(BF16)
    out_ref[:, :width] = grad
    grad = grad.astype(F32)
    grad_mean = jnp.sum(grad * total_ref[...], axis=1, keepdims=True) / features
    cross_mean = jnp.sum(grad * inputs, axis=1, keepdims=True) / features
    out_ref[:, width:] = put_scalars([grad_mean, cross_mean], 2 * count).astype(BF16)


def merge_grad_kernel(*refs, size, bases):
    gain_ref, merged_ref, scalar_ref, weight_ref, *part_refs, out_ref = refs
    rows, features = merged_ref.shape
    width = weight_ref.shape[1]
    depth, patches = out_ref.shape
    row_share = part_refs[0].shape[0] // 2
    blocks = {}
    for base, ref in zip(bases, part_refs):
        part = ref[...].astype(F32)
        blocks[base] = part[:row_share]
        blocks[base ^ len(bases)] = part[row_share:]
    parts = jnp.concatenate([blocks[k] for k in sorted(blocks)], axis=0).astype(BF16)
    normed_grad = dot_nt(parts[:, :width], weight_ref[...]) * flat_gain(gain_ref)
    means = parts[:, width:].astype(F32)
    scalars = scalar_ref[:, width:].astype(F32)
    inv_std = get_scalar(scalars, 1)
    normed = (merged_ref[...].astype(F32) - get_scalar(scalars, 0)) * inv_std
    grad = inv_std * (normed_grad - get_scalar(means, 0) - normed * get_scalar(means, 1))
    high = grad.astype(BF16)
    low = (grad - high.astype(F32)).astype(BF16)
    line = iota((patches, rows), 1)
    line = ((line // row_share) ^ lax.axis_index("expert")) * row_share + line % row_share
    unfold = (iota((patches, rows), 0) // 4 == line).astype(F32)
    spot = iota((patches, features), 1) // size % 4 == iota((patches, features), 0) % 4
    row, col = iota((depth, features), 0), iota((depth, features), 1)
    place = (col // (4 * size) == row // size) & (col % size == row % size)
    place = place.astype(F32).astype(BF16)
    out = jnp.zeros((depth, patches), F32)
    for piece in (high, low):
        wide = jnp.where(spot, dot(unfold, piece), 0.0).astype(BF16)
        out = out + dot_nt(place, wide)
    out_ref[...] = out


def whole(memory_space=pltpu.VMEM):
    return pl.BlockSpec(memory_space=memory_space)


def run(kernel, outs, *args, far=(), scratch=(), cost=1.0, vmem=VMEM_BYTES, name=None):
    specs = [whole()] * len(args)
    for place in far:
        specs[place] = whole(pl.ANY)
    return pl.pallas_call(
        kernel,
        out_shape=outs,
        in_specs=specs,
        out_specs=jax.tree.map(lambda _: whole(), outs),
        scratch_shapes=scratch,
        compiler_params=pltpu.CompilerParams(vmem_limit_bytes=vmem),
        cost_estimate=microseconds(cost),
        name=name,
    )(*args)


def to_sibling(parts, deps, name):
    rows, width = parts[0].shape
    half = run(
        functools.partial(other_half_kernel, count=len(parts)),
        shape((len(parts) * rows // 2, width)), *parts, *deps,
        far=range(len(parts), len(parts) + len(deps)), cost=0.01, name=name,
    )
    return swap(half, "blk", 1)


def microseconds(time):
    return pl.CostEstimate(flops=0, transcendentals=0, bytes_accessed=int(time * 3e6))


def after(values, deps):
    count = len(values)
    return pl.pallas_call(
        lambda *refs: None,
        out_shape=[shape(value.shape, value.dtype) for value in values],
        in_specs=[whole(pl.ANY)] * (count + len(deps)),
        out_specs=[whole(pl.ANY)] * count,
        input_output_aliases={i: i for i in range(count)},
        compiler_params=pltpu.CompilerParams(vmem_limit_bytes=VMEM_BYTES),
        cost_estimate=microseconds(0.1),
        name="after",
    )(*values, *deps)


def shape(dims, dtype=BF16):
    return jax.ShapeDtypeStruct(dims, dtype)


def swap(value, axis, step):
    count = lax.axis_size(axis)
    return lax.ppermute(value, axis, [(i, i ^ step) for i in range(count)])


def trade(parts, axis):
    return [parts[0]] + [swap(parts[k], axis, k) for k in range(1, len(parts))]


def spread_out(value, axis):
    return trade([value] * lax.axis_size(axis), axis)


def gather_blocks(value, deps=None):
    own = [value] + [swap(value, "blk", k) for k in range(2, lax.axis_size("blk"), 2)]
    if deps is not None:
        own = own[:1] + list(after(own[1:], deps))
    sibling = [swap(part, "blk", 1) for part in own]
    return [part for pair in zip(own, sibling) for part in pair]


def to_chips(parts):
    return [parts[0]] + [swap(parts[k], "blk", 2 * k) for k in range(1, len(parts))]


def body(
    queries, keys, values, image_ids, placement, merge_gain, merge_weight, text, norm_gain,
    w_gate, w_up, w_down, routes, route_gates, cotangent,
):
    blocks = lax.axis_size("blk")
    share = lax.axis_size("expert")
    heads, size, patches = queries.shape
    depth = heads * size
    rows = image_ids.shape[0]
    row_share = rows // share
    tokens, width = text.shape
    part = tokens // share
    all_rows = blocks * rows
    features = heads * 4 * size
    hidden = w_gate.shape[1]
    slot_count = blocks * SLOTS
    groups = share // 2
    routes_t, gates_t, gain_row = routes.T, route_gates.T, norm_gain[None]

    small = [
        keys.reshape(depth, patches), values.reshape(depth, patches),
        image_ids[None], placement.reshape(1, rows), routes_t,
    ]
    local = run(
        pack_kernel, shape((2 * depth + 16, patches)), *small, far=range(5),
        scratch=[pltpu.VMEM(array.shape, array.dtype) for array in small]
        + [pltpu.SemaphoreType.DMA((5,))],
        vmem=PACK_BYTES, name="pack",
    )
    comb, pick, factor = run(
        functools.partial(route_kernel, groups=groups, share=share),
        [
            shape((2, slot_count, tokens)), shape((2, blocks * SEND, tokens)),
            shape((blocks * SEND, 128), F32),
        ],
        routes_t, gates_t, cost=3.0, name="route",
    )
    send = run(
        dispatch_kernel, [shape((2 * SEND, width))] * (blocks // 2),
        pick, factor, text, gain_row, cotangent, cost=2.0, name="dispatch",
    )
    near = gather_blocks(local, send)
    early = to_chips(after(send, near[2::2]))

    weight_flat = merge_weight.reshape(features, width)
    message_width = width + width // row_share + 128
    merged, meta, left, local_scalars = run(
        functools.partial(attend_kernel, blocks=blocks, row_share=row_share),
        [
            shape((rows, features)), shape((blocks * 16, patches)), shape((rows + 16, features)),
            shape((rows, 128), F32),
        ],
        queries, merge_gain, *small, *near[1:], cost=3.0, name="attend",
    )
    message = run(
        project_kernel, [shape((row_share, message_width))] * share,
        left, local_scalars, weight_flat, early[1], far=(3,), cost=2.0, name="project",
    )
    slots, placed, back_cots = run(
        functools.partial(
            plan_kernel, blocks=blocks, groups=groups, merged_rows=rows, row_share=row_share
        ),
        [
            shape((slot_count, all_rows)), shape((tokens, all_rows)),
            shape((blocks * row_share, width)),
        ],
        meta, cotangent, cost=1.5, name="plan",
    )
    message = trade(message, "expert")
    early = early[:1] + list(after(early[1:], message[1:]))
    own, gain_total = run(
        functools.partial(merge_kernel, width=width, features=features),
        [
            shape((row_share, width + 128)), shape((1, width), F32),
        ],
        early[1], *message, far=(0,), cost=0.2, name="merge",
    )
    owns = spread_out(own, "expert")
    block_rows = run(
        stack_kernel, shape((rows, width + 128)), *owns, cost=0.2, name="stack",
    )
    text_rows, act_grad = run(
        early_kernel, [shape((slot_count, width)), shape((slot_count, hidden), F32)],
        w_down, *early, to_sibling(early, owns[1:], "early_half"), cost=3.0, name="early",
    )

    vision = gather_blocks(block_rows, [text_rows, slots])
    gate_pre, up_proj, *down = run(
        functools.partial(forward_kernel, blocks=blocks),
        [
            shape((slot_count, hidden), F32), shape((slot_count, hidden), F32),
        ] + [shape((2 * SLOTS, width))] * (blocks // 2),
        slots, gain_row, w_gate, w_up, w_down, text_rows, *vision,
        scratch=[pltpu.VMEM((slot_count, width), BF16), pltpu.VMEM((slot_count, width), F32)],
        cost=4.0, name="forward",
    )
    returned = to_chips(down)
    block = rows + row_share
    even, odd = run(
        functools.partial(backward_kernel, blocks=blocks),
        [shape((blocks // 2 * block, width))] * 2,
        slots, act_grad, gate_pre, up_proj, back_cots, w_gate, w_up,
        scratch=[pltpu.VMEM((slot_count, width), F32)],
        cost=4.0, name="backward",
    )
    grads = run(
        pair_sum_kernel, [shape((block, width))] * (blocks // 2), even, swap(odd, "blk", 1),
        cost=0.2, name="pair_sum",
    )
    grads = to_chips(grads)
    count = tokens // 4
    pieces = [shape((count, width), F32)] * 2 + [shape((count, width))] * 2
    low, high, sent_low, sent_high = run(
        combine_kernel, pieces, comb, *returned,
        to_sibling(returned, grads[:1], "returned_half"), cost=0.01, name="combine",
    )
    step = 1
    arrived_high = swap(sent_high, "expert", step)
    first_arrived = arrived_high
    arrived_low = swap(sent_low, "expert", step)
    while count > part:
        count //= 2
        step *= 2
        pieces = [shape((count, width), F32)] * 2 + [shape((count, width))] * 2
        low, high, sent_low, sent_high = run(
            halve_kernel, pieces, low, high, arrived_low, arrived_high, cost=0.3, name="halve"
        )
        arrived_high = swap(sent_high, "expert", step)
        arrived_low = swap(sent_low, "expert", step)
    step *= 2

    def add(own_part, arrived, gate, name):
        return run(
            add_kernel, shape((part, width)), own_part, arrived, *gate,
            far=range(2, 2 + len(gate)), cost=0.3, name=name,
        )

    sum_high = add(high, arrived_high, grads[1:], "add_high")
    cot_rows, keep, sent = run(
        functools.partial(chip_sum_kernel, count=blocks // 2, order=halving_order(share)),
        [
            shape((row_share, width)), shape((rows // 2, width), F32), shape((rows // 2, width)),
        ],
        *grads, first_arrived, far=(blocks // 2,), cost=0.2, name="chip_sum",
    )
    bit, kept_rows = 1, rows // 2
    while kept_rows > 2 * row_share:
        kept_rows //= 2
        keep, sent = run(
            grad_halve_kernel, [shape((kept_rows, width), F32), shape((kept_rows, width))],
            keep, swap(sent, "expert", bit), cost=0.2, name="grad_halve",
        )
        bit *= 2
    joined = run(
        grad_join_kernel, shape((3 * row_share, width)),
        keep, swap(sent, "expert", bit), cot_rows, cost=0.2, name="grad_join",
    )
    other = swap(joined, "expert", share // 2)
    sums = [add(low, arrived_low, [other], "add_low"), sum_high]
    others = [swap(value, "expert", step) for value in sums][::-1]
    vision_grad = run(
        functools.partial(norm_grad_kernel, features=share * features),
        shape((2 * row_share, width + 128)),
        joined, other, block_rows, gain_row, gain_total, cost=0.3, name="norm_grad",
    )
    vision_grads, bit = {0: vision_grad}, share // 4
    while bit:
        vision_grads.update({k + bit: swap(vision_grads[k], "expert", bit) for k in list(vision_grads)})
        bit //= 2
    bases = sorted(vision_grads)
    vision_grads = [vision_grads[k] for k in bases]
    attn_grad = run(
        functools.partial(merge_grad_kernel, size=size, bases=tuple(bases)),
        shape((depth, patches), F32),
        merge_gain, merged, block_rows, weight_flat, *vision_grads, cost=4.0, name="merge_grad",
    )

    laid = {}
    for turn, value, other, gate in zip((0, step), sums, others, ([other], vision_grads[1:])):
        laid[turn] = run(
            functools.partial(finish_kernel, blocks=blocks, turn=turn), shape((part, width)),
            placed, text, value, other, *vision, *gate,
            far=range(4 + blocks, 4 + blocks + len(gate)), cost=1.0, name="finish",
        )
    while step > 1:
        step //= 2
        laid.update({k + step: swap(laid[k], "expert", step) for k in list(laid)})
    llm_out = run(
        lay_kernel, shape((tokens, width)), *[laid[k] for k in sorted(laid)], cost=1.0, name="lay"
    )
    return llm_out, attn_grad.reshape(heads, size, patches)


def solution(mesh):
    return jax.shard_map(
        body,
        mesh=mesh,
        in_specs=(
            P("expert", None, "blk"),
            P("expert", None, "blk"),
            P("expert", None, "blk"),
            P("blk"),
            P("blk", None),
            P("expert", None),
            P("expert", None, None),
            P("blk", None),
            P(),
            P("blk", "expert", None),
            P("blk", "expert", None),
            P("blk", "expert", None),
            P("blk", None),
            P("blk", None),
            P("blk", None),
        ),
        out_specs=(P("blk", None), P("expert", None, "blk")),
        check_vma=False,
    )
```

```python
import functools

import jax
import jax.numpy as jnp
from jax import lax
from jax.experimental import pallas as pl
from jax.experimental.pallas import tpu as pltpu
from jax.sharding import PartitionSpec as P

CAPX = 10
SLOTS = 12
SEND = 24
EPS = 1e-06
VMEM_BYTES = 16 * 1024 * 1024
PACK_BYTES = 60 * 1024 * 1024
F32 = jnp.float32
BF16 = jnp.bfloat16


def iota(shape, dim):
    return lax.broadcasted_iota(jnp.int32, shape, dim)


def dot(a, b):
    return jnp.dot(a.astype(BF16), b.astype(BF16), preferred_element_type=F32)


def dot_nt(a, b):
    return lax.dot_general(a, b, (((1,), (1,)), ((), ())), preferred_element_type=F32)


def dot_tn(a, b):
    return lax.dot_general(a, b, (((0,), (0,)), ((), ())), preferred_element_type=F32)


def three(value):
    first = value.astype(BF16).astype(F32)
    second = (value - first).astype(BF16).astype(F32)
    return first, second, value - first - second


def put_scalars(columns, rows):
    lane = iota((rows, 128), 1)
    out = jnp.zeros((rows, 128), F32)
    place = 0
    for column in columns:
        for piece in three(column):
            out = jnp.where(lane == place, piece, out)
            place += 1
    return out


def get_scalar(block, which):
    lane = iota(block.shape, 1)
    return jnp.sum(jnp.where(lane // 3 == which, block, 0.0), axis=1, keepdims=True)


def bring(far_refs, near_refs, sems):
    copies = [
        pltpu.make_async_copy(far, near, sems.at[i])
        for i, (far, near) in enumerate(zip(far_refs, near_refs))
    ]
    for copy in copies:
        copy.start()
    return copies


def pack_kernel(*refs):
    far_refs, out_ref, near_refs, sems = refs[:5], refs[5], refs[6:11], refs[11]
    for copy in bring(far_refs, near_refs, sems):
        copy.wait()
    out_ref[...] = packed(*near_refs).astype(BF16)


def packed(keys_ref, values_ref, images_ref, placement_ref, routes_ref):
    rows = images_ref.shape[1]
    patches = keys_ref.shape[1]
    repeat = (iota((rows, patches), 0) == iota((rows, patches), 1) // 4).astype(F32)
    keep = (iota((rows, patches), 0) == iota((rows, patches), 1)).astype(F32)
    patch_ids = dot(images_ref[...].astype(F32), repeat)
    dest = dot(placement_ref[...].astype(F32), keep)
    line = iota((8, patches), 0)
    rest = jnp.where(line == 0, patch_ids, jnp.where(line == 1, dest, 0.0))
    parts = [keys_ref[...], values_ref[...], routes_ref[...], rest]
    return jnp.concatenate([part.astype(F32) for part in parts], axis=0)


def route_kernel(routes_ref, gates_ref, comb_ref, pick_ref, factor_ref, *, groups, share):
    blocks = comb_ref.shape[1] // SLOTS
    tokens = routes_ref.shape[1]
    me, expert_index = lax.axis_index("blk"), lax.axis_index("expert")
    member = expert_index // groups
    before = (iota((tokens, tokens), 0) < iota((tokens, tokens), 1)).astype(BF16)
    pair_of = 2 * (iota((blocks, tokens), 0) ^ me) + member
    out_hit = jnp.zeros((blocks, tokens), F32)
    out_gate = jnp.zeros((blocks, tokens), F32)
    for k in range(routes_ref.shape[0]):
        same = pair_of == routes_ref[k : k + 1, :]
        out_hit = out_hit + same.astype(F32)
        out_gate = out_gate + jnp.where(same, gates_ref[k : k + 1, :], 0.0)
    out_rank = dot(out_hit, before)

    def expand(stride):
        count = blocks * stride
        pick = (iota((count, blocks), 0) // stride == iota((count, blocks), 1)).astype(BF16)
        gate = sum(dot(pick, piece) for piece in three(out_gate))
        return dot(pick, out_hit), dot(pick, out_rank).astype(jnp.int32), gate

    hits, ranks, gates = expand(SLOTS)
    live = jnp.where(ranks == iota(hits.shape, 0) % SLOTS, hits, 0.0)
    weight = live * gates
    high = weight.astype(BF16).astype(F32)
    part = tokens // share
    col = iota((tokens, tokens), 1)
    turned = (col // part * 0).astype(jnp.int32)
    for place, k in enumerate(halving_order(share)):
        turned = jnp.where(col // part == place, k, turned)
    turned = (iota((tokens, tokens), 0) == (turned ^ expert_index) * part + col % part)
    turned = turned.astype(F32)
    comb_ref[0] = dot(high, turned).astype(BF16)
    comb_ref[1] = dot(weight - high, turned).astype(BF16)

    hits, ranks, gates = expand(SEND)
    place = iota(hits.shape, 0) % SEND
    input_pick = jnp.where((place < CAPX) & (ranks == place), hits, 0.0)
    back_pick = jnp.where((place >= CAPX) & (place < 2 * CAPX) & (ranks == place - CAPX), hits, 0.0)
    pick_ref[0] = input_pick.astype(BF16)
    pick_ref[1] = back_pick.astype(BF16)
    factor = jnp.sum(back_pick * gates, axis=1, keepdims=True)
    factor_ref[...] = jnp.broadcast_to(factor, factor_ref.shape)


def dispatch_kernel(pick_ref, factor_ref, text_ref, gain_ref, cot_ref, *send_refs):
    text = text_ref[...].astype(F32)
    scale = lax.rsqrt(jnp.mean(text * text, axis=1, keepdims=True) + EPS)
    h_rows = (text * scale * gain_ref[...]).astype(BF16)
    factor = factor_ref[:, :1]
    send = dot(pick_ref[0], h_rows) + factor * dot(pick_ref[1], cot_ref[...])
    send = send.astype(BF16)
    count = 2 * SEND
    for k, ref in enumerate(send_refs):
        ref[...] = send[k * count : (k + 1) * count]


def plan_kernel(
    meta_ref, cot_ref, slots_ref, placed_ref, back_ref, *, blocks, groups, merged_rows, row_share
):
    tokens = cot_ref.shape[0]
    rows = blocks * merged_rows
    me, expert_index = lax.axis_index("blk"), lax.axis_index("expert")
    member = expert_index // groups
    meta = [meta_ref[k * 16 : (k + 1) * 16].astype(F32) for k in range(blocks)]
    mine = (2 * me + member).astype(F32)
    hits = [jnp.sum((part[:8] == mine).astype(F32), axis=0, keepdims=True) for part in meta]
    hit = jnp.concatenate(hits, axis=0)
    dest = jnp.concatenate([part[9:10] for part in meta], axis=0)
    before = (iota((tokens, tokens), 0) < iota((tokens, tokens), 1)).astype(BF16)
    rank = dot(hit, before)

    def row_of(col):
        inner = col % merged_rows
        return ((inner // row_share) ^ expert_index) * row_share + inner % row_share

    def place_of(col):
        return ((col // merged_rows) ^ me) * merged_rows + row_of(col)

    spread = (iota((128, rows), 0) == row_of(iota((128, rows), 1))).astype(F32)
    own_block = iota((blocks, rows), 1) // merged_rows == iota((blocks, rows), 0)
    dest_row = jnp.sum(jnp.where(own_block, dot(dest, spread), 0.0), axis=0, keepdims=True)
    dest_row = dest_row.astype(jnp.int32) ^ me
    dest_hit = (iota((blocks, rows), 0) == dest_row).astype(F32)
    rows_before = place_of(iota((rows, rows), 0)) < place_of(iota((rows, rows), 1))
    earlier = dot(dest_hit, rows_before.astype(F32))
    slot = jnp.sum(dest_hit * earlier, axis=0, keepdims=True).astype(jnp.int32)
    at_token = (iota((tokens, rows), 0) == slot).astype(F32)
    row_hit = jnp.sum(dest_hit * dot(hit, at_token), axis=0, keepdims=True)
    row_rank = jnp.sum(dest_hit * dot(rank, at_token), axis=0, keepdims=True).astype(jnp.int32)
    slot_id = dest_row * SLOTS + row_rank
    slot_count = slots_ref.shape[0]
    chosen = (iota((slot_count, rows), 0) == slot_id) & (row_hit > 0.5)
    slots_ref[...] = chosen.astype(F32).astype(BF16)
    placed = jnp.where(dest_row == 0, at_token, 0.0).astype(BF16)
    placed_ref[...] = placed
    back_rows = blocks * row_share
    source = iota((back_rows, rows), 0)
    wanted = source // row_share * merged_rows + source % row_share
    row_pick = (iota((back_rows, rows), 1) == wanted).astype(F32).astype(BF16)
    back_ref[...] = dot(dot_nt(row_pick, placed), cot_ref[...]).astype(BF16)


def flat_gain(gain_ref):
    return jnp.concatenate([gain_ref[h : h + 1] for h in range(gain_ref.shape[0])], axis=1)


def attend_kernel(*refs, blocks, row_share):
    query_ref, gain_ref = refs[:2]
    near_refs = refs[7 : 6 + blocks]
    merged_ref, meta_ref, left_ref, scalar_ref = refs[6 + blocks :]
    heads, size, patches = query_ref.shape
    rows, features = merged_ref.shape
    depth = heads * size
    near = [packed(*refs[2:7])] + [ref[...].astype(F32) for ref in near_refs]
    meta_ref[...] = jnp.concatenate([part[2 * depth :] for part in near], axis=0).astype(BF16)
    key_ids = jnp.concatenate([part[2 * depth + 8 : 2 * depth + 9] for part in near], axis=1)
    eye = iota((patches, patches), 0) == iota((patches, patches), 1)
    own_ids = jnp.sum(jnp.where(eye, key_ids[:, :patches], 0.0), axis=1, keepdims=True)
    same = own_ids == key_ids
    spread = jnp.zeros((patches, features), F32)
    place_row, place_col = iota((size, features), 0), iota((size, features), 1)
    for head in range(heads):
        first = head * size
        keys = jnp.concatenate([part[first : first + size] for part in near], axis=1)
        first = depth + head * size
        values = jnp.concatenate([part[first : first + size] for part in near], axis=1)
        query = query_ref[head].astype(F32).T.astype(BF16)
        scores = dot(query, keys) * (size**-0.5)
        scores = jnp.where(same, scores, -1e30)
        weights = jnp.exp(scores - jnp.max(scores, axis=1, keepdims=True))
        total = jnp.sum(weights, axis=1, keepdims=True)
        attn = dot_nt(weights.astype(BF16), values.astype(BF16)) / total
        place = (place_col % size == place_row) & (place_col // (4 * size) == head)
        spread = spread + dot(attn, place.astype(F32))
    spot = iota((patches, features), 1) // size % 4 == iota((patches, features), 0) % 4
    line = iota((rows, patches), 0)
    line = ((line // row_share) ^ lax.axis_index("expert")) * row_share + line % row_share
    fold = (iota((rows, patches), 1) // 4 == line).astype(F32)
    merged = dot(fold, jnp.where(spot, spread, 0.0))
    merged_ref[...] = merged.astype(BF16)
    local_mean = jnp.sum(merged, axis=1, keepdims=True) / features
    centered = merged - local_mean
    squares = jnp.sum(centered * centered, axis=1, keepdims=True)
    gain = flat_gain(gain_ref)
    gain_high = gain.astype(BF16).astype(F32)
    extra = iota((16, features), 0)
    gain_rows = jnp.where(extra == 0, gain_high, jnp.where(extra == 1, gain - gain_high, 0.0))
    left_ref[...] = jnp.concatenate([centered * gain, gain_rows], axis=0).astype(BF16)
    scalar_ref[...] = put_scalars([local_mean, squares], rows)


def project_kernel(left_ref, scalar_ref, weight_ref, _, *message_refs):
    rows = scalar_ref.shape[0]
    width = weight_ref.shape[1]
    row_share = rows // len(message_refs)
    product = dot(left_ref[...], weight_ref[...])
    gain_sum = product[rows : rows + 1] + product[rows + 1 : rows + 2]
    piece = width // row_share
    pieces = [gain_sum[:, j * piece : (j + 1) * piece] for j in range(row_share)]
    pieces = jnp.concatenate(pieces, axis=0).astype(BF16)
    scalars = scalar_ref[...].astype(BF16)
    for k, message_ref in enumerate(message_refs):
        mine = slice(k * row_share, (k + 1) * row_share)
        message_ref[:, :width] = product[mine].astype(BF16)
        message_ref[:, width : width + piece] = pieces
        message_ref[:, width + piece :] = scalars[mine]


def merge_kernel(_, *refs, width, features):
    *message_refs, out_ref, gain_ref = refs
    share, row_share = len(message_refs), out_ref.shape[0]
    piece = width // row_share
    parts = [ref[...].astype(F32) for ref in message_refs]
    scalars = [part[:, width + piece :] for part in parts]
    means = [get_scalar(block, 0) for block in scalars]
    squares = [get_scalar(block, 1) for block in scalars]
    mean = sum(means) / share
    spread = sum(q + features * (m - mean) * (m - mean) for q, m in zip(squares, means))
    inv_std = lax.rsqrt(spread / (share * features) + EPS)
    total = jnp.zeros((row_share, width), F32)
    gain_total = jnp.zeros((1, width), F32)
    for part, local in zip(parts, means):
        tail = part[:, width : width + piece]
        gain_sum = jnp.concatenate([tail[j : j + 1] for j in range(row_share)], axis=1)
        total = total + part[:, :width] + (local - mean) * gain_sum
        gain_total = gain_total + gain_sum
    gain_ref[...] = gain_total
    out_ref[:, :width] = (total * inv_std).astype(BF16)
    out_ref[:, width:] = put_scalars([mean, inv_std], row_share).astype(BF16)


def stack_kernel(*refs):
    *part_refs, out_ref = refs
    out_ref[...] = stacked(part_refs)


def stacked(part_refs):
    return jnp.concatenate([ref[...].astype(F32) for ref in part_refs], axis=0).astype(BF16)


def by_chip(own_refs, sibling_ref):
    parts = []
    sibling = sibling_ref[...].astype(F32)
    for k, own_ref in enumerate(own_refs):
        half = own_ref.shape[0] // 2
        parts.append(own_ref[...].astype(F32)[:half])
        parts.append(sibling[k * half : (k + 1) * half])
    return jnp.concatenate(parts, axis=0).astype(BF16)


def other_half_kernel(*refs, count):
    out_ref = refs[-1]
    parts = [ref[...].astype(F32)[ref.shape[0] // 2 :] for ref in refs[:count]]
    out_ref[...] = jnp.concatenate(parts, axis=0).astype(BF16)


def slot_pick(slot_count, send_rows, shift):
    row, col = iota((slot_count, send_rows), 0), iota((slot_count, send_rows), 1)
    place = row % SLOTS
    pick = (col == row // SLOTS * SEND + place + shift) & (place < CAPX)
    return pick.astype(F32)


def early_kernel(down_ref, *refs):
    *early_refs, sibling_ref, text_out, grad_out = refs
    slot_count = text_out.shape[0]
    early = by_chip(early_refs, sibling_ref)
    text_out[...] = dot(slot_pick(slot_count, early.shape[0], 0), early).astype(BF16)
    back_rows = dot(slot_pick(slot_count, early.shape[0], CAPX), early).astype(BF16)
    grad_out[...] = dot_nt(back_rows, down_ref[0])


def forward_kernel(*refs, blocks):
    slots_ref, gain_ref, gate_ref, up_ref, down_ref, text_ref = refs[:6]
    vision_refs = refs[6 : 6 + blocks]
    gate_out, up_out, *down_refs = refs[6 + blocks : -2]
    h_ref, sum_ref = refs[-2:]
    _, hidden, width = gate_ref.shape
    chosen = slots_ref[...]
    is_vision = jnp.sum(chosen.astype(F32), axis=1, keepdims=True) > 0.5
    vision = jnp.concatenate([ref[:, :width] for ref in vision_refs], axis=0)
    inputs = dot(chosen, vision)
    scale = lax.rsqrt(jnp.mean(inputs * inputs, axis=1, keepdims=True) + EPS)
    normed = inputs * scale * gain_ref[...]
    h_ref[...] = jnp.where(is_vision, normed, text_ref[...].astype(F32)).astype(BF16)
    tile = tile_of(hidden)
    for i in range(hidden // tile):
        mine = slice(i * tile, (i + 1) * tile)
        gate_pre = dot_nt(h_ref[...], gate_ref[0, mine])
        up_proj = dot_nt(h_ref[...], up_ref[0, mine])
        gate_out[:, mine] = gate_pre
        up_out[:, mine] = up_proj
        activated = gate_pre * jax.nn.sigmoid(gate_pre) * up_proj
        product = dot(activated, down_ref[0, mine])
        sum_ref[...] = product if i == 0 else sum_ref[...] + product
    count = 2 * SLOTS
    for k, ref in enumerate(down_refs):
        ref[...] = sum_ref[k * count : (k + 1) * count].astype(BF16)


def backward_kernel(
    slots_ref, grad_ref, gate_in, up_in, cot_ref, gate_ref, up_ref, even_ref, odd_ref, sum_ref,
    *, blocks,
):
    hidden = gate_ref.shape[1]
    tile = tile_of(hidden)
    for i in range(hidden // tile):
        mine = slice(i * tile, (i + 1) * tile)
        act_grad = grad_ref[:, mine]
        gate_pre, up_proj = gate_in[:, mine], up_in[:, mine]
        sigmoid = jax.nn.sigmoid(gate_pre)
        gate_grad = act_grad * up_proj * sigmoid * (1.0 + gate_pre * (1.0 - sigmoid))
        up_grad = act_grad * gate_pre * sigmoid
        product = dot(gate_grad, gate_ref[0, mine]) + dot(up_grad, up_ref[0, mine])
        sum_ref[...] = product if i == 0 else sum_ref[...] + product
    grads = dot_tn(slots_ref[...], sum_ref[...].astype(BF16))
    cots = cot_ref[...].astype(F32)
    rows, row_share = grads.shape[0] // blocks, cots.shape[0] // blocks
    parts = ([], [])
    for k in range(blocks):
        parts[k % 2].append(grads[k * rows : (k + 1) * rows])
        parts[k % 2].append(cots[k * row_share : (k + 1) * row_share])
    even_ref[...] = jnp.concatenate(parts[0], axis=0).astype(BF16)
    odd_ref[...] = jnp.concatenate(parts[1], axis=0).astype(BF16)


def tile_of(hidden):
    return 256 if hidden % 256 == 0 else hidden


def halving_order(share):
    order = [0]
    step = share // 2
    while step:
        order = order + [k + step for k in order]
        step //= 2
    return [sum(1 << j for j in range(share.bit_length() - 1) if k >> j & 1) for k in order]


def pair_sum_kernel(own_ref, sibling_ref, *out_refs):
    rows = out_refs[0].shape[0]
    total = own_ref[...].astype(F32) + sibling_ref[...].astype(F32)
    for k, out_ref in enumerate(out_refs):
        out_ref[...] = total[k * rows : (k + 1) * rows].astype(BF16)


def total_of(part_refs):
    total = part_refs[0][...].astype(F32)
    for ref in part_refs[1:]:
        total = total + ref[...].astype(F32)
    return total


def chip_sum_kernel(*refs, count, order):
    cot_ref, keep_ref, send_ref = refs[count + 1 :]
    total = total_of(refs[:count])
    rows = cot_ref.shape[0]
    turned = jnp.concatenate([total[k * rows : (k + 1) * rows] for k in order], axis=0)
    half = turned.shape[0] // 2
    keep_ref[...] = turned[:half]
    send_ref[...] = turned[half:].astype(BF16)
    cot_ref[...] = total[len(order) * rows :].astype(BF16)


def grad_halve_kernel(keep_ref, arrived_ref, *refs):
    quarters(keep_ref[...] + arrived_ref[...].astype(F32), refs)


def grad_join_kernel(keep_ref, arrived_ref, cot_ref, out_ref):
    total = keep_ref[...] + arrived_ref[...].astype(F32)
    out_ref[...] = jnp.concatenate([total, cot_ref[...].astype(F32)], axis=0).astype(BF16)


def quarters(total, out_refs):
    count = out_refs[0].shape[0]
    for k, ref in enumerate(out_refs):
        ref[...] = total[k * count : (k + 1) * count].astype(ref.dtype)


def combine_kernel(comb_ref, *refs):
    *part_refs, sibling_ref = refs[:-4]
    rows = by_chip(part_refs, sibling_ref)
    quarters(dot_tn(comb_ref[0], rows) + dot_tn(comb_ref[1], rows), refs[-4:])


def halve_kernel(*refs):
    low, high, arrived_low, arrived_high = [ref[...].astype(F32) for ref in refs[:4]]
    quarters(jnp.concatenate([low + arrived_low, high + arrived_high], axis=0), refs[4:])


def add_kernel(own_ref, arrived_ref, *refs):
    refs[-1][...] = (own_ref[...] + arrived_ref[...].astype(F32)).astype(BF16)


def finish_kernel(placed_ref, text_ref, own_ref, arrived_ref, *refs, blocks, turn):
    vision_refs, out_ref = refs[:blocks], refs[-1]
    count, width = out_ref.shape
    tokens = placed_ref.shape[0]
    first = (lax.axis_index("expert") ^ turn) * count
    pick = iota((count, tokens), 1) == iota((count, tokens), 0) + first
    pick = pick.astype(F32)
    placed = dot(pick, placed_ref[...])
    is_vision = jnp.sum(placed, axis=1, keepdims=True) > 0.5
    vision = jnp.concatenate([ref[:, :width] for ref in vision_refs], axis=0)
    inputs = jnp.where(is_vision, dot(placed, vision), dot(pick, text_ref[...]))
    out_ref[...] = (inputs + (own_ref[...].astype(F32) + arrived_ref[...].astype(F32))).astype(BF16)


def lay_kernel(*refs):
    *part_refs, out_ref = refs
    count = part_refs[0].shape[0]
    for k, ref in enumerate(part_refs):
        first = pl.multiple_of((lax.axis_index("expert") ^ k) * count, count)
        out_ref[pl.ds(first, count), :] = ref[...]


def norm_grad_kernel(
    joined_ref, other_ref, rows_ref, gain_ref, total_ref, out_ref, *, features
):
    width = gain_ref.shape[1]
    count = out_ref.shape[0] // 2
    far = rows_ref.shape[0] // 2
    joined, other = joined_ref[...].astype(F32), other_ref[...].astype(F32)
    turned = jnp.concatenate([other[count : 2 * count], other[:count]], axis=0)
    hidden = joined[: 2 * count] + turned
    cotangent = jnp.concatenate([joined[2 * count :], other[2 * count :]], axis=0)
    rows = rows_ref[:, :width].astype(F32)
    inputs = jnp.concatenate([rows[:count], rows[far : far + count]], axis=0)
    scale = lax.rsqrt(jnp.mean(inputs * inputs, axis=1, keepdims=True) + EPS)
    pulled = hidden * gain_ref[...]
    cross = jnp.mean(pulled * inputs, axis=1, keepdims=True)
    grad = cotangent + scale * pulled - inputs * (scale * scale * scale) * cross
    grad = grad.astype(BF16)
    out_ref[:, :width] = grad
    grad = grad.astype(F32)
    grad_mean = jnp.sum(grad * total_ref[...], axis=1, keepdims=True) / features
    cross_mean = jnp.sum(grad * inputs, axis=1, keepdims=True) / features
    out_ref[:, width:] = put_scalars([grad_mean, cross_mean], 2 * count).astype(BF16)


def merge_grad_kernel(*refs, size, bases):
    gain_ref, merged_ref, scalar_ref, weight_ref, *part_refs, out_ref = refs
    rows, features = merged_ref.shape
    width = weight_ref.shape[1]
    depth, patches = out_ref.shape
    row_share = part_refs[0].shape[0] // 2
    blocks = {}
    for base, ref in zip(bases, part_refs):
        part = ref[...].astype(F32)
        blocks[base] = part[:row_share]
        blocks[base ^ len(bases)] = part[row_share:]
    parts = jnp.concatenate([blocks[k] for k in sorted(blocks)], axis=0).astype(BF16)
    normed_grad = dot_nt(parts[:, :width], weight_ref[...]) * flat_gain(gain_ref)
    means = parts[:, width:].astype(F32)
    scalars = scalar_ref[:, width:].astype(F32)
    inv_std = get_scalar(scalars, 1)
    normed = (merged_ref[...].astype(F32) - get_scalar(scalars, 0)) * inv_std
    grad = inv_std * (normed_grad - get_scalar(means, 0) - normed * get_scalar(means, 1))
    high = grad.astype(BF16)
    low = (grad - high.astype(F32)).astype(BF16)
    line = iota((patches, rows), 1)
    line = ((line // row_share) ^ lax.axis_index("expert")) * row_share + line % row_share
    unfold = (iota((patches, rows), 0) // 4 == line).astype(F32)
    spot = iota((patches, features), 1) // size % 4 == iota((patches, features), 0) % 4
    row, col = iota((depth, features), 0), iota((depth, features), 1)
    place = (col // (4 * size) == row // size) & (col % size == row % size)
    place = place.astype(F32).astype(BF16)
    out = jnp.zeros((depth, patches), F32)
    for piece in (high, low):
        wide = jnp.where(spot, dot(unfold, piece), 0.0).astype(BF16)
        out = out + dot_nt(place, wide)
    out_ref[...] = out


def whole(memory_space=pltpu.VMEM):
    return pl.BlockSpec(memory_space=memory_space)


def run(kernel, outs, *args, far=(), scratch=(), cost=1.0, vmem=VMEM_BYTES, name=None):
    specs = [whole()] * len(args)
    for place in far:
        specs[place] = whole(pl.ANY)
    return pl.pallas_call(
        kernel,
        out_shape=outs,
        in_specs=specs,
        out_specs=jax.tree.map(lambda _: whole(), outs),
        scratch_shapes=scratch,
        compiler_params=pltpu.CompilerParams(vmem_limit_bytes=vmem),
        cost_estimate=microseconds(cost),
        name=name,
    )(*args)


def to_sibling(parts, deps, name):
    rows, width = parts[0].shape
    half = run(
        functools.partial(other_half_kernel, count=len(parts)),
        shape((len(parts) * rows // 2, width)), *parts, *deps,
        far=range(len(parts), len(parts) + len(deps)), cost=0.01, name=name,
    )
    return swap(half, "blk", 1)


def microseconds(time):
    return pl.CostEstimate(flops=0, transcendentals=0, bytes_accessed=int(time * 3e6))


def after(values, deps):
    count = len(values)
    return pl.pallas_call(
        lambda *refs: None,
        out_shape=[shape(value.shape, value.dtype) for value in values],
        in_specs=[whole(pl.ANY)] * (count + len(deps)),
        out_specs=[whole(pl.ANY)] * count,
        input_output_aliases={i: i for i in range(count)},
        compiler_params=pltpu.CompilerParams(vmem_limit_bytes=VMEM_BYTES),
        cost_estimate=microseconds(0.1),
        name="after",
    )(*values, *deps)


def shape(dims, dtype=BF16):
    return jax.ShapeDtypeStruct(dims, dtype)


def swap(value, axis, step):
    count = lax.axis_size(axis)
    return lax.ppermute(value, axis, [(i, i ^ step) for i in range(count)])


def trade(parts, axis):
    return [parts[0]] + [swap(parts[k], axis, k) for k in range(1, len(parts))]


def spread_out(value, axis):
    return trade([value] * lax.axis_size(axis), axis)


def gather_blocks(value, deps=None):
    own = [value] + [swap(value, "blk", k) for k in range(2, lax.axis_size("blk"), 2)]
    if deps is not None:
        own = own[:1] + list(after(own[1:], deps))
    sibling = [swap(part, "blk", 1) for part in own]
    return [part for pair in zip(own, sibling) for part in pair]


def to_chips(parts):
    return [parts[0]] + [swap(parts[k], "blk", 2 * k) for k in range(1, len(parts))]


def body(
    queries, keys, values, image_ids, placement, merge_gain, merge_weight, text, norm_gain,
    w_gate, w_up, w_down, routes, route_gates, cotangent,
):
    blocks = lax.axis_size("blk")
    share = lax.axis_size("expert")
    heads, size, patches = queries.shape
    depth = heads * size
    rows = image_ids.shape[0]
    row_share = rows // share
    tokens, width = text.shape
    part = tokens // share
    all_rows = blocks * rows
    features = heads * 4 * size
    hidden = w_gate.shape[1]
    slot_count = blocks * SLOTS
    groups = share // 2
    routes_t, gates_t, gain_row = routes.T, route_gates.T, norm_gain[None]

    small = [
        keys.reshape(depth, patches), values.reshape(depth, patches),
        image_ids[None], placement.reshape(1, rows), routes_t,
    ]
    local = run(
        pack_kernel, shape((2 * depth + 16, patches)), *small, far=range(5),
        scratch=[pltpu.VMEM(array.shape, array.dtype) for array in small]
        + [pltpu.SemaphoreType.DMA((5,))],
        vmem=PACK_BYTES, name="pack",
    )
    comb, pick, factor = run(
        functools.partial(route_kernel, groups=groups, share=share),
        [
            shape((2, slot_count, tokens)), shape((2, blocks * SEND, tokens)),
            shape((blocks * SEND, 128), F32),
        ],
        routes_t, gates_t, cost=3.0, name="route",
    )
    send = run(
        dispatch_kernel, [shape((2 * SEND, width))] * (blocks // 2),
        pick, factor, text, gain_row, cotangent, cost=2.0, name="dispatch",
    )
    near = gather_blocks(local, send)
    early = to_chips(after(send, near[2::2]))

    weight_flat = merge_weight.reshape(features, width)
    message_width = width + width // row_share + 128
    merged, meta, left, local_scalars = run(
        functools.partial(attend_kernel, blocks=blocks, row_share=row_share),
        [
            shape((rows, features)), shape((blocks * 16, patches)), shape((rows + 16, features)),
            shape((rows, 128), F32),
        ],
        queries, merge_gain, *small, *near[1:], cost=3.0, name="attend",
    )
    message = run(
        project_kernel, [shape((row_share, message_width))] * share,
        left, local_scalars, weight_flat, early[1], far=(3,), cost=2.0, name="project",
    )
    slots, placed, back_cots = run(
        functools.partial(
            plan_kernel, blocks=blocks, groups=groups, merged_rows=rows, row_share=row_share
        ),
        [
            shape((slot_count, all_rows)), shape((tokens, all_rows)),
            shape((blocks * row_share, width)),
        ],
        meta, cotangent, cost=1.5, name="plan",
    )
    message = trade(message, "expert")
    early = early[:1] + list(after(early[1:], message[1:]))
    own, gain_total = run(
        functools.partial(merge_kernel, width=width, features=features),
        [
            shape((row_share, width + 128)), shape((1, width), F32),
        ],
        early[1], *message, far=(0,), cost=0.2, name="merge",
    )
    owns = spread_out(own, "expert")
    block_rows = run(
        stack_kernel, shape((rows, width + 128)), *owns, cost=0.2, name="stack",
    )
    text_rows, act_grad = run(
        early_kernel, [shape((slot_count, width)), shape((slot_count, hidden), F32)],
        w_down, *early, to_sibling(early, owns[1:], "early_half"), cost=3.0, name="early",
    )

    vision = gather_blocks(block_rows, [text_rows, slots])
    gate_pre, up_proj, *down = run(
        functools.partial(forward_kernel, blocks=blocks),
        [
            shape((slot_count, hidden), F32), shape((slot_count, hidden), F32),
        ] + [shape((2 * SLOTS, width))] * (blocks // 2),
        slots, gain_row, w_gate, w_up, w_down, text_rows, *vision,
        scratch=[pltpu.VMEM((slot_count, width), BF16), pltpu.VMEM((slot_count, width), F32)],
        cost=4.0, name="forward",
    )
    returned = to_chips(down)
    block = rows + row_share
    even, odd = run(
        functools.partial(backward_kernel, blocks=blocks),
        [shape((blocks // 2 * block, width))] * 2,
        slots, act_grad, gate_pre, up_proj, back_cots, w_gate, w_up,
        scratch=[pltpu.VMEM((slot_count, width), F32)],
        cost=4.0, name="backward",
    )
    grads = run(
        pair_sum_kernel, [shape((block, width))] * (blocks // 2), even, swap(odd, "blk", 1),
        cost=0.2, name="pair_sum",
    )
    grads = to_chips(grads)
    count = tokens // 4
    pieces = [shape((count, width), F32)] * 2 + [shape((count, width))] * 2
    low, high, sent_low, sent_high = run(
        combine_kernel, pieces, comb, *returned,
        to_sibling(returned, grads[:1], "returned_half"), cost=0.01, name="combine",
    )
    step = 1
    arrived_high = swap(sent_high, "expert", step)
    first_arrived = arrived_high
    arrived_low = swap(sent_low, "expert", step)
    while count > part:
        count //= 2
        step *= 2
        pieces = [shape((count, width), F32)] * 2 + [shape((count, width))] * 2
        low, high, sent_low, sent_high = run(
            halve_kernel, pieces, low, high, arrived_low, arrived_high, cost=0.3, name="halve"
        )
        arrived_high = swap(sent_high, "expert", step)
        arrived_low = swap(sent_low, "expert", step)
    step *= 2

    def add(own_part, arrived, gate, name):
        return run(
            add_kernel, shape((part, width)), own_part, arrived, *gate,
            far=range(2, 2 + len(gate)), cost=0.3, name=name,
        )

    sum_high = add(high, arrived_high, [], "add_high")
    other_low = swap(sum_high, "expert", step)
    cot_rows, keep, sent = run(
        functools.partial(chip_sum_kernel, count=blocks // 2, order=halving_order(share)),
        [
            shape((row_share, width)), shape((rows // 2, width), F32), shape((rows // 2, width)),
        ],
        *grads, first_arrived, far=(blocks // 2,), cost=0.2, name="chip_sum",
    )
    bit, kept_rows = 1, rows // 2
    while kept_rows > 2 * row_share:
        kept_rows //= 2
        keep, sent = run(
            grad_halve_kernel, [shape((kept_rows, width), F32), shape((kept_rows, width))],
            keep, swap(sent, "expert", bit), cost=0.2, name="grad_halve",
        )
        bit *= 2
    joined = run(
        grad_join_kernel, shape((3 * row_share, width)),
        keep, swap(sent, "expert", bit), cot_rows, cost=0.2, name="grad_join",
    )
    other = swap(joined, "expert", share // 2)
    sums = [add(low, arrived_low, [other_low], "add_low"), sum_high]
    others = [other_low, swap(sums[0], "expert", step)]
    vision_grad = run(
        functools.partial(norm_grad_kernel, features=share * features),
        shape((2 * row_share, width + 128)),
        joined, other, block_rows, gain_row, gain_total, cost=0.3, name="norm_grad",
    )
    vision_grads, bit = {0: vision_grad}, share // 4
    while bit:
        vision_grads.update({k + bit: swap(vision_grads[k], "expert", bit) for k in list(vision_grads)})
        bit //= 2
    bases = sorted(vision_grads)
    vision_grads = [vision_grads[k] for k in bases]
    attn_grad = run(
        functools.partial(merge_grad_kernel, size=size, bases=tuple(bases)),
        shape((depth, patches), F32),
        merge_gain, merged, block_rows, weight_flat, *vision_grads, cost=4.0, name="merge_grad",
    )

    laid = {}
    for turn, value, other, gate in zip((0, step), sums, others, ([other], vision_grads[1:])):
        laid[turn] = run(
            functools.partial(finish_kernel, blocks=blocks, turn=turn), shape((part, width)),
            placed, text, value, other, *vision, *gate,
            far=range(4 + blocks, 4 + blocks + len(gate)), cost=1.0, name="finish",
        )
    while step > 1:
        step //= 2
        laid.update({k + step: swap(laid[k], "expert", step) for k in list(laid)})
    llm_out = run(
        lay_kernel, shape((tokens, width)), *[laid[k] for k in sorted(laid)], cost=1.0, name="lay"
    )
    return llm_out, attn_grad.reshape(heads, size, patches)


def solution(mesh):
    return jax.shard_map(
        body,
        mesh=mesh,
        in_specs=(
            P("expert", None, "blk"),
            P("expert", None, "blk"),
            P("expert", None, "blk"),
            P("blk"),
            P("blk", None),
            P("expert", None),
            P("expert", None, None),
            P("blk", None),
            P(),
            P("blk", "expert", None),
            P("blk", "expert", None),
            P("blk", "expert", None),
            P("blk", None),
            P("blk", None),
            P("blk", None),
        ),
        out_specs=(P("blk", None), P("expert", None, "blk")),
        check_vma=False,
    )
```

```python
import functools

import jax
import jax.numpy as jnp
from jax import lax
from jax.experimental import pallas as pl
from jax.experimental.pallas import tpu as pltpu
from jax.sharding import PartitionSpec as P

CAPX = 10
SLOTS = 12
SEND = 24
EPS = 1e-06
VMEM_BYTES = 16 * 1024 * 1024
PACK_BYTES = 60 * 1024 * 1024
F32 = jnp.float32
BF16 = jnp.bfloat16


def iota(shape, dim):
    return lax.broadcasted_iota(jnp.int32, shape, dim)


def dot(a, b):
    return jnp.dot(a.astype(BF16), b.astype(BF16), preferred_element_type=F32)


def dot_nt(a, b):
    return lax.dot_general(a, b, (((1,), (1,)), ((), ())), preferred_element_type=F32)


def dot_tn(a, b):
    return lax.dot_general(a, b, (((0,), (0,)), ((), ())), preferred_element_type=F32)


def three(value):
    first = value.astype(BF16).astype(F32)
    second = (value - first).astype(BF16).astype(F32)
    return first, second, value - first - second


def put_scalars(columns, rows):
    lane = iota((rows, 128), 1)
    out = jnp.zeros((rows, 128), F32)
    place = 0
    for column in columns:
        for piece in three(column):
            out = jnp.where(lane == place, piece, out)
            place += 1
    return out


def get_scalar(block, which):
    lane = iota(block.shape, 1)
    return jnp.sum(jnp.where(lane // 3 == which, block, 0.0), axis=1, keepdims=True)


def bring(far_refs, near_refs, sems):
    copies = [
        pltpu.make_async_copy(far, near, sems.at[i])
        for i, (far, near) in enumerate(zip(far_refs, near_refs))
    ]
    for copy in copies:
        copy.start()
    return copies


def pack_kernel(*refs):
    far_refs, out_ref, near_refs, sems = refs[:5], refs[5], refs[6:11], refs[11]
    for copy in bring(far_refs, near_refs, sems):
        copy.wait()
    out_ref[...] = packed(*near_refs).astype(BF16)


def packed(keys_ref, values_ref, images_ref, placement_ref, routes_ref):
    rows = images_ref.shape[1]
    patches = keys_ref.shape[1]
    repeat = (iota((rows, patches), 0) == iota((rows, patches), 1) // 4).astype(F32)
    keep = (iota((rows, patches), 0) == iota((rows, patches), 1)).astype(F32)
    patch_ids = dot(images_ref[...].astype(F32), repeat)
    dest = dot(placement_ref[...].astype(F32), keep)
    line = iota((8, patches), 0)
    rest = jnp.where(line == 0, patch_ids, jnp.where(line == 1, dest, 0.0))
    parts = [keys_ref[...], values_ref[...], routes_ref[...], rest]
    return jnp.concatenate([part.astype(F32) for part in parts], axis=0)


def route_kernel(routes_ref, gates_ref, comb_ref, pick_ref, factor_ref, *, groups, share):
    blocks = comb_ref.shape[1] // SLOTS
    tokens = routes_ref.shape[1]
    me, expert_index = lax.axis_index("blk"), lax.axis_index("expert")
    member = expert_index // groups
    before = (iota((tokens, tokens), 0) < iota((tokens, tokens), 1)).astype(BF16)
    pair_of = 2 * (iota((blocks, tokens), 0) ^ me) + member
    out_hit = jnp.zeros((blocks, tokens), F32)
    out_gate = jnp.zeros((blocks, tokens), F32)
    for k in range(routes_ref.shape[0]):
        same = pair_of == routes_ref[k : k + 1, :]
        out_hit = out_hit + same.astype(F32)
        out_gate = out_gate + jnp.where(same, gates_ref[k : k + 1, :], 0.0)
    out_rank = dot(out_hit, before)

    def expand(stride):
        count = blocks * stride
        pick = (iota((count, blocks), 0) // stride == iota((count, blocks), 1)).astype(BF16)
        gate = sum(dot(pick, piece) for piece in three(out_gate))
        return dot(pick, out_hit), dot(pick, out_rank).astype(jnp.int32), gate

    hits, ranks, gates = expand(SLOTS)
    live = jnp.where(ranks == iota(hits.shape, 0) % SLOTS, hits, 0.0)
    weight = live * gates
    high = weight.astype(BF16).astype(F32)
    part = tokens // share
    col = iota((tokens, tokens), 1)
    turned = (col // part * 0).astype(jnp.int32)
    for place, k in enumerate(halving_order(share)):
        turned = jnp.where(col // part == place, k, turned)
    turned = (iota((tokens, tokens), 0) == (turned ^ expert_index) * part + col % part)
    turned = turned.astype(F32)
    comb_ref[0] = dot(high, turned).astype(BF16)
    comb_ref[1] = dot(weight - high, turned).astype(BF16)

    hits, ranks, gates = expand(SEND)
    place = iota(hits.shape, 0) % SEND
    input_pick = jnp.where((place < CAPX) & (ranks == place), hits, 0.0)
    back_pick = jnp.where((place >= CAPX) & (place < 2 * CAPX) & (ranks == place - CAPX), hits, 0.0)
    pick_ref[0] = input_pick.astype(BF16)
    pick_ref[1] = back_pick.astype(BF16)
    factor = jnp.sum(back_pick * gates, axis=1, keepdims=True)
    factor_ref[...] = jnp.broadcast_to(factor, factor_ref.shape)


def dispatch_kernel(pick_ref, factor_ref, text_ref, gain_ref, cot_ref, *send_refs):
    text = text_ref[...].astype(F32)
    scale = lax.rsqrt(jnp.mean(text * text, axis=1, keepdims=True) + EPS)
    h_rows = (text * scale * gain_ref[...]).astype(BF16)
    factor = factor_ref[:, :1]
    send = dot(pick_ref[0], h_rows) + factor * dot(pick_ref[1], cot_ref[...])
    send = send.astype(BF16)
    count = 2 * SEND
    for k, ref in enumerate(send_refs):
        ref[...] = send[k * count : (k + 1) * count]


def plan_kernel(
    meta_ref, cot_ref, slots_ref, placed_ref, back_ref, *, blocks, groups, merged_rows, row_share
):
    tokens = cot_ref.shape[0]
    rows = blocks * merged_rows
    me, expert_index = lax.axis_index("blk"), lax.axis_index("expert")
    member = expert_index // groups
    meta = [meta_ref[k * 16 : (k + 1) * 16].astype(F32) for k in range(blocks)]
    mine = (2 * me + member).astype(F32)
    hits = [jnp.sum((part[:8] == mine).astype(F32), axis=0, keepdims=True) for part in meta]
    hit = jnp.concatenate(hits, axis=0)
    dest = jnp.concatenate([part[9:10] for part in meta], axis=0)
    before = (iota((tokens, tokens), 0) < iota((tokens, tokens), 1)).astype(BF16)
    rank = dot(hit, before)

    def row_of(col):
        inner = col % merged_rows
        return ((inner // row_share) ^ expert_index) * row_share + inner % row_share

    def place_of(col):
        return ((col // merged_rows) ^ me) * merged_rows + row_of(col)

    spread = (iota((128, rows), 0) == row_of(iota((128, rows), 1))).astype(F32)
    own_block = iota((blocks, rows), 1) // merged_rows == iota((blocks, rows), 0)
    dest_row = jnp.sum(jnp.where(own_block, dot(dest, spread), 0.0), axis=0, keepdims=True)
    dest_row = dest_row.astype(jnp.int32) ^ me
    dest_hit = (iota((blocks, rows), 0) == dest_row).astype(F32)
    rows_before = place_of(iota((rows, rows), 0)) < place_of(iota((rows, rows), 1))
    earlier = dot(dest_hit, rows_before.astype(F32))
    slot = jnp.sum(dest_hit * earlier, axis=0, keepdims=True).astype(jnp.int32)
    at_token = (iota((tokens, rows), 0) == slot).astype(F32)
    row_hit = jnp.sum(dest_hit * dot(hit, at_token), axis=0, keepdims=True)
    row_rank = jnp.sum(dest_hit * dot(rank, at_token), axis=0, keepdims=True).astype(jnp.int32)
    slot_id = dest_row * SLOTS + row_rank
    slot_count = slots_ref.shape[0]
    chosen = (iota((slot_count, rows), 0) == slot_id) & (row_hit > 0.5)
    slots_ref[...] = chosen.astype(F32).astype(BF16)
    placed = jnp.where(dest_row == 0, at_token, 0.0).astype(BF16)
    placed_ref[...] = placed
    back_rows = blocks * row_share
    source = iota((back_rows, rows), 0)
    wanted = source // row_share * merged_rows + source % row_share
    row_pick = (iota((back_rows, rows), 1) == wanted).astype(F32).astype(BF16)
    back_ref[...] = dot(dot_nt(row_pick, placed), cot_ref[...]).astype(BF16)


def flat_gain(gain_ref):
    return jnp.concatenate([gain_ref[h : h + 1] for h in range(gain_ref.shape[0])], axis=1)


def attend_kernel(*refs, blocks, row_share):
    query_ref, gain_ref = refs[:2]
    near_refs = refs[7 : 6 + blocks]
    merged_ref, meta_ref, left_ref, scalar_ref = refs[6 + blocks :]
    heads, size, patches = query_ref.shape
    rows, features = merged_ref.shape
    depth = heads * size
    near = [packed(*refs[2:7])] + [ref[...].astype(F32) for ref in near_refs]
    meta_ref[...] = jnp.concatenate([part[2 * depth :] for part in near], axis=0).astype(BF16)
    key_ids = jnp.concatenate([part[2 * depth + 8 : 2 * depth + 9] for part in near], axis=1)
    eye = iota((patches, patches), 0) == iota((patches, patches), 1)
    own_ids = jnp.sum(jnp.where(eye, key_ids[:, :patches], 0.0), axis=1, keepdims=True)
    same = own_ids == key_ids
    spread = jnp.zeros((patches, features), F32)
    place_row, place_col = iota((size, features), 0), iota((size, features), 1)
    for head in range(heads):
        first = head * size
        keys = jnp.concatenate([part[first : first + size] for part in near], axis=1)
        first = depth + head * size
        values = jnp.concatenate([part[first : first + size] for part in near], axis=1)
        query = query_ref[head].astype(F32).T.astype(BF16)
        scores = dot(query, keys) * (size**-0.5)
        scores = jnp.where(same, scores, -1e30)
        weights = jnp.exp(scores - jnp.max(scores, axis=1, keepdims=True))
        total = jnp.sum(weights, axis=1, keepdims=True)
        attn = dot_nt(weights.astype(BF16), values.astype(BF16)) / total
        place = (place_col % size == place_row) & (place_col // (4 * size) == head)
        spread = spread + dot(attn, place.astype(F32))
    spot = iota((patches, features), 1) // size % 4 == iota((patches, features), 0) % 4
    line = iota((rows, patches), 0)
    line = ((line // row_share) ^ lax.axis_index("expert")) * row_share + line % row_share
    fold = (iota((rows, patches), 1) // 4 == line).astype(F32)
    merged = dot(fold, jnp.where(spot, spread, 0.0))
    merged_ref[...] = merged.astype(BF16)
    local_mean = jnp.sum(merged, axis=1, keepdims=True) / features
    centered = merged - local_mean
    squares = jnp.sum(centered * centered, axis=1, keepdims=True)
    gain = flat_gain(gain_ref)
    gain_high = gain.astype(BF16).astype(F32)
    extra = iota((16, features), 0)
    gain_rows = jnp.where(extra == 0, gain_high, jnp.where(extra == 1, gain - gain_high, 0.0))
    left_ref[...] = jnp.concatenate([centered * gain, gain_rows], axis=0).astype(BF16)
    scalar_ref[...] = put_scalars([local_mean, squares], rows)


def project_kernel(left_ref, scalar_ref, weight_ref, _, *message_refs):
    rows = scalar_ref.shape[0]
    width = weight_ref.shape[1]
    row_share = rows // len(message_refs)
    product = dot(left_ref[...], weight_ref[...])
    gain_sum = product[rows : rows + 1] + product[rows + 1 : rows + 2]
    piece = width // row_share
    pieces = [gain_sum[:, j * piece : (j + 1) * piece] for j in range(row_share)]
    pieces = jnp.concatenate(pieces, axis=0).astype(BF16)
    scalars = scalar_ref[...].astype(BF16)
    for k, message_ref in enumerate(message_refs):
        mine = slice(k * row_share, (k + 1) * row_share)
        message_ref[:, :width] = product[mine].astype(BF16)
        message_ref[:, width : width + piece] = pieces
        message_ref[:, width + piece :] = scalars[mine]


def merge_kernel(_, *refs, width, features):
    *message_refs, out_ref, gain_ref = refs
    share, row_share = len(message_refs), out_ref.shape[0]
    piece = width // row_share
    parts = [ref[...].astype(F32) for ref in message_refs]
    scalars = [part[:, width + piece :] for part in parts]
    means = [get_scalar(block, 0) for block in scalars]
    squares = [get_scalar(block, 1) for block in scalars]
    mean = sum(means) / share
    spread = sum(q + features * (m - mean) * (m - mean) for q, m in zip(squares, means))
    inv_std = lax.rsqrt(spread / (share * features) + EPS)
    total = jnp.zeros((row_share, width), F32)
    gain_total = jnp.zeros((1, width), F32)
    for part, local in zip(parts, means):
        tail = part[:, width : width + piece]
        gain_sum = jnp.concatenate([tail[j : j + 1] for j in range(row_share)], axis=1)
        total = total + part[:, :width] + (local - mean) * gain_sum
        gain_total = gain_total + gain_sum
    gain_ref[...] = gain_total
    out_ref[:, :width] = (total * inv_std).astype(BF16)
    out_ref[:, width:] = put_scalars([mean, inv_std], row_share).astype(BF16)


def stack_kernel(*refs):
    *part_refs, out_ref, scalar_ref = refs
    width = out_ref.shape[1]
    rows = jnp.concatenate([ref[...].astype(F32) for ref in part_refs], axis=0)
    out_ref[...] = rows[:, :width].astype(BF16)
    scalar_ref[...] = rows[:, width:].astype(BF16)


def by_chip(own_refs, sibling_ref):
    parts = []
    sibling = sibling_ref[...].astype(F32)
    for k, own_ref in enumerate(own_refs):
        half = own_ref.shape[0] // 2
        parts.append(own_ref[...].astype(F32)[:half])
        parts.append(sibling[k * half : (k + 1) * half])
    return jnp.concatenate(parts, axis=0).astype(BF16)


def other_half_kernel(*refs, count):
    out_ref = refs[-1]
    parts = [ref[...].astype(F32)[ref.shape[0] // 2 :] for ref in refs[:count]]
    out_ref[...] = jnp.concatenate(parts, axis=0).astype(BF16)


def slot_pick(slot_count, send_rows, shift):
    row, col = iota((slot_count, send_rows), 0), iota((slot_count, send_rows), 1)
    place = row % SLOTS
    pick = (col == row // SLOTS * SEND + place + shift) & (place < CAPX)
    return pick.astype(F32)


def early_kernel(down_ref, *refs):
    *early_refs, sibling_ref, text_out, grad_out = refs
    slot_count = text_out.shape[0]
    early = by_chip(early_refs, sibling_ref)
    text_out[...] = dot(slot_pick(slot_count, early.shape[0], 0), early).astype(BF16)
    back_rows = dot(slot_pick(slot_count, early.shape[0], CAPX), early).astype(BF16)
    grad_out[...] = dot_nt(back_rows, down_ref[0])


def forward_kernel(*refs, blocks):
    slots_ref, gain_ref, gate_ref, up_ref, down_ref, text_ref = refs[:6]
    vision_refs = refs[6 : 6 + blocks]
    gate_out, up_out, *down_refs = refs[6 + blocks : -2]
    h_ref, sum_ref = refs[-2:]
    _, hidden, width = gate_ref.shape
    chosen = slots_ref[...]
    is_vision = jnp.sum(chosen.astype(F32), axis=1, keepdims=True) > 0.5
    vision = jnp.concatenate([ref[:, :width] for ref in vision_refs], axis=0)
    inputs = dot(chosen, vision)
    scale = lax.rsqrt(jnp.mean(inputs * inputs, axis=1, keepdims=True) + EPS)
    normed = inputs * scale * gain_ref[...]
    h_ref[...] = jnp.where(is_vision, normed, text_ref[...].astype(F32)).astype(BF16)
    tile = tile_of(hidden)
    for i in range(hidden // tile):
        mine = slice(i * tile, (i + 1) * tile)
        gate_pre = dot_nt(h_ref[...], gate_ref[0, mine])
        up_proj = dot_nt(h_ref[...], up_ref[0, mine])
        gate_out[:, mine] = gate_pre
        up_out[:, mine] = up_proj
        activated = gate_pre * jax.nn.sigmoid(gate_pre) * up_proj
        product = dot(activated, down_ref[0, mine])
        sum_ref[...] = product if i == 0 else sum_ref[...] + product
    count = 2 * SLOTS
    for k, ref in enumerate(down_refs):
        ref[...] = sum_ref[k * count : (k + 1) * count].astype(BF16)


def backward_kernel(
    slots_ref, grad_ref, gate_in, up_in, cot_ref, gate_ref, up_ref, even_ref, odd_ref, sum_ref,
    *, blocks,
):
    hidden = gate_ref.shape[1]
    tile = tile_of(hidden)
    for i in range(hidden // tile):
        mine = slice(i * tile, (i + 1) * tile)
        act_grad = grad_ref[:, mine]
        gate_pre, up_proj = gate_in[:, mine], up_in[:, mine]
        sigmoid = jax.nn.sigmoid(gate_pre)
        gate_grad = act_grad * up_proj * sigmoid * (1.0 + gate_pre * (1.0 - sigmoid))
        up_grad = act_grad * gate_pre * sigmoid
        product = dot(gate_grad, gate_ref[0, mine]) + dot(up_grad, up_ref[0, mine])
        sum_ref[...] = product if i == 0 else sum_ref[...] + product
    grads = dot_tn(slots_ref[...], sum_ref[...].astype(BF16))
    cots = cot_ref[...].astype(F32)
    rows, row_share = grads.shape[0] // blocks, cots.shape[0] // blocks
    parts = ([], [])
    for k in range(blocks):
        parts[k % 2].append(grads[k * rows : (k + 1) * rows])
        parts[k % 2].append(cots[k * row_share : (k + 1) * row_share])
    even_ref[...] = jnp.concatenate(parts[0], axis=0).astype(BF16)
    odd_ref[...] = jnp.concatenate(parts[1], axis=0).astype(BF16)


def tile_of(hidden):
    return 256 if hidden % 256 == 0 else hidden


def halving_order(share):
    order = [0]
    step = share // 2
    while step:
        order = order + [k + step for k in order]
        step //= 2
    return [sum(1 << j for j in range(share.bit_length() - 1) if k >> j & 1) for k in order]


def pair_sum_kernel(own_ref, sibling_ref, *out_refs):
    rows = out_refs[0].shape[0]
    total = own_ref[...].astype(F32) + sibling_ref[...].astype(F32)
    for k, out_ref in enumerate(out_refs):
        out_ref[...] = total[k * rows : (k + 1) * rows].astype(BF16)


def total_of(part_refs):
    total = part_refs[0][...].astype(F32)
    for ref in part_refs[1:]:
        total = total + ref[...].astype(F32)
    return total


def chip_sum_kernel(*refs, count, order):
    cot_ref, keep_ref, send_ref = refs[count + 1 :]
    total = total_of(refs[:count])
    rows = cot_ref.shape[0]
    turned = jnp.concatenate([total[k * rows : (k + 1) * rows] for k in order], axis=0)
    half = turned.shape[0] // 2
    keep_ref[...] = turned[:half]
    send_ref[...] = turned[half:].astype(BF16)
    cot_ref[...] = total[len(order) * rows :].astype(BF16)


def grad_halve_kernel(keep_ref, arrived_ref, *refs):
    quarters(keep_ref[...] + arrived_ref[...].astype(F32), refs)


def grad_join_kernel(keep_ref, arrived_ref, cot_ref, out_ref):
    total = keep_ref[...] + arrived_ref[...].astype(F32)
    out_ref[...] = jnp.concatenate([total, cot_ref[...].astype(F32)], axis=0).astype(BF16)


def quarters(total, out_refs):
    count = out_refs[0].shape[0]
    for k, ref in enumerate(out_refs):
        ref[...] = total[k * count : (k + 1) * count].astype(ref.dtype)


def combine_kernel(comb_ref, *refs):
    *part_refs, sibling_ref = refs[:-4]
    rows = by_chip(part_refs, sibling_ref)
    quarters(dot_tn(comb_ref[0], rows) + dot_tn(comb_ref[1], rows), refs[-4:])


def halve_kernel(*refs):
    low, high, arrived_low, arrived_high = [ref[...].astype(F32) for ref in refs[:4]]
    quarters(jnp.concatenate([low + arrived_low, high + arrived_high], axis=0), refs[4:])


def add_kernel(own_ref, arrived_ref, *refs):
    refs[-1][...] = (own_ref[...] + arrived_ref[...].astype(F32)).astype(BF16)


def finish_kernel(placed_ref, text_ref, own_ref, arrived_ref, *refs, blocks, turn):
    vision_refs, out_ref = refs[:blocks], refs[-1]
    count, width = out_ref.shape
    tokens = placed_ref.shape[0]
    first = (lax.axis_index("expert") ^ turn) * count
    pick = iota((count, tokens), 1) == iota((count, tokens), 0) + first
    pick = pick.astype(F32)
    placed = dot(pick, placed_ref[...])
    is_vision = jnp.sum(placed, axis=1, keepdims=True) > 0.5
    vision = jnp.concatenate([ref[:, :width] for ref in vision_refs], axis=0)
    inputs = jnp.where(is_vision, dot(placed, vision), dot(pick, text_ref[...]))
    out_ref[...] = (inputs + (own_ref[...].astype(F32) + arrived_ref[...].astype(F32))).astype(BF16)


def lay_kernel(*refs):
    *part_refs, out_ref = refs
    count = part_refs[0].shape[0]
    for k, ref in enumerate(part_refs):
        first = pl.multiple_of((lax.axis_index("expert") ^ k) * count, count)
        out_ref[pl.ds(first, count), :] = ref[...]


def norm_grad_kernel(
    joined_ref, other_ref, rows_ref, gain_ref, total_ref, out_ref, *, features
):
    width = gain_ref.shape[1]
    count = out_ref.shape[0] // 2
    far = rows_ref.shape[0] // 2
    joined, other = joined_ref[...].astype(F32), other_ref[...].astype(F32)
    turned = jnp.concatenate([other[count : 2 * count], other[:count]], axis=0)
    hidden = joined[: 2 * count] + turned
    cotangent = jnp.concatenate([joined[2 * count :], other[2 * count :]], axis=0)
    rows = rows_ref[:, :width].astype(F32)
    inputs = jnp.concatenate([rows[:count], rows[far : far + count]], axis=0)
    scale = lax.rsqrt(jnp.mean(inputs * inputs, axis=1, keepdims=True) + EPS)
    pulled = hidden * gain_ref[...]
    cross = jnp.mean(pulled * inputs, axis=1, keepdims=True)
    grad = cotangent + scale * pulled - inputs * (scale * scale * scale) * cross
    grad = grad.astype(BF16)
    out_ref[:, :width] = grad
    grad = grad.astype(F32)
    grad_mean = jnp.sum(grad * total_ref[...], axis=1, keepdims=True) / features
    cross_mean = jnp.sum(grad * inputs, axis=1, keepdims=True) / features
    out_ref[:, width:] = put_scalars([grad_mean, cross_mean], 2 * count).astype(BF16)


def merge_grad_kernel(*refs, size, bases):
    gain_ref, merged_ref, scalar_ref, weight_ref, *part_refs, out_ref = refs
    rows, features = merged_ref.shape
    width = weight_ref.shape[1]
    depth, patches = out_ref.shape
    row_share = part_refs[0].shape[0] // 2
    blocks = {}
    for base, ref in zip(bases, part_refs):
        part = ref[...].astype(F32)
        blocks[base] = part[:row_share]
        blocks[base ^ len(bases)] = part[row_share:]
    parts = jnp.concatenate([blocks[k] for k in sorted(blocks)], axis=0).astype(BF16)
    normed_grad = dot_nt(parts[:, :width], weight_ref[...]) * flat_gain(gain_ref)
    means = parts[:, width:].astype(F32)
    scalars = scalar_ref[...].astype(F32)
    inv_std = get_scalar(scalars, 1)
    normed = (merged_ref[...].astype(F32) - get_scalar(scalars, 0)) * inv_std
    grad = inv_std * (normed_grad - get_scalar(means, 0) - normed * get_scalar(means, 1))
    high = grad.astype(BF16)
    low = (grad - high.astype(F32)).astype(BF16)
    line = iota((patches, rows), 1)
    line = ((line // row_share) ^ lax.axis_index("expert")) * row_share + line % row_share
    unfold = (iota((patches, rows), 0) // 4 == line).astype(F32)
    spot = iota((patches, features), 1) // size % 4 == iota((patches, features), 0) % 4
    row, col = iota((depth, features), 0), iota((depth, features), 1)
    place = (col // (4 * size) == row // size) & (col % size == row % size)
    place = place.astype(F32).astype(BF16)
    out = jnp.zeros((depth, patches), F32)
    for piece in (high, low):
        wide = jnp.where(spot, dot(unfold, piece), 0.0).astype(BF16)
        out = out + dot_nt(place, wide)
    out_ref[...] = out


def whole(memory_space=pltpu.VMEM):
    return pl.BlockSpec(memory_space=memory_space)


def run(kernel, outs, *args, far=(), scratch=(), cost=1.0, vmem=VMEM_BYTES, name=None):
    specs = [whole()] * len(args)
    for place in far:
        specs[place] = whole(pl.ANY)
    return pl.pallas_call(
        kernel,
        out_shape=outs,
        in_specs=specs,
        out_specs=jax.tree.map(lambda _: whole(), outs),
        scratch_shapes=scratch,
        compiler_params=pltpu.CompilerParams(vmem_limit_bytes=vmem),
        cost_estimate=microseconds(cost),
        name=name,
    )(*args)


def to_sibling(parts, deps, name):
    rows, width = parts[0].shape
    half = run(
        functools.partial(other_half_kernel, count=len(parts)),
        shape((len(parts) * rows // 2, width)), *parts, *deps,
        far=range(len(parts), len(parts) + len(deps)), cost=0.01, name=name,
    )
    return swap(half, "blk", 1)


def microseconds(time):
    return pl.CostEstimate(flops=0, transcendentals=0, bytes_accessed=int(time * 3e6))


def after(values, deps):
    count = len(values)
    return pl.pallas_call(
        lambda *refs: None,
        out_shape=[shape(value.shape, value.dtype) for value in values],
        in_specs=[whole(pl.ANY)] * (count + len(deps)),
        out_specs=[whole(pl.ANY)] * count,
        input_output_aliases={i: i for i in range(count)},
        compiler_params=pltpu.CompilerParams(vmem_limit_bytes=VMEM_BYTES),
        cost_estimate=microseconds(0.1),
        name="after",
    )(*values, *deps)


def shape(dims, dtype=BF16):
    return jax.ShapeDtypeStruct(dims, dtype)


def swap(value, axis, step):
    count = lax.axis_size(axis)
    return lax.ppermute(value, axis, [(i, i ^ step) for i in range(count)])


def trade(parts, axis):
    return [parts[0]] + [swap(parts[k], axis, k) for k in range(1, len(parts))]


def spread_out(value, axis):
    return trade([value] * lax.axis_size(axis), axis)


def gather_blocks(value, deps=None):
    own = [value] + [swap(value, "blk", k) for k in range(2, lax.axis_size("blk"), 2)]
    if deps is not None:
        own = own[:1] + list(after(own[1:], deps))
    sibling = [swap(part, "blk", 1) for part in own]
    return [part for pair in zip(own, sibling) for part in pair]


def to_chips(parts):
    return [parts[0]] + [swap(parts[k], "blk", 2 * k) for k in range(1, len(parts))]


def body(
    queries, keys, values, image_ids, placement, merge_gain, merge_weight, text, norm_gain,
    w_gate, w_up, w_down, routes, route_gates, cotangent,
):
    blocks = lax.axis_size("blk")
    share = lax.axis_size("expert")
    heads, size, patches = queries.shape
    depth = heads * size
    rows = image_ids.shape[0]
    row_share = rows // share
    tokens, width = text.shape
    part = tokens // share
    all_rows = blocks * rows
    features = heads * 4 * size
    hidden = w_gate.shape[1]
    slot_count = blocks * SLOTS
    groups = share // 2
    routes_t, gates_t, gain_row = routes.T, route_gates.T, norm_gain[None]

    small = [
        keys.reshape(depth, patches), values.reshape(depth, patches),
        image_ids[None], placement.reshape(1, rows), routes_t,
    ]
    local = run(
        pack_kernel, shape((2 * depth + 16, patches)), *small, far=range(5),
        scratch=[pltpu.VMEM(array.shape, array.dtype) for array in small]
        + [pltpu.SemaphoreType.DMA((5,))],
        vmem=PACK_BYTES, name="pack",
    )
    comb, pick, factor = run(
        functools.partial(route_kernel, groups=groups, share=share),
        [
            shape((2, slot_count, tokens)), shape((2, blocks * SEND, tokens)),
            shape((blocks * SEND, 128), F32),
        ],
        routes_t, gates_t, cost=3.0, name="route",
    )
    send = run(
        dispatch_kernel, [shape((2 * SEND, width))] * (blocks // 2),
        pick, factor, text, gain_row, cotangent, cost=2.0, name="dispatch",
    )
    near = gather_blocks(local, send)
    early = to_chips(after(send, near[2::2]))

    weight_flat = merge_weight.reshape(features, width)
    message_width = width + width // row_share + 128
    merged, meta, left, local_scalars = run(
        functools.partial(attend_kernel, blocks=blocks, row_share=row_share),
        [
            shape((rows, features)), shape((blocks * 16, patches)), shape((rows + 16, features)),
            shape((rows, 128), F32),
        ],
        queries, merge_gain, *small, *near[1:], cost=3.0, name="attend",
    )
    message = run(
        project_kernel, [shape((row_share, message_width))] * share,
        left, local_scalars, weight_flat, early[1], far=(3,), cost=2.0, name="project",
    )
    slots, placed, back_cots = run(
        functools.partial(
            plan_kernel, blocks=blocks, groups=groups, merged_rows=rows, row_share=row_share
        ),
        [
            shape((slot_count, all_rows)), shape((tokens, all_rows)),
            shape((blocks * row_share, width)),
        ],
        meta, cotangent, cost=1.5, name="plan",
    )
    message = trade(message, "expert")
    early = early[:1] + list(after(early[1:], message[1:]))
    own, gain_total = run(
        functools.partial(merge_kernel, width=width, features=features),
        [
            shape((row_share, width + 128)), shape((1, width), F32),
        ],
        early[1], *message, far=(0,), cost=0.2, name="merge",
    )
    owns = spread_out(own, "expert")
    block_rows, row_scalars = run(
        stack_kernel, [shape((rows, width)), shape((rows, 128))], *owns, cost=0.2, name="stack",
    )
    text_rows, act_grad = run(
        early_kernel, [shape((slot_count, width)), shape((slot_count, hidden), F32)],
        w_down, *early, to_sibling(early, owns[1:], "early_half"), cost=3.0, name="early",
    )

    vision = gather_blocks(block_rows, [text_rows, slots])
    gate_pre, up_proj, *down = run(
        functools.partial(forward_kernel, blocks=blocks),
        [
            shape((slot_count, hidden), F32), shape((slot_count, hidden), F32),
        ] + [shape((2 * SLOTS, width))] * (blocks // 2),
        slots, gain_row, w_gate, w_up, w_down, text_rows, *vision,
        scratch=[pltpu.VMEM((slot_count, width), BF16), pltpu.VMEM((slot_count, width), F32)],
        cost=4.0, name="forward",
    )
    returned = to_chips(down)
    block = rows + row_share
    even, odd = run(
        functools.partial(backward_kernel, blocks=blocks),
        [shape((blocks // 2 * block, width))] * 2,
        slots, act_grad, gate_pre, up_proj, back_cots, w_gate, w_up,
        scratch=[pltpu.VMEM((slot_count, width), F32)],
        cost=4.0, name="backward",
    )
    grads = run(
        pair_sum_kernel, [shape((block, width))] * (blocks // 2), even, swap(odd, "blk", 1),
        cost=0.2, name="pair_sum",
    )
    grads = to_chips(grads)
    count = tokens // 4
    pieces = [shape((count, width), F32)] * 2 + [shape((count, width))] * 2
    low, high, sent_low, sent_high = run(
        combine_kernel, pieces, comb, *returned,
        to_sibling(returned, grads[:1], "returned_half"), cost=0.01, name="combine",
    )
    step = 1
    arrived_high = swap(sent_high, "expert", step)
    first_arrived = arrived_high
    arrived_low = swap(sent_low, "expert", step)
    while count > part:
        count //= 2
        step *= 2
        pieces = [shape((count, width), F32)] * 2 + [shape((count, width))] * 2
        low, high, sent_low, sent_high = run(
            halve_kernel, pieces, low, high, arrived_low, arrived_high, cost=0.3, name="halve"
        )
        arrived_high = swap(sent_high, "expert", step)
        arrived_low = swap(sent_low, "expert", step)
    step *= 2

    def add(own_part, arrived, gate, name):
        return run(
            add_kernel, shape((part, width)), own_part, arrived, *gate,
            far=range(2, 2 + len(gate)), cost=0.3, name=name,
        )

    sum_high = add(high, arrived_high, [], "add_high")
    other_low = swap(sum_high, "expert", step)
    cot_rows, keep, sent = run(
        functools.partial(chip_sum_kernel, count=blocks // 2, order=halving_order(share)),
        [
            shape((row_share, width)), shape((rows // 2, width), F32), shape((rows // 2, width)),
        ],
        *grads, first_arrived, far=(blocks // 2,), cost=0.2, name="chip_sum",
    )
    bit, kept_rows = 1, rows // 2
    while kept_rows > 2 * row_share:
        kept_rows //= 2
        keep, sent = run(
            grad_halve_kernel, [shape((kept_rows, width), F32), shape((kept_rows, width))],
            keep, swap(sent, "expert", bit), cost=0.2, name="grad_halve",
        )
        bit *= 2
    joined = run(
        grad_join_kernel, shape((3 * row_share, width)),
        keep, swap(sent, "expert", bit), cot_rows, cost=0.2, name="grad_join",
    )
    other = swap(joined, "expert", share // 2)
    sums = [add(low, arrived_low, [other_low], "add_low"), sum_high]
    others = [other_low, swap(sums[0], "expert", step)]
    vision_grad = run(
        functools.partial(norm_grad_kernel, features=share * features),
        shape((2 * row_share, width + 128)),
        joined, other, block_rows, gain_row, gain_total, cost=0.3, name="norm_grad",
    )
    vision_grads, bit = {0: vision_grad}, share // 4
    while bit:
        vision_grads.update({k + bit: swap(vision_grads[k], "expert", bit) for k in list(vision_grads)})
        bit //= 2
    bases = sorted(vision_grads)
    vision_grads = [vision_grads[k] for k in bases]
    attn_grad = run(
        functools.partial(merge_grad_kernel, size=size, bases=tuple(bases)),
        shape((depth, patches), F32),
        merge_gain, merged, row_scalars, weight_flat, *vision_grads, cost=4.0, name="merge_grad",
    )

    laid = {}
    for turn, value, other, gate in zip((0, step), sums, others, ([other], vision_grads[1:])):
        laid[turn] = run(
            functools.partial(finish_kernel, blocks=blocks, turn=turn), shape((part, width)),
            placed, text, value, other, *vision, *gate,
            far=range(4 + blocks, 4 + blocks + len(gate)), cost=1.0, name="finish",
        )
    while step > 1:
        step //= 2
        laid.update({k + step: swap(laid[k], "expert", step) for k in list(laid)})
    llm_out = run(
        lay_kernel, shape((tokens, width)), *[laid[k] for k in sorted(laid)], cost=1.0, name="lay"
    )
    return llm_out, attn_grad.reshape(heads, size, patches)


def solution(mesh):
    return jax.shard_map(
        body,
        mesh=mesh,
        in_specs=(
            P("expert", None, "blk"),
            P("expert", None, "blk"),
            P("expert", None, "blk"),
            P("blk"),
            P("blk", None),
            P("expert", None),
            P("expert", None, None),
            P("blk", None),
            P(),
            P("blk", "expert", None),
            P("blk", "expert", None),
            P("blk", "expert", None),
            P("blk", None),
            P("blk", None),
            P("blk", None),
        ),
        out_specs=(P("blk", None), P("expert", None, "blk")),
        check_vma=False,
    )
```

```python
import functools

import jax
import jax.numpy as jnp
from jax import lax
from jax.experimental import pallas as pl
from jax.experimental.pallas import tpu as pltpu
from jax.sharding import PartitionSpec as P

CAPX = 10
SLOTS = 12
SEND = 24
EPS = 1e-06
VMEM_BYTES = 16 * 1024 * 1024
PACK_BYTES = 60 * 1024 * 1024
F32 = jnp.float32
BF16 = jnp.bfloat16


def iota(shape, dim):
    return lax.broadcasted_iota(jnp.int32, shape, dim)


def dot(a, b):
    return jnp.dot(a.astype(BF16), b.astype(BF16), preferred_element_type=F32)


def dot_nt(a, b):
    return lax.dot_general(a, b, (((1,), (1,)), ((), ())), preferred_element_type=F32)


def dot_tn(a, b):
    return lax.dot_general(a, b, (((0,), (0,)), ((), ())), preferred_element_type=F32)


def three(value):
    first = value.astype(BF16).astype(F32)
    second = (value - first).astype(BF16).astype(F32)
    return first, second, value - first - second


def put_scalars(columns, rows):
    lane = iota((rows, 128), 1)
    out = jnp.zeros((rows, 128), F32)
    place = 0
    for column in columns:
        for piece in three(column):
            out = jnp.where(lane == place, piece, out)
            place += 1
    return out


def get_scalar(block, which):
    lane = iota(block.shape, 1)
    return jnp.sum(jnp.where(lane // 3 == which, block, 0.0), axis=1, keepdims=True)


def bring(far_refs, near_refs, sems):
    copies = [
        pltpu.make_async_copy(far, near, sems.at[i])
        for i, (far, near) in enumerate(zip(far_refs, near_refs))
    ]
    for copy in copies:
        copy.start()
    return copies


def pack_kernel(*refs):
    far_refs, out_ref, near_refs, sems = refs[:5], refs[5], refs[6:11], refs[11]
    for copy in bring(far_refs, near_refs, sems):
        copy.wait()
    out_ref[...] = packed(*near_refs).astype(BF16)


def packed(keys_ref, values_ref, images_ref, placement_ref, routes_ref):
    rows = images_ref.shape[1]
    patches = keys_ref.shape[1]
    repeat = (iota((rows, patches), 0) == iota((rows, patches), 1) // 4).astype(F32)
    keep = (iota((rows, patches), 0) == iota((rows, patches), 1)).astype(F32)
    patch_ids = dot(images_ref[...].astype(F32), repeat)
    dest = dot(placement_ref[...].astype(F32), keep)
    line = iota((8, patches), 0)
    rest = jnp.where(line == 0, patch_ids, jnp.where(line == 1, dest, 0.0))
    parts = [keys_ref[...], values_ref[...], routes_ref[...], rest]
    return jnp.concatenate([part.astype(F32) for part in parts], axis=0)


def route_kernel(routes_ref, gates_ref, comb_ref, pick_ref, factor_ref, *, groups, share):
    blocks = comb_ref.shape[1] // SLOTS
    tokens = routes_ref.shape[1]
    me, expert_index = lax.axis_index("blk"), lax.axis_index("expert")
    member = expert_index // groups
    before = (iota((tokens, tokens), 0) < iota((tokens, tokens), 1)).astype(BF16)
    pair_of = 2 * (iota((blocks, tokens), 0) ^ me) + member
    out_hit = jnp.zeros((blocks, tokens), F32)
    out_gate = jnp.zeros((blocks, tokens), F32)
    for k in range(routes_ref.shape[0]):
        same = pair_of == routes_ref[k : k + 1, :]
        out_hit = out_hit + same.astype(F32)
        out_gate = out_gate + jnp.where(same, gates_ref[k : k + 1, :], 0.0)
    out_rank = dot(out_hit, before)

    def expand(stride):
        count = blocks * stride
        pick = (iota((count, blocks), 0) // stride == iota((count, blocks), 1)).astype(BF16)
        gate = sum(dot(pick, piece) for piece in three(out_gate))
        return dot(pick, out_hit), dot(pick, out_rank).astype(jnp.int32), gate

    hits, ranks, gates = expand(SLOTS)
    live = jnp.where(ranks == iota(hits.shape, 0) % SLOTS, hits, 0.0)
    weight = live * gates
    high = weight.astype(BF16).astype(F32)
    part = tokens // share
    col = iota((tokens, tokens), 1)
    turned = (col // part * 0).astype(jnp.int32)
    for place, k in enumerate(halving_order(share)):
        turned = jnp.where(col // part == place, k, turned)
    turned = (iota((tokens, tokens), 0) == (turned ^ expert_index) * part + col % part)
    turned = turned.astype(F32)
    comb_ref[0] = dot(high, turned).astype(BF16)
    comb_ref[1] = dot(weight - high, turned).astype(BF16)

    hits, ranks, gates = expand(SEND)
    place = iota(hits.shape, 0) % SEND
    input_pick = jnp.where((place < CAPX) & (ranks == place), hits, 0.0)
    back_pick = jnp.where((place >= CAPX) & (place < 2 * CAPX) & (ranks == place - CAPX), hits, 0.0)
    pick_ref[0] = input_pick.astype(BF16)
    pick_ref[1] = back_pick.astype(BF16)
    factor = jnp.sum(back_pick * gates, axis=1, keepdims=True)
    factor_ref[...] = jnp.broadcast_to(factor, factor_ref.shape)


def dispatch_kernel(pick_ref, factor_ref, text_ref, gain_ref, cot_ref, *send_refs):
    text = text_ref[...].astype(F32)
    scale = lax.rsqrt(jnp.mean(text * text, axis=1, keepdims=True) + EPS)
    h_rows = (text * scale * gain_ref[...]).astype(BF16)
    factor = factor_ref[:, :1]
    send = dot(pick_ref[0], h_rows) + factor * dot(pick_ref[1], cot_ref[...])
    send = send.astype(BF16)
    count = 2 * SEND
    for k, ref in enumerate(send_refs):
        ref[...] = send[k * count : (k + 1) * count]


def plan_kernel(
    meta_ref, cot_ref, slots_ref, placed_ref, back_ref, *, blocks, groups, merged_rows, row_share
):
    tokens = cot_ref.shape[0]
    rows = blocks * merged_rows
    me, expert_index = lax.axis_index("blk"), lax.axis_index("expert")
    member = expert_index // groups
    meta = [meta_ref[k * 16 : (k + 1) * 16].astype(F32) for k in range(blocks)]
    mine = (2 * me + member).astype(F32)
    hits = [jnp.sum((part[:8] == mine).astype(F32), axis=0, keepdims=True) for part in meta]
    hit = jnp.concatenate(hits, axis=0)
    dest = jnp.concatenate([part[9:10] for part in meta], axis=0)
    before = (iota((tokens, tokens), 0) < iota((tokens, tokens), 1)).astype(BF16)
    rank = dot(hit, before)

    def row_of(col):
        inner = col % merged_rows
        return ((inner // row_share) ^ expert_index) * row_share + inner % row_share

    def place_of(col):
        return ((col // merged_rows) ^ me) * merged_rows + row_of(col)

    spread = (iota((128, rows), 0) == row_of(iota((128, rows), 1))).astype(F32)
    own_block = iota((blocks, rows), 1) // merged_rows == iota((blocks, rows), 0)
    dest_row = jnp.sum(jnp.where(own_block, dot(dest, spread), 0.0), axis=0, keepdims=True)
    dest_row = dest_row.astype(jnp.int32) ^ me
    dest_hit = (iota((blocks, rows), 0) == dest_row).astype(F32)
    rows_before = place_of(iota((rows, rows), 0)) < place_of(iota((rows, rows), 1))
    earlier = dot(dest_hit, rows_before.astype(F32))
    slot = jnp.sum(dest_hit * earlier, axis=0, keepdims=True).astype(jnp.int32)
    at_token = (iota((tokens, rows), 0) == slot).astype(F32)
    row_hit = jnp.sum(dest_hit * dot(hit, at_token), axis=0, keepdims=True)
    row_rank = jnp.sum(dest_hit * dot(rank, at_token), axis=0, keepdims=True).astype(jnp.int32)
    slot_id = dest_row * SLOTS + row_rank
    slot_count = slots_ref.shape[0]
    chosen = (iota((slot_count, rows), 0) == slot_id) & (row_hit > 0.5)
    slots_ref[...] = chosen.astype(F32).astype(BF16)
    placed = jnp.where(dest_row == 0, at_token, 0.0).astype(BF16)
    placed_ref[...] = placed
    back_rows = blocks * row_share
    source = iota((back_rows, rows), 0)
    wanted = source // row_share * merged_rows + source % row_share
    row_pick = (iota((back_rows, rows), 1) == wanted).astype(F32).astype(BF16)
    back_ref[...] = dot(dot_nt(row_pick, placed), cot_ref[...]).astype(BF16)


def flat_gain(gain_ref):
    return jnp.concatenate([gain_ref[h : h + 1] for h in range(gain_ref.shape[0])], axis=1)


def attend_kernel(*refs, blocks, row_share):
    query_ref, gain_ref = refs[:2]
    near_refs = refs[7 : 6 + blocks]
    merged_ref, meta_ref, left_ref, scalar_ref = refs[6 + blocks :]
    heads, size, patches = query_ref.shape
    rows, features = merged_ref.shape
    depth = heads * size
    near = [packed(*refs[2:7])] + [ref[...].astype(F32) for ref in near_refs]
    meta_ref[...] = jnp.concatenate([part[2 * depth :] for part in near], axis=0).astype(BF16)
    key_ids = jnp.concatenate([part[2 * depth + 8 : 2 * depth + 9] for part in near], axis=1)
    eye = iota((patches, patches), 0) == iota((patches, patches), 1)
    own_ids = jnp.sum(jnp.where(eye, key_ids[:, :patches], 0.0), axis=1, keepdims=True)
    same = own_ids == key_ids
    spread = jnp.zeros((patches, features), F32)
    place_row, place_col = iota((size, features), 0), iota((size, features), 1)
    for head in range(heads):
        first = head * size
        keys = jnp.concatenate([part[first : first + size] for part in near], axis=1)
        first = depth + head * size
        values = jnp.concatenate([part[first : first + size] for part in near], axis=1)
        query = query_ref[head].astype(F32).T.astype(BF16)
        scores = dot(query, keys) * (size**-0.5)
        scores = jnp.where(same, scores, -1e30)
        weights = jnp.exp(scores - jnp.max(scores, axis=1, keepdims=True))
        total = jnp.sum(weights, axis=1, keepdims=True)
        attn = dot_nt(weights.astype(BF16), values.astype(BF16)) / total
        place = (place_col % size == place_row) & (place_col // (4 * size) == head)
        spread = spread + dot(attn, place.astype(F32))
    spot = iota((patches, features), 1) // size % 4 == iota((patches, features), 0) % 4
    line = iota((rows, patches), 0)
    line = ((line // row_share) ^ lax.axis_index("expert")) * row_share + line % row_share
    fold = (iota((rows, patches), 1) // 4 == line).astype(F32)
    merged = dot(fold, jnp.where(spot, spread, 0.0))
    merged_ref[...] = merged.astype(BF16)
    local_mean = jnp.sum(merged, axis=1, keepdims=True) / features
    centered = merged - local_mean
    squares = jnp.sum(centered * centered, axis=1, keepdims=True)
    gain = flat_gain(gain_ref)
    gain_high = gain.astype(BF16).astype(F32)
    extra = iota((16, features), 0)
    gain_rows = jnp.where(extra == 0, gain_high, jnp.where(extra == 1, gain - gain_high, 0.0))
    left_ref[...] = jnp.concatenate([centered * gain, gain_rows], axis=0).astype(BF16)
    scalar_ref[...] = put_scalars([local_mean, squares], rows)


def project_kernel(left_ref, scalar_ref, weight_ref, _, *message_refs):
    rows = scalar_ref.shape[0]
    width = weight_ref.shape[1]
    row_share = rows // len(message_refs)
    product = dot(left_ref[...], weight_ref[...])
    gain_sum = product[rows : rows + 1] + product[rows + 1 : rows + 2]
    piece = width // row_share
    pieces = [gain_sum[:, j * piece : (j + 1) * piece] for j in range(row_share)]
    pieces = jnp.concatenate(pieces, axis=0).astype(BF16)
    scalars = scalar_ref[...].astype(BF16)
    for k, message_ref in enumerate(message_refs):
        mine = slice(k * row_share, (k + 1) * row_share)
        message_ref[:, :width] = product[mine].astype(BF16)
        message_ref[:, width : width + piece] = pieces
        message_ref[:, width + piece :] = scalars[mine]


def merge_kernel(_, *refs, width, features):
    *message_refs, out_ref, gain_ref = refs
    share, row_share = len(message_refs), out_ref.shape[0]
    piece = width // row_share
    parts = [ref[...].astype(F32) for ref in message_refs]
    scalars = [part[:, width + piece :] for part in parts]
    means = [get_scalar(block, 0) for block in scalars]
    squares = [get_scalar(block, 1) for block in scalars]
    mean = sum(means) / share
    spread = sum(q + features * (m - mean) * (m - mean) for q, m in zip(squares, means))
    inv_std = lax.rsqrt(spread / (share * features) + EPS)
    total = jnp.zeros((row_share, width), F32)
    gain_total = jnp.zeros((1, width), F32)
    for part, local in zip(parts, means):
        tail = part[:, width : width + piece]
        gain_sum = jnp.concatenate([tail[j : j + 1] for j in range(row_share)], axis=1)
        total = total + part[:, :width] + (local - mean) * gain_sum
        gain_total = gain_total + gain_sum
    gain_ref[...] = gain_total
    out_ref[:, :width] = (total * inv_std).astype(BF16)
    out_ref[:, width:] = put_scalars([mean, inv_std], row_share).astype(BF16)


def stack_kernel(*refs):
    *part_refs, out_ref, scalar_ref = refs
    width = out_ref.shape[1]
    rows = jnp.concatenate([ref[...].astype(F32) for ref in part_refs], axis=0)
    out_ref[...] = rows[:, :width].astype(BF16)
    scalar_ref[...] = rows[:, width:].astype(BF16)


def by_chip(own_refs, sibling_ref):
    parts = []
    sibling = sibling_ref[...].astype(F32)
    for k, own_ref in enumerate(own_refs):
        half = own_ref.shape[0] // 2
        parts.append(own_ref[...].astype(F32)[:half])
        parts.append(sibling[k * half : (k + 1) * half])
    return jnp.concatenate(parts, axis=0).astype(BF16)


def other_half_kernel(*refs, count):
    out_ref = refs[-1]
    parts = [ref[...].astype(F32)[ref.shape[0] // 2 :] for ref in refs[:count]]
    out_ref[...] = jnp.concatenate(parts, axis=0).astype(BF16)


def slot_pick(slot_count, send_rows, shift):
    row, col = iota((slot_count, send_rows), 0), iota((slot_count, send_rows), 1)
    place = row % SLOTS
    pick = (col == row // SLOTS * SEND + place + shift) & (place < CAPX)
    return pick.astype(F32)


def early_kernel(down_ref, *refs):
    *early_refs, sibling_ref, text_out, grad_out = refs
    slot_count = text_out.shape[0]
    early = by_chip(early_refs, sibling_ref)
    text_out[...] = dot(slot_pick(slot_count, early.shape[0], 0), early).astype(BF16)
    back_rows = dot(slot_pick(slot_count, early.shape[0], CAPX), early).astype(BF16)
    grad_out[...] = dot_nt(back_rows, down_ref[0])


def forward_kernel(*refs, blocks):
    slots_ref, gain_ref, gate_ref, up_ref, down_ref, text_ref = refs[:6]
    vision_refs = refs[6 : 6 + blocks]
    gate_out, up_out, *down_refs = refs[6 + blocks : -2]
    h_ref, sum_ref = refs[-2:]
    _, hidden, width = gate_ref.shape
    chosen = slots_ref[...]
    is_vision = jnp.sum(chosen.astype(F32), axis=1, keepdims=True) > 0.5
    vision = jnp.concatenate([ref[:, :width] for ref in vision_refs], axis=0)
    inputs = dot(chosen, vision)
    scale = lax.rsqrt(jnp.mean(inputs * inputs, axis=1, keepdims=True) + EPS)
    normed = inputs * scale * gain_ref[...]
    h_ref[...] = jnp.where(is_vision, normed, text_ref[...].astype(F32)).astype(BF16)
    tile = tile_of(hidden)
    for i in range(hidden // tile):
        mine = slice(i * tile, (i + 1) * tile)
        gate_pre = dot_nt(h_ref[...], gate_ref[0, mine])
        up_proj = dot_nt(h_ref[...], up_ref[0, mine])
        gate_out[:, mine] = gate_pre
        up_out[:, mine] = up_proj
        activated = gate_pre * jax.nn.sigmoid(gate_pre) * up_proj
        product = dot(activated, down_ref[0, mine])
        sum_ref[...] = product if i == 0 else sum_ref[...] + product
    count = 2 * SLOTS
    for k, ref in enumerate(down_refs):
        ref[...] = sum_ref[k * count : (k + 1) * count].astype(BF16)


def backward_kernel(
    slots_ref, grad_ref, gate_in, up_in, cot_ref, gate_ref, up_ref, even_ref, odd_ref, sum_ref,
    *, blocks,
):
    hidden = gate_ref.shape[1]
    tile = tile_of(hidden)
    for i in range(hidden // tile):
        mine = slice(i * tile, (i + 1) * tile)
        act_grad = grad_ref[:, mine]
        gate_pre, up_proj = gate_in[:, mine], up_in[:, mine]
        sigmoid = jax.nn.sigmoid(gate_pre)
        gate_grad = act_grad * up_proj * sigmoid * (1.0 + gate_pre * (1.0 - sigmoid))
        up_grad = act_grad * gate_pre * sigmoid
        product = dot(gate_grad, gate_ref[0, mine]) + dot(up_grad, up_ref[0, mine])
        sum_ref[...] = product if i == 0 else sum_ref[...] + product
    grads = dot_tn(slots_ref[...], sum_ref[...].astype(BF16))
    cots = cot_ref[...].astype(F32)
    rows, row_share = grads.shape[0] // blocks, cots.shape[0] // blocks
    parts = ([], [])
    for k in range(blocks):
        parts[k % 2].append(grads[k * rows : (k + 1) * rows])
        parts[k % 2].append(cots[k * row_share : (k + 1) * row_share])
    even_ref[...] = jnp.concatenate(parts[0], axis=0).astype(BF16)
    odd_ref[...] = jnp.concatenate(parts[1], axis=0).astype(BF16)


def tile_of(hidden):
    return 256 if hidden % 256 == 0 else hidden


def halving_order(share):
    order = [0]
    step = share // 2
    while step:
        order = order + [k + step for k in order]
        step //= 2
    return [sum(1 << j for j in range(share.bit_length() - 1) if k >> j & 1) for k in order]


def pair_sum_kernel(own_ref, sibling_ref, *out_refs):
    rows = out_refs[0].shape[0]
    total = own_ref[...].astype(F32) + sibling_ref[...].astype(F32)
    for k, out_ref in enumerate(out_refs):
        out_ref[...] = total[k * rows : (k + 1) * rows].astype(BF16)


def total_of(part_refs):
    total = part_refs[0][...].astype(F32)
    for ref in part_refs[1:]:
        total = total + ref[...].astype(F32)
    return total


def chip_sum_kernel(*refs, count, order):
    cot_ref, keep_ref, send_ref = refs[count + 1 :]
    total = total_of(refs[:count])
    rows = cot_ref.shape[0]
    turned = jnp.concatenate([total[k * rows : (k + 1) * rows] for k in order], axis=0)
    half = turned.shape[0] // 2
    keep_ref[...] = turned[:half]
    send_ref[...] = turned[half:].astype(BF16)
    cot_ref[...] = total[len(order) * rows :].astype(BF16)


def grad_halve_kernel(keep_ref, arrived_ref, *refs):
    quarters(keep_ref[...] + arrived_ref[...].astype(F32), refs)


def grad_join_kernel(keep_ref, arrived_ref, cot_ref, out_ref):
    total = keep_ref[...] + arrived_ref[...].astype(F32)
    out_ref[...] = jnp.concatenate([total, cot_ref[...].astype(F32)], axis=0).astype(BF16)


def quarters(total, out_refs):
    count = out_refs[0].shape[0]
    for k, ref in enumerate(out_refs):
        ref[...] = total[k * count : (k + 1) * count].astype(ref.dtype)


def combine_kernel(comb_ref, *refs):
    *part_refs, sibling_ref = refs[:-4]
    rows = by_chip(part_refs, sibling_ref)
    quarters(dot_tn(comb_ref[0], rows) + dot_tn(comb_ref[1], rows), refs[-4:])


def halve_kernel(*refs):
    low, high, arrived_low, arrived_high = [ref[...].astype(F32) for ref in refs[:4]]
    quarters(jnp.concatenate([low + arrived_low, high + arrived_high], axis=0), refs[4:])


def add_kernel(own_ref, arrived_ref, *refs):
    refs[-1][...] = (own_ref[...] + arrived_ref[...].astype(F32)).astype(BF16)


def finish_kernel(placed_ref, text_ref, own_ref, arrived_ref, *refs, blocks, turn):
    vision_refs, out_ref = refs[:blocks], refs[-1]
    count, width = out_ref.shape
    tokens = placed_ref.shape[0]
    first = (lax.axis_index("expert") ^ turn) * count
    pick = iota((count, tokens), 1) == iota((count, tokens), 0) + first
    pick = pick.astype(F32)
    placed = dot(pick, placed_ref[...])
    is_vision = jnp.sum(placed, axis=1, keepdims=True) > 0.5
    vision = jnp.concatenate([ref[:, :width] for ref in vision_refs], axis=0)
    inputs = jnp.where(is_vision, dot(placed, vision), dot(pick, text_ref[...]))
    out_ref[...] = (inputs + (own_ref[...].astype(F32) + arrived_ref[...].astype(F32))).astype(BF16)


def lay_kernel(*refs):
    *part_refs, out_ref = refs
    count = part_refs[0].shape[0]
    for k, ref in enumerate(part_refs):
        first = pl.multiple_of((lax.axis_index("expert") ^ k) * count, count)
        out_ref[pl.ds(first, count), :] = ref[...]


def norm_grad_kernel(
    joined_ref, other_ref, rows_ref, gain_ref, total_ref, out_ref, *, features
):
    width = gain_ref.shape[1]
    count = out_ref.shape[0] // 2
    far = rows_ref.shape[0] // 2
    joined, other = joined_ref[...].astype(F32), other_ref[...].astype(F32)
    turned = jnp.concatenate([other[count : 2 * count], other[:count]], axis=0)
    hidden = joined[: 2 * count] + turned
    cotangent = jnp.concatenate([joined[2 * count :], other[2 * count :]], axis=0)
    rows = rows_ref[:, :width].astype(F32)
    inputs = jnp.concatenate([rows[:count], rows[far : far + count]], axis=0)
    scale = lax.rsqrt(jnp.mean(inputs * inputs, axis=1, keepdims=True) + EPS)
    pulled = hidden * gain_ref[...]
    cross = jnp.mean(pulled * inputs, axis=1, keepdims=True)
    grad = cotangent + scale * pulled - inputs * (scale * scale * scale) * cross
    grad = grad.astype(BF16)
    out_ref[:, :width] = grad
    grad = grad.astype(F32)
    grad_mean = jnp.sum(grad * total_ref[...], axis=1, keepdims=True) / features
    cross_mean = jnp.sum(grad * inputs, axis=1, keepdims=True) / features
    out_ref[:, width:] = put_scalars([grad_mean, cross_mean], 2 * count).astype(BF16)


def merge_grad_kernel(*refs, size, bases):
    gain_ref, merged_ref, scalar_ref, weight_ref, *part_refs, out_ref = refs
    rows, features = merged_ref.shape
    width = weight_ref.shape[1]
    depth, patches = out_ref.shape
    row_share = part_refs[0].shape[0] // 2
    blocks = {}
    for base, ref in zip(bases, part_refs):
        part = ref[...].astype(F32)
        blocks[base] = part[:row_share]
        blocks[base ^ len(bases)] = part[row_share:]
    parts = jnp.concatenate([blocks[k] for k in sorted(blocks)], axis=0).astype(BF16)
    normed_grad = dot_nt(parts[:, :width], weight_ref[...]) * flat_gain(gain_ref)
    means = parts[:, width:].astype(F32)
    scalars = scalar_ref[...].astype(F32)
    inv_std = get_scalar(scalars, 1)
    normed = (merged_ref[...].astype(F32) - get_scalar(scalars, 0)) * inv_std
    grad = inv_std * (normed_grad - get_scalar(means, 0) - normed * get_scalar(means, 1))
    high = grad.astype(BF16)
    low = (grad - high.astype(F32)).astype(BF16)
    line = iota((patches, rows), 1)
    line = ((line // row_share) ^ lax.axis_index("expert")) * row_share + line % row_share
    unfold = (iota((patches, rows), 0) // 4 == line).astype(F32)
    spot = iota((patches, features), 1) // size % 4 == iota((patches, features), 0) % 4
    row, col = iota((depth, features), 0), iota((depth, features), 1)
    place = (col // (4 * size) == row // size) & (col % size == row % size)
    place = place.astype(F32).astype(BF16)
    out = jnp.zeros((depth, patches), F32)
    for piece in (high, low):
        wide = jnp.where(spot, dot(unfold, piece), 0.0).astype(BF16)
        out = out + dot_nt(place, wide)
    out_ref[...] = out


def whole(memory_space=pltpu.VMEM):
    return pl.BlockSpec(memory_space=memory_space)


def run(kernel, outs, *args, far=(), scratch=(), cost=1.0, vmem=VMEM_BYTES, name=None):
    specs = [whole()] * len(args)
    for place in far:
        specs[place] = whole(pl.ANY)
    return pl.pallas_call(
        kernel,
        out_shape=outs,
        in_specs=specs,
        out_specs=jax.tree.map(lambda _: whole(), outs),
        scratch_shapes=scratch,
        compiler_params=pltpu.CompilerParams(vmem_limit_bytes=vmem),
        cost_estimate=microseconds(cost),
        name=name,
    )(*args)


def to_sibling(parts, deps, name):
    rows, width = parts[0].shape
    half = run(
        functools.partial(other_half_kernel, count=len(parts)),
        shape((len(parts) * rows // 2, width)), *parts, *deps,
        far=range(len(parts), len(parts) + len(deps)), cost=0.01, name=name,
    )
    return swap(half, "blk", 1)


def microseconds(time):
    return pl.CostEstimate(flops=0, transcendentals=0, bytes_accessed=int(time * 3e6))


def after(values, deps):
    count = len(values)
    return pl.pallas_call(
        lambda *refs: None,
        out_shape=[shape(value.shape, value.dtype) for value in values],
        in_specs=[whole(pl.ANY)] * (count + len(deps)),
        out_specs=[whole(pl.ANY)] * count,
        input_output_aliases={i: i for i in range(count)},
        compiler_params=pltpu.CompilerParams(vmem_limit_bytes=VMEM_BYTES),
        cost_estimate=microseconds(0.1),
        name="after",
    )(*values, *deps)


def shape(dims, dtype=BF16):
    return jax.ShapeDtypeStruct(dims, dtype)


def swap(value, axis, step):
    count = lax.axis_size(axis)
    return lax.ppermute(value, axis, [(i, i ^ step) for i in range(count)])


def trade(parts, axis):
    return [parts[0]] + [swap(parts[k], axis, k) for k in range(1, len(parts))]


def spread_out(value, axis):
    return trade([value] * lax.axis_size(axis), axis)


def gather_blocks(value, deps=None):
    own = [value] + [swap(value, "blk", k) for k in range(2, lax.axis_size("blk"), 2)]
    if deps is not None:
        own = own[:1] + list(after(own[1:], deps))
    sibling = [swap(part, "blk", 1) for part in own]
    return [part for pair in zip(own, sibling) for part in pair]


def to_chips(parts):
    return [parts[0]] + [swap(parts[k], "blk", 2 * k) for k in range(1, len(parts))]


def body(
    queries, keys, values, image_ids, placement, merge_gain, merge_weight, text, norm_gain,
    w_gate, w_up, w_down, routes, route_gates, cotangent,
):
    blocks = lax.axis_size("blk")
    share = lax.axis_size("expert")
    heads, size, patches = queries.shape
    depth = heads * size
    rows = image_ids.shape[0]
    row_share = rows // share
    tokens, width = text.shape
    part = tokens // share
    all_rows = blocks * rows
    features = heads * 4 * size
    hidden = w_gate.shape[1]
    slot_count = blocks * SLOTS
    groups = share // 2
    routes_t, gates_t, gain_row = routes.T, route_gates.T, norm_gain[None]

    small = [
        keys.reshape(depth, patches), values.reshape(depth, patches),
        image_ids[None], placement.reshape(1, rows), routes_t,
    ]
    local = run(
        pack_kernel, shape((2 * depth + 16, patches)), *small, far=range(5),
        scratch=[pltpu.VMEM(array.shape, array.dtype) for array in small]
        + [pltpu.SemaphoreType.DMA((5,))],
        vmem=PACK_BYTES, name="pack",
    )
    comb, pick, factor = run(
        functools.partial(route_kernel, groups=groups, share=share),
        [
            shape((2, slot_count, tokens)), shape((2, blocks * SEND, tokens)),
            shape((blocks * SEND, 128), F32),
        ],
        routes_t, gates_t, cost=3.0, name="route",
    )
    send = run(
        dispatch_kernel, [shape((2 * SEND, width))] * (blocks // 2),
        pick, factor, text, gain_row, cotangent, cost=2.0, name="dispatch",
    )
    near = gather_blocks(local, send)
    early = to_chips(after(send, near[2::2]))

    weight_flat = merge_weight.reshape(features, width)
    message_width = width + width // row_share + 128
    merged, meta, left, local_scalars = run(
        functools.partial(attend_kernel, blocks=blocks, row_share=row_share),
        [
            shape((rows, features)), shape((blocks * 16, patches)), shape((rows + 16, features)),
            shape((rows, 128), F32),
        ],
        queries, merge_gain, *small, *near[1:], cost=3.0, name="attend",
    )
    message = run(
        project_kernel, [shape((row_share, message_width))] * share,
        left, local_scalars, weight_flat, early[1], far=(3,), cost=2.0, name="project",
    )
    slots, placed, back_cots = run(
        functools.partial(
            plan_kernel, blocks=blocks, groups=groups, merged_rows=rows, row_share=row_share
        ),
        [
            shape((slot_count, all_rows)), shape((tokens, all_rows)),
            shape((blocks * row_share, width)),
        ],
        meta, cotangent, cost=1.5, name="plan",
    )
    message = trade(message, "expert")
    early = early[:1] + list(after(early[1:], message[1:]))
    own, gain_total = run(
        functools.partial(merge_kernel, width=width, features=features),
        [
            shape((row_share, width + 128)), shape((1, width), F32),
        ],
        early[1], *message, far=(0,), cost=0.2, name="merge",
    )
    owns = spread_out(own, "expert")
    block_rows, row_scalars = run(
        stack_kernel, [shape((rows, width)), shape((rows, 128))], *owns, cost=0.2, name="stack",
    )
    text_rows, act_grad = run(
        early_kernel, [shape((slot_count, width)), shape((slot_count, hidden), F32)],
        w_down, *early, to_sibling(early, owns[1:], "early_half"), cost=3.0, name="early",
    )

    vision = gather_blocks(block_rows, [text_rows, slots])
    gate_pre, up_proj, *down = run(
        functools.partial(forward_kernel, blocks=blocks),
        [
            shape((slot_count, hidden), F32), shape((slot_count, hidden), F32),
        ] + [shape((2 * SLOTS, width))] * (blocks // 2),
        slots, gain_row, w_gate, w_up, w_down, text_rows, *vision,
        scratch=[pltpu.VMEM((slot_count, width), BF16), pltpu.VMEM((slot_count, width), F32)],
        cost=4.0, name="forward",
    )
    returned = to_chips(down)
    block = rows + row_share
    even, odd = run(
        functools.partial(backward_kernel, blocks=blocks),
        [shape((blocks // 2 * block, width))] * 2,
        slots, act_grad, gate_pre, up_proj, back_cots, w_gate, w_up,
        scratch=[pltpu.VMEM((slot_count, width), F32)],
        cost=4.0, name="backward",
    )
    grads = run(
        pair_sum_kernel, [shape((block, width))] * (blocks // 2), even, swap(odd, "blk", 1),
        cost=0.2, name="pair_sum",
    )
    grads = to_chips(grads)
    count = tokens // 4
    pieces = [shape((count, width), F32)] * 2 + [shape((count, width))] * 2
    low, high, sent_low, sent_high = run(
        combine_kernel, pieces, comb, *returned,
        to_sibling(returned, grads[:1], "returned_half"), cost=0.01, name="combine",
    )
    step = 1
    arrived_high = swap(sent_high, "expert", step)
    first_arrived = arrived_high
    arrived_low = swap(sent_low, "expert", step)
    while count > part:
        count //= 2
        step *= 2
        pieces = [shape((count, width), F32)] * 2 + [shape((count, width))] * 2
        low, high, sent_low, sent_high = run(
            halve_kernel, pieces, low, high, arrived_low, arrived_high, cost=0.3, name="halve"
        )
        arrived_high = swap(sent_high, "expert", step)
        arrived_low = swap(sent_low, "expert", step)
    step *= 2

    def add(own_part, arrived, gate, name):
        return run(
            add_kernel, shape((part, width)), own_part, arrived, *gate,
            far=range(2, 2 + len(gate)), cost=0.3, name=name,
        )

    sum_high = add(high, arrived_high, [], "add_high")
    other_low = swap(sum_high, "expert", step)
    cot_rows, keep, sent = run(
        functools.partial(chip_sum_kernel, count=blocks // 2, order=halving_order(share)),
        [
            shape((row_share, width)), shape((rows // 2, width), F32), shape((rows // 2, width)),
        ],
        *grads, first_arrived, far=(blocks // 2,), cost=0.2, name="chip_sum",
    )
    bit, kept_rows = 1, rows // 2
    while kept_rows > 2 * row_share:
        kept_rows //= 2
        keep, sent = run(
            grad_halve_kernel, [shape((kept_rows, width), F32), shape((kept_rows, width))],
            keep, swap(sent, "expert", bit), cost=0.2, name="grad_halve",
        )
        bit *= 2
    joined = run(
        grad_join_kernel, shape((3 * row_share, width)),
        keep, swap(sent, "expert", bit), cot_rows, cost=0.2, name="grad_join",
    )
    other = swap(joined, "expert", share // 2)
    sums = [add(low, arrived_low, [other_low, other], "add_low"), sum_high]
    others = [other_low, swap(sums[0], "expert", step)]
    vision_grad = run(
        functools.partial(norm_grad_kernel, features=share * features),
        shape((2 * row_share, width + 128)),
        joined, other, block_rows, gain_row, gain_total, cost=0.3, name="norm_grad",
    )
    vision_grads, bit = {0: vision_grad}, share // 4
    while bit:
        vision_grads.update({k + bit: swap(vision_grads[k], "expert", bit) for k in list(vision_grads)})
        bit //= 2
    bases = sorted(vision_grads)
    vision_grads = [vision_grads[k] for k in bases]
    attn_grad = run(
        functools.partial(merge_grad_kernel, size=size, bases=tuple(bases)),
        shape((depth, patches), F32),
        merge_gain, merged, row_scalars, weight_flat, *vision_grads, cost=4.0, name="merge_grad",
    )

    laid = {}
    for turn, value, other, gate in zip((0, step), sums, others, ([other], vision_grads[1:])):
        laid[turn] = run(
            functools.partial(finish_kernel, blocks=blocks, turn=turn), shape((part, width)),
            placed, text, value, other, *vision, *gate,
            far=range(4 + blocks, 4 + blocks + len(gate)), cost=1.0, name="finish",
        )
    while step > 1:
        step //= 2
        laid.update({k + step: swap(laid[k], "expert", step) for k in list(laid)})
    llm_out = run(
        lay_kernel, shape((tokens, width)), *[laid[k] for k in sorted(laid)], cost=1.0, name="lay"
    )
    return llm_out, attn_grad.reshape(heads, size, patches)


def solution(mesh):
    return jax.shard_map(
        body,
        mesh=mesh,
        in_specs=(
            P("expert", None, "blk"),
            P("expert", None, "blk"),
            P("expert", None, "blk"),
            P("blk"),
            P("blk", None),
            P("expert", None),
            P("expert", None, None),
            P("blk", None),
            P(),
            P("blk", "expert", None),
            P("blk", "expert", None),
            P("blk", "expert", None),
            P("blk", None),
            P("blk", None),
            P("blk", None),
        ),
        out_specs=(P("blk", None), P("expert", None, "blk")),
        check_vma=False,
    )
```

```python
import functools

import jax
import jax.numpy as jnp
from jax import lax
from jax.experimental import pallas as pl
from jax.experimental.pallas import tpu as pltpu
from jax.sharding import PartitionSpec as P

CAPX = 10
SLOTS = 12
SEND = 24
EPS = 1e-06
VMEM_BYTES = 16 * 1024 * 1024
PACK_BYTES = 60 * 1024 * 1024
F32 = jnp.float32
BF16 = jnp.bfloat16


def iota(shape, dim):
    return lax.broadcasted_iota(jnp.int32, shape, dim)


def dot(a, b):
    return jnp.dot(a.astype(BF16), b.astype(BF16), preferred_element_type=F32)


def dot_nt(a, b):
    return lax.dot_general(a, b, (((1,), (1,)), ((), ())), preferred_element_type=F32)


def dot_tn(a, b):
    return lax.dot_general(a, b, (((0,), (0,)), ((), ())), preferred_element_type=F32)


def three(value):
    first = value.astype(BF16).astype(F32)
    second = (value - first).astype(BF16).astype(F32)
    return first, second, value - first - second


def put_scalars(columns, rows):
    lane = iota((rows, 128), 1)
    out = jnp.zeros((rows, 128), F32)
    place = 0
    for column in columns:
        for piece in three(column):
            out = jnp.where(lane == place, piece, out)
            place += 1
    return out


def get_scalar(block, which):
    lane = iota(block.shape, 1)
    return jnp.sum(jnp.where(lane // 3 == which, block, 0.0), axis=1, keepdims=True)


def bring(far_refs, near_refs, sems):
    copies = [
        pltpu.make_async_copy(far, near, sems.at[i])
        for i, (far, near) in enumerate(zip(far_refs, near_refs))
    ]
    for copy in copies:
        copy.start()
    return copies


def pack_kernel(*refs):
    far_refs, out_ref, near_refs, sems = refs[:5], refs[5], refs[6:11], refs[11]
    for copy in bring(far_refs, near_refs, sems):
        copy.wait()
    out_ref[...] = packed(*near_refs).astype(BF16)


def packed(keys_ref, values_ref, images_ref, placement_ref, routes_ref):
    rows = images_ref.shape[1]
    patches = keys_ref.shape[1]
    repeat = (iota((rows, patches), 0) == iota((rows, patches), 1) // 4).astype(F32)
    keep = (iota((rows, patches), 0) == iota((rows, patches), 1)).astype(F32)
    patch_ids = dot(images_ref[...].astype(F32), repeat)
    dest = dot(placement_ref[...].astype(F32), keep)
    line = iota((8, patches), 0)
    rest = jnp.where(line == 0, patch_ids, jnp.where(line == 1, dest, 0.0))
    parts = [keys_ref[...], values_ref[...], routes_ref[...], rest]
    return jnp.concatenate([part.astype(F32) for part in parts], axis=0)


def route_kernel(routes_ref, gates_ref, comb_ref, pick_ref, factor_ref, *, groups, share):
    blocks = comb_ref.shape[1] // SLOTS
    tokens = routes_ref.shape[1]
    me, expert_index = lax.axis_index("blk"), lax.axis_index("expert")
    member = expert_index // groups
    before = (iota((tokens, tokens), 0) < iota((tokens, tokens), 1)).astype(BF16)
    pair_of = 2 * (iota((blocks, tokens), 0) ^ me) + member
    out_hit = jnp.zeros((blocks, tokens), F32)
    out_gate = jnp.zeros((blocks, tokens), F32)
    for k in range(routes_ref.shape[0]):
        same = pair_of == routes_ref[k : k + 1, :]
        out_hit = out_hit + same.astype(F32)
        out_gate = out_gate + jnp.where(same, gates_ref[k : k + 1, :], 0.0)
    out_rank = dot(out_hit, before)

    def expand(stride):
        count = blocks * stride
        pick = (iota((count, blocks), 0) // stride == iota((count, blocks), 1)).astype(BF16)
        gate = sum(dot(pick, piece) for piece in three(out_gate))
        return dot(pick, out_hit), dot(pick, out_rank).astype(jnp.int32), gate

    hits, ranks, gates = expand(SLOTS)
    live = jnp.where(ranks == iota(hits.shape, 0) % SLOTS, hits, 0.0)
    weight = live * gates
    high = weight.astype(BF16).astype(F32)
    part = tokens // share
    col = iota((tokens, tokens), 1)
    turned = (col // part * 0).astype(jnp.int32)
    for place, k in enumerate(halving_order(share)):
        turned = jnp.where(col // part == place, k, turned)
    turned = (iota((tokens, tokens), 0) == (turned ^ expert_index) * part + col % part)
    turned = turned.astype(F32)
    comb_ref[0] = dot(high, turned).astype(BF16)
    comb_ref[1] = dot(weight - high, turned).astype(BF16)

    hits, ranks, gates = expand(SEND)
    place = iota(hits.shape, 0) % SEND
    input_pick = jnp.where((place < CAPX) & (ranks == place), hits, 0.0)
    back_pick = jnp.where((place >= CAPX) & (place < 2 * CAPX) & (ranks == place - CAPX), hits, 0.0)
    pick_ref[0] = input_pick.astype(BF16)
    pick_ref[1] = back_pick.astype(BF16)
    factor = jnp.sum(back_pick * gates, axis=1, keepdims=True)
    factor_ref[...] = jnp.broadcast_to(factor, factor_ref.shape)


def dispatch_kernel(pick_ref, factor_ref, text_ref, gain_ref, cot_ref, *send_refs):
    text = text_ref[...].astype(F32)
    scale = lax.rsqrt(jnp.mean(text * text, axis=1, keepdims=True) + EPS)
    h_rows = (text * scale * gain_ref[...]).astype(BF16)
    factor = factor_ref[:, :1]
    send = dot(pick_ref[0], h_rows) + factor * dot(pick_ref[1], cot_ref[...])
    send = send.astype(BF16)
    count = 2 * SEND
    for k, ref in enumerate(send_refs):
        ref[...] = send[k * count : (k + 1) * count]


def plan_kernel(
    meta_ref, cot_ref, slots_ref, placed_ref, back_ref, *, blocks, groups, merged_rows, row_share
):
    tokens = cot_ref.shape[0]
    rows = blocks * merged_rows
    me, expert_index = lax.axis_index("blk"), lax.axis_index("expert")
    member = expert_index // groups
    meta = [meta_ref[k * 16 : (k + 1) * 16].astype(F32) for k in range(blocks)]
    mine = (2 * me + member).astype(F32)
    hits = [jnp.sum((part[:8] == mine).astype(F32), axis=0, keepdims=True) for part in meta]
    hit = jnp.concatenate(hits, axis=0)
    dest = jnp.concatenate([part[9:10] for part in meta], axis=0)
    before = (iota((tokens, tokens), 0) < iota((tokens, tokens), 1)).astype(BF16)
    rank = dot(hit, before)

    def row_of(col):
        inner = col % merged_rows
        return ((inner // row_share) ^ expert_index) * row_share + inner % row_share

    def place_of(col):
        return ((col // merged_rows) ^ me) * merged_rows + row_of(col)

    spread = (iota((128, rows), 0) == row_of(iota((128, rows), 1))).astype(F32)
    own_block = iota((blocks, rows), 1) // merged_rows == iota((blocks, rows), 0)
    dest_row = jnp.sum(jnp.where(own_block, dot(dest, spread), 0.0), axis=0, keepdims=True)
    dest_row = dest_row.astype(jnp.int32) ^ me
    dest_hit = (iota((blocks, rows), 0) == dest_row).astype(F32)
    rows_before = place_of(iota((rows, rows), 0)) < place_of(iota((rows, rows), 1))
    earlier = dot(dest_hit, rows_before.astype(F32))
    slot = jnp.sum(dest_hit * earlier, axis=0, keepdims=True).astype(jnp.int32)
    at_token = (iota((tokens, rows), 0) == slot).astype(F32)
    row_hit = jnp.sum(dest_hit * dot(hit, at_token), axis=0, keepdims=True)
    row_rank = jnp.sum(dest_hit * dot(rank, at_token), axis=0, keepdims=True).astype(jnp.int32)
    slot_id = dest_row * SLOTS + row_rank
    slot_count = slots_ref.shape[0]
    chosen = (iota((slot_count, rows), 0) == slot_id) & (row_hit > 0.5)
    slots_ref[...] = chosen.astype(F32).astype(BF16)
    placed = jnp.where(dest_row == 0, at_token, 0.0).astype(BF16)
    placed_ref[...] = placed
    back_rows = blocks * row_share
    source = iota((back_rows, rows), 0)
    wanted = source // row_share * merged_rows + source % row_share
    row_pick = (iota((back_rows, rows), 1) == wanted).astype(F32).astype(BF16)
    back_ref[...] = dot(dot_nt(row_pick, placed), cot_ref[...]).astype(BF16)


def flat_gain(gain_ref):
    return jnp.concatenate([gain_ref[h : h + 1] for h in range(gain_ref.shape[0])], axis=1)


def attend_kernel(*refs, blocks, row_share):
    query_ref, gain_ref = refs[:2]
    near_refs = refs[7 : 6 + blocks]
    merged_ref, meta_ref, left_ref, scalar_ref = refs[6 + blocks :]
    heads, size, patches = query_ref.shape
    rows, features = merged_ref.shape
    depth = heads * size
    near = [packed(*refs[2:7])] + [ref[...].astype(F32) for ref in near_refs]
    meta_ref[...] = jnp.concatenate([part[2 * depth :] for part in near], axis=0).astype(BF16)
    key_ids = jnp.concatenate([part[2 * depth + 8 : 2 * depth + 9] for part in near], axis=1)
    eye = iota((patches, patches), 0) == iota((patches, patches), 1)
    own_ids = jnp.sum(jnp.where(eye, key_ids[:, :patches], 0.0), axis=1, keepdims=True)
    same = own_ids == key_ids
    spread = jnp.zeros((patches, features), F32)
    place_row, place_col = iota((size, features), 0), iota((size, features), 1)
    for head in range(heads):
        first = head * size
        keys = jnp.concatenate([part[first : first + size] for part in near], axis=1)
        first = depth + head * size
        values = jnp.concatenate([part[first : first + size] for part in near], axis=1)
        query = query_ref[head].astype(F32).T.astype(BF16)
        scores = dot(query, keys) * (size**-0.5)
        scores = jnp.where(same, scores, -1e30)
        weights = jnp.exp(scores - jnp.max(scores, axis=1, keepdims=True))
        total = jnp.sum(weights, axis=1, keepdims=True)
        attn = dot_nt(weights.astype(BF16), values.astype(BF16)) / total
        place = (place_col % size == place_row) & (place_col // (4 * size) == head)
        spread = spread + dot(attn, place.astype(F32))
    spot = iota((patches, features), 1) // size % 4 == iota((patches, features), 0) % 4
    line = iota((rows, patches), 0)
    line = ((line // row_share) ^ lax.axis_index("expert")) * row_share + line % row_share
    fold = (iota((rows, patches), 1) // 4 == line).astype(F32)
    merged = dot(fold, jnp.where(spot, spread, 0.0))
    merged_ref[...] = merged.astype(BF16)
    local_mean = jnp.sum(merged, axis=1, keepdims=True) / features
    centered = merged - local_mean
    squares = jnp.sum(centered * centered, axis=1, keepdims=True)
    gain = flat_gain(gain_ref)
    gain_high = gain.astype(BF16).astype(F32)
    extra = iota((16, features), 0)
    gain_rows = jnp.where(extra == 0, gain_high, jnp.where(extra == 1, gain - gain_high, 0.0))
    left_ref[...] = jnp.concatenate([centered * gain, gain_rows], axis=0).astype(BF16)
    scalar_ref[...] = put_scalars([local_mean, squares], rows)


def project_kernel(left_ref, scalar_ref, weight_ref, _, *message_refs):
    rows = scalar_ref.shape[0]
    width = weight_ref.shape[1]
    row_share = rows // len(message_refs)
    product = dot(left_ref[...], weight_ref[...])
    gain_sum = product[rows : rows + 1] + product[rows + 1 : rows + 2]
    piece = width // row_share
    pieces = [gain_sum[:, j * piece : (j + 1) * piece] for j in range(row_share)]
    pieces = jnp.concatenate(pieces, axis=0).astype(BF16)
    scalars = scalar_ref[...].astype(BF16)
    for k, message_ref in enumerate(message_refs):
        mine = slice(k * row_share, (k + 1) * row_share)
        message_ref[:, :width] = product[mine].astype(BF16)
        message_ref[:, width : width + piece] = pieces
        message_ref[:, width + piece :] = scalars[mine]


def merge_kernel(_, *refs, width, features):
    *message_refs, out_ref, gain_ref = refs
    share, row_share = len(message_refs), out_ref.shape[0]
    piece = width // row_share
    parts = [ref[...].astype(F32) for ref in message_refs]
    scalars = [part[:, width + piece :] for part in parts]
    means = [get_scalar(block, 0) for block in scalars]
    squares = [get_scalar(block, 1) for block in scalars]
    mean = sum(means) / share
    spread = sum(q + features * (m - mean) * (m - mean) for q, m in zip(squares, means))
    inv_std = lax.rsqrt(spread / (share * features) + EPS)
    total = jnp.zeros((row_share, width), F32)
    gain_total = jnp.zeros((1, width), F32)
    for part, local in zip(parts, means):
        tail = part[:, width : width + piece]
        gain_sum = jnp.concatenate([tail[j : j + 1] for j in range(row_share)], axis=1)
        total = total + part[:, :width] + (local - mean) * gain_sum
        gain_total = gain_total + gain_sum
    gain_ref[...] = gain_total
    out_ref[:, :width] = (total * inv_std).astype(BF16)
    out_ref[:, width:] = put_scalars([mean, inv_std], row_share).astype(BF16)


def stack_kernel(*refs):
    *part_refs, out_ref, scalar_ref = refs
    width = out_ref.shape[1]
    rows = jnp.concatenate([ref[...].astype(F32) for ref in part_refs], axis=0)
    out_ref[...] = rows[:, :width].astype(BF16)
    scalar_ref[...] = rows[:, width:].astype(BF16)


def by_chip(own_refs, sibling_ref):
    parts = []
    sibling = sibling_ref[...].astype(F32)
    for k, own_ref in enumerate(own_refs):
        half = own_ref.shape[0] // 2
        parts.append(own_ref[...].astype(F32)[:half])
        parts.append(sibling[k * half : (k + 1) * half])
    return jnp.concatenate(parts, axis=0).astype(BF16)


def other_half_kernel(*refs, count):
    out_ref = refs[-1]
    parts = [ref[...].astype(F32)[ref.shape[0] // 2 :] for ref in refs[:count]]
    out_ref[...] = jnp.concatenate(parts, axis=0).astype(BF16)


def slot_pick(slot_count, send_rows, shift):
    row, col = iota((slot_count, send_rows), 0), iota((slot_count, send_rows), 1)
    place = row % SLOTS
    pick = (col == row // SLOTS * SEND + place + shift) & (place < CAPX)
    return pick.astype(F32)


def early_kernel(down_ref, *refs):
    *early_refs, sibling_ref, text_out, grad_out = refs
    slot_count = text_out.shape[0]
    early = by_chip(early_refs, sibling_ref)
    text_out[...] = dot(slot_pick(slot_count, early.shape[0], 0), early).astype(BF16)
    back_rows = dot(slot_pick(slot_count, early.shape[0], CAPX), early).astype(BF16)
    grad_out[...] = dot_nt(back_rows, down_ref[0])


def forward_kernel(*refs, blocks):
    slots_ref, gain_ref, gate_ref, up_ref, down_ref, text_ref = refs[:6]
    vision_refs = refs[6 : 6 + blocks]
    gate_out, up_out, *down_refs = refs[6 + blocks : -2]
    h_ref, sum_ref = refs[-2:]
    _, hidden, width = gate_ref.shape
    chosen = slots_ref[...]
    is_vision = jnp.sum(chosen.astype(F32), axis=1, keepdims=True) > 0.5
    vision = jnp.concatenate([ref[:, :width] for ref in vision_refs], axis=0)
    inputs = dot(chosen, vision)
    scale = lax.rsqrt(jnp.mean(inputs * inputs, axis=1, keepdims=True) + EPS)
    normed = inputs * scale * gain_ref[...]
    h_ref[...] = jnp.where(is_vision, normed, text_ref[...].astype(F32)).astype(BF16)
    tile = tile_of(hidden)
    for i in range(hidden // tile):
        mine = slice(i * tile, (i + 1) * tile)
        gate_pre = dot_nt(h_ref[...], gate_ref[0, mine])
        up_proj = dot_nt(h_ref[...], up_ref[0, mine])
        gate_out[:, mine] = gate_pre
        up_out[:, mine] = up_proj
        activated = gate_pre * jax.nn.sigmoid(gate_pre) * up_proj
        product = dot(activated, down_ref[0, mine])
        sum_ref[...] = product if i == 0 else sum_ref[...] + product
    count = 2 * SLOTS
    for k, ref in enumerate(down_refs):
        ref[...] = sum_ref[k * count : (k + 1) * count].astype(BF16)


def backward_kernel(
    slots_ref, grad_ref, gate_in, up_in, cot_ref, gate_ref, up_ref, even_ref, odd_ref, sum_ref,
    *, blocks,
):
    hidden = gate_ref.shape[1]
    tile = tile_of(hidden)
    for i in range(hidden // tile):
        mine = slice(i * tile, (i + 1) * tile)
        act_grad = grad_ref[:, mine]
        gate_pre, up_proj = gate_in[:, mine], up_in[:, mine]
        sigmoid = jax.nn.sigmoid(gate_pre)
        gate_grad = act_grad * up_proj * sigmoid * (1.0 + gate_pre * (1.0 - sigmoid))
        up_grad = act_grad * gate_pre * sigmoid
        product = dot(gate_grad, gate_ref[0, mine]) + dot(up_grad, up_ref[0, mine])
        sum_ref[...] = product if i == 0 else sum_ref[...] + product
    grads = dot_tn(slots_ref[...], sum_ref[...].astype(BF16))
    cots = cot_ref[...].astype(F32)
    rows, row_share = grads.shape[0] // blocks, cots.shape[0] // blocks
    parts = ([], [])
    for k in range(blocks):
        parts[k % 2].append(grads[k * rows : (k + 1) * rows])
        parts[k % 2].append(cots[k * row_share : (k + 1) * row_share])
    even_ref[...] = jnp.concatenate(parts[0], axis=0).astype(BF16)
    odd_ref[...] = jnp.concatenate(parts[1], axis=0).astype(BF16)


def tile_of(hidden):
    return 256 if hidden % 256 == 0 else hidden


def halving_order(share):
    order = [0]
    step = share // 2
    while step:
        order = order + [k + step for k in order]
        step //= 2
    return [sum(1 << j for j in range(share.bit_length() - 1) if k >> j & 1) for k in order]


def pair_sum_kernel(own_ref, sibling_ref, *out_refs):
    rows = out_refs[0].shape[0]
    total = own_ref[...].astype(F32) + sibling_ref[...].astype(F32)
    for k, out_ref in enumerate(out_refs):
        out_ref[...] = total[k * rows : (k + 1) * rows].astype(BF16)


def total_of(part_refs):
    total = part_refs[0][...].astype(F32)
    for ref in part_refs[1:]:
        total = total + ref[...].astype(F32)
    return total


def chip_sum_kernel(*refs, count, order):
    cot_ref, keep_ref, send_ref = refs[count + 1 :]
    total = total_of(refs[:count])
    rows = cot_ref.shape[0]
    turned = jnp.concatenate([total[k * rows : (k + 1) * rows] for k in order], axis=0)
    half = turned.shape[0] // 2
    keep_ref[...] = turned[:half]
    send_ref[...] = turned[half:].astype(BF16)
    cot_ref[...] = total[len(order) * rows :].astype(BF16)


def grad_halve_kernel(keep_ref, arrived_ref, *refs):
    quarters(keep_ref[...] + arrived_ref[...].astype(F32), refs)


def grad_join_kernel(keep_ref, arrived_ref, cot_ref, out_ref):
    total = keep_ref[...] + arrived_ref[...].astype(F32)
    out_ref[...] = jnp.concatenate([total, cot_ref[...].astype(F32)], axis=0).astype(BF16)


def quarters(total, out_refs):
    count = out_refs[0].shape[0]
    for k, ref in enumerate(out_refs):
        ref[...] = total[k * count : (k + 1) * count].astype(ref.dtype)


def combine_kernel(comb_ref, *refs):
    *part_refs, sibling_ref = refs[:-4]
    rows = by_chip(part_refs, sibling_ref)
    quarters(dot_tn(comb_ref[0], rows) + dot_tn(comb_ref[1], rows), refs[-4:])


def halve_kernel(*refs):
    low, high, arrived_low, arrived_high = [ref[...].astype(F32) for ref in refs[:4]]
    quarters(jnp.concatenate([low + arrived_low, high + arrived_high], axis=0), refs[4:])


def add_kernel(own_ref, arrived_ref, *refs):
    refs[-1][...] = (own_ref[...] + arrived_ref[...].astype(F32)).astype(BF16)


def finish_kernel(placed_ref, text_ref, own_ref, arrived_ref, *refs, blocks, turn):
    vision_refs, out_ref = refs[:blocks], refs[-1]
    count, width = out_ref.shape
    tokens = placed_ref.shape[0]
    first = (lax.axis_index("expert") ^ turn) * count
    pick = iota((count, tokens), 1) == iota((count, tokens), 0) + first
    pick = pick.astype(F32)
    placed = dot(pick, placed_ref[...])
    is_vision = jnp.sum(placed, axis=1, keepdims=True) > 0.5
    vision = jnp.concatenate([ref[:, :width] for ref in vision_refs], axis=0)
    inputs = jnp.where(is_vision, dot(placed, vision), dot(pick, text_ref[...]))
    out_ref[...] = (inputs + (own_ref[...].astype(F32) + arrived_ref[...].astype(F32))).astype(BF16)


def lay_kernel(*refs):
    *part_refs, out_ref = refs
    count = part_refs[0].shape[0]
    for k, ref in enumerate(part_refs):
        first = pl.multiple_of((lax.axis_index("expert") ^ k) * count, count)
        out_ref[pl.ds(first, count), :] = ref[...]


def norm_grad_kernel(
    joined_ref, other_ref, rows_ref, gain_ref, total_ref, out_ref, *, features
):
    width = gain_ref.shape[1]
    count = out_ref.shape[0] // 2
    far = rows_ref.shape[0] // 2
    joined, other = joined_ref[...].astype(F32), other_ref[...].astype(F32)
    turned = jnp.concatenate([other[count : 2 * count], other[:count]], axis=0)
    hidden = joined[: 2 * count] + turned
    cotangent = jnp.concatenate([joined[2 * count :], other[2 * count :]], axis=0)
    rows = rows_ref[:, :width].astype(F32)
    inputs = jnp.concatenate([rows[:count], rows[far : far + count]], axis=0)
    scale = lax.rsqrt(jnp.mean(inputs * inputs, axis=1, keepdims=True) + EPS)
    pulled = hidden * gain_ref[...]
    cross = jnp.mean(pulled * inputs, axis=1, keepdims=True)
    grad = cotangent + scale * pulled - inputs * (scale * scale * scale) * cross
    grad = grad.astype(BF16)
    out_ref[:, :width] = grad
    grad = grad.astype(F32)
    grad_mean = jnp.sum(grad * total_ref[...], axis=1, keepdims=True) / features
    cross_mean = jnp.sum(grad * inputs, axis=1, keepdims=True) / features
    out_ref[:, width:] = put_scalars([grad_mean, cross_mean], 2 * count).astype(BF16)


def merge_grad_kernel(*refs, size, bases):
    gain_ref, merged_ref, scalar_ref, weight_ref, *part_refs, out_ref = refs
    rows, features = merged_ref.shape
    width = weight_ref.shape[1]
    depth, patches = out_ref.shape
    row_share = part_refs[0].shape[0] // 2
    blocks = {}
    for base, ref in zip(bases, part_refs):
        part = ref[...].astype(F32)
        blocks[base] = part[:row_share]
        blocks[base ^ len(bases)] = part[row_share:]
    parts = jnp.concatenate([blocks[k] for k in sorted(blocks)], axis=0).astype(BF16)
    normed_grad = dot_nt(parts[:, :width], weight_ref[...]) * flat_gain(gain_ref)
    means = parts[:, width:].astype(F32)
    scalars = scalar_ref[...].astype(F32)
    inv_std = get_scalar(scalars, 1)
    normed = (merged_ref[...].astype(F32) - get_scalar(scalars, 0)) * inv_std
    grad = inv_std * (normed_grad - get_scalar(means, 0) - normed * get_scalar(means, 1))
    high = grad.astype(BF16)
    low = (grad - high.astype(F32)).astype(BF16)
    line = iota((patches, rows), 1)
    line = ((line // row_share) ^ lax.axis_index("expert")) * row_share + line % row_share
    unfold = (iota((patches, rows), 0) // 4 == line).astype(F32)
    spot = iota((patches, features), 1) // size % 4 == iota((patches, features), 0) % 4
    row, col = iota((depth, features), 0), iota((depth, features), 1)
    place = (col // (4 * size) == row // size) & (col % size == row % size)
    place = place.astype(F32).astype(BF16)
    out = jnp.zeros((depth, patches), F32)
    for piece in (high, low):
        wide = jnp.where(spot, dot(unfold, piece), 0.0).astype(BF16)
        out = out + dot_nt(place, wide)
    out_ref[...] = out


def whole(memory_space=pltpu.VMEM):
    return pl.BlockSpec(memory_space=memory_space)


def run(kernel, outs, *args, far=(), scratch=(), cost=1.0, vmem=VMEM_BYTES, name=None):
    specs = [whole()] * len(args)
    for place in far:
        specs[place] = whole(pl.ANY)
    return pl.pallas_call(
        kernel,
        out_shape=outs,
        in_specs=specs,
        out_specs=jax.tree.map(lambda _: whole(), outs),
        scratch_shapes=scratch,
        compiler_params=pltpu.CompilerParams(vmem_limit_bytes=vmem),
        cost_estimate=microseconds(cost),
        name=name,
    )(*args)


def to_sibling(parts, deps, name):
    rows, width = parts[0].shape
    half = run(
        functools.partial(other_half_kernel, count=len(parts)),
        shape((len(parts) * rows // 2, width)), *parts, *deps,
        far=range(len(parts), len(parts) + len(deps)), cost=0.01, name=name,
    )
    return swap(half, "blk", 1)


def microseconds(time):
    return pl.CostEstimate(flops=0, transcendentals=0, bytes_accessed=int(time * 3e6))


def after(values, deps):
    count = len(values)
    return pl.pallas_call(
        lambda *refs: None,
        out_shape=[shape(value.shape, value.dtype) for value in values],
        in_specs=[whole(pl.ANY)] * (count + len(deps)),
        out_specs=[whole(pl.ANY)] * count,
        input_output_aliases={i: i for i in range(count)},
        compiler_params=pltpu.CompilerParams(vmem_limit_bytes=VMEM_BYTES),
        cost_estimate=microseconds(0.1),
        name="after",
    )(*values, *deps)


def shape(dims, dtype=BF16):
    return jax.ShapeDtypeStruct(dims, dtype)


def swap(value, axis, step):
    count = lax.axis_size(axis)
    return lax.ppermute(value, axis, [(i, i ^ step) for i in range(count)])


def trade(parts, axis):
    return [parts[0]] + [swap(parts[k], axis, k) for k in range(1, len(parts))]


def spread_out(value, axis):
    return trade([value] * lax.axis_size(axis), axis)


def gather_blocks(value, deps=None):
    own = [value] + [swap(value, "blk", k) for k in range(2, lax.axis_size("blk"), 2)]
    if deps is not None:
        own = own[:1] + list(after(own[1:], deps))
    sibling = [swap(part, "blk", 1) for part in own]
    return [part for pair in zip(own, sibling) for part in pair]


def to_chips(parts):
    return [parts[0]] + [swap(parts[k], "blk", 2 * k) for k in range(1, len(parts))]


def body(
    queries, keys, values, image_ids, placement, merge_gain, merge_weight, text, norm_gain,
    w_gate, w_up, w_down, routes, route_gates, cotangent,
):
    blocks = lax.axis_size("blk")
    share = lax.axis_size("expert")
    heads, size, patches = queries.shape
    depth = heads * size
    rows = image_ids.shape[0]
    row_share = rows // share
    tokens, width = text.shape
    part = tokens // share
    all_rows = blocks * rows
    features = heads * 4 * size
    hidden = w_gate.shape[1]
    slot_count = blocks * SLOTS
    groups = share // 2
    routes_t, gates_t, gain_row = routes.T, route_gates.T, norm_gain[None]

    small = [
        keys.reshape(depth, patches), values.reshape(depth, patches),
        image_ids[None], placement.reshape(1, rows), routes_t,
    ]
    local = run(
        pack_kernel, shape((2 * depth + 16, patches)), *small, far=range(5),
        scratch=[pltpu.VMEM(array.shape, array.dtype) for array in small]
        + [pltpu.SemaphoreType.DMA((5,))],
        vmem=PACK_BYTES, name="pack",
    )
    comb, pick, factor = run(
        functools.partial(route_kernel, groups=groups, share=share),
        [
            shape((2, slot_count, tokens)), shape((2, blocks * SEND, tokens)),
            shape((blocks * SEND, 128), F32),
        ],
        routes_t, gates_t, cost=3.0, name="route",
    )
    send = run(
        dispatch_kernel, [shape((2 * SEND, width))] * (blocks // 2),
        pick, factor, text, gain_row, cotangent, cost=2.0, name="dispatch",
    )
    near = gather_blocks(local, send)
    early = to_chips(after(send, near[2::2]))

    weight_flat = merge_weight.reshape(features, width)
    message_width = width + width // row_share + 128
    merged, meta, left, local_scalars = run(
        functools.partial(attend_kernel, blocks=blocks, row_share=row_share),
        [
            shape((rows, features)), shape((blocks * 16, patches)), shape((rows + 16, features)),
            shape((rows, 128), F32),
        ],
        queries, merge_gain, *small, *near[1:], cost=3.0, name="attend",
    )
    message = run(
        project_kernel, [shape((row_share, message_width))] * share,
        left, local_scalars, weight_flat, early[1], far=(3,), cost=2.0, name="project",
    )
    slots, placed, back_cots = run(
        functools.partial(
            plan_kernel, blocks=blocks, groups=groups, merged_rows=rows, row_share=row_share
        ),
        [
            shape((slot_count, all_rows)), shape((tokens, all_rows)),
            shape((blocks * row_share, width)),
        ],
        meta, cotangent, cost=1.5, name="plan",
    )
    message = trade(message, "expert")
    early = early[:1] + list(after(early[1:], message[1:]))
    own, gain_total = run(
        functools.partial(merge_kernel, width=width, features=features),
        [
            shape((row_share, width + 128)), shape((1, width), F32),
        ],
        early[1], *message, far=(0,), cost=0.2, name="merge",
    )
    owns = spread_out(own, "expert")
    block_rows, row_scalars = run(
        stack_kernel, [shape((rows, width)), shape((rows, 128))], *owns, cost=0.2, name="stack",
    )
    text_rows, act_grad = run(
        early_kernel, [shape((slot_count, width)), shape((slot_count, hidden), F32)],
        w_down, *early, to_sibling(early, owns[1:], "early_half"), cost=3.0, name="early",
    )

    vision = gather_blocks(block_rows, [text_rows, slots])
    gate_pre, up_proj, *down = run(
        functools.partial(forward_kernel, blocks=blocks),
        [
            shape((slot_count, hidden), F32), shape((slot_count, hidden), F32),
        ] + [shape((2 * SLOTS, width))] * (blocks // 2),
        slots, gain_row, w_gate, w_up, w_down, text_rows, *vision,
        scratch=[pltpu.VMEM((slot_count, width), BF16), pltpu.VMEM((slot_count, width), F32)],
        cost=4.0, name="forward",
    )
    returned = to_chips(down)
    block = rows + row_share
    even, odd = run(
        functools.partial(backward_kernel, blocks=blocks),
        [shape((blocks // 2 * block, width))] * 2,
        slots, act_grad, gate_pre, up_proj, back_cots, w_gate, w_up,
        scratch=[pltpu.VMEM((slot_count, width), F32)],
        cost=4.0, name="backward",
    )
    grads = run(
        pair_sum_kernel, [shape((block, width))] * (blocks // 2), even, swap(odd, "blk", 1),
        cost=0.2, name="pair_sum",
    )
    grads = to_chips(grads)
    count = tokens // 4
    pieces = [shape((count, width), F32)] * 2 + [shape((count, width))] * 2
    low, high, sent_low, sent_high = run(
        combine_kernel, pieces, comb, *returned,
        to_sibling(returned, grads[:1], "returned_half"), cost=0.01, name="combine",
    )
    step = 1
    arrived_high = swap(sent_high, "expert", step)
    first_arrived = arrived_high
    arrived_low = swap(sent_low, "expert", step)
    while count > part:
        count //= 2
        step *= 2
        pieces = [shape((count, width), F32)] * 2 + [shape((count, width))] * 2
        low, high, sent_low, sent_high = run(
            halve_kernel, pieces, low, high, arrived_low, arrived_high, cost=0.3, name="halve"
        )
        arrived_high = swap(sent_high, "expert", step)
        arrived_low = swap(sent_low, "expert", step)
    step *= 2

    def add(own_part, arrived, gate, name):
        return run(
            add_kernel, shape((part, width)), own_part, arrived, *gate,
            far=range(2, 2 + len(gate)), cost=0.3, name=name,
        )

    sum_high = add(high, arrived_high, [], "add_high")
    other_low = swap(sum_high, "expert", step)
    cot_rows, keep, sent = run(
        functools.partial(chip_sum_kernel, count=blocks // 2, order=halving_order(share)),
        [
            shape((row_share, width)), shape((rows // 2, width), F32), shape((rows // 2, width)),
        ],
        *grads, first_arrived, far=(blocks // 2,), cost=0.2, name="chip_sum",
    )
    bit, kept_rows = 1, rows // 2
    while kept_rows > 2 * row_share:
        kept_rows //= 2
        keep, sent = run(
            grad_halve_kernel, [shape((kept_rows, width), F32), shape((kept_rows, width))],
            keep, swap(sent, "expert", bit), cost=0.2, name="grad_halve",
        )
        bit *= 2
    joined = run(
        grad_join_kernel, shape((3 * row_share, width)),
        keep, swap(sent, "expert", bit), cot_rows, cost=0.2, name="grad_join",
    )
    other = swap(joined, "expert", share // 2)
    sums = [add(low, arrived_low, [other_low], "add_low"), sum_high]
    others = [other_low, swap(sums[0], "expert", step)]
    vision_grad = run(
        functools.partial(norm_grad_kernel, features=share * features),
        shape((2 * row_share, width + 128)),
        joined, other, block_rows, gain_row, gain_total, cost=0.3, name="norm_grad",
    )
    vision_grads, bit = {0: vision_grad}, share // 4
    while bit:
        vision_grads.update({k + bit: swap(vision_grads[k], "expert", bit) for k in list(vision_grads)})
        bit //= 2
    bases = sorted(vision_grads)
    vision_grads = [vision_grads[k] for k in bases]
    attn_grad = run(
        functools.partial(merge_grad_kernel, size=size, bases=tuple(bases)),
        shape((depth, patches), F32),
        merge_gain, merged, row_scalars, weight_flat, *vision_grads, cost=4.0, name="merge_grad",
    )

    laid = {}
    for turn, value, other, gate in zip((0, step), sums, others, ([], vision_grads[1:])):
        laid[turn] = run(
            functools.partial(finish_kernel, blocks=blocks, turn=turn), shape((part, width)),
            placed, text, value, other, *vision, *gate,
            far=range(4 + blocks, 4 + blocks + len(gate)), cost=1.0, name="finish",
        )
    while step > 1:
        step //= 2
        laid.update({k + step: swap(laid[k], "expert", step) for k in list(laid)})
    llm_out = run(
        lay_kernel, shape((tokens, width)), *[laid[k] for k in sorted(laid)], cost=1.0, name="lay"
    )
    return llm_out, attn_grad.reshape(heads, size, patches)


def solution(mesh):
    return jax.shard_map(
        body,
        mesh=mesh,
        in_specs=(
            P("expert", None, "blk"),
            P("expert", None, "blk"),
            P("expert", None, "blk"),
            P("blk"),
            P("blk", None),
            P("expert", None),
            P("expert", None, None),
            P("blk", None),
            P(),
            P("blk", "expert", None),
            P("blk", "expert", None),
            P("blk", "expert", None),
            P("blk", None),
            P("blk", None),
            P("blk", None),
        ),
        out_specs=(P("blk", None), P("expert", None, "blk")),
        check_vma=False,
    )
```
